128 devices in a mesh: heads: 4 (over x), ctx: 32 (over z, y, core).
Axes of the slice: x: 4, y: 4, z: 4, core: 2. Of those that a mesh axis runs over, the one named last changes fastest.
Arguments:
- queries: bfloat16 [16384, 1536], P('ctx', 'heads'), may hold values from -8 to 8
- key_rows: bfloat16 [16384, 1536], P('ctx', 'heads'), may hold values from -8 to 8
- value_rows: bfloat16 [16384, 1536], P('ctx', 'heads'), may hold values from -6 to 6
- out_weight: bfloat16 [1536, 3072], P('heads'), may hold values from -0.15625 to 0.15625
- tile_masks: int32 [2, 128, 128], replicated, may hold values from 0 to 1, as said below
- head_pattern: int32 [12], P('heads'), may hold values from 0 to 1
Outputs:
- mixed: bfloat16 [16384, 3072], P('ctx', 'heads')
The draws below stay inside these ranges and needn't reach their ends.
Inputs may be any that keep to these rules, and one draw needn't show every extreme that they name: tile_masks[k, i, i] = 1 for every pattern k and tile i.
All inputs are finite; a program needn't handle non-finite values.
Results may differ from the reference program's by a relative error of at most 0.015.
Values may be sent and summed in bfloat16 or wider, within the bound.
A program may use at most 128 MiB of HBM per device.

```python
import math
import jax
import jax.numpy as jnp
from jax import lax

D = 3072
HEADS = 12
DH = 128
TILE = 128
SPATIAL = 512
FRAMES = 32
TOKENS = 16384
TILES = 128


def draw_queries(key, part):
    key = jax.random.fold_in(key, 3)
    first_key = jax.random.fold_in(key, 0)
    field = jnp.clip(2.0 * jax.random.normal(first_key, (TOKENS, HEADS * DH), jnp.float32), -8.0, 8.0)
    return field.astype(jnp.bfloat16)


def draw_key_rows(key, part):
    key = jax.random.fold_in(key, 5)
    first_key = jax.random.fold_in(key, 0)
    field = jnp.clip(2.0 * jax.random.normal(first_key, (TOKENS, HEADS * DH), jnp.float32), -8.0, 8.0)
    return field.astype(jnp.bfloat16)


def draw_tile_masks(key, part):
    key = jax.random.fold_in(key, 7)
    count = TOKENS // TILE
    rolls = jax.random.randint(key, (2, count, count), 0, 1000, dtype=jnp.int32)
    query_tile = jnp.arange(count, dtype=jnp.int32)[None, :, None]
    key_tile = jnp.arange(count, dtype=jnp.int32)[None, None, :]
    pattern = jnp.arange(2, dtype=jnp.int32)[:, None, None]
    limit = 60 + 540 * query_tile // count
    band = jnp.where(pattern == 0, jnp.abs(query_tile - key_tile) <= 2, (query_tile - key_tile) % 8 == 0)
    keep = (rolls < limit) | band
    return keep.astype(jnp.int32)


def with_ends(drawn, own_key, low, top_value):
    extent = drawn.shape
    index_at = [jax.random.randint(jax.random.fold_in(own_key, axis), (), 0, extent[axis]) for axis in range(len(extent))]
    drawn = drawn.at[tuple(index_at)].set(low)
    longest = extent.index(max(extent))
    index_at[longest] = (index_at[longest] + 1) % extent[longest]
    return drawn.at[tuple(index_at)].set(top_value)


def level_of(own_key, shape, shards, low, largest):
    factor_of = 1.0
    for dim, shards_of in shards:
        steps = jax.random.uniform(jax.random.fold_in(jax.random.fold_in(own_key, 6), dim), (shards_of,), jnp.float32, low / len(shards), largest / len(shards))
        factor_of = factor_of * jnp.repeat(jnp.exp(steps), shape[dim] // shards_of).reshape((-1,) + (1,) * (len(shape) - 1 - dim))
    return factor_of


def noise(own_key, extent, deviation, most, shards=(), held_as=jnp.bfloat16):
    values = jax.random.normal(own_key, extent, jnp.float32) * deviation
    if len(shards) > 0:
        values = level_of(own_key, extent, shards, -0.22, 0.18) * values
    return jnp.clip(values, min=-most, max=most).astype(held_as)


def setup_inputs(seed: int = 0) -> dict:
    key_list = jax.random.split(jax.random.key(seed), 7)
    queries = draw_queries(jax.random.fold_in(key_list[6], 71), 0)
    key_rows = draw_key_rows(jax.random.fold_in(key_list[6], 71), 0)
    value_rows = noise(key_list[2], (TOKENS, HEADS * DH), 1.0, 6.0, ((0, 32), (1, 4)))
    out_weight = noise(key_list[3], (HEADS * DH, D), (HEADS * DH) ** -0.5, 0.15625, ((0, 4),))
    tile_masks = draw_tile_masks(jax.random.fold_in(key_list[6], 71), 0)
    head_pattern = with_ends(jax.random.randint(key_list[5], (HEADS,), 0, 2), jax.random.fold_in(key_list[5], 1), 0, 1).astype(jnp.int32)
    return {"queries": queries, "key_rows": key_rows, "value_rows": value_rows, "out_weight": out_weight, "tile_masks": tile_masks, "head_pattern": head_pattern}


def to_spatial(field):
    columns = field.shape[1]
    return field.reshape(FRAMES, SPATIAL, columns).transpose(1, 0, 2).reshape(TOKENS, columns)

def to_frames(field):
    columns = field.shape[1]
    return field.reshape(SPATIAL, FRAMES, columns).transpose(1, 0, 2).reshape(TOKENS, columns)

def reference(queries, key_rows, value_rows, out_weight, tile_masks, head_pattern):
    query_s = to_spatial(queries).reshape(TOKENS, HEADS, DH)
    key_all = to_spatial(key_rows).reshape(TOKENS, HEADS, DH).astype(jnp.float32)
    value_all = to_spatial(value_rows).reshape(TOKENS, HEADS, DH).astype(jnp.float32)
    head_masks = tile_masks[head_pattern]

    def one_block(block_index):
        first_row = block_index * TILE
        query_block = lax.dynamic_slice_in_dim(query_s, first_row, TILE, 0).astype(jnp.float32)
        scores = jnp.einsum('qhd,khd->hqk', query_block, key_all) / math.sqrt(DH)
        tile_row = head_masks[:, block_index, :]
        allowed = jnp.repeat(tile_row, TILE, axis=1) == 1
        allowed = allowed[:, None, :]
        row_peak = lax.optimization_barrier(jnp.max(jnp.where(allowed, scores, jnp.float32(-1e+30)), axis=-1, keepdims=True))
        weights = jnp.where(allowed, jnp.exp(scores - row_peak), jnp.float32(0.0))
        totals = lax.optimization_barrier(jnp.sum(weights, axis=-1))
        weights_b = weights.astype(jnp.bfloat16)
        block_out = jnp.einsum('hqk,khd->hqd', weights_b.astype(jnp.float32), value_all)
        block_out = block_out / totals[:, :, None]
        return block_out.transpose(1, 0, 2).reshape(TILE, HEADS * DH).astype(jnp.bfloat16)
    attn_s = lax.map(one_block, jnp.arange(TILES, dtype=jnp.int32)).reshape(TOKENS, HEADS * DH)
    attn = to_frames(attn_s)
    return jnp.dot(attn, out_weight, preferred_element_type=jnp.float32).astype(jnp.bfloat16)
```

```python
import math

import jax
import jax.numpy as jnp
from jax import lax
from jax.experimental import pallas as pl
from jax.experimental.pallas import tpu as pltpu
from jax.sharding import PartitionSpec as P

MESH = pl.DeviceIdType.MESH
DH = 128
TILE = 128
SPOTS = 4
FRAMES = 32
TILES = 128
PLANES = 4
SIDE = 4
HEADS_HERE = 3
WORKERS = 2 * SIDE
SLOTS = TILES // WORKERS
PARTS = 4
PART = 2 * TILES // PARTS
PIECE = TILE // WORKERS
GROUP = 16
STEPS = TILES // GROUP
LOW = -1e30
SCALE2 = math.log2(math.e) / math.sqrt(DH)
BF16 = jnp.bfloat16
F32 = jnp.float32


def where_is(device):
    return lax.div(device, WORKERS), lax.rem(lax.div(device, 2), SIDE), lax.rem(device, 2)


def device_at(row, column, core):
    return (lax.rem(row, SIDE) * SIDE + lax.rem(column, SIDE)) * 2 + core


def spread_kernel(
    q_ref, kv_ref, w_ref, q_all, kv_all, w_all,
    q_send, q_recv, z_send, z_recv, y_send, y_recv, far_send, far_recv,
    core_send, core_recv, w_send, w_recv, w_core_send, w_core_recv, own_sem,
):
    plane = lax.axis_index("heads")
    me = lax.axis_index("ctx")
    row, column, core = where_is(me)
    working = row < HEADS_HERE
    own_row = jnp.minimum(row, HEADS_HERE - 1)
    depth = w_ref.shape[0]
    width = w_all.shape[1]
    sides = (1, SIDE - 1)

    barrier = pltpu.get_barrier_semaphore()

    def greet(step, carry):
        pl.semaphore_signal(
            barrier, inc=1, device_id=(plane, lax.rem(me + step, FRAMES)), device_id_type=MESH
        )
        return carry

    lax.fori_loop(1, FRAMES, greet, 0)
    for hop in range(1, PLANES):
        pl.semaphore_signal(
            barrier, inc=1, device_id=(lax.rem(plane + hop, PLANES), me), device_id_type=MESH
        )
    pl.semaphore_wait(barrier, FRAMES - 1 + PLANES - 1)

    def span(part):
        return pl.ds(part * PART, PART)

    own_copy = pltpu.make_async_copy(
        kv_ref.at[own_row], kv_all.at[column * 2 + core, :, 0], own_sem
    )

    def z_copy(part, hop):
        there = lax.rem(row + hop, SIDE)
        return pltpu.make_async_remote_copy(
            src_ref=kv_ref.at[there, span(part)],
            dst_ref=kv_all.at[column * 2 + core, span(part), hop],
            send_sem=z_send.at[part, hop],
            recv_sem=z_recv.at[part, hop],
            device_id=(plane, device_at(there, column, core)),
            device_id_type=MESH,
        )

    def piece(number, away):
        source = kv_all.at[lax.rem(column + away, SIDE) * 2 + core]
        if number == 0:
            return source.at[:, 0]
        return source.at[span(number - 1), pl.ds(1, SIDE - 1)]

    def y_copy(number, side):
        return pltpu.make_async_remote_copy(
            src_ref=kv_ref.at[own_row] if number == 0 else piece(number, 0),
            dst_ref=piece(number, 0),
            send_sem=y_send.at[number, side],
            recv_sem=y_recv.at[number, side],
            device_id=(plane, device_at(row, column + sides[side], core)),
            device_id_type=MESH,
        )

    def far_copy(number, side):
        source = kv_all.at[lax.rem(column + sides[1 - side], SIDE) * 2 + core]
        if number == 0:
            chunk = source.at[pl.ds(side * TILES, TILES), 0]
        else:
            chunk = source.at[
                pl.ds((number - 1) * PART + side * (PART // 2), PART // 2), pl.ds(1, SIDE - 1)
            ]
        return pltpu.make_async_remote_copy(
            src_ref=chunk,
            dst_ref=chunk,
            send_sem=far_send.at[number, side],
            recv_sem=far_recv.at[number, side],
            device_id=(plane, device_at(row, column + sides[side], core)),
            device_id_type=MESH,
        )

    def core_copy(number, away):
        return pltpu.make_async_remote_copy(
            src_ref=piece(number, away),
            dst_ref=piece(number, away),
            send_sem=core_send.at[number, away],
            recv_sem=core_recv,
            device_id=(plane, device_at(row, column, 1 - core)),
            device_id_type=MESH,
        )

    half = depth // 2

    def w_rows(source, part):
        return w_all.at[pl.ds(pl.multiple_of(source * depth + part * half, 16), half)]

    def w_copy(hop):
        there = lax.rem(plane + hop, PLANES)
        return pltpu.make_async_remote_copy(
            src_ref=w_ref.at[
                pl.ds(pl.multiple_of(core * half, 16), half),
                pl.ds(pl.multiple_of(there * width, 128), width),
            ],
            dst_ref=w_rows(plane, core),
            send_sem=w_send.at[hop],
            recv_sem=w_recv.at[hop],
            device_id=(there, me),
            device_id_type=MESH,
        )

    def w_core_copy(hop):
        rows = w_rows(lax.rem(plane + PLANES - hop, PLANES), core)
        return pltpu.make_async_remote_copy(
            src_ref=rows,
            dst_ref=rows,
            send_sem=w_core_send.at[hop],
            recv_sem=w_core_recv.at[hop],
            device_id=(plane, device_at(row, column, 1 - core)),
            device_id_type=MESH,
        )

    own_w = pltpu.make_async_copy(
        w_ref.at[:, pl.ds(pl.multiple_of(plane * width, 128), width)],
        w_all.at[pl.ds(pl.multiple_of(plane * depth, 128), depth)],
        w_recv.at[0],
    )

    def q_copy(step):
        there = lax.rem(me + step, FRAMES)
        row_there, column_there, core_there = where_is(there)
        return row_there < HEADS_HERE, pltpu.make_async_remote_copy(
            src_ref=q_ref.at[
                jnp.minimum(row_there, HEADS_HERE - 1), :, column_there * 2 + core_there
            ],
            dst_ref=q_all.at[:, me],
            send_sem=q_send.at[step],
            recv_sem=q_recv,
            device_id=(plane, there),
            device_id_type=MESH,
        )

    def to_rows(part, work):
        for hop in range(1, SIDE):

            @pl.when(lax.rem(row + hop, SIDE) < HEADS_HERE)
            def _():
                work(z_copy(part, hop))

    def send_q(step, carry):
        wanted, copy = q_copy(step)

        @pl.when(wanted)
        def _():
            copy.start()

        return carry

    def sent_q(step, carry):
        wanted, copy = q_copy(step)

        @pl.when(wanted)
        def _():
            copy.wait_send()

        return carry

    def send_small():
        for hop in range(1, PLANES):
            w_copy(hop).start()
        own_w.start()
        lax.fori_loop(1, FRAMES, send_q, 0)

    @pl.when(working)
    def _():
        own_copy.start()
        for side in range(2):
            y_copy(0, side).start()

    to_rows(0, lambda copy: copy.start())
    send_small()

    def next_rows(part):
        to_rows(part, lambda copy: copy.wait_send())
        if part + 1 < PARTS:
            to_rows(part + 1, lambda copy: copy.start())

    @pl.when(jnp.logical_not(working))
    def _():
        for part in range(PARTS):
            next_rows(part)

    @pl.when(working)
    def _():
        pltpu.make_async_copy(
            q_ref.at[own_row, :, column * 2 + core], q_all.at[:, me], q_recv
        ).start()
        own_copy.wait()
        core_copy(0, 0).start()

        def pass_on(number):
            for side in range(2):
                y_copy(number, side).wait_recv()
                far_copy(number, side).start()
            for side in range(2):
                core_copy(number, sides[1 - side]).start()

        for part in range(PARTS):
            next_rows(part)
            for hop in range(1, SIDE):
                landed = kv_all.at[column * 2 + core, span(part), hop]
                pltpu.make_async_copy(landed, landed, z_recv.at[part, hop]).wait()
            for side in range(2):
                y_copy(part + 1, side).start()
            core_copy(part + 1, 0).start()
            pass_on(part)
        pass_on(PARTS)
        for number in range(PARTS + 1):
            for side in range(2):
                far_copy(number, side).wait_recv()
            core_copy(number, 2).start()

    for hop in range(1, PLANES):
        w_copy(hop).wait_recv()
        w_core_copy(hop).start()

    @pl.when(working)
    def _():
        pltpu.make_async_copy(q_all, q_all, q_recv).wait()
        other = kv_all.at[pl.ds(0, SIDE)]
        pltpu.make_async_copy(other, other, core_recv).wait()
        for number in range(PARTS + 1):
            for side in range(2):
                y_copy(number, side).wait_send()
                far_copy(number, side).wait_send()
            for away in range(SIDE):
                core_copy(number, away).wait_send()

    own_w.wait()
    lax.fori_loop(1, FRAMES, sent_q, 0)
    for hop in range(1, PLANES):
        w_copy(hop).wait_send()
        w_core_copy(hop).wait()


def spread(q_parts, kv_parts, out_weight):
    depth, columns = out_weight.shape
    return pl.pallas_call(
        spread_kernel,
        out_shape=(
            jax.ShapeDtypeStruct((SLOTS, FRAMES, SPOTS, DH), BF16),
            jax.ShapeDtypeStruct((WORKERS, 2 * TILES, SIDE, SPOTS, DH), BF16),
            jax.ShapeDtypeStruct((depth * PLANES, columns // PLANES), BF16),
        ),
        in_specs=[pl.BlockSpec(memory_space=pl.ANY)] * 3,
        out_specs=(pl.BlockSpec(memory_space=pl.ANY),) * 3,
        scratch_shapes=[
            pltpu.SemaphoreType.DMA((FRAMES,)),
            pltpu.SemaphoreType.DMA,
            pltpu.SemaphoreType.DMA((PARTS, SIDE)),
            pltpu.SemaphoreType.DMA((PARTS, SIDE)),
            pltpu.SemaphoreType.DMA((PARTS + 1, 2)),
            pltpu.SemaphoreType.DMA((PARTS + 1, 2)),
            pltpu.SemaphoreType.DMA((PARTS + 1, 2)),
            pltpu.SemaphoreType.DMA((PARTS + 1, 2)),
            pltpu.SemaphoreType.DMA((PARTS + 1, SIDE)),
            pltpu.SemaphoreType.DMA,
            pltpu.SemaphoreType.DMA((PLANES,)),
            pltpu.SemaphoreType.DMA((PLANES,)),
            pltpu.SemaphoreType.DMA((PLANES,)),
            pltpu.SemaphoreType.DMA((PLANES,)),
            pltpu.SemaphoreType.DMA,
        ],
        compiler_params=pltpu.CompilerParams(
            collective_id=0, has_side_effects=True, vmem_limit_bytes=4 * 1024 * 1024
        ),
    )(q_parts, kv_parts, out_weight)


def attend_kernel(
    list_ref, q_ref, kv_ref, o_ref, even_ref, odd_ref, even_peak, odd_peak,
    base_ref, sum_ref,
):
    kept = ((even_ref, even_peak), (odd_ref, odd_peak))

    def count_of(slot):
        return list_ref[SLOTS, slot]

    def steps_of(slot):
        return lax.div(count_of(slot) + GROUP - 1, GROUP)

    def tile_of(slot, number, first):
        start = pl.multiple_of((first + list_ref[slot, number]) * PIECE, PIECE)
        return jnp.concatenate(
            [kv_ref[worker, pl.ds(start, PIECE), :] for worker in range(WORKERS)], axis=0
        )

    def score(slot, side, step):
        score_ref, peak_ref = kept[side]
        query = q_ref[pl.ds(pl.multiple_of(slot * TILE, TILE), TILE), :]
        keys = [tile_of(slot, step * GROUP + u, 0) for u in range(GROUP)]
        scores = lax.dot_general(
            query,
            jnp.concatenate(keys, axis=0),
            (((1,), (1,)), ((), ())),
            preferred_element_type=F32,
        )
        peak = peak_ref[...]
        for u in range(GROUP):
            part = scores[:, u * TILE : (u + 1) * TILE]
            score_ref[step, :, u * TILE : (u + 1) * TILE] = part
            peak = jnp.maximum(peak, part)
        peak_ref[...] = peak

    def gather(slot, side, step):
        score_ref = kept[side][0]
        base = base_ref[...]
        count = count_of(slot)
        weights, values = [], []
        for u in range(GROUP):
            part = score_ref[step, :, u * TILE : (u + 1) * TILE]
            weights.append(jnp.exp2(part * SCALE2 - base).astype(BF16))
            listed = step * GROUP + u < count
            value = jnp.where(listed, tile_of(slot, step * GROUP + u, TILES), 0).astype(BF16)
            ones = jnp.broadcast_to(jnp.where(listed, 1.0, 0.0).astype(BF16), (TILE, DH))
            values.append(jnp.concatenate([value, ones], axis=1))
        sum_ref[...] += jnp.dot(
            jnp.concatenate(weights, axis=1),
            jnp.concatenate(values, axis=0),
            preferred_element_type=F32,
        )

    def loop(first, last, work):
        def one(step, carry):
            work(step)
            return carry

        lax.fori_loop(first, last, one, 0)

    def one_slot(slot, side, ahead):
        here = steps_of(slot)
        both = jnp.minimum(here, ahead)
        base = jnp.max(kept[side][1][...], axis=1, keepdims=True) * SCALE2
        base_ref[...] = jnp.broadcast_to(base, (TILE, TILE))
        sum_ref[...] = jnp.zeros((TILE, 2 * DH), F32)
        kept[1 - side][1][...] = jnp.full((TILE, TILE), LOW, F32)

        def pair(step):
            gather(slot, side, step)
            score(slot + 1, 1 - side, step)

        loop(0, both, pair)
        loop(both, ahead, lambda step: score(slot + 1, 1 - side, step))
        loop(both, here, lambda step: gather(slot, side, step))
        o_ref[pl.ds(pl.multiple_of(slot * TILE, TILE), TILE), :] = (
            sum_ref[:, :DH] / sum_ref[:, DH:]
        ).astype(BF16)

    even_peak[...] = jnp.full((TILE, TILE), LOW, F32)
    loop(0, steps_of(0), lambda step: score(0, 0, step))

    def two_slots(turn, carry):
        slot = turn * 2
        one_slot(slot, 0, steps_of(slot + 1))
        follows = jnp.minimum(slot + 2, SLOTS - 1)
        one_slot(slot + 1, 1, jnp.where(slot + 2 < SLOTS, steps_of(follows), 0))
        return carry

    lax.fori_loop(0, SLOTS // 2, two_slots, 0)
    if SLOTS % 2:
        one_slot(SLOTS - 1, 0, 0)


def attend(lists, query, kv):
    return pl.pallas_call(
        attend_kernel,
        out_shape=jax.ShapeDtypeStruct(query.shape, BF16),
        in_specs=[
            pl.BlockSpec(memory_space=pltpu.SMEM),
            pl.BlockSpec(memory_space=pltpu.VMEM),
            pl.BlockSpec(memory_space=pltpu.VMEM),
        ],
        out_specs=pl.BlockSpec(memory_space=pltpu.VMEM),
        scratch_shapes=[
            pltpu.VMEM((STEPS, TILE, GROUP * TILE), F32),
            pltpu.VMEM((STEPS, TILE, GROUP * TILE), F32),
            pltpu.VMEM((TILE, TILE), F32),
            pltpu.VMEM((TILE, TILE), F32),
            pltpu.VMEM((TILE, TILE), F32),
            pltpu.VMEM((TILE, 2 * DH), F32),
        ],
        compiler_params=pltpu.CompilerParams(vmem_limit_bytes=40 * 1024 * 1024),
    )(lists, query, kv)


def collect_kernel(o_ref, attn, send, recv, x_send, x_recv):
    plane = lax.axis_index("heads")
    me = lax.axis_index("ctx")
    row, column, core = where_is(me)
    barrier = pltpu.get_barrier_semaphore()

    def greet(step, carry):
        pl.semaphore_signal(
            barrier, inc=1, device_id=(plane, lax.rem(me + step, FRAMES)), device_id_type=MESH
        )
        return carry

    lax.fori_loop(1, FRAMES, greet, 0)
    sides = (lax.rem(plane + 1, PLANES), lax.rem(plane + PLANES - 1, PLANES))
    for there in sides:
        pl.semaphore_signal(barrier, inc=1, device_id=(there, me), device_id_type=MESH)
    pl.semaphore_wait(barrier, FRAMES - 1 + 2)

    mine = jnp.minimum(row, HEADS_HERE - 1)
    goal = attn.at[plane * HEADS_HERE + mine, :, column * 2 + core]

    def back(step):
        there = lax.rem(me + step, FRAMES)
        return pltpu.make_async_remote_copy(
            src_ref=o_ref.at[:, there],
            dst_ref=goal,
            send_sem=send.at[step],
            recv_sem=recv.at[mine],
            device_id=(plane, there),
            device_id_type=MESH,
        )

    def start(step, carry):
        back(step).start()
        return carry

    def end(step, carry):
        back(step).wait_send()
        return carry

    working = row < HEADS_HERE

    @pl.when(working)
    def _():
        lax.fori_loop(1, FRAMES, start, 0)
        pltpu.make_async_copy(o_ref.at[:, me], goal, recv.at[mine]).start()

    cut = SLOTS // 2

    def near(head, side):
        part = attn.at[plane * HEADS_HERE + head]
        return pltpu.make_async_remote_copy(
            src_ref=part,
            dst_ref=part,
            send_sem=x_send.at[head, side],
            recv_sem=x_recv.at[head, side],
            device_id=(sides[side], me),
            device_id_type=MESH,
        )

    def far(head, side):
        part = attn.at[sides[1 - side] * HEADS_HERE + head]
        part = part.at[pl.ds(0, cut)] if side == 0 else part.at[pl.ds(cut, SLOTS - cut)]
        return pltpu.make_async_remote_copy(
            src_ref=part,
            dst_ref=part,
            send_sem=x_send.at[head, 2 + side],
            recv_sem=x_recv.at[head, 2 + side],
            device_id=(sides[side], me),
            device_id_type=MESH,
        )

    for head in range(HEADS_HERE):
        part = attn.at[plane * HEADS_HERE + head]
        pltpu.make_async_copy(part, part, recv.at[head]).wait()
        for side in range(2):
            near(head, side).start()
    for head in range(HEADS_HERE):
        for side in range(2):
            near(head, side).wait_recv()
            far(head, side).start()

    @pl.when(working)
    def _():
        lax.fori_loop(1, FRAMES, end, 0)

    for head in range(HEADS_HERE):
        for side in range(2):
            near(head, side).wait_send()
            far(head, side).wait()


def collect(attended):
    return pl.pallas_call(
        collect_kernel,
        out_shape=jax.ShapeDtypeStruct(
            (PLANES * HEADS_HERE, SLOTS, WORKERS, SPOTS, DH), BF16
        ),
        in_specs=[pl.BlockSpec(memory_space=pl.ANY)],
        out_specs=pl.BlockSpec(memory_space=pl.ANY),
        scratch_shapes=[
            pltpu.SemaphoreType.DMA((FRAMES,)),
            pltpu.SemaphoreType.DMA((HEADS_HERE,)),
            pltpu.SemaphoreType.DMA((HEADS_HERE, 4)),
            pltpu.SemaphoreType.DMA((HEADS_HERE, 4)),
        ],
        compiler_params=pltpu.CompilerParams(
            collective_id=1, has_side_effects=True, vmem_limit_bytes=4 * 1024 * 1024
        ),
    )(attended)


def project_kernel(attn_ref, w_ref, out_ref):
    rows = out_ref.shape[0]
    heads = attn_ref.shape[0]
    wide = jnp.concatenate([attn_ref[h, :rows, :] for h in range(heads)], axis=1)
    out_ref[...] = jnp.dot(wide, w_ref[...], preferred_element_type=F32).astype(BF16)


def project(attn, weight, rows):
    columns = weight.shape[1]
    block = 256
    heads = attn.shape[0]
    return pl.pallas_call(
        project_kernel,
        out_shape=jax.ShapeDtypeStruct((rows, columns), BF16),
        grid=(columns // block,),
        in_specs=[
            pl.BlockSpec((heads, attn.shape[1], DH), lambda i: (0, 0, 0)),
            pl.BlockSpec((weight.shape[0], block), lambda i: (0, i)),
        ],
        out_specs=pl.BlockSpec((rows, block), lambda i: (0, i)),
        compiler_params=pltpu.CompilerParams(vmem_limit_bytes=24 * 1024 * 1024),
    )(attn, weight)


def arrange_kernel(pattern_ref, mask_ref, q_ref, k_ref, v_ref, q_out, kv_out, list_ref):
    me = lax.axis_index("ctx")
    row, column, core = where_is(me)
    rows = q_ref.shape[0]
    for head in range(HEADS_HERE):
        columns = slice(head * DH, (head + 1) * DH)
        q_out[head] = q_ref[:, columns]
        kv_out[head, :rows, :] = k_ref[:, columns]
        kv_out[head, rows:, :] = v_ref[:, columns]

    pattern = pattern_ref[jnp.minimum(row, HEADS_HERE - 1)]
    masks = []
    tiles = [slot * WORKERS + column * 2 + core for slot in range(SLOTS)]
    for tile in tiles:
        masks.append(jnp.where(row < HEADS_HERE, mask_ref[pattern, pl.ds(tile, 1), :], 0))
    seen = jnp.concatenate(masks, axis=0) == 1
    seen = jnp.where(seen, 1.0, 0.0).astype(F32)
    down = lax.broadcasted_iota(jnp.int32, (TILES, TILES), 0)
    along = lax.broadcasted_iota(jnp.int32, (TILES, TILES), 1)
    both = (((1,), (1,)), ((), ()))
    upto = jnp.where(along <= down, 1.0, 0.0).astype(BF16)
    same = jnp.where(along == down, 1.0, 0.0).astype(BF16)
    rank = lax.dot_general(upto, seen.astype(BF16), both, preferred_element_type=F32)
    turned = lax.dot_general(same, seen.astype(BF16), both, preferred_element_type=F32)
    rank = rank.astype(jnp.int32)
    spot = jnp.where(turned > 0.5, rank - 1, -1)
    for slot in range(SLOTS):
        hit = spot[:, slot : slot + 1] == along
        listed = jnp.sum(jnp.where(hit, down, 0), axis=0, keepdims=True)
        spare = along[:1, :] >= rank[TILES - 1 :, slot : slot + 1]
        list_ref[slot : slot + 1, :] = jnp.where(spare, tiles[slot], listed)
    last = jnp.concatenate(
        [rank[TILES - 1 :, :], jnp.zeros((1, TILES - SLOTS), jnp.int32)], axis=1
    )
    list_ref[SLOTS : SLOTS + 1, :] = last


def arrange(head_pattern, tile_masks, queries, key_rows, value_rows):
    rows = queries.shape[0]
    return pl.pallas_call(
        arrange_kernel,
        out_shape=(
            jax.ShapeDtypeStruct((HEADS_HERE, rows, DH), BF16),
            jax.ShapeDtypeStruct((HEADS_HERE, 2 * rows, DH), BF16),
            jax.ShapeDtypeStruct((SLOTS + 1, TILES), jnp.int32),
        ),
        in_specs=[pl.BlockSpec(memory_space=pltpu.SMEM)]
        + [pl.BlockSpec(memory_space=pltpu.VMEM)] * 4,
        out_specs=(pl.BlockSpec(memory_space=pltpu.VMEM),) * 3,
        compiler_params=pltpu.CompilerParams(vmem_limit_bytes=16 * 1024 * 1024),
    )(head_pattern, tile_masks, queries, key_rows, value_rows)


def body(queries, key_rows, value_rows, out_weight, tile_masks, head_pattern):
    rows = queries.shape[0]
    q_parts, kv_parts, lists = arrange(head_pattern, tile_masks, queries, key_rows, value_rows)
    q_all, kv_all, w_all = spread(
        q_parts.reshape(HEADS_HERE, SLOTS, WORKERS, SPOTS, DH),
        kv_parts.reshape(HEADS_HERE, 2 * TILES, SPOTS, DH),
        out_weight,
    )
    attended = attend(
        lists, q_all.reshape(SLOTS * TILE, DH), kv_all.reshape(WORKERS, 2 * TILES * PIECE, DH)
    )
    attn = collect(attended.reshape(SLOTS, FRAMES, SPOTS, DH))
    attn = attn.reshape(PLANES * HEADS_HERE, rows, DH)
    return project(attn, w_all, rows)


def solution(mesh):
    placed = (
        P("ctx", "heads"),
        P("ctx", "heads"),
        P("ctx", "heads"),
        P("heads", None),
        P(),
        P("heads"),
    )
    return jax.shard_map(
        body, mesh=mesh, in_specs=placed, out_specs=P("ctx", "heads"), check_vma=False
    )
```

```python
import math

import jax
import jax.numpy as jnp
from jax import lax
from jax.experimental import pallas as pl
from jax.experimental.pallas import tpu as pltpu
from jax.sharding import PartitionSpec as P

MESH = pl.DeviceIdType.MESH
DH = 128
TILE = 128
SPOTS = 4
FRAMES = 32
TILES = 128
PLANES = 4
SIDE = 4
HEADS_HERE = 3
WORKERS = 2 * SIDE
SLOTS = TILES // WORKERS
PARTS = 4
PART = 2 * TILES // PARTS
PIECE = TILE // WORKERS
GROUP = 16
STEPS = TILES // GROUP
LOW = -1e30
SCALE2 = math.log2(math.e) / math.sqrt(DH)
BF16 = jnp.bfloat16
F32 = jnp.float32


def where_is(device):
    return lax.div(device, WORKERS), lax.rem(lax.div(device, 2), SIDE), lax.rem(device, 2)


def device_at(row, column, core):
    return (lax.rem(row, SIDE) * SIDE + lax.rem(column, SIDE)) * 2 + core


def spread_kernel(
    q_ref, kv_ref, w_ref, q_all, kv_all, w_all,
    q_send, q_recv, z_send, z_recv, y_send, y_recv, far_send, far_recv,
    core_send, core_recv, w_send, w_recv, w_core_send, w_core_recv, own_sem,
):
    plane = lax.axis_index("heads")
    me = lax.axis_index("ctx")
    row, column, core = where_is(me)
    working = row < HEADS_HERE
    own_row = jnp.minimum(row, HEADS_HERE - 1)
    depth = w_ref.shape[0]
    width = w_all.shape[1]
    sides = (1, SIDE - 1)

    barrier = pltpu.get_barrier_semaphore()

    def greet(step, carry):
        pl.semaphore_signal(
            barrier, inc=1, device_id=(plane, lax.rem(me + step, FRAMES)), device_id_type=MESH
        )
        return carry

    lax.fori_loop(1, FRAMES, greet, 0)
    for hop in range(1, PLANES):
        pl.semaphore_signal(
            barrier, inc=1, device_id=(lax.rem(plane + hop, PLANES), me), device_id_type=MESH
        )
    pl.semaphore_wait(barrier, FRAMES - 1 + PLANES - 1)

    def span(part):
        return pl.ds(part * PART, PART)

    own_copy = pltpu.make_async_copy(
        kv_ref.at[own_row], kv_all.at[column * 2 + core, :, 0], own_sem
    )

    def z_copy(part, hop):
        there = lax.rem(row + hop, SIDE)
        return pltpu.make_async_remote_copy(
            src_ref=kv_ref.at[there, span(part)],
            dst_ref=kv_all.at[column * 2 + core, span(part), hop],
            send_sem=z_send.at[part, hop],
            recv_sem=z_recv.at[part, hop],
            device_id=(plane, device_at(there, column, core)),
            device_id_type=MESH,
        )

    def piece(number, away):
        source = kv_all.at[lax.rem(column + away, SIDE) * 2 + core]
        if number == 0:
            return source.at[:, 0]
        return source.at[span(number - 1), pl.ds(1, SIDE - 1)]

    def y_copy(number, side):
        return pltpu.make_async_remote_copy(
            src_ref=kv_ref.at[own_row] if number == 0 else piece(number, 0),
            dst_ref=piece(number, 0),
            send_sem=y_send.at[number, side],
            recv_sem=y_recv.at[number, side],
            device_id=(plane, device_at(row, column + sides[side], core)),
            device_id_type=MESH,
        )

    def far_copy(number, side):
        source = kv_all.at[lax.rem(column + sides[1 - side], SIDE) * 2 + core]
        if number == 0:
            chunk = source.at[pl.ds(side * TILES, TILES), 0]
        else:
            chunk = source.at[
                pl.ds((number - 1) * PART + side * (PART // 2), PART // 2), pl.ds(1, SIDE - 1)
            ]
        return pltpu.make_async_remote_copy(
            src_ref=chunk,
            dst_ref=chunk,
            send_sem=far_send.at[number, side],
            recv_sem=far_recv.at[number, side],
            device_id=(plane, device_at(row, column + sides[side], core)),
            device_id_type=MESH,
        )

    def core_copy(number, away):
        return pltpu.make_async_remote_copy(
            src_ref=piece(number, away),
            dst_ref=piece(number, away),
            send_sem=core_send.at[number, away],
            recv_sem=core_recv,
            device_id=(plane, device_at(row, column, 1 - core)),
            device_id_type=MESH,
        )

    half = depth // 2

    def w_rows(source, part):
        return w_all.at[pl.ds(pl.multiple_of(source * depth + part * half, 16), half)]

    def w_copy(hop):
        there = lax.rem(plane + hop, PLANES)
        return pltpu.make_async_remote_copy(
            src_ref=w_ref.at[
                pl.ds(pl.multiple_of(core * half, 16), half),
                pl.ds(pl.multiple_of(there * width, 128), width),
            ],
            dst_ref=w_rows(plane, core),
            send_sem=w_send.at[hop],
            recv_sem=w_recv.at[hop],
            device_id=(there, me),
            device_id_type=MESH,
        )

    def w_core_copy(hop):
        rows = w_rows(lax.rem(plane + PLANES - hop, PLANES), core)
        return pltpu.make_async_remote_copy(
            src_ref=rows,
            dst_ref=rows,
            send_sem=w_core_send.at[hop],
            recv_sem=w_core_recv.at[hop],
            device_id=(plane, device_at(row, column, 1 - core)),
            device_id_type=MESH,
        )

    own_w = pltpu.make_async_copy(
        w_ref.at[:, pl.ds(pl.multiple_of(plane * width, 128), width)],
        w_all.at[pl.ds(pl.multiple_of(plane * depth, 128), depth)],
        w_recv.at[0],
    )

    def q_copy(step):
        there = lax.rem(me + step, FRAMES)
        row_there, column_there, core_there = where_is(there)
        return row_there < HEADS_HERE, pltpu.make_async_remote_copy(
            src_ref=q_ref.at[
                jnp.minimum(row_there, HEADS_HERE - 1), :, column_there * 2 + core_there
            ],
            dst_ref=q_all.at[:, me],
            send_sem=q_send.at[step],
            recv_sem=q_recv,
            device_id=(plane, there),
            device_id_type=MESH,
        )

    def to_rows(part, work):
        for hop in range(1, SIDE):

            @pl.when(lax.rem(row + hop, SIDE) < HEADS_HERE)
            def _():
                work(z_copy(part, hop))

    def send_q(step, carry):
        wanted, copy = q_copy(step)

        @pl.when(wanted)
        def _():
            copy.start()

        return carry

    def sent_q(step, carry):
        wanted, copy = q_copy(step)

        @pl.when(wanted)
        def _():
            copy.wait_send()

        return carry

    def send_small():
        for hop in range(1, PLANES):
            w_copy(hop).start()
        own_w.start()
        lax.fori_loop(1, FRAMES, send_q, 0)

    @pl.when(working)
    def _():
        own_copy.start()
        for side in range(2):
            y_copy(0, side).start()

    to_rows(0, lambda copy: copy.start())
    send_small()

    def next_rows(part):
        to_rows(part, lambda copy: copy.wait_send())
        if part + 1 < PARTS:
            to_rows(part + 1, lambda copy: copy.start())

    @pl.when(jnp.logical_not(working))
    def _():
        for part in range(PARTS):
            next_rows(part)

    @pl.when(working)
    def _():
        pltpu.make_async_copy(
            q_ref.at[own_row, :, column * 2 + core], q_all.at[:, me], q_recv
        ).start()
        own_copy.wait()
        core_copy(0, 0).start()

        def pass_on(number):
            for side in range(2):
                y_copy(number, side).wait_recv()
                far_copy(number, side).start()
            for side in range(2):
                core_copy(number, sides[1 - side]).start()

        for part in range(PARTS):
            next_rows(part)
            for hop in range(1, SIDE):
                landed = kv_all.at[column * 2 + core, span(part), hop]
                pltpu.make_async_copy(landed, landed, z_recv.at[part, hop]).wait()
            for side in range(2):
                y_copy(part + 1, side).start()
            core_copy(part + 1, 0).start()
            pass_on(part)
        pass_on(PARTS)
        for number in range(PARTS + 1):
            for side in range(2):
                far_copy(number, side).wait_recv()
            core_copy(number, 2).start()

    for hop in range(1, PLANES):
        w_copy(hop).wait_recv()
        w_core_copy(hop).start()

    @pl.when(working)
    def _():
        pltpu.make_async_copy(q_all, q_all, q_recv).wait()
        other = kv_all.at[pl.ds(0, SIDE)]
        pltpu.make_async_copy(other, other, core_recv).wait()
        for number in range(PARTS + 1):
            for side in range(2):
                y_copy(number, side).wait_send()
                far_copy(number, side).wait_send()
            for away in range(SIDE):
                core_copy(number, away).wait_send()

    own_w.wait()
    lax.fori_loop(1, FRAMES, sent_q, 0)
    for hop in range(1, PLANES):
        w_copy(hop).wait_send()
        w_core_copy(hop).wait()


def spread(q_parts, kv_parts, out_weight):
    depth, columns = out_weight.shape
    return pl.pallas_call(
        spread_kernel,
        out_shape=(
            jax.ShapeDtypeStruct((SLOTS, FRAMES, SPOTS, DH), BF16),
            jax.ShapeDtypeStruct((WORKERS, 2 * TILES, SIDE, SPOTS, DH), BF16),
            jax.ShapeDtypeStruct((depth * PLANES, columns // PLANES), BF16),
        ),
        in_specs=[pl.BlockSpec(memory_space=pl.ANY)] * 3,
        out_specs=(pl.BlockSpec(memory_space=pl.ANY),) * 3,
        scratch_shapes=[
            pltpu.SemaphoreType.DMA((FRAMES,)),
            pltpu.SemaphoreType.DMA,
            pltpu.SemaphoreType.DMA((PARTS, SIDE)),
            pltpu.SemaphoreType.DMA((PARTS, SIDE)),
            pltpu.SemaphoreType.DMA((PARTS + 1, 2)),
            pltpu.SemaphoreType.DMA((PARTS + 1, 2)),
            pltpu.SemaphoreType.DMA((PARTS + 1, 2)),
            pltpu.SemaphoreType.DMA((PARTS + 1, 2)),
            pltpu.SemaphoreType.DMA((PARTS + 1, SIDE)),
            pltpu.SemaphoreType.DMA,
            pltpu.SemaphoreType.DMA((PLANES,)),
            pltpu.SemaphoreType.DMA((PLANES,)),
            pltpu.SemaphoreType.DMA((PLANES,)),
            pltpu.SemaphoreType.DMA((PLANES,)),
            pltpu.SemaphoreType.DMA,
        ],
        compiler_params=pltpu.CompilerParams(
            collective_id=0, has_side_effects=True, vmem_limit_bytes=4 * 1024 * 1024
        ),
    )(q_parts, kv_parts, out_weight)


def attend_kernel(
    list_ref, q_ref, kv_ref, o_ref, turned_ref, even_ref, odd_ref, even_peak, odd_peak,
    base_ref, sum_ref,
):
    kept = ((even_ref, even_peak), (odd_ref, odd_peak))

    def count_of(slot):
        return list_ref[SLOTS, slot]

    def steps_of(slot):
        return lax.div(count_of(slot) + GROUP - 1, GROUP)

    def tile_at(tile):
        start = pl.multiple_of(tile * PIECE, PIECE)
        return jnp.concatenate(
            [kv_ref[worker, pl.ds(start, PIECE), :] for worker in range(WORKERS)], axis=0
        )

    def score(slot, side, step):
        score_ref, peak_ref = kept[side]
        query = q_ref[pl.ds(pl.multiple_of(slot * TILE, TILE), TILE), :]
        keys = [turned_ref[list_ref[slot, step * GROUP + u]] for u in range(GROUP)]
        scores = jnp.dot(query, jnp.concatenate(keys, axis=1), preferred_element_type=F32)
        peak = peak_ref[...]
        for u in range(GROUP):
            part = scores[:, u * TILE : (u + 1) * TILE]
            score_ref[step, :, u * TILE : (u + 1) * TILE] = part
            peak = jnp.maximum(peak, part)
        peak_ref[...] = peak

    def gather(slot, side, step):
        score_ref = kept[side][0]
        base = base_ref[...]
        count = count_of(slot)
        weights, values = [], []
        for u in range(GROUP):
            part = score_ref[step, :, u * TILE : (u + 1) * TILE]
            weights.append(jnp.exp2(part * SCALE2 - base).astype(BF16))
            listed = step * GROUP + u < count
            value = jnp.where(listed, tile_at(TILES + list_ref[slot, step * GROUP + u]), 0).astype(BF16)
            ones = jnp.broadcast_to(jnp.where(listed, 1.0, 0.0).astype(BF16), (TILE, DH))
            values.append(jnp.concatenate([value, ones], axis=1))
        sum_ref[...] += jnp.dot(
            jnp.concatenate(weights, axis=1),
            jnp.concatenate(values, axis=0),
            preferred_element_type=F32,
        )

    def loop(first, last, work):
        def one(step, carry):
            work(step)
            return carry

        lax.fori_loop(first, last, one, 0)

    def one_slot(slot, side, ahead):
        here = steps_of(slot)
        both = jnp.minimum(here, ahead)
        base = jnp.max(kept[side][1][...], axis=1, keepdims=True) * SCALE2
        base_ref[...] = jnp.broadcast_to(base, (TILE, TILE))
        sum_ref[...] = jnp.zeros((TILE, 2 * DH), F32)
        kept[1 - side][1][...] = jnp.full((TILE, TILE), LOW, F32)

        def pair(step):
            gather(slot, side, step)
            score(slot + 1, 1 - side, step)

        loop(0, both, pair)
        loop(both, ahead, lambda step: score(slot + 1, 1 - side, step))
        loop(both, here, lambda step: gather(slot, side, step))
        o_ref[pl.ds(pl.multiple_of(slot * TILE, TILE), TILE), :] = (
            sum_ref[:, :DH] / sum_ref[:, DH:]
        ).astype(BF16)

    def turn(step):
        for u in range(GROUP):
            tile = step * GROUP + u
            turned_ref[tile] = tile_at(tile).T

    loop(0, jnp.where(count_of(0) > 0, STEPS, 0), turn)
    even_peak[...] = jnp.full((TILE, TILE), LOW, F32)
    loop(0, steps_of(0), lambda step: score(0, 0, step))

    def two_slots(turn, carry):
        slot = turn * 2
        one_slot(slot, 0, steps_of(slot + 1))
        follows = jnp.minimum(slot + 2, SLOTS - 1)
        one_slot(slot + 1, 1, jnp.where(slot + 2 < SLOTS, steps_of(follows), 0))
        return carry

    lax.fori_loop(0, SLOTS // 2, two_slots, 0)
    if SLOTS % 2:
        one_slot(SLOTS - 1, 0, 0)


def attend(lists, query, kv):
    return pl.pallas_call(
        attend_kernel,
        out_shape=jax.ShapeDtypeStruct(query.shape, BF16),
        in_specs=[
            pl.BlockSpec(memory_space=pltpu.SMEM),
            pl.BlockSpec(memory_space=pltpu.VMEM),
            pl.BlockSpec(memory_space=pltpu.VMEM),
        ],
        out_specs=pl.BlockSpec(memory_space=pltpu.VMEM),
        scratch_shapes=[
            pltpu.VMEM((TILES, DH, TILE), BF16),
            pltpu.VMEM((STEPS, TILE, GROUP * TILE), F32),
            pltpu.VMEM((STEPS, TILE, GROUP * TILE), F32),
            pltpu.VMEM((TILE, TILE), F32),
            pltpu.VMEM((TILE, TILE), F32),
            pltpu.VMEM((TILE, TILE), F32),
            pltpu.VMEM((TILE, 2 * DH), F32),
        ],
        compiler_params=pltpu.CompilerParams(vmem_limit_bytes=40 * 1024 * 1024),
    )(lists, query, kv)


def collect_kernel(o_ref, attn, send, recv, x_send, x_recv):
    plane = lax.axis_index("heads")
    me = lax.axis_index("ctx")
    row, column, core = where_is(me)
    barrier = pltpu.get_barrier_semaphore()

    def greet(step, carry):
        pl.semaphore_signal(
            barrier, inc=1, device_id=(plane, lax.rem(me + step, FRAMES)), device_id_type=MESH
        )
        return carry

    lax.fori_loop(1, FRAMES, greet, 0)
    sides = (lax.rem(plane + 1, PLANES), lax.rem(plane + PLANES - 1, PLANES))
    for there in sides:
        pl.semaphore_signal(barrier, inc=1, device_id=(there, me), device_id_type=MESH)
    pl.semaphore_wait(barrier, FRAMES - 1 + 2)

    mine = jnp.minimum(row, HEADS_HERE - 1)
    goal = attn.at[plane * HEADS_HERE + mine, :, column * 2 + core]

    def back(step):
        there = lax.rem(me + step, FRAMES)
        return pltpu.make_async_remote_copy(
            src_ref=o_ref.at[:, there],
            dst_ref=goal,
            send_sem=send.at[step],
            recv_sem=recv.at[mine],
            device_id=(plane, there),
            device_id_type=MESH,
        )

    def start(step, carry):
        back(step).start()
        return carry

    def end(step, carry):
        back(step).wait_send()
        return carry

    working = row < HEADS_HERE

    @pl.when(working)
    def _():
        lax.fori_loop(1, FRAMES, start, 0)
        pltpu.make_async_copy(o_ref.at[:, me], goal, recv.at[mine]).start()

    cut = SLOTS // 2

    def near(head, side):
        part = attn.at[plane * HEADS_HERE + head]
        return pltpu.make_async_remote_copy(
            src_ref=part,
            dst_ref=part,
            send_sem=x_send.at[head, side],
            recv_sem=x_recv.at[head, side],
            device_id=(sides[side], me),
            device_id_type=MESH,
        )

    def far(head, side):
        part = attn.at[sides[1 - side] * HEADS_HERE + head]
        part = part.at[pl.ds(0, cut)] if side == 0 else part.at[pl.ds(cut, SLOTS - cut)]
        return pltpu.make_async_remote_copy(
            src_ref=part,
            dst_ref=part,
            send_sem=x_send.at[head, 2 + side],
            recv_sem=x_recv.at[head, 2 + side],
            device_id=(sides[side], me),
            device_id_type=MESH,
        )

    for head in range(HEADS_HERE):
        part = attn.at[plane * HEADS_HERE + head]
        pltpu.make_async_copy(part, part, recv.at[head]).wait()
        for side in range(2):
            near(head, side).start()
    for head in range(HEADS_HERE):
        for side in range(2):
            near(head, side).wait_recv()
            far(head, side).start()

    @pl.when(working)
    def _():
        lax.fori_loop(1, FRAMES, end, 0)

    for head in range(HEADS_HERE):
        for side in range(2):
            near(head, side).wait_send()
            far(head, side).wait()


def collect(attended):
    return pl.pallas_call(
        collect_kernel,
        out_shape=jax.ShapeDtypeStruct(
            (PLANES * HEADS_HERE, SLOTS, WORKERS, SPOTS, DH), BF16
        ),
        in_specs=[pl.BlockSpec(memory_space=pl.ANY)],
        out_specs=pl.BlockSpec(memory_space=pl.ANY),
        scratch_shapes=[
            pltpu.SemaphoreType.DMA((FRAMES,)),
            pltpu.SemaphoreType.DMA((HEADS_HERE,)),
            pltpu.SemaphoreType.DMA((HEADS_HERE, 4)),
            pltpu.SemaphoreType.DMA((HEADS_HERE, 4)),
        ],
        compiler_params=pltpu.CompilerParams(
            collective_id=1, has_side_effects=True, vmem_limit_bytes=4 * 1024 * 1024
        ),
    )(attended)


def project_kernel(attn_ref, w_ref, out_ref):
    rows = out_ref.shape[0]
    heads = attn_ref.shape[0]
    wide = jnp.concatenate([attn_ref[h, :rows, :] for h in range(heads)], axis=1)
    out_ref[...] = jnp.dot(wide, w_ref[...], preferred_element_type=F32).astype(BF16)


def project(attn, weight, rows):
    columns = weight.shape[1]
    block = 256
    heads = attn.shape[0]
    return pl.pallas_call(
        project_kernel,
        out_shape=jax.ShapeDtypeStruct((rows, columns), BF16),
        grid=(columns // block,),
        in_specs=[
            pl.BlockSpec((heads, attn.shape[1], DH), lambda i: (0, 0, 0)),
            pl.BlockSpec((weight.shape[0], block), lambda i: (0, i)),
        ],
        out_specs=pl.BlockSpec((rows, block), lambda i: (0, i)),
        compiler_params=pltpu.CompilerParams(vmem_limit_bytes=24 * 1024 * 1024),
    )(attn, weight)


def arrange_kernel(pattern_ref, mask_ref, q_ref, k_ref, v_ref, q_out, kv_out, list_ref):
    me = lax.axis_index("ctx")
    row, column, core = where_is(me)
    rows = q_ref.shape[0]
    for head in range(HEADS_HERE):
        columns = slice(head * DH, (head + 1) * DH)
        q_out[head] = q_ref[:, columns]
        kv_out[head, :rows, :] = k_ref[:, columns]
        kv_out[head, rows:, :] = v_ref[:, columns]

    pattern = pattern_ref[jnp.minimum(row, HEADS_HERE - 1)]
    masks = []
    tiles = [slot * WORKERS + column * 2 + core for slot in range(SLOTS)]
    for tile in tiles:
        masks.append(jnp.where(row < HEADS_HERE, mask_ref[pattern, pl.ds(tile, 1), :], 0))
    seen = jnp.concatenate(masks, axis=0) == 1
    seen = jnp.where(seen, 1.0, 0.0).astype(F32)
    down = lax.broadcasted_iota(jnp.int32, (TILES, TILES), 0)
    along = lax.broadcasted_iota(jnp.int32, (TILES, TILES), 1)
    both = (((1,), (1,)), ((), ()))
    upto = jnp.where(along <= down, 1.0, 0.0).astype(BF16)
    same = jnp.where(along == down, 1.0, 0.0).astype(BF16)
    rank = lax.dot_general(upto, seen.astype(BF16), both, preferred_element_type=F32)
    turned = lax.dot_general(same, seen.astype(BF16), both, preferred_element_type=F32)
    rank = rank.astype(jnp.int32)
    spot = jnp.where(turned > 0.5, rank - 1, -1)
    for slot in range(SLOTS):
        hit = spot[:, slot : slot + 1] == along
        listed = jnp.sum(jnp.where(hit, down, 0), axis=0, keepdims=True)
        spare = along[:1, :] >= rank[TILES - 1 :, slot : slot + 1]
        list_ref[slot : slot + 1, :] = jnp.where(spare, tiles[slot], listed)
    last = jnp.concatenate(
        [rank[TILES - 1 :, :], jnp.zeros((1, TILES - SLOTS), jnp.int32)], axis=1
    )
    list_ref[SLOTS : SLOTS + 1, :] = last


def arrange(head_pattern, tile_masks, queries, key_rows, value_rows):
    rows = queries.shape[0]
    return pl.pallas_call(
        arrange_kernel,
        out_shape=(
            jax.ShapeDtypeStruct((HEADS_HERE, rows, DH), BF16),
            jax.ShapeDtypeStruct((HEADS_HERE, 2 * rows, DH), BF16),
            jax.ShapeDtypeStruct((SLOTS + 1, TILES), jnp.int32),
        ),
        in_specs=[pl.BlockSpec(memory_space=pltpu.SMEM)]
        + [pl.BlockSpec(memory_space=pltpu.VMEM)] * 4,
        out_specs=(pl.BlockSpec(memory_space=pltpu.VMEM),) * 3,
        compiler_params=pltpu.CompilerParams(vmem_limit_bytes=16 * 1024 * 1024),
    )(head_pattern, tile_masks, queries, key_rows, value_rows)


def body(queries, key_rows, value_rows, out_weight, tile_masks, head_pattern):
    rows = queries.shape[0]
    q_parts, kv_parts, lists = arrange(head_pattern, tile_masks, queries, key_rows, value_rows)
    q_all, kv_all, w_all = spread(
        q_parts.reshape(HEADS_HERE, SLOTS, WORKERS, SPOTS, DH),
        kv_parts.reshape(HEADS_HERE, 2 * TILES, SPOTS, DH),
        out_weight,
    )
    attended = attend(
        lists, q_all.reshape(SLOTS * TILE, DH), kv_all.reshape(WORKERS, 2 * TILES * PIECE, DH)
    )
    attn = collect(attended.reshape(SLOTS, FRAMES, SPOTS, DH))
    attn = attn.reshape(PLANES * HEADS_HERE, rows, DH)
    return project(attn, w_all, rows)


def solution(mesh):
    placed = (
        P("ctx", "heads"),
        P("ctx", "heads"),
        P("ctx", "heads"),
        P("heads", None),
        P(),
        P("heads"),
    )
    return jax.shard_map(
        body, mesh=mesh, in_specs=placed, out_specs=P("ctx", "heads"), check_vma=False
    )
```

```python
import math

import jax
import jax.numpy as jnp
from jax import lax
from jax.experimental import pallas as pl
from jax.experimental.pallas import tpu as pltpu
from jax.sharding import PartitionSpec as P

MESH = pl.DeviceIdType.MESH
DH = 128
TILE = 128
SPOTS = 4
FRAMES = 32
TILES = 128
PLANES = 4
SIDE = 4
HEADS_HERE = 3
WORKERS = 2 * SIDE
SLOTS = TILES // WORKERS
PARTS = 4
PART = 2 * TILES // PARTS
PIECE = TILE // WORKERS
GROUP = 8
BESIDE = 4
FAR = 64.0
SCALE2 = math.log2(math.e) / math.sqrt(DH)
BF16 = jnp.bfloat16
F32 = jnp.float32


def where_is(device):
    return lax.div(device, WORKERS), lax.rem(lax.div(device, 2), SIDE), lax.rem(device, 2)


def device_at(row, column, core):
    return (lax.rem(row, SIDE) * SIDE + lax.rem(column, SIDE)) * 2 + core


def spread_kernel(
    q_ref, kv_ref, w_ref, q_all, kv_all, w_all,
    q_send, q_recv, z_send, z_recv, y_send, y_recv, far_send, far_recv,
    core_send, core_recv, w_send, w_recv, w_core_send, w_core_recv, own_sem,
):
    plane = lax.axis_index("heads")
    me = lax.axis_index("ctx")
    row, column, core = where_is(me)
    working = row < HEADS_HERE
    own_row = jnp.minimum(row, HEADS_HERE - 1)
    depth = w_ref.shape[0]
    width = w_all.shape[1]
    sides = (1, SIDE - 1)

    barrier = pltpu.get_barrier_semaphore()

    def greet(step, carry):
        pl.semaphore_signal(
            barrier, inc=1, device_id=(plane, lax.rem(me + step, FRAMES)), device_id_type=MESH
        )
        return carry

    lax.fori_loop(1, FRAMES, greet, 0)
    for hop in range(1, PLANES):
        pl.semaphore_signal(
            barrier, inc=1, device_id=(lax.rem(plane + hop, PLANES), me), device_id_type=MESH
        )
    pl.semaphore_wait(barrier, FRAMES - 1 + PLANES - 1)

    def span(part):
        return pl.ds(part * PART, PART)

    own_copy = pltpu.make_async_copy(
        kv_ref.at[own_row], kv_all.at[column * 2 + core, :, 0], own_sem
    )

    def z_copy(part, hop):
        there = lax.rem(row + hop, SIDE)
        return pltpu.make_async_remote_copy(
            src_ref=kv_ref.at[there, span(part)],
            dst_ref=kv_all.at[column * 2 + core, span(part), hop],
            send_sem=z_send.at[part, hop],
            recv_sem=z_recv.at[part, hop],
            device_id=(plane, device_at(there, column, core)),
            device_id_type=MESH,
        )

    def piece(number, away):
        source = kv_all.at[lax.rem(column + away, SIDE) * 2 + core]
        if number == 0:
            return source.at[:, 0]
        return source.at[span(number - 1), pl.ds(1, SIDE - 1)]

    def y_copy(number, side):
        return pltpu.make_async_remote_copy(
            src_ref=kv_ref.at[own_row] if number == 0 else piece(number, 0),
            dst_ref=piece(number, 0),
            send_sem=y_send.at[number, side],
            recv_sem=y_recv.at[number, side],
            device_id=(plane, device_at(row, column + sides[side], core)),
            device_id_type=MESH,
        )

    def far_copy(number, side):
        source = kv_all.at[lax.rem(column + sides[1 - side], SIDE) * 2 + core]
        if number == 0:
            chunk = source.at[pl.ds(side * TILES, TILES), 0]
        else:
            chunk = source.at[
                pl.ds((number - 1) * PART + side * (PART // 2), PART // 2), pl.ds(1, SIDE - 1)
            ]
        return pltpu.make_async_remote_copy(
            src_ref=chunk,
            dst_ref=chunk,
            send_sem=far_send.at[number, side],
            recv_sem=far_recv.at[number, side],
            device_id=(plane, device_at(row, column + sides[side], core)),
            device_id_type=MESH,
        )

    def core_copy(number, away):
        return pltpu.make_async_remote_copy(
            src_ref=piece(number, away),
            dst_ref=piece(number, away),
            send_sem=core_send.at[number, away],
            recv_sem=core_recv,
            device_id=(plane, device_at(row, column, 1 - core)),
            device_id_type=MESH,
        )

    half = depth // 2

    def w_rows(source, part):
        return w_all.at[pl.ds(pl.multiple_of(source * depth + part * half, 16), half)]

    def w_copy(hop):
        there = lax.rem(plane + hop, PLANES)
        return pltpu.make_async_remote_copy(
            src_ref=w_ref.at[
                pl.ds(pl.multiple_of(core * half, 16), half),
                pl.ds(pl.multiple_of(there * width, 128), width),
            ],
            dst_ref=w_rows(plane, core),
            send_sem=w_send.at[hop],
            recv_sem=w_recv.at[hop],
            device_id=(there, me),
            device_id_type=MESH,
        )

    def w_core_copy(hop):
        rows = w_rows(lax.rem(plane + PLANES - hop, PLANES), core)
        return pltpu.make_async_remote_copy(
            src_ref=rows,
            dst_ref=rows,
            send_sem=w_core_send.at[hop],
            recv_sem=w_core_recv.at[hop],
            device_id=(plane, device_at(row, column, 1 - core)),
            device_id_type=MESH,
        )

    own_w = pltpu.make_async_copy(
        w_ref.at[:, pl.ds(pl.multiple_of(plane * width, 128), width)],
        w_all.at[pl.ds(pl.multiple_of(plane * depth, 128), depth)],
        w_recv.at[0],
    )

    def q_copy(step):
        there = lax.rem(me + step, FRAMES)
        row_there, column_there, core_there = where_is(there)
        return row_there < HEADS_HERE, pltpu.make_async_remote_copy(
            src_ref=q_ref.at[
                jnp.minimum(row_there, HEADS_HERE - 1), :, column_there * 2 + core_there
            ],
            dst_ref=q_all.at[:, me],
            send_sem=q_send.at[step],
            recv_sem=q_recv,
            device_id=(plane, there),
            device_id_type=MESH,
        )

    def to_rows(part, work):
        for hop in range(1, SIDE):

            @pl.when(lax.rem(row + hop, SIDE) < HEADS_HERE)
            def _():
                work(z_copy(part, hop))

    def send_q(step, carry):
        wanted, copy = q_copy(step)

        @pl.when(wanted)
        def _():
            copy.start()

        return carry

    def sent_q(step, carry):
        wanted, copy = q_copy(step)

        @pl.when(wanted)
        def _():
            copy.wait_send()

        return carry

    def send_small():
        for hop in range(1, PLANES):
            w_copy(hop).start()
        own_w.start()
        lax.fori_loop(1, FRAMES, send_q, 0)

    @pl.when(working)
    def _():
        own_copy.start()
        for side in range(2):
            y_copy(0, side).start()

    to_rows(0, lambda copy: copy.start())
    send_small()

    def next_rows(part):
        to_rows(part, lambda copy: copy.wait_send())
        if part + 1 < PARTS:
            to_rows(part + 1, lambda copy: copy.start())

    @pl.when(jnp.logical_not(working))
    def _():
        for part in range(PARTS):
            next_rows(part)

    @pl.when(working)
    def _():
        pltpu.make_async_copy(
            q_ref.at[own_row, :, column * 2 + core], q_all.at[:, me], q_recv
        ).start()
        own_copy.wait()
        core_copy(0, 0).start()

        def pass_on(number):
            for side in range(2):
                y_copy(number, side).wait_recv()
                far_copy(number, side).start()
            for side in range(2):
                core_copy(number, sides[1 - side]).start()

        for part in range(PARTS):
            next_rows(part)
            for hop in range(1, SIDE):
                landed = kv_all.at[column * 2 + core, span(part), hop]
                pltpu.make_async_copy(landed, landed, z_recv.at[part, hop]).wait()
            for side in range(2):
                y_copy(part + 1, side).start()
            core_copy(part + 1, 0).start()
            pass_on(part)
        pass_on(PARTS)
        for number in range(PARTS + 1):
            for side in range(2):
                far_copy(number, side).wait_recv()
            core_copy(number, 2).start()

    for hop in range(1, PLANES):
        w_copy(hop).wait_recv()
        w_core_copy(hop).start()

    @pl.when(working)
    def _():
        pltpu.make_async_copy(q_all, q_all, q_recv).wait()
        other = kv_all.at[pl.ds(0, SIDE)]
        pltpu.make_async_copy(other, other, core_recv).wait()
        for number in range(PARTS + 1):
            for side in range(2):
                y_copy(number, side).wait_send()
                far_copy(number, side).wait_send()
            for away in range(SIDE):
                core_copy(number, away).wait_send()

    own_w.wait()
    lax.fori_loop(1, FRAMES, sent_q, 0)
    for hop in range(1, PLANES):
        w_copy(hop).wait_send()
        w_core_copy(hop).wait()


def spread(q_parts, kv_parts, out_weight):
    depth, columns = out_weight.shape
    return pl.pallas_call(
        spread_kernel,
        out_shape=(
            jax.ShapeDtypeStruct((SLOTS, FRAMES, SPOTS, DH), BF16),
            jax.ShapeDtypeStruct((WORKERS, 2 * TILES, SIDE, SPOTS, DH), BF16),
            jax.ShapeDtypeStruct((depth * PLANES, columns // PLANES), BF16),
        ),
        in_specs=[pl.BlockSpec(memory_space=pl.ANY)] * 3,
        out_specs=(pl.BlockSpec(memory_space=pl.ANY),) * 3,
        scratch_shapes=[
            pltpu.SemaphoreType.DMA((FRAMES,)),
            pltpu.SemaphoreType.DMA,
            pltpu.SemaphoreType.DMA((PARTS, SIDE)),
            pltpu.SemaphoreType.DMA((PARTS, SIDE)),
            pltpu.SemaphoreType.DMA((PARTS + 1, 2)),
            pltpu.SemaphoreType.DMA((PARTS + 1, 2)),
            pltpu.SemaphoreType.DMA((PARTS + 1, 2)),
            pltpu.SemaphoreType.DMA((PARTS + 1, 2)),
            pltpu.SemaphoreType.DMA((PARTS + 1, SIDE)),
            pltpu.SemaphoreType.DMA,
            pltpu.SemaphoreType.DMA((PLANES,)),
            pltpu.SemaphoreType.DMA((PLANES,)),
            pltpu.SemaphoreType.DMA((PLANES,)),
            pltpu.SemaphoreType.DMA((PLANES,)),
            pltpu.SemaphoreType.DMA,
        ],
        compiler_params=pltpu.CompilerParams(
            collective_id=0, has_side_effects=True, vmem_limit_bytes=4 * 1024 * 1024
        ),
    )(q_parts, kv_parts, out_weight)


def attend_kernel(
    list_ref, q_ref, kv_ref, o_ref, turned_ref, base_ref, peak_ref, sum_ref,
    slot_of, first_of, listed_of,
):
    _, column, core = where_is(lax.axis_index("ctx"))

    def loop(count, work):
        def one(step, carry):
            work(step)
            return carry

        lax.fori_loop(0, count, one, 0)

    def rows_of(slot):
        return pl.ds(pl.multiple_of(slot * TILE, TILE), TILE)

    def tile_at(tile):
        start = pl.multiple_of(tile * PIECE, PIECE)
        return jnp.concatenate(
            [kv_ref[worker, pl.ds(start, PIECE), :] for worker in range(WORKERS)], axis=0
        )

    def enlist(slot, total):
        count = list_ref[SLOTS, slot]
        steps = lax.div(count + GROUP - 1, GROUP)

        def one(step, carry):
            slot_of[total + step] = slot
            first_of[total + step] = step * GROUP
            listed_of[total + step] = count - step * GROUP
            return carry

        lax.fori_loop(0, steps, one, 0)
        return total + steps

    total = lax.fori_loop(0, SLOTS, enlist, 0)
    for spare in range(BESIDE - 1):
        slot_of[total + spare] = 0
        first_of[total + spare] = 0
        listed_of[total + spare] = 0
    turns = lax.div(total + BESIDE - 1, BESIDE)
    busy = jnp.where(total > 0, 1, 0)

    def turn(step):
        for u in range(GROUP):
            tile = step * GROUP + u
            turned_ref[tile] = tile_at(tile).T

    loop(busy * (TILES // GROUP), turn)

    def own_scores(step):
        for u in range(BESIDE):
            slot = step * BESIDE + u
            own = turned_ref[slot * WORKERS + column * 2 + core]
            peak_ref[slot] = jnp.dot(q_ref[rows_of(slot), :], own, preferred_element_type=F32)

    loop(busy * (SLOTS // BESIDE), own_scores)

    def start(step):
        for u in range(BESIDE):
            slot = step * BESIDE + u
            base = jnp.max(peak_ref[slot], axis=1, keepdims=True) * SCALE2
            base_ref[slot] = jnp.broadcast_to(base, (TILE, TILE))
            sum_ref[slot] = jnp.zeros((TILE, 2 * DH), F32)

    def attend_steps(step):
        found = []
        for beside in range(BESIDE):
            number = step * BESIDE + beside
            slot, first, listed = slot_of[number], first_of[number], listed_of[number]
            tiles = [list_ref[slot, first + u] for u in range(GROUP)]
            keys = jnp.concatenate([turned_ref[tile] for tile in tiles], axis=1)
            scores = jnp.dot(q_ref[rows_of(slot), :], keys, preferred_element_type=F32)
            base = base_ref[slot]
            peak, weights, values = None, [], []
            for u in range(GROUP):
                part = scores[:, u * TILE : (u + 1) * TILE]
                peak = part if peak is None else jnp.maximum(peak, part)
                weights.append(jnp.exp2(part * SCALE2 - base).astype(BF16))
                value = jnp.where(u < listed, tile_at(TILES + tiles[u]), 0).astype(BF16)
                ones = jnp.where(u < listed, 1.0, 0.0).astype(BF16)
                ones = jnp.broadcast_to(ones, (TILE, DH))
                values.append(jnp.concatenate([value, ones], axis=1))
            added = jnp.dot(
                jnp.concatenate(weights, axis=1),
                jnp.concatenate(values, axis=0),
                preferred_element_type=F32,
            )
            found.append((slot, peak, added))
        for slot, peak, added in found:
            peak_ref[slot] = jnp.maximum(peak_ref[slot], peak)
            sum_ref[slot] += added

    def attempt(number, needed):
        loop(needed * (SLOTS // BESIDE), start)
        loop(needed * turns, attend_steps)
        above = peak_ref[0] * SCALE2 - base_ref[0]
        for slot in range(1, SLOTS):
            above = jnp.maximum(above, peak_ref[slot] * SCALE2 - base_ref[slot])
        return needed * jnp.where(jnp.max(above) > FAR, 1, 0)

    lax.fori_loop(0, 2, attempt, busy)

    def finish(step):
        for u in range(BESIDE):
            slot = step * BESIDE + u
            o_ref[rows_of(slot), :] = (sum_ref[slot, :, :DH] / sum_ref[slot, :, DH:]).astype(BF16)

    loop(busy * (SLOTS // BESIDE), finish)


def attend(lists, query, kv):
    most = SLOTS * (TILES // GROUP) + BESIDE
    return pl.pallas_call(
        attend_kernel,
        out_shape=jax.ShapeDtypeStruct(query.shape, BF16),
        in_specs=[
            pl.BlockSpec(memory_space=pltpu.SMEM),
            pl.BlockSpec(memory_space=pltpu.VMEM),
            pl.BlockSpec(memory_space=pltpu.VMEM),
        ],
        out_specs=pl.BlockSpec(memory_space=pltpu.VMEM),
        scratch_shapes=[
            pltpu.VMEM((TILES, DH, TILE), BF16),
            pltpu.VMEM((SLOTS, TILE, TILE), F32),
            pltpu.VMEM((SLOTS, TILE, TILE), F32),
            pltpu.VMEM((SLOTS, TILE, 2 * DH), F32),
            pltpu.SMEM((most,), jnp.int32),
            pltpu.SMEM((most,), jnp.int32),
            pltpu.SMEM((most,), jnp.int32),
        ],
        compiler_params=pltpu.CompilerParams(vmem_limit_bytes=40 * 1024 * 1024),
    )(lists, query, kv)


def collect_kernel(o_ref, attn, send, recv, x_send, x_recv):
    plane = lax.axis_index("heads")
    me = lax.axis_index("ctx")
    row, column, core = where_is(me)
    barrier = pltpu.get_barrier_semaphore()

    def greet(step, carry):
        pl.semaphore_signal(
            barrier, inc=1, device_id=(plane, lax.rem(me + step, FRAMES)), device_id_type=MESH
        )
        return carry

    lax.fori_loop(1, FRAMES, greet, 0)
    sides = (lax.rem(plane + 1, PLANES), lax.rem(plane + PLANES - 1, PLANES))
    for there in sides:
        pl.semaphore_signal(barrier, inc=1, device_id=(there, me), device_id_type=MESH)
    pl.semaphore_wait(barrier, FRAMES - 1 + 2)

    mine = jnp.minimum(row, HEADS_HERE - 1)
    goal = attn.at[plane * HEADS_HERE + mine, :, column * 2 + core]

    def back(step):
        there = lax.rem(me + step, FRAMES)
        return pltpu.make_async_remote_copy(
            src_ref=o_ref.at[:, there],
            dst_ref=goal,
            send_sem=send.at[step],
            recv_sem=recv.at[mine],
            device_id=(plane, there),
            device_id_type=MESH,
        )

    def start(step, carry):
        back(step).start()
        return carry

    def end(step, carry):
        back(step).wait_send()
        return carry

    working = row < HEADS_HERE

    @pl.when(working)
    def _():
        lax.fori_loop(1, FRAMES, start, 0)
        pltpu.make_async_copy(o_ref.at[:, me], goal, recv.at[mine]).start()

    cut = SLOTS // 2

    def near(head, side):
        part = attn.at[plane * HEADS_HERE + head]
        return pltpu.make_async_remote_copy(
            src_ref=part,
            dst_ref=part,
            send_sem=x_send.at[head, side],
            recv_sem=x_recv.at[head, side],
            device_id=(sides[side], me),
            device_id_type=MESH,
        )

    def far(head, side):
        part = attn.at[sides[1 - side] * HEADS_HERE + head]
        part = part.at[pl.ds(0, cut)] if side == 0 else part.at[pl.ds(cut, SLOTS - cut)]
        return pltpu.make_async_remote_copy(
            src_ref=part,
            dst_ref=part,
            send_sem=x_send.at[head, 2 + side],
            recv_sem=x_recv.at[head, 2 + side],
            device_id=(sides[side], me),
            device_id_type=MESH,
        )

    for head in range(HEADS_HERE):
        part = attn.at[plane * HEADS_HERE + head]
        pltpu.make_async_copy(part, part, recv.at[head]).wait()
        for side in range(2):
            near(head, side).start()
    for head in range(HEADS_HERE):
        for side in range(2):
            near(head, side).wait_recv()
            far(head, side).start()

    @pl.when(working)
    def _():
        lax.fori_loop(1, FRAMES, end, 0)

    for head in range(HEADS_HERE):
        for side in range(2):
            near(head, side).wait_send()
            far(head, side).wait()


def collect(attended):
    return pl.pallas_call(
        collect_kernel,
        out_shape=jax.ShapeDtypeStruct(
            (PLANES * HEADS_HERE, SLOTS, WORKERS, SPOTS, DH), BF16
        ),
        in_specs=[pl.BlockSpec(memory_space=pl.ANY)],
        out_specs=pl.BlockSpec(memory_space=pl.ANY),
        scratch_shapes=[
            pltpu.SemaphoreType.DMA((FRAMES,)),
            pltpu.SemaphoreType.DMA((HEADS_HERE,)),
            pltpu.SemaphoreType.DMA((HEADS_HERE, 4)),
            pltpu.SemaphoreType.DMA((HEADS_HERE, 4)),
        ],
        compiler_params=pltpu.CompilerParams(
            collective_id=1, has_side_effects=True, vmem_limit_bytes=4 * 1024 * 1024
        ),
    )(attended)


def project_kernel(attn_ref, w_ref, out_ref):
    rows = out_ref.shape[0]
    heads = attn_ref.shape[0]
    wide = jnp.concatenate([attn_ref[h, :rows, :] for h in range(heads)], axis=1)
    out_ref[...] = jnp.dot(wide, w_ref[...], preferred_element_type=F32).astype(BF16)


def project(attn, weight, rows):
    columns = weight.shape[1]
    block = 256
    heads = attn.shape[0]
    return pl.pallas_call(
        project_kernel,
        out_shape=jax.ShapeDtypeStruct((rows, columns), BF16),
        grid=(columns // block,),
        in_specs=[
            pl.BlockSpec((heads, attn.shape[1], DH), lambda i: (0, 0, 0)),
            pl.BlockSpec((weight.shape[0], block), lambda i: (0, i)),
        ],
        out_specs=pl.BlockSpec((rows, block), lambda i: (0, i)),
        compiler_params=pltpu.CompilerParams(vmem_limit_bytes=24 * 1024 * 1024),
    )(attn, weight)


def arrange_kernel(pattern_ref, mask_ref, q_ref, k_ref, v_ref, q_out, kv_out, list_ref):
    me = lax.axis_index("ctx")
    row, column, core = where_is(me)
    rows = q_ref.shape[0]
    for head in range(HEADS_HERE):
        columns = slice(head * DH, (head + 1) * DH)
        q_out[head] = q_ref[:, columns]
        kv_out[head, :rows, :] = k_ref[:, columns]
        kv_out[head, rows:, :] = v_ref[:, columns]

    pattern = pattern_ref[jnp.minimum(row, HEADS_HERE - 1)]
    masks = []
    tiles = [slot * WORKERS + column * 2 + core for slot in range(SLOTS)]
    for tile in tiles:
        masks.append(jnp.where(row < HEADS_HERE, mask_ref[pattern, pl.ds(tile, 1), :], 0))
    seen = jnp.concatenate(masks, axis=0) == 1
    seen = jnp.where(seen, 1.0, 0.0).astype(F32)
    down = lax.broadcasted_iota(jnp.int32, (TILES, TILES), 0)
    along = lax.broadcasted_iota(jnp.int32, (TILES, TILES), 1)
    both = (((1,), (1,)), ((), ()))
    upto = jnp.where(along <= down, 1.0, 0.0).astype(BF16)
    same = jnp.where(along == down, 1.0, 0.0).astype(BF16)
    rank = lax.dot_general(upto, seen.astype(BF16), both, preferred_element_type=F32)
    turned = lax.dot_general(same, seen.astype(BF16), both, preferred_element_type=F32)
    rank = rank.astype(jnp.int32)
    spot = jnp.where(turned > 0.5, rank - 1, -1)
    for slot in range(SLOTS):
        hit = spot[:, slot : slot + 1] == along
        listed = jnp.sum(jnp.where(hit, down, 0), axis=0, keepdims=True)
        spare = along[:1, :] >= rank[TILES - 1 :, slot : slot + 1]
        list_ref[slot : slot + 1, :] = jnp.where(spare, tiles[slot], listed)
    last = jnp.concatenate(
        [rank[TILES - 1 :, :], jnp.zeros((1, TILES - SLOTS), jnp.int32)], axis=1
    )
    list_ref[SLOTS : SLOTS + 1, :] = last


def arrange(head_pattern, tile_masks, queries, key_rows, value_rows):
    rows = queries.shape[0]
    return pl.pallas_call(
        arrange_kernel,
        out_shape=(
            jax.ShapeDtypeStruct((HEADS_HERE, rows, DH), BF16),
            jax.ShapeDtypeStruct((HEADS_HERE, 2 * rows, DH), BF16),
            jax.ShapeDtypeStruct((SLOTS + 1, TILES), jnp.int32),
        ),
        in_specs=[pl.BlockSpec(memory_space=pltpu.SMEM)]
        + [pl.BlockSpec(memory_space=pltpu.VMEM)] * 4,
        out_specs=(pl.BlockSpec(memory_space=pltpu.VMEM),) * 3,
        compiler_params=pltpu.CompilerParams(vmem_limit_bytes=16 * 1024 * 1024),
    )(head_pattern, tile_masks, queries, key_rows, value_rows)


def body(queries, key_rows, value_rows, out_weight, tile_masks, head_pattern):
    rows = queries.shape[0]
    q_parts, kv_parts, lists = arrange(head_pattern, tile_masks, queries, key_rows, value_rows)
    q_all, kv_all, w_all = spread(
        q_parts.reshape(HEADS_HERE, SLOTS, WORKERS, SPOTS, DH),
        kv_parts.reshape(HEADS_HERE, 2 * TILES, SPOTS, DH),
        out_weight,
    )
    attended = attend(
        lists, q_all.reshape(SLOTS * TILE, DH), kv_all.reshape(WORKERS, 2 * TILES * PIECE, DH)
    )
    attn = collect(attended.reshape(SLOTS, FRAMES, SPOTS, DH))
    attn = attn.reshape(PLANES * HEADS_HERE, rows, DH)
    return project(attn, w_all, rows)


def solution(mesh):
    placed = (
        P("ctx", "heads"),
        P("ctx", "heads"),
        P("ctx", "heads"),
        P("heads", None),
        P(),
        P("heads"),
    )
    return jax.shard_map(
        body, mesh=mesh, in_specs=placed, out_specs=P("ctx", "heads"), check_vma=False
    )
```

```python
import math

import jax
import jax.numpy as jnp
from jax import lax
from jax.experimental import pallas as pl
from jax.experimental.pallas import tpu as pltpu
from jax.sharding import PartitionSpec as P

MESH = pl.DeviceIdType.MESH
DH = 128
TILE = 128
SPOTS = 4
FRAMES = 32
TILES = 128
PLANES = 4
SIDE = 4
HEADS_HERE = 3
WORKERS = 2 * SIDE
SLOTS = TILES // WORKERS
PARTS = 4
PART = 2 * TILES // PARTS
PIECE = TILE // WORKERS
GROUP = 8
BESIDE = 4
FAR = 2.0**64
LOW = -1e30
SCALE2 = math.log2(math.e) / math.sqrt(DH)
BF16 = jnp.bfloat16
F32 = jnp.float32


def where_is(device):
    return lax.div(device, WORKERS), lax.rem(lax.div(device, 2), SIDE), lax.rem(device, 2)


def device_at(row, column, core):
    return (lax.rem(row, SIDE) * SIDE + lax.rem(column, SIDE)) * 2 + core


def spread_kernel(
    q_ref, kv_ref, w_ref, q_all, kv_all, w_all,
    q_send, q_recv, z_send, z_recv, y_send, y_recv, far_send, far_recv,
    core_send, core_recv, w_send, w_recv, w_core_send, w_core_recv, own_sem,
):
    plane = lax.axis_index("heads")
    me = lax.axis_index("ctx")
    row, column, core = where_is(me)
    working = row < HEADS_HERE
    own_row = jnp.minimum(row, HEADS_HERE - 1)
    depth = w_ref.shape[0]
    width = w_all.shape[1]
    sides = (1, SIDE - 1)

    barrier = pltpu.get_barrier_semaphore()

    def greet(step, carry):
        pl.semaphore_signal(
            barrier, inc=1, device_id=(plane, lax.rem(me + step, FRAMES)), device_id_type=MESH
        )
        return carry

    lax.fori_loop(1, FRAMES, greet, 0)
    for hop in range(1, PLANES):
        pl.semaphore_signal(
            barrier, inc=1, device_id=(lax.rem(plane + hop, PLANES), me), device_id_type=MESH
        )
    pl.semaphore_wait(barrier, FRAMES - 1 + PLANES - 1)

    def span(part):
        return pl.ds(part * PART, PART)

    own_copy = pltpu.make_async_copy(
        kv_ref.at[own_row], kv_all.at[column * 2 + core, :, 0], own_sem
    )

    def z_copy(part, hop):
        there = lax.rem(row + hop, SIDE)
        return pltpu.make_async_remote_copy(
            src_ref=kv_ref.at[there, span(part)],
            dst_ref=kv_all.at[column * 2 + core, span(part), hop],
            send_sem=z_send.at[part, hop],
            recv_sem=z_recv.at[part, hop],
            device_id=(plane, device_at(there, column, core)),
            device_id_type=MESH,
        )

    def piece(number, away):
        source = kv_all.at[lax.rem(column + away, SIDE) * 2 + core]
        if number == 0:
            return source.at[:, 0]
        return source.at[span(number - 1), pl.ds(1, SIDE - 1)]

    def y_copy(number, side):
        return pltpu.make_async_remote_copy(
            src_ref=kv_ref.at[own_row] if number == 0 else piece(number, 0),
            dst_ref=piece(number, 0),
            send_sem=y_send.at[number, side],
            recv_sem=y_recv.at[number, side],
            device_id=(plane, device_at(row, column + sides[side], core)),
            device_id_type=MESH,
        )

    def far_copy(number, side):
        source = kv_all.at[lax.rem(column + sides[1 - side], SIDE) * 2 + core]
        if number == 0:
            chunk = source.at[pl.ds(side * TILES, TILES), 0]
        else:
            chunk = source.at[
                pl.ds((number - 1) * PART + side * (PART // 2), PART // 2), pl.ds(1, SIDE - 1)
            ]
        return pltpu.make_async_remote_copy(
            src_ref=chunk,
            dst_ref=chunk,
            send_sem=far_send.at[number, side],
            recv_sem=far_recv.at[number, side],
            device_id=(plane, device_at(row, column + sides[side], core)),
            device_id_type=MESH,
        )

    def core_copy(number, away):
        return pltpu.make_async_remote_copy(
            src_ref=piece(number, away),
            dst_ref=piece(number, away),
            send_sem=core_send.at[number, away],
            recv_sem=core_recv,
            device_id=(plane, device_at(row, column, 1 - core)),
            device_id_type=MESH,
        )

    half = depth // 2

    def w_rows(source, part):
        return w_all.at[pl.ds(pl.multiple_of(source * depth + part * half, 16), half)]

    def w_copy(hop):
        there = lax.rem(plane + hop, PLANES)
        return pltpu.make_async_remote_copy(
            src_ref=w_ref.at[
                pl.ds(pl.multiple_of(core * half, 16), half),
                pl.ds(pl.multiple_of(there * width, 128), width),
            ],
            dst_ref=w_rows(plane, core),
            send_sem=w_send.at[hop],
            recv_sem=w_recv.at[hop],
            device_id=(there, me),
            device_id_type=MESH,
        )

    def w_core_copy(hop):
        rows = w_rows(lax.rem(plane + PLANES - hop, PLANES), core)
        return pltpu.make_async_remote_copy(
            src_ref=rows,
            dst_ref=rows,
            send_sem=w_core_send.at[hop],
            recv_sem=w_core_recv.at[hop],
            device_id=(plane, device_at(row, column, 1 - core)),
            device_id_type=MESH,
        )

    own_w = pltpu.make_async_copy(
        w_ref.at[:, pl.ds(pl.multiple_of(plane * width, 128), width)],
        w_all.at[pl.ds(pl.multiple_of(plane * depth, 128), depth)],
        w_recv.at[0],
    )

    def q_copy(step):
        there = lax.rem(me + step, FRAMES)
        row_there, column_there, core_there = where_is(there)
        return row_there < HEADS_HERE, pltpu.make_async_remote_copy(
            src_ref=q_ref.at[
                jnp.minimum(row_there, HEADS_HERE - 1), :, column_there * 2 + core_there
            ],
            dst_ref=q_all.at[:, me],
            send_sem=q_send.at[step],
            recv_sem=q_recv,
            device_id=(plane, there),
            device_id_type=MESH,
        )

    def to_rows(part, work):
        for hop in range(1, SIDE):

            @pl.when(lax.rem(row + hop, SIDE) < HEADS_HERE)
            def _():
                work(z_copy(part, hop))

    def send_q(step, carry):
        wanted, copy = q_copy(step)

        @pl.when(wanted)
        def _():
            copy.start()

        return carry

    def sent_q(step, carry):
        wanted, copy = q_copy(step)

        @pl.when(wanted)
        def _():
            copy.wait_send()

        return carry

    def send_small():
        for hop in range(1, PLANES):
            w_copy(hop).start()
        own_w.start()
        lax.fori_loop(1, FRAMES, send_q, 0)

    @pl.when(working)
    def _():
        own_copy.start()
        for side in range(2):
            y_copy(0, side).start()

    to_rows(0, lambda copy: copy.start())
    send_small()

    def next_rows(part):
        to_rows(part, lambda copy: copy.wait_send())
        if part + 1 < PARTS:
            to_rows(part + 1, lambda copy: copy.start())

    @pl.when(jnp.logical_not(working))
    def _():
        for part in range(PARTS):
            next_rows(part)

    @pl.when(working)
    def _():
        pltpu.make_async_copy(
            q_ref.at[own_row, :, column * 2 + core], q_all.at[:, me], q_recv
        ).start()
        own_copy.wait()
        core_copy(0, 0).start()

        def pass_on(number):
            for side in range(2):
                y_copy(number, side).wait_recv()
                far_copy(number, side).start()
            for side in range(2):
                core_copy(number, sides[1 - side]).start()

        for part in range(PARTS):
            next_rows(part)
            for hop in range(1, SIDE):
                landed = kv_all.at[column * 2 + core, span(part), hop]
                pltpu.make_async_copy(landed, landed, z_recv.at[part, hop]).wait()
            for side in range(2):
                y_copy(part + 1, side).start()
            core_copy(part + 1, 0).start()
            pass_on(part)
        pass_on(PARTS)
        for number in range(PARTS + 1):
            for side in range(2):
                far_copy(number, side).wait_recv()
            core_copy(number, 2).start()

    for hop in range(1, PLANES):
        w_copy(hop).wait_recv()
        w_core_copy(hop).start()

    @pl.when(working)
    def _():
        pltpu.make_async_copy(q_all, q_all, q_recv).wait()
        other = kv_all.at[pl.ds(0, SIDE)]
        pltpu.make_async_copy(other, other, core_recv).wait()
        for number in range(PARTS + 1):
            for side in range(2):
                y_copy(number, side).wait_send()
                far_copy(number, side).wait_send()
            for away in range(SIDE):
                core_copy(number, away).wait_send()

    own_w.wait()
    lax.fori_loop(1, FRAMES, sent_q, 0)
    for hop in range(1, PLANES):
        w_copy(hop).wait_send()
        w_core_copy(hop).wait()


def spread(q_parts, kv_parts, out_weight):
    depth, columns = out_weight.shape
    return pl.pallas_call(
        spread_kernel,
        out_shape=(
            jax.ShapeDtypeStruct((SLOTS, FRAMES, SPOTS, DH), BF16),
            jax.ShapeDtypeStruct((WORKERS, 2 * TILES, SIDE, SPOTS, DH), BF16),
            jax.ShapeDtypeStruct((depth * PLANES, columns // PLANES), BF16),
        ),
        in_specs=[pl.BlockSpec(memory_space=pl.ANY)] * 3,
        out_specs=(pl.BlockSpec(memory_space=pl.ANY),) * 3,
        scratch_shapes=[
            pltpu.SemaphoreType.DMA((FRAMES,)),
            pltpu.SemaphoreType.DMA,
            pltpu.SemaphoreType.DMA((PARTS, SIDE)),
            pltpu.SemaphoreType.DMA((PARTS, SIDE)),
            pltpu.SemaphoreType.DMA((PARTS + 1, 2)),
            pltpu.SemaphoreType.DMA((PARTS + 1, 2)),
            pltpu.SemaphoreType.DMA((PARTS + 1, 2)),
            pltpu.SemaphoreType.DMA((PARTS + 1, 2)),
            pltpu.SemaphoreType.DMA((PARTS + 1, SIDE)),
            pltpu.SemaphoreType.DMA,
            pltpu.SemaphoreType.DMA((PLANES,)),
            pltpu.SemaphoreType.DMA((PLANES,)),
            pltpu.SemaphoreType.DMA((PLANES,)),
            pltpu.SemaphoreType.DMA((PLANES,)),
            pltpu.SemaphoreType.DMA,
        ],
        compiler_params=pltpu.CompilerParams(
            collective_id=0, has_side_effects=True, vmem_limit_bytes=4 * 1024 * 1024
        ),
    )(q_parts, kv_parts, out_weight)


def attend_kernel(
    list_ref, q_ref, kv_ref, o_ref, keys_ref, values_ref, wide_ref, base_ref, peak_ref, sum_ref,
    slot_of, first_of, listed_of,
):
    _, column, core = where_is(lax.axis_index("ctx"))

    def loop(count, work):
        def one(step, carry):
            work(step)
            return carry

        lax.fori_loop(0, count, one, 0)

    def rows_of(slot):
        return pl.ds(pl.multiple_of(slot * TILE, TILE), TILE)

    def tile_at(tile):
        start = pl.multiple_of(tile * PIECE, PIECE)
        return jnp.concatenate(
            [kv_ref[worker, pl.ds(start, PIECE), :] for worker in range(WORKERS)], axis=0
        )

    def enlist(slot, total):
        count = list_ref[SLOTS, slot]
        steps = lax.div(count + GROUP - 1, GROUP)

        def one(step, carry):
            slot_of[total + step] = slot
            first_of[total + step] = step * GROUP
            listed_of[total + step] = count - step * GROUP
            return carry

        lax.fori_loop(0, steps, one, 0)
        return total + steps

    total = lax.fori_loop(0, SLOTS, enlist, 0)
    for spare in range(BESIDE - 1):
        slot_of[total + spare] = 0
        first_of[total + spare] = 0
        listed_of[total + spare] = 0
    turns = lax.div(total + BESIDE - 1, BESIDE)
    busy = jnp.where(total > 0, 1, 0)

    down = lax.broadcasted_iota(jnp.int32, (DH, TILE), 0)
    last_row = jnp.where(down == DH - 1, 1.0, 0.0).astype(BF16)
    other_rows = jnp.where(down == DH - 1, 0.0, 1.0).astype(BF16)
    ones = jnp.ones((TILE, DH), BF16)
    values_ref[TILES] = jnp.zeros((TILE, 2 * DH), BF16)

    def unpack(step):
        for u in range(GROUP):
            tile = step * GROUP + u
            keys = tile_at(tile).T
            keys_ref[tile, :DH, :] = keys
            keys_ref[tile, DH:, :] = keys * other_rows + last_row
            values_ref[tile, :, :DH] = tile_at(TILES + tile)
            values_ref[tile, :, DH:] = ones

    loop(busy * (TILES // GROUP), unpack)

    along = lax.broadcasted_iota(jnp.int32, (TILE, DH), 1)

    def widen(slot, base):
        query = q_ref[rows_of(slot), :].astype(F32) * SCALE2
        high = query.astype(BF16)
        low = query - high.astype(F32)
        return jnp.concatenate([high, jnp.where(along == DH - 1, -base, low).astype(BF16)], axis=1)

    def set_base(slot, base):
        base = jnp.broadcast_to(base, (TILE, TILE)).astype(BF16).astype(F32)
        base_ref[slot] = base
        wide_ref[rows_of(slot), :] = widen(slot, base)

    def own_base(step):
        for u in range(BESIDE):
            slot = step * BESIDE + u
            own = keys_ref[slot * WORKERS + column * 2 + core]
            scores = jnp.dot(widen(slot, 0.0), own, preferred_element_type=F32)
            set_base(slot, jnp.max(scores, axis=1, keepdims=True))

    loop(busy * (SLOTS // BESIDE), own_base)

    def scores_of(number):
        slot, first = slot_of[number], first_of[number]
        tiles = [list_ref[slot, first + u] for u in range(GROUP)]
        keys = jnp.concatenate([keys_ref[tile] for tile in tiles], axis=1)
        scores = jnp.dot(wide_ref[rows_of(slot), :], keys, preferred_element_type=F32)
        return slot, tiles, scores

    def attend_steps(step):
        found = []
        for beside in range(BESIDE):
            number = step * BESIDE + beside
            slot, tiles, scores = scores_of(number)
            listed = listed_of[number]
            values = [values_ref[jnp.where(u < listed, tiles[u], TILES)] for u in range(GROUP)]
            weights = jnp.exp2(scores).astype(BF16)
            added = jnp.dot(
                weights, jnp.concatenate(values, axis=0), preferred_element_type=F32
            )
            found.append((slot, added))
        for slot, added in found:
            sum_ref[slot] += added

    def peak_steps(step):
        for beside in range(BESIDE):
            slot, _, scores = scores_of(step * BESIDE + beside)
            peak = peak_ref[slot]
            for u in range(GROUP):
                peak = jnp.maximum(peak, scores[:, u * TILE : (u + 1) * TILE])
            peak_ref[slot] = peak

    def attempt(number, needed):
        def clear(slot):
            sum_ref[slot] = jnp.zeros((TILE, 2 * DH), F32)
            peak_ref[slot] = jnp.full((TILE, TILE), LOW, F32)

        loop(needed * SLOTS, clear)
        loop(needed * turns, attend_steps)
        beyond = jnp.zeros((TILE, DH), F32)
        for slot in range(SLOTS):
            beyond = jnp.where(sum_ref[slot, :, DH:] <= FAR, beyond, 1.0)
        again = needed * jnp.where(jnp.max(beyond) > 0.0, 1, 0)
        loop(again * turns, peak_steps)

        def rebase(slot):
            above = jnp.max(peak_ref[slot], axis=1, keepdims=True)
            set_base(slot, base_ref[slot] + above)

        loop(again * SLOTS, rebase)
        return again

    lax.fori_loop(0, 2, attempt, busy)

    def finish(step):
        for u in range(BESIDE):
            slot = step * BESIDE + u
            o_ref[rows_of(slot), :] = (sum_ref[slot, :, :DH] / sum_ref[slot, :, DH:]).astype(BF16)

    loop(busy * (SLOTS // BESIDE), finish)


def attend(lists, query, kv):
    most = SLOTS * (TILES // GROUP) + BESIDE
    return pl.pallas_call(
        attend_kernel,
        out_shape=jax.ShapeDtypeStruct(query.shape, BF16),
        in_specs=[
            pl.BlockSpec(memory_space=pltpu.SMEM),
            pl.BlockSpec(memory_space=pltpu.VMEM),
            pl.BlockSpec(memory_space=pltpu.VMEM),
        ],
        out_specs=pl.BlockSpec(memory_space=pltpu.VMEM),
        scratch_shapes=[
            pltpu.VMEM((TILES, 2 * DH, TILE), BF16),
            pltpu.VMEM((TILES + 1, TILE, 2 * DH), BF16),
            pltpu.VMEM((SLOTS * TILE, 2 * DH), BF16),
            pltpu.VMEM((SLOTS, TILE, TILE), F32),
            pltpu.VMEM((SLOTS, TILE, TILE), F32),
            pltpu.VMEM((SLOTS, TILE, 2 * DH), F32),
            pltpu.SMEM((most,), jnp.int32),
            pltpu.SMEM((most,), jnp.int32),
            pltpu.SMEM((most,), jnp.int32),
        ],
        compiler_params=pltpu.CompilerParams(vmem_limit_bytes=40 * 1024 * 1024),
    )(lists, query, kv)


def collect_kernel(o_ref, attn, send, recv, x_send, x_recv):
    plane = lax.axis_index("heads")
    me = lax.axis_index("ctx")
    row, column, core = where_is(me)
    barrier = pltpu.get_barrier_semaphore()

    def greet(step, carry):
        pl.semaphore_signal(
            barrier, inc=1, device_id=(plane, lax.rem(me + step, FRAMES)), device_id_type=MESH
        )
        return carry

    lax.fori_loop(1, FRAMES, greet, 0)
    sides = (lax.rem(plane + 1, PLANES), lax.rem(plane + PLANES - 1, PLANES))
    for there in sides:
        pl.semaphore_signal(barrier, inc=1, device_id=(there, me), device_id_type=MESH)
    pl.semaphore_wait(barrier, FRAMES - 1 + 2)

    mine = jnp.minimum(row, HEADS_HERE - 1)
    goal = attn.at[plane * HEADS_HERE + mine, :, column * 2 + core]

    def back(step):
        there = lax.rem(me + step, FRAMES)
        return pltpu.make_async_remote_copy(
            src_ref=o_ref.at[:, there],
            dst_ref=goal,
            send_sem=send.at[step],
            recv_sem=recv.at[mine],
            device_id=(plane, there),
            device_id_type=MESH,
        )

    def start(step, carry):
        back(step).start()
        return carry

    def end(step, carry):
        back(step).wait_send()
        return carry

    working = row < HEADS_HERE

    @pl.when(working)
    def _():
        lax.fori_loop(1, FRAMES, start, 0)
        pltpu.make_async_copy(o_ref.at[:, me], goal, recv.at[mine]).start()

    cut = SLOTS // 2

    def near(head, side):
        part = attn.at[plane * HEADS_HERE + head]
        return pltpu.make_async_remote_copy(
            src_ref=part,
            dst_ref=part,
            send_sem=x_send.at[head, side],
            recv_sem=x_recv.at[head, side],
            device_id=(sides[side], me),
            device_id_type=MESH,
        )

    def far(head, side):
        part = attn.at[sides[1 - side] * HEADS_HERE + head]
        part = part.at[pl.ds(0, cut)] if side == 0 else part.at[pl.ds(cut, SLOTS - cut)]
        return pltpu.make_async_remote_copy(
            src_ref=part,
            dst_ref=part,
            send_sem=x_send.at[head, 2 + side],
            recv_sem=x_recv.at[head, 2 + side],
            device_id=(sides[side], me),
            device_id_type=MESH,
        )

    for head in range(HEADS_HERE):
        part = attn.at[plane * HEADS_HERE + head]
        pltpu.make_async_copy(part, part, recv.at[head]).wait()
        for side in range(2):
            near(head, side).start()
    for head in range(HEADS_HERE):
        for side in range(2):
            near(head, side).wait_recv()
            far(head, side).start()

    @pl.when(working)
    def _():
        lax.fori_loop(1, FRAMES, end, 0)

    for head in range(HEADS_HERE):
        for side in range(2):
            near(head, side).wait_send()
            far(head, side).wait()


def collect(attended):
    return pl.pallas_call(
        collect_kernel,
        out_shape=jax.ShapeDtypeStruct(
            (PLANES * HEADS_HERE, SLOTS, WORKERS, SPOTS, DH), BF16
        ),
        in_specs=[pl.BlockSpec(memory_space=pl.ANY)],
        out_specs=pl.BlockSpec(memory_space=pl.ANY),
        scratch_shapes=[
            pltpu.SemaphoreType.DMA((FRAMES,)),
            pltpu.SemaphoreType.DMA((HEADS_HERE,)),
            pltpu.SemaphoreType.DMA((HEADS_HERE, 4)),
            pltpu.SemaphoreType.DMA((HEADS_HERE, 4)),
        ],
        compiler_params=pltpu.CompilerParams(
            collective_id=1, has_side_effects=True, vmem_limit_bytes=4 * 1024 * 1024
        ),
    )(attended)


def project_kernel(attn_ref, w_ref, out_ref):
    rows = out_ref.shape[0]
    heads = attn_ref.shape[0]
    wide = jnp.concatenate([attn_ref[h, :rows, :] for h in range(heads)], axis=1)
    out_ref[...] = jnp.dot(wide, w_ref[...], preferred_element_type=F32).astype(BF16)


def project(attn, weight, rows):
    columns = weight.shape[1]
    block = 256
    heads = attn.shape[0]
    return pl.pallas_call(
        project_kernel,
        out_shape=jax.ShapeDtypeStruct((rows, columns), BF16),
        grid=(columns // block,),
        in_specs=[
            pl.BlockSpec((heads, attn.shape[1], DH), lambda i: (0, 0, 0)),
            pl.BlockSpec((weight.shape[0], block), lambda i: (0, i)),
        ],
        out_specs=pl.BlockSpec((rows, block), lambda i: (0, i)),
        compiler_params=pltpu.CompilerParams(vmem_limit_bytes=24 * 1024 * 1024),
    )(attn, weight)


def arrange_kernel(pattern_ref, mask_ref, q_ref, k_ref, v_ref, q_out, kv_out, list_ref):
    me = lax.axis_index("ctx")
    row, column, core = where_is(me)
    rows = q_ref.shape[0]
    for head in range(HEADS_HERE):
        columns = slice(head * DH, (head + 1) * DH)
        q_out[head] = q_ref[:, columns]
        kv_out[head, :rows, :] = k_ref[:, columns]
        kv_out[head, rows:, :] = v_ref[:, columns]

    pattern = pattern_ref[jnp.minimum(row, HEADS_HERE - 1)]
    masks = []
    tiles = [slot * WORKERS + column * 2 + core for slot in range(SLOTS)]
    for tile in tiles:
        masks.append(jnp.where(row < HEADS_HERE, mask_ref[pattern, pl.ds(tile, 1), :], 0))
    seen = jnp.concatenate(masks, axis=0) == 1
    seen = jnp.where(seen, 1.0, 0.0).astype(F32)
    down = lax.broadcasted_iota(jnp.int32, (TILES, TILES), 0)
    along = lax.broadcasted_iota(jnp.int32, (TILES, TILES), 1)
    both = (((1,), (1,)), ((), ()))
    upto = jnp.where(along <= down, 1.0, 0.0).astype(BF16)
    same = jnp.where(along == down, 1.0, 0.0).astype(BF16)
    rank = lax.dot_general(upto, seen.astype(BF16), both, preferred_element_type=F32)
    turned = lax.dot_general(same, seen.astype(BF16), both, preferred_element_type=F32)
    rank = rank.astype(jnp.int32)
    spot = jnp.where(turned > 0.5, rank - 1, -1)
    for slot in range(SLOTS):
        hit = spot[:, slot : slot + 1] == along
        listed = jnp.sum(jnp.where(hit, down, 0), axis=0, keepdims=True)
        spare = along[:1, :] >= rank[TILES - 1 :, slot : slot + 1]
        list_ref[slot : slot + 1, :] = jnp.where(spare, tiles[slot], listed)
    last = jnp.concatenate(
        [rank[TILES - 1 :, :], jnp.zeros((1, TILES - SLOTS), jnp.int32)], axis=1
    )
    list_ref[SLOTS : SLOTS + 1, :] = last


def arrange(head_pattern, tile_masks, queries, key_rows, value_rows):
    rows = queries.shape[0]
    return pl.pallas_call(
        arrange_kernel,
        out_shape=(
            jax.ShapeDtypeStruct((HEADS_HERE, rows, DH), BF16),
            jax.ShapeDtypeStruct((HEADS_HERE, 2 * rows, DH), BF16),
            jax.ShapeDtypeStruct((SLOTS + 1, TILES), jnp.int32),
        ),
        in_specs=[pl.BlockSpec(memory_space=pltpu.SMEM)]
        + [pl.BlockSpec(memory_space=pltpu.VMEM)] * 4,
        out_specs=(pl.BlockSpec(memory_space=pltpu.VMEM),) * 3,
        compiler_params=pltpu.CompilerParams(vmem_limit_bytes=16 * 1024 * 1024),
    )(head_pattern, tile_masks, queries, key_rows, value_rows)


def body(queries, key_rows, value_rows, out_weight, tile_masks, head_pattern):
    rows = queries.shape[0]
    q_parts, kv_parts, lists = arrange(head_pattern, tile_masks, queries, key_rows, value_rows)
    q_all, kv_all, w_all = spread(
        q_parts.reshape(HEADS_HERE, SLOTS, WORKERS, SPOTS, DH),
        kv_parts.reshape(HEADS_HERE, 2 * TILES, SPOTS, DH),
        out_weight,
    )
    attended = attend(
        lists, q_all.reshape(SLOTS * TILE, DH), kv_all.reshape(WORKERS, 2 * TILES * PIECE, DH)
    )
    attn = collect(attended.reshape(SLOTS, FRAMES, SPOTS, DH))
    attn = attn.reshape(PLANES * HEADS_HERE, rows, DH)
    return project(attn, w_all, rows)


def solution(mesh):
    placed = (
        P("ctx", "heads"),
        P("ctx", "heads"),
        P("ctx", "heads"),
        P("heads", None),
        P(),
        P("heads"),
    )
    return jax.shard_map(
        body, mesh=mesh, in_specs=placed, out_specs=P("ctx", "heads"), check_vma=False
    )
```

```python
import math

import jax
import jax.numpy as jnp
from jax import lax
from jax.experimental import pallas as pl
from jax.experimental.pallas import tpu as pltpu
from jax.sharding import PartitionSpec as P

MESH = pl.DeviceIdType.MESH
DH = 128
TILE = 128
SPOTS = 4
FRAMES = 32
TILES = 128
PLANES = 4
SIDE = 4
HEADS_HERE = 3
WORKERS = 2 * SIDE
SLOTS = TILES // WORKERS
PARTS = 4
PART = 2 * TILES // PARTS
PIECE = TILE // WORKERS
GROUP = 8
BESIDE = 4
FAR = 2.0**64
LOW = -1e30
SCALE2 = math.log2(math.e) / math.sqrt(DH)
BF16 = jnp.bfloat16
F32 = jnp.float32


def where_is(device):
    return lax.div(device, WORKERS), lax.rem(lax.div(device, 2), SIDE), lax.rem(device, 2)


def device_at(row, column, core):
    return (lax.rem(row, SIDE) * SIDE + lax.rem(column, SIDE)) * 2 + core


def spread_kernel(
    q_ref, kv_ref, w_ref, q_all, kv_all, w_all,
    q_send, q_recv, z_send, z_recv, y_send, y_recv, far_send, far_recv,
    core_send, core_recv, w_send, w_recv, w_core_send, w_core_recv, own_sem,
):
    plane = lax.axis_index("heads")
    me = lax.axis_index("ctx")
    row, column, core = where_is(me)
    working = row < HEADS_HERE
    own_row = jnp.minimum(row, HEADS_HERE - 1)
    depth = w_ref.shape[0]
    width = w_all.shape[1]
    sides = (1, SIDE - 1)

    barrier = pltpu.get_barrier_semaphore()

    def greet(step, carry):
        pl.semaphore_signal(
            barrier, inc=1, device_id=(plane, lax.rem(me + step, FRAMES)), device_id_type=MESH
        )
        return carry

    lax.fori_loop(1, FRAMES, greet, 0)
    for hop in range(1, PLANES):
        pl.semaphore_signal(
            barrier, inc=1, device_id=(lax.rem(plane + hop, PLANES), me), device_id_type=MESH
        )
    pl.semaphore_wait(barrier, FRAMES - 1 + PLANES - 1)

    def span(part):
        return pl.ds(part * PART, PART)

    own_copy = pltpu.make_async_copy(
        kv_ref.at[own_row], kv_all.at[column * 2 + core, :, 0], own_sem
    )

    def z_copy(part, hop):
        there = lax.rem(row + hop, SIDE)
        return pltpu.make_async_remote_copy(
            src_ref=kv_ref.at[there, span(part)],
            dst_ref=kv_all.at[column * 2 + core, span(part), hop],
            send_sem=z_send.at[part, hop],
            recv_sem=z_recv.at[part, hop],
            device_id=(plane, device_at(there, column, core)),
            device_id_type=MESH,
        )

    def piece(number, away):
        source = kv_all.at[lax.rem(column + away, SIDE) * 2 + core]
        if number == 0:
            return source.at[:, 0]
        return source.at[span(number - 1), pl.ds(1, SIDE - 1)]

    def y_copy(number, side):
        return pltpu.make_async_remote_copy(
            src_ref=kv_ref.at[own_row] if number == 0 else piece(number, 0),
            dst_ref=piece(number, 0),
            send_sem=y_send.at[number, side],
            recv_sem=y_recv.at[number, side],
            device_id=(plane, device_at(row, column + sides[side], core)),
            device_id_type=MESH,
        )

    def far_copy(number, side):
        source = kv_all.at[lax.rem(column + sides[1 - side], SIDE) * 2 + core]
        if number == 0:
            chunk = source.at[pl.ds(side * TILES, TILES), 0]
        else:
            chunk = source.at[
                pl.ds((number - 1) * PART + side * (PART // 2), PART // 2), pl.ds(1, SIDE - 1)
            ]
        return pltpu.make_async_remote_copy(
            src_ref=chunk,
            dst_ref=chunk,
            send_sem=far_send.at[number, side],
            recv_sem=far_recv.at[number, side],
            device_id=(plane, device_at(row, column + sides[side], core)),
            device_id_type=MESH,
        )

    def core_copy(number, away):
        return pltpu.make_async_remote_copy(
            src_ref=piece(number, away),
            dst_ref=piece(number, away),
            send_sem=core_send.at[number, away],
            recv_sem=core_recv,
            device_id=(plane, device_at(row, column, 1 - core)),
            device_id_type=MESH,
        )

    half = depth // 2

    def w_rows(source, part):
        return w_all.at[pl.ds(pl.multiple_of(source * depth + part * half, 16), half)]

    def w_copy(hop):
        there = lax.rem(plane + hop, PLANES)
        return pltpu.make_async_remote_copy(
            src_ref=w_ref.at[
                pl.ds(pl.multiple_of(core * half, 16), half),
                pl.ds(pl.multiple_of(there * width, 128), width),
            ],
            dst_ref=w_rows(plane, core),
            send_sem=w_send.at[hop],
            recv_sem=w_recv.at[hop],
            device_id=(there, me),
            device_id_type=MESH,
        )

    def w_core_copy(hop):
        rows = w_rows(lax.rem(plane + PLANES - hop, PLANES), core)
        return pltpu.make_async_remote_copy(
            src_ref=rows,
            dst_ref=rows,
            send_sem=w_core_send.at[hop],
            recv_sem=w_core_recv.at[hop],
            device_id=(plane, device_at(row, column, 1 - core)),
            device_id_type=MESH,
        )

    own_w = pltpu.make_async_copy(
        w_ref.at[:, pl.ds(pl.multiple_of(plane * width, 128), width)],
        w_all.at[pl.ds(pl.multiple_of(plane * depth, 128), depth)],
        w_recv.at[0],
    )

    def q_copy(step):
        there = lax.rem(me + step, FRAMES)
        row_there, column_there, core_there = where_is(there)
        return row_there < HEADS_HERE, pltpu.make_async_remote_copy(
            src_ref=q_ref.at[
                jnp.minimum(row_there, HEADS_HERE - 1), :, column_there * 2 + core_there
            ],
            dst_ref=q_all.at[:, me],
            send_sem=q_send.at[step],
            recv_sem=q_recv,
            device_id=(plane, there),
            device_id_type=MESH,
        )

    def to_rows(part, work):
        for hop in range(1, SIDE):

            @pl.when(lax.rem(row + hop, SIDE) < HEADS_HERE)
            def _():
                work(z_copy(part, hop))

    def send_q(step, carry):
        wanted, copy = q_copy(step)

        @pl.when(wanted)
        def _():
            copy.start()

        return carry

    def sent_q(step, carry):
        wanted, copy = q_copy(step)

        @pl.when(wanted)
        def _():
            copy.wait_send()

        return carry

    def send_small():
        for hop in range(1, PLANES):
            w_copy(hop).start()
        own_w.start()
        lax.fori_loop(1, FRAMES, send_q, 0)

    @pl.when(working)
    def _():
        own_copy.start()
        for side in range(2):
            y_copy(0, side).start()

    to_rows(0, lambda copy: copy.start())
    send_small()

    def next_rows(part):
        to_rows(part, lambda copy: copy.wait_send())
        if part + 1 < PARTS:
            to_rows(part + 1, lambda copy: copy.start())

    @pl.when(jnp.logical_not(working))
    def _():
        for part in range(PARTS):
            next_rows(part)

    @pl.when(working)
    def _():
        pltpu.make_async_copy(
            q_ref.at[own_row, :, column * 2 + core], q_all.at[:, me], q_recv
        ).start()
        own_copy.wait()
        core_copy(0, 0).start()

        def pass_on(number):
            for side in range(2):
                y_copy(number, side).wait_recv()
                far_copy(number, side).start()
            for side in range(2):
                core_copy(number, sides[1 - side]).start()

        for part in range(PARTS):
            next_rows(part)
            for hop in range(1, SIDE):
                landed = kv_all.at[column * 2 + core, span(part), hop]
                pltpu.make_async_copy(landed, landed, z_recv.at[part, hop]).wait()
            for side in range(2):
                y_copy(part + 1, side).start()
            core_copy(part + 1, 0).start()
            pass_on(part)
        pass_on(PARTS)
        for number in range(PARTS + 1):
            for side in range(2):
                far_copy(number, side).wait_recv()
            core_copy(number, 2).start()

    for hop in range(1, PLANES):
        w_copy(hop).wait_recv()
        w_core_copy(hop).start()

    @pl.when(working)
    def _():
        pltpu.make_async_copy(q_all, q_all, q_recv).wait()
        other = kv_all.at[pl.ds(0, SIDE)]
        pltpu.make_async_copy(other, other, core_recv).wait()
        for number in range(PARTS + 1):
            for side in range(2):
                y_copy(number, side).wait_send()
                far_copy(number, side).wait_send()
            for away in range(SIDE):
                core_copy(number, away).wait_send()

    own_w.wait()
    lax.fori_loop(1, FRAMES, sent_q, 0)
    for hop in range(1, PLANES):
        w_copy(hop).wait_send()
        w_core_copy(hop).wait()


def spread(q_parts, kv_parts, out_weight):
    depth, columns = out_weight.shape
    return pl.pallas_call(
        spread_kernel,
        out_shape=(
            jax.ShapeDtypeStruct((SLOTS, FRAMES, SPOTS, DH), BF16),
            jax.ShapeDtypeStruct((WORKERS, 2 * TILES, SIDE, SPOTS, DH), BF16),
            jax.ShapeDtypeStruct((depth * PLANES, columns // PLANES), BF16),
        ),
        in_specs=[pl.BlockSpec(memory_space=pl.ANY)] * 3,
        out_specs=(pl.BlockSpec(memory_space=pl.ANY),) * 3,
        scratch_shapes=[
            pltpu.SemaphoreType.DMA((FRAMES,)),
            pltpu.SemaphoreType.DMA,
            pltpu.SemaphoreType.DMA((PARTS, SIDE)),
            pltpu.SemaphoreType.DMA((PARTS, SIDE)),
            pltpu.SemaphoreType.DMA((PARTS + 1, 2)),
            pltpu.SemaphoreType.DMA((PARTS + 1, 2)),
            pltpu.SemaphoreType.DMA((PARTS + 1, 2)),
            pltpu.SemaphoreType.DMA((PARTS + 1, 2)),
            pltpu.SemaphoreType.DMA((PARTS + 1, SIDE)),
            pltpu.SemaphoreType.DMA,
            pltpu.SemaphoreType.DMA((PLANES,)),
            pltpu.SemaphoreType.DMA((PLANES,)),
            pltpu.SemaphoreType.DMA((PLANES,)),
            pltpu.SemaphoreType.DMA((PLANES,)),
            pltpu.SemaphoreType.DMA,
        ],
        compiler_params=pltpu.CompilerParams(
            collective_id=0, has_side_effects=True, vmem_limit_bytes=4 * 1024 * 1024
        ),
    )(q_parts, kv_parts, out_weight)


def attend_kernel(
    list_ref, q_ref, kv_ref, o_ref, keys_ref, values_ref, base_ref, peak_ref, sum_ref,
    slot_of, first_of, listed_of,
):
    _, column, core = where_is(lax.axis_index("ctx"))

    def loop(count, work):
        def one(step, carry):
            work(step)
            return carry

        lax.fori_loop(0, count, one, 0)

    def rows_of(slot):
        return pl.ds(pl.multiple_of(slot * TILE, TILE), TILE)

    def tile_at(tile):
        start = pl.multiple_of(tile * PIECE, PIECE)
        return jnp.concatenate(
            [kv_ref[worker, pl.ds(start, PIECE), :] for worker in range(WORKERS)], axis=0
        )

    def enlist(slot, total):
        count = list_ref[SLOTS, slot]
        steps = lax.div(count + GROUP - 1, GROUP)

        def one(step, carry):
            slot_of[total + step] = slot
            first_of[total + step] = step * GROUP
            listed_of[total + step] = count - step * GROUP
            return carry

        lax.fori_loop(0, steps, one, 0)
        return total + steps

    total = lax.fori_loop(0, SLOTS, enlist, 0)
    for spare in range(BESIDE - 1):
        slot_of[total + spare] = 0
        first_of[total + spare] = 0
        listed_of[total + spare] = 0
    turns = lax.div(total + BESIDE - 1, BESIDE)
    busy = jnp.where(total > 0, 1, 0)

    values_ref[TILES] = jnp.zeros((TILE, DH), BF16)

    def unpack(step):
        for u in range(GROUP):
            tile = step * GROUP + u
            keys_ref[tile] = tile_at(tile).T
            values_ref[tile] = tile_at(TILES + tile)

    loop(busy * (TILES // GROUP), unpack)

    def set_base(slot, base):
        base_ref[slot] = jnp.broadcast_to(base * SCALE2, (TILE, TILE))

    def own_base(step):
        for u in range(BESIDE):
            slot = step * BESIDE + u
            own = keys_ref[slot * WORKERS + column * 2 + core]
            scores = jnp.dot(q_ref[rows_of(slot), :], own, preferred_element_type=F32)
            set_base(slot, jnp.max(scores, axis=1, keepdims=True))

    loop(busy * (SLOTS // BESIDE), own_base)

    def tiles_of(number):
        slot, first = slot_of[number], first_of[number]
        return slot, [list_ref[slot, first + u] for u in range(GROUP)]

    def scores_of(slot, tiles):
        keys = jnp.concatenate([keys_ref[tile] for tile in tiles], axis=1)
        return jnp.dot(q_ref[rows_of(slot), :], keys, preferred_element_type=F32)

    def attend_steps(step):
        found = []
        for beside in range(BESIDE):
            number = step * BESIDE + beside
            slot, tiles = tiles_of(number)
            listed = listed_of[number]
            base = base_ref[slot]
            base = jnp.concatenate([base, base], axis=1)
            weights, values = [], []
            for u in range(0, GROUP, 2):
                scores = scores_of(slot, tiles[u : u + 2])
                weights.append(jnp.exp2(scores * SCALE2 - base).astype(BF16))
            for u in range(GROUP):
                value = values_ref[jnp.where(u < listed, tiles[u], TILES)]
                ones = jnp.where(u < listed, 1.0, 0.0).astype(BF16)
                ones = jnp.broadcast_to(ones, (TILE, DH))
                values.append(jnp.concatenate([value, ones], axis=1))
            added = jnp.dot(
                jnp.concatenate(weights, axis=1),
                jnp.concatenate(values, axis=0),
                preferred_element_type=F32,
            )
            found.append((slot, added))
        for slot, added in found:
            sum_ref[slot] += added

    def peak_steps(step):
        for beside in range(BESIDE):
            slot, tiles = tiles_of(step * BESIDE + beside)
            scores = scores_of(slot, tiles)
            peak = peak_ref[slot]
            for u in range(GROUP):
                peak = jnp.maximum(peak, scores[:, u * TILE : (u + 1) * TILE])
            peak_ref[slot] = peak

    def attempt(number, needed):
        def clear(slot):
            sum_ref[slot] = jnp.zeros((TILE, 2 * DH), F32)
            peak_ref[slot] = jnp.full((TILE, TILE), LOW, F32)

        loop(needed * SLOTS, clear)
        loop(needed * turns, attend_steps)
        beyond = jnp.zeros((TILE, DH), F32)
        for slot in range(SLOTS):
            beyond = jnp.where(sum_ref[slot, :, DH:] <= FAR, beyond, 1.0)
        again = needed * jnp.where(jnp.max(beyond) > 0.0, 1, 0)
        loop(again * turns, peak_steps)

        def rebase(slot):
            set_base(slot, jnp.max(peak_ref[slot], axis=1, keepdims=True))

        loop(again * SLOTS, rebase)
        return again

    lax.fori_loop(0, 2, attempt, busy)

    def finish(step):
        for u in range(BESIDE):
            slot = step * BESIDE + u
            o_ref[rows_of(slot), :] = (sum_ref[slot, :, :DH] / sum_ref[slot, :, DH:]).astype(BF16)

    loop(busy * (SLOTS // BESIDE), finish)


def attend(lists, query, kv):
    most = SLOTS * (TILES // GROUP) + BESIDE
    return pl.pallas_call(
        attend_kernel,
        out_shape=jax.ShapeDtypeStruct(query.shape, BF16),
        in_specs=[
            pl.BlockSpec(memory_space=pltpu.SMEM),
            pl.BlockSpec(memory_space=pltpu.VMEM),
            pl.BlockSpec(memory_space=pltpu.VMEM),
        ],
        out_specs=pl.BlockSpec(memory_space=pltpu.VMEM),
        scratch_shapes=[
            pltpu.VMEM((TILES, DH, TILE), BF16),
            pltpu.VMEM((TILES + 1, TILE, DH), BF16),
            pltpu.VMEM((SLOTS, TILE, TILE), F32),
            pltpu.VMEM((SLOTS, TILE, TILE), F32),
            pltpu.VMEM((SLOTS, TILE, 2 * DH), F32),
            pltpu.SMEM((most,), jnp.int32),
            pltpu.SMEM((most,), jnp.int32),
            pltpu.SMEM((most,), jnp.int32),
        ],
        compiler_params=pltpu.CompilerParams(vmem_limit_bytes=40 * 1024 * 1024),
    )(lists, query, kv)


def collect_kernel(o_ref, attn, send, recv, x_send, x_recv):
    plane = lax.axis_index("heads")
    me = lax.axis_index("ctx")
    row, column, core = where_is(me)
    barrier = pltpu.get_barrier_semaphore()

    def greet(step, carry):
        pl.semaphore_signal(
            barrier, inc=1, device_id=(plane, lax.rem(me + step, FRAMES)), device_id_type=MESH
        )
        return carry

    lax.fori_loop(1, FRAMES, greet, 0)
    sides = (lax.rem(plane + 1, PLANES), lax.rem(plane + PLANES - 1, PLANES))
    for there in sides:
        pl.semaphore_signal(barrier, inc=1, device_id=(there, me), device_id_type=MESH)
    pl.semaphore_wait(barrier, FRAMES - 1 + 2)

    mine = jnp.minimum(row, HEADS_HERE - 1)
    goal = attn.at[plane * HEADS_HERE + mine, :, column * 2 + core]

    def back(step):
        there = lax.rem(me + step, FRAMES)
        return pltpu.make_async_remote_copy(
            src_ref=o_ref.at[:, there],
            dst_ref=goal,
            send_sem=send.at[step],
            recv_sem=recv.at[mine],
            device_id=(plane, there),
            device_id_type=MESH,
        )

    def start(step, carry):
        back(step).start()
        return carry

    def end(step, carry):
        back(step).wait_send()
        return carry

    working = row < HEADS_HERE

    @pl.when(working)
    def _():
        lax.fori_loop(1, FRAMES, start, 0)
        pltpu.make_async_copy(o_ref.at[:, me], goal, recv.at[mine]).start()

    cut = SLOTS // 2

    def near(head, side):
        part = attn.at[plane * HEADS_HERE + head]
        return pltpu.make_async_remote_copy(
            src_ref=part,
            dst_ref=part,
            send_sem=x_send.at[head, side],
            recv_sem=x_recv.at[head, side],
            device_id=(sides[side], me),
            device_id_type=MESH,
        )

    def far(head, side):
        part = attn.at[sides[1 - side] * HEADS_HERE + head]
        part = part.at[pl.ds(0, cut)] if side == 0 else part.at[pl.ds(cut, SLOTS - cut)]
        return pltpu.make_async_remote_copy(
            src_ref=part,
            dst_ref=part,
            send_sem=x_send.at[head, 2 + side],
            recv_sem=x_recv.at[head, 2 + side],
            device_id=(sides[side], me),
            device_id_type=MESH,
        )

    for head in range(HEADS_HERE):
        part = attn.at[plane * HEADS_HERE + head]
        pltpu.make_async_copy(part, part, recv.at[head]).wait()
        for side in range(2):
            near(head, side).start()
    for head in range(HEADS_HERE):
        for side in range(2):
            near(head, side).wait_recv()
            far(head, side).start()

    @pl.when(working)
    def _():
        lax.fori_loop(1, FRAMES, end, 0)

    for head in range(HEADS_HERE):
        for side in range(2):
            near(head, side).wait_send()
            far(head, side).wait()


def collect(attended):
    return pl.pallas_call(
        collect_kernel,
        out_shape=jax.ShapeDtypeStruct(
            (PLANES * HEADS_HERE, SLOTS, WORKERS, SPOTS, DH), BF16
        ),
        in_specs=[pl.BlockSpec(memory_space=pl.ANY)],
        out_specs=pl.BlockSpec(memory_space=pl.ANY),
        scratch_shapes=[
            pltpu.SemaphoreType.DMA((FRAMES,)),
            pltpu.SemaphoreType.DMA((HEADS_HERE,)),
            pltpu.SemaphoreType.DMA((HEADS_HERE, 4)),
            pltpu.SemaphoreType.DMA((HEADS_HERE, 4)),
        ],
        compiler_params=pltpu.CompilerParams(
            collective_id=1, has_side_effects=True, vmem_limit_bytes=4 * 1024 * 1024
        ),
    )(attended)


def project_kernel(attn_ref, w_ref, out_ref):
    rows = out_ref.shape[0]
    heads = attn_ref.shape[0]
    wide = jnp.concatenate([attn_ref[h, :rows, :] for h in range(heads)], axis=1)
    out_ref[...] = jnp.dot(wide, w_ref[...], preferred_element_type=F32).astype(BF16)


def project(attn, weight, rows):
    columns = weight.shape[1]
    block = 256
    heads = attn.shape[0]
    return pl.pallas_call(
        project_kernel,
        out_shape=jax.ShapeDtypeStruct((rows, columns), BF16),
        grid=(columns // block,),
        in_specs=[
            pl.BlockSpec((heads, attn.shape[1], DH), lambda i: (0, 0, 0)),
            pl.BlockSpec((weight.shape[0], block), lambda i: (0, i)),
        ],
        out_specs=pl.BlockSpec((rows, block), lambda i: (0, i)),
        compiler_params=pltpu.CompilerParams(vmem_limit_bytes=24 * 1024 * 1024),
    )(attn, weight)


def arrange_kernel(pattern_ref, mask_ref, q_ref, k_ref, v_ref, q_out, kv_out, list_ref):
    me = lax.axis_index("ctx")
    row, column, core = where_is(me)
    rows = q_ref.shape[0]
    for head in range(HEADS_HERE):
        columns = slice(head * DH, (head + 1) * DH)
        q_out[head] = q_ref[:, columns]
        kv_out[head, :rows, :] = k_ref[:, columns]
        kv_out[head, rows:, :] = v_ref[:, columns]

    pattern = pattern_ref[jnp.minimum(row, HEADS_HERE - 1)]
    masks = []
    tiles = [slot * WORKERS + column * 2 + core for slot in range(SLOTS)]
    for tile in tiles:
        masks.append(jnp.where(row < HEADS_HERE, mask_ref[pattern, pl.ds(tile, 1), :], 0))
    seen = jnp.concatenate(masks, axis=0) == 1
    seen = jnp.where(seen, 1.0, 0.0).astype(F32)
    down = lax.broadcasted_iota(jnp.int32, (TILES, TILES), 0)
    along = lax.broadcasted_iota(jnp.int32, (TILES, TILES), 1)
    both = (((1,), (1,)), ((), ()))
    upto = jnp.where(along <= down, 1.0, 0.0).astype(BF16)
    same = jnp.where(along == down, 1.0, 0.0).astype(BF16)
    rank = lax.dot_general(upto, seen.astype(BF16), both, preferred_element_type=F32)
    turned = lax.dot_general(same, seen.astype(BF16), both, preferred_element_type=F32)
    rank = rank.astype(jnp.int32)
    spot = jnp.where(turned > 0.5, rank - 1, -1)
    for slot in range(SLOTS):
        hit = spot[:, slot : slot + 1] == along
        listed = jnp.sum(jnp.where(hit, down, 0), axis=0, keepdims=True)
        spare = along[:1, :] >= rank[TILES - 1 :, slot : slot + 1]
        list_ref[slot : slot + 1, :] = jnp.where(spare, tiles[slot], listed)
    last = jnp.concatenate(
        [rank[TILES - 1 :, :], jnp.zeros((1, TILES - SLOTS), jnp.int32)], axis=1
    )
    list_ref[SLOTS : SLOTS + 1, :] = last


def arrange(head_pattern, tile_masks, queries, key_rows, value_rows):
    rows = queries.shape[0]
    return pl.pallas_call(
        arrange_kernel,
        out_shape=(
            jax.ShapeDtypeStruct((HEADS_HERE, rows, DH), BF16),
            jax.ShapeDtypeStruct((HEADS_HERE, 2 * rows, DH), BF16),
            jax.ShapeDtypeStruct((SLOTS + 1, TILES), jnp.int32),
        ),
        in_specs=[pl.BlockSpec(memory_space=pltpu.SMEM)]
        + [pl.BlockSpec(memory_space=pltpu.VMEM)] * 4,
        out_specs=(pl.BlockSpec(memory_space=pltpu.VMEM),) * 3,
        compiler_params=pltpu.CompilerParams(vmem_limit_bytes=16 * 1024 * 1024),
    )(head_pattern, tile_masks, queries, key_rows, value_rows)


def body(queries, key_rows, value_rows, out_weight, tile_masks, head_pattern):
    rows = queries.shape[0]
    q_parts, kv_parts, lists = arrange(head_pattern, tile_masks, queries, key_rows, value_rows)
    q_all, kv_all, w_all = spread(
        q_parts.reshape(HEADS_HERE, SLOTS, WORKERS, SPOTS, DH),
        kv_parts.reshape(HEADS_HERE, 2 * TILES, SPOTS, DH),
        out_weight,
    )
    attended = attend(
        lists, q_all.reshape(SLOTS * TILE, DH), kv_all.reshape(WORKERS, 2 * TILES * PIECE, DH)
    )
    attn = collect(attended.reshape(SLOTS, FRAMES, SPOTS, DH))
    attn = attn.reshape(PLANES * HEADS_HERE, rows, DH)
    return project(attn, w_all, rows)


def solution(mesh):
    placed = (
        P("ctx", "heads"),
        P("ctx", "heads"),
        P("ctx", "heads"),
        P("heads", None),
        P(),
        P("heads"),
    )
    return jax.shard_map(
        body, mesh=mesh, in_specs=placed, out_specs=P("ctx", "heads"), check_vma=False
    )
```

```python
import math

import jax
import jax.numpy as jnp
from jax import lax
from jax.experimental import pallas as pl
from jax.experimental.pallas import tpu as pltpu
from jax.sharding import PartitionSpec as P

MESH = pl.DeviceIdType.MESH
DH = 128
TILE = 128
SPOTS = 4
FRAMES = 32
TILES = 128
PLANES = 4
SIDE = 4
HEADS_HERE = 3
WORKERS = 2 * SIDE
SLOTS = TILES // WORKERS
PARTS = 4
PART = 2 * TILES // PARTS
DETOURS = 2
PIECE = TILE // WORKERS
GROUP = 8
BESIDE = 4
FAR = 2.0**64
LOW = -1e30
SCALE2 = math.log2(math.e) / math.sqrt(DH)
BF16 = jnp.bfloat16
F32 = jnp.float32


def where_is(device, plane):
    z, y = lax.div(device, 2 * SIDE), lax.rem(lax.div(device, 2), SIDE)
    odd = lax.rem(plane, 2)
    return z + odd * (y - z), y + odd * (z - y), lax.rem(device, 2)


def device_at(row, column, core, plane):
    row, column = lax.rem(row, SIDE), lax.rem(column, SIDE)
    odd = lax.rem(plane, 2)
    return ((row + odd * (column - row)) * SIDE + column + odd * (row - column)) * 2 + core


def spread_kernel(
    q_ref, kv_ref, w_ref, q_all, kv_all, w_all,
    q_send, q_recv, z_send, z_recv, y_send, y_recv, far_send, far_recv,
    core_send, core_recv, w_send, w_recv, w_core_send, w_core_recv, own_sem,
    held, passed, leg_send, leg_recv,
):
    plane = lax.axis_index("heads")
    me = lax.axis_index("ctx")
    row, column, core = where_is(me, plane)
    working = row < HEADS_HERE
    own_row = jnp.minimum(row, HEADS_HERE - 1)
    depth = w_ref.shape[0]
    width = w_all.shape[1]
    sides = (1, SIDE - 1)

    barrier = pltpu.get_barrier_semaphore()

    def greet(step, carry):
        pl.semaphore_signal(
            barrier, inc=1, device_id=(plane, lax.rem(me + step, FRAMES)), device_id_type=MESH
        )
        return carry

    lax.fori_loop(1, FRAMES, greet, 0)
    for hop in range(1, PLANES):
        pl.semaphore_signal(
            barrier, inc=1, device_id=(lax.rem(plane + hop, PLANES), me), device_id_type=MESH
        )
    pl.semaphore_wait(barrier, FRAMES - 1 + PLANES - 1)

    def span(part):
        return pl.ds(part * PART, PART)

    own_copy = pltpu.make_async_copy(
        kv_ref.at[own_row], kv_all.at[column * 2 + core, :, 0], own_sem
    )

    def z_copy(part, hop):
        there = lax.rem(row + hop, SIDE)
        return pltpu.make_async_remote_copy(
            src_ref=kv_ref.at[there, span(part)],
            dst_ref=kv_all.at[column * 2 + core, span(part), hop],
            send_sem=z_send.at[part, hop],
            recv_sem=z_recv.at[part, hop],
            device_id=(plane, device_at(there, column, core, plane)),
            device_id_type=MESH,
        )

    def piece(number, away):
        source = kv_all.at[lax.rem(column + away, SIDE) * 2 + core]
        if number == 0:
            return source.at[:, 0]
        return source.at[span(number - 1), pl.ds(1, SIDE - 1)]

    def y_copy(number, side):
        return pltpu.make_async_remote_copy(
            src_ref=kv_ref.at[own_row] if number == 0 else piece(number, 0),
            dst_ref=piece(number, 0),
            send_sem=y_send.at[number, side],
            recv_sem=y_recv.at[number, side],
            device_id=(plane, device_at(row, column + sides[side], core, plane)),
            device_id_type=MESH,
        )

    def far_copy(number, side):
        source = kv_all.at[lax.rem(column + sides[1 - side], SIDE) * 2 + core]
        if number == 0:
            chunk = source.at[pl.ds(side * TILES, TILES), 0]
        else:
            chunk = source.at[
                pl.ds((number - 1) * PART + side * (PART // 2), PART // 2), pl.ds(1, SIDE - 1)
            ]
        return pltpu.make_async_remote_copy(
            src_ref=chunk,
            dst_ref=chunk,
            send_sem=far_send.at[number, side],
            recv_sem=far_recv.at[number, side],
            device_id=(plane, device_at(row, column + sides[side], core, plane)),
            device_id_type=MESH,
        )

    other_row, other_column, _ = where_is(me, plane + 1)
    relaying = other_row < HEADS_HERE

    def next_plane(side):
        return lax.rem(plane + sides[side], PLANES)

    def first_leg(number, side):
        return pltpu.make_async_remote_copy(
            src_ref=piece(number, 0),
            dst_ref=held.at[number - 1, side],
            send_sem=leg_send.at[0, number - 1, side],
            recv_sem=leg_recv.at[0, number - 1, side],
            device_id=(next_plane(side), me),
            device_id_type=MESH,
        )

    def second_leg(number, side):
        there = device_at(other_row, other_column + sides[side], core, plane + 1)
        return pltpu.make_async_remote_copy(
            src_ref=held.at[number - 1, side],
            dst_ref=passed.at[number - 1, side],
            send_sem=leg_send.at[1, number - 1, side],
            recv_sem=leg_recv.at[1, number - 1, side],
            device_id=(plane, there),
            device_id_type=MESH,
        )

    def third_leg(number, side):
        source = lax.rem(other_column + sides[1 - side], SIDE) * 2 + core
        return pltpu.make_async_remote_copy(
            src_ref=passed.at[number - 1, side],
            dst_ref=kv_all.at[source, span(number - 1), pl.ds(1, SIDE - 1)],
            send_sem=leg_send.at[2, number - 1, side],
            recv_sem=y_recv.at[number, side],
            device_id=(next_plane(1 - side), me),
            device_id_type=MESH,
        )

    def relay(leg, number):
        @pl.when(relaying)
        def _():
            for side in range(2):
                if leg == 1:
                    first_leg(number, side).wait_recv()
                    second_leg(number, side).start()
                else:
                    second_leg(number, side).wait_recv()
                    third_leg(number, side).start()

    def core_copy(number, away):
        return pltpu.make_async_remote_copy(
            src_ref=piece(number, away),
            dst_ref=piece(number, away),
            send_sem=core_send.at[number, away],
            recv_sem=core_recv,
            device_id=(plane, device_at(row, column, 1 - core, plane)),
            device_id_type=MESH,
        )

    half = depth // 2

    def w_rows(source, part):
        return w_all.at[pl.ds(pl.multiple_of(source * depth + part * half, 16), half)]

    def w_copy(hop):
        there = lax.rem(plane + hop, PLANES)
        return pltpu.make_async_remote_copy(
            src_ref=w_ref.at[
                pl.ds(pl.multiple_of(core * half, 16), half),
                pl.ds(pl.multiple_of(there * width, 128), width),
            ],
            dst_ref=w_rows(plane, core),
            send_sem=w_send.at[hop],
            recv_sem=w_recv.at[hop],
            device_id=(there, me),
            device_id_type=MESH,
        )

    def w_core_copy(hop):
        rows = w_rows(lax.rem(plane + PLANES - hop, PLANES), core)
        return pltpu.make_async_remote_copy(
            src_ref=rows,
            dst_ref=rows,
            send_sem=w_core_send.at[hop],
            recv_sem=w_core_recv.at[hop],
            device_id=(plane, device_at(row, column, 1 - core, plane)),
            device_id_type=MESH,
        )

    own_w = pltpu.make_async_copy(
        w_ref.at[:, pl.ds(pl.multiple_of(plane * width, 128), width)],
        w_all.at[pl.ds(pl.multiple_of(plane * depth, 128), depth)],
        w_recv.at[0],
    )

    def q_copy(step):
        there = lax.rem(me + step, FRAMES)
        row_there, column_there, core_there = where_is(there, plane)
        return row_there < HEADS_HERE, pltpu.make_async_remote_copy(
            src_ref=q_ref.at[
                jnp.minimum(row_there, HEADS_HERE - 1), :, column_there * 2 + core_there
            ],
            dst_ref=q_all.at[:, me],
            send_sem=q_send.at[step],
            recv_sem=q_recv,
            device_id=(plane, there),
            device_id_type=MESH,
        )

    def to_rows(part, work):
        for hop in range(1, SIDE):

            @pl.when(lax.rem(row + hop, SIDE) < HEADS_HERE)
            def _():
                work(z_copy(part, hop))

    def send_q(step, carry):
        wanted, copy = q_copy(step)

        @pl.when(wanted)
        def _():
            copy.start()

        return carry

    def sent_q(step, carry):
        wanted, copy = q_copy(step)

        @pl.when(wanted)
        def _():
            copy.wait_send()

        return carry

    def send_small():
        for hop in range(1, PLANES):
            w_copy(hop).start()
        own_w.start()
        lax.fori_loop(1, FRAMES, send_q, 0)

    @pl.when(working)
    def _():
        own_copy.start()
        for side in range(2):
            y_copy(0, side).start()

    to_rows(0, lambda copy: copy.start())
    send_small()

    def next_rows(part):
        to_rows(part, lambda copy: copy.wait_send())
        if part + 1 < PARTS:
            to_rows(part + 1, lambda copy: copy.start())

    @pl.when(working)
    def _():
        pltpu.make_async_copy(
            q_ref.at[own_row, :, column * 2 + core], q_all.at[:, me], q_recv
        ).start()
        own_copy.wait()
        core_copy(0, 0).start()

    def gathered(part):
        next_rows(part)

        @pl.when(working)
        def _():
            for hop in range(1, SIDE):
                landed = kv_all.at[column * 2 + core, span(part), hop]
                pltpu.make_async_copy(landed, landed, z_recv.at[part, hop]).wait()
            for side in range(2):
                if part < DETOURS:
                    first_leg(part + 1, side).start()
                else:
                    y_copy(part + 1, side).start()
            core_copy(part + 1, 0).start()

    def pass_on(number):
        @pl.when(working)
        def _():
            for side in range(2):
                y_copy(number, side).wait_recv()
                far_copy(number, side).start()
            for side in range(2):
                core_copy(number, sides[1 - side]).start()

    gathered(0)
    gathered(1)
    pass_on(0)
    relay(1, 1)
    gathered(2)
    relay(1, 2)
    gathered(3)
    relay(2, 1)
    pass_on(3)
    relay(2, 2)
    pass_on(1)
    pass_on(4)
    pass_on(2)

    @pl.when(working)
    def _():
        for number in (0, 3, 1, 4, 2):
            for side in range(2):
                far_copy(number, side).wait_recv()
            core_copy(number, 2).start()

    for hop in range(1, PLANES):
        w_copy(hop).wait_recv()
        w_core_copy(hop).start()

    @pl.when(working)
    def _():
        pltpu.make_async_copy(q_all, q_all, q_recv).wait()
        other = kv_all.at[pl.ds(0, SIDE)]
        pltpu.make_async_copy(other, other, core_recv).wait()
        for number in range(PARTS + 1):
            for side in range(2):
                if 0 < number <= DETOURS:
                    first_leg(number, side).wait_send()
                else:
                    y_copy(number, side).wait_send()
                far_copy(number, side).wait_send()
            for away in range(SIDE):
                core_copy(number, away).wait_send()

    @pl.when(relaying)
    def _():
        for number in range(1, DETOURS + 1):
            for side in range(2):
                second_leg(number, side).wait_send()
                third_leg(number, side).wait_send()

    own_w.wait()
    lax.fori_loop(1, FRAMES, sent_q, 0)
    for hop in range(1, PLANES):
        w_copy(hop).wait_send()
        w_core_copy(hop).wait()


def spread(q_parts, kv_parts, out_weight):
    depth, columns = out_weight.shape
    return pl.pallas_call(
        spread_kernel,
        out_shape=(
            jax.ShapeDtypeStruct((SLOTS, FRAMES, SPOTS, DH), BF16),
            jax.ShapeDtypeStruct((WORKERS, 2 * TILES, SIDE, SPOTS, DH), BF16),
            jax.ShapeDtypeStruct((depth * PLANES, columns // PLANES), BF16),
        ),
        in_specs=[pl.BlockSpec(memory_space=pl.ANY)] * 3,
        out_specs=(pl.BlockSpec(memory_space=pl.ANY),) * 3,
        scratch_shapes=[
            pltpu.SemaphoreType.DMA((FRAMES,)),
            pltpu.SemaphoreType.DMA,
            pltpu.SemaphoreType.DMA((PARTS, SIDE)),
            pltpu.SemaphoreType.DMA((PARTS, SIDE)),
            pltpu.SemaphoreType.DMA((PARTS + 1, 2)),
            pltpu.SemaphoreType.DMA((PARTS + 1, 2)),
            pltpu.SemaphoreType.DMA((PARTS + 1, 2)),
            pltpu.SemaphoreType.DMA((PARTS + 1, 2)),
            pltpu.SemaphoreType.DMA((PARTS + 1, SIDE)),
            pltpu.SemaphoreType.DMA,
            pltpu.SemaphoreType.DMA((PLANES,)),
            pltpu.SemaphoreType.DMA((PLANES,)),
            pltpu.SemaphoreType.DMA((PLANES,)),
            pltpu.SemaphoreType.DMA((PLANES,)),
            pltpu.SemaphoreType.DMA,
            pltpu.VMEM((DETOURS, 2, PART, SIDE - 1, SPOTS, DH), BF16),
            pltpu.VMEM((DETOURS, 2, PART, SIDE - 1, SPOTS, DH), BF16),
            pltpu.SemaphoreType.DMA((3, DETOURS, 2)),
            pltpu.SemaphoreType.DMA((2, DETOURS, 2)),
        ],
        compiler_params=pltpu.CompilerParams(
            collective_id=0, has_side_effects=True, vmem_limit_bytes=12 * 1024 * 1024
        ),
    )(q_parts, kv_parts, out_weight)


def attend_kernel(
    list_ref, q_ref, kv_ref, o_ref, keys_ref, values_ref, base_ref, peak_ref, sum_ref,
    slot_of, first_of, listed_of,
):
    _, column, core = where_is(lax.axis_index("ctx"), lax.axis_index("heads"))

    def loop(count, work):
        def one(step, carry):
            work(step)
            return carry

        lax.fori_loop(0, count, one, 0)

    def rows_of(slot):
        return pl.ds(pl.multiple_of(slot * TILE, TILE), TILE)

    def tile_at(tile):
        start = pl.multiple_of(tile * PIECE, PIECE)
        return jnp.concatenate(
            [kv_ref[worker, pl.ds(start, PIECE), :] for worker in range(WORKERS)], axis=0
        )

    def enlist(slot, total):
        count = list_ref[SLOTS, slot]
        steps = lax.div(count + GROUP - 1, GROUP)

        def one(step, carry):
            slot_of[total + step] = slot
            first_of[total + step] = step * GROUP
            listed_of[total + step] = count - step * GROUP
            return carry

        lax.fori_loop(0, steps, one, 0)
        return total + steps

    total = lax.fori_loop(0, SLOTS, enlist, 0)
    for spare in range(BESIDE - 1):
        slot_of[total + spare] = 0
        first_of[total + spare] = 0
        listed_of[total + spare] = 0
    turns = lax.div(total + BESIDE - 1, BESIDE)
    busy = jnp.where(total > 0, 1, 0)

    values_ref[TILES] = jnp.zeros((TILE, DH), BF16)

    def unpack(step):
        for u in range(GROUP):
            tile = step * GROUP + u
            keys_ref[tile] = tile_at(tile).T
            values_ref[tile] = tile_at(TILES + tile)

    loop(busy * (TILES // GROUP), unpack)

    def set_base(slot, base):
        base_ref[slot] = jnp.broadcast_to(base * SCALE2, (TILE, TILE))

    def own_base(step):
        for u in range(BESIDE):
            slot = step * BESIDE + u
            own = keys_ref[slot * WORKERS + column * 2 + core]
            scores = jnp.dot(q_ref[rows_of(slot), :], own, preferred_element_type=F32)
            set_base(slot, jnp.max(scores, axis=1, keepdims=True))

    loop(busy * (SLOTS // BESIDE), own_base)

    def tiles_of(number):
        slot, first = slot_of[number], first_of[number]
        return slot, [list_ref[slot, first + u] for u in range(GROUP)]

    def scores_of(slot, tiles):
        keys = jnp.concatenate([keys_ref[tile] for tile in tiles], axis=1)
        return jnp.dot(q_ref[rows_of(slot), :], keys, preferred_element_type=F32)

    def attend_steps(step):
        found = []
        for beside in range(BESIDE):
            number = step * BESIDE + beside
            slot, tiles = tiles_of(number)
            listed = listed_of[number]
            base = base_ref[slot]
            base = jnp.concatenate([base, base], axis=1)
            weights, values = [], []
            for u in range(0, GROUP, 2):
                scores = scores_of(slot, tiles[u : u + 2])
                weights.append(jnp.exp2(scores * SCALE2 - base).astype(BF16))
            for u in range(GROUP):
                value = values_ref[jnp.where(u < listed, tiles[u], TILES)]
                ones = jnp.where(u < listed, 1.0, 0.0).astype(BF16)
                ones = jnp.broadcast_to(ones, (TILE, DH))
                values.append(jnp.concatenate([value, ones], axis=1))
            added = jnp.dot(
                jnp.concatenate(weights, axis=1),
                jnp.concatenate(values, axis=0),
                preferred_element_type=F32,
            )
            found.append((slot, added))
        for slot, added in found:
            sum_ref[slot] += added

    def peak_steps(step):
        for beside in range(BESIDE):
            slot, tiles = tiles_of(step * BESIDE + beside)
            scores = scores_of(slot, tiles)
            peak = peak_ref[slot]
            for u in range(GROUP):
                peak = jnp.maximum(peak, scores[:, u * TILE : (u + 1) * TILE])
            peak_ref[slot] = peak

    def attempt(number, needed):
        def clear(slot):
            sum_ref[slot] = jnp.zeros((TILE, 2 * DH), F32)
            peak_ref[slot] = jnp.full((TILE, TILE), LOW, F32)

        loop(needed * SLOTS, clear)
        loop(needed * turns, attend_steps)
        beyond = jnp.zeros((TILE, DH), F32)
        for slot in range(SLOTS):
            beyond = jnp.where(sum_ref[slot, :, DH:] <= FAR, beyond, 1.0)
        again = needed * jnp.where(jnp.max(beyond) > 0.0, 1, 0)
        loop(again * turns, peak_steps)

        def rebase(slot):
            set_base(slot, jnp.max(peak_ref[slot], axis=1, keepdims=True))

        loop(again * SLOTS, rebase)
        return again

    lax.fori_loop(0, 2, attempt, busy)

    def finish(step):
        for u in range(BESIDE):
            slot = step * BESIDE + u
            o_ref[rows_of(slot), :] = (sum_ref[slot, :, :DH] / sum_ref[slot, :, DH:]).astype(BF16)

    loop(busy * (SLOTS // BESIDE), finish)


def attend(lists, query, kv):
    most = SLOTS * (TILES // GROUP) + BESIDE
    return pl.pallas_call(
        attend_kernel,
        out_shape=jax.ShapeDtypeStruct(query.shape, BF16),
        in_specs=[
            pl.BlockSpec(memory_space=pltpu.SMEM),
            pl.BlockSpec(memory_space=pltpu.VMEM),
            pl.BlockSpec(memory_space=pltpu.VMEM),
        ],
        out_specs=pl.BlockSpec(memory_space=pltpu.VMEM),
        scratch_shapes=[
            pltpu.VMEM((TILES, DH, TILE), BF16),
            pltpu.VMEM((TILES + 1, TILE, DH), BF16),
            pltpu.VMEM((SLOTS, TILE, TILE), F32),
            pltpu.VMEM((SLOTS, TILE, TILE), F32),
            pltpu.VMEM((SLOTS, TILE, 2 * DH), F32),
            pltpu.SMEM((most,), jnp.int32),
            pltpu.SMEM((most,), jnp.int32),
            pltpu.SMEM((most,), jnp.int32),
        ],
        compiler_params=pltpu.CompilerParams(vmem_limit_bytes=40 * 1024 * 1024),
    )(lists, query, kv)


def collect_kernel(o_ref, attn, send, recv, x_send, x_recv):
    plane = lax.axis_index("heads")
    me = lax.axis_index("ctx")
    row, column, core = where_is(me, plane)
    barrier = pltpu.get_barrier_semaphore()

    def greet(step, carry):
        pl.semaphore_signal(
            barrier, inc=1, device_id=(plane, lax.rem(me + step, FRAMES)), device_id_type=MESH
        )
        return carry

    lax.fori_loop(1, FRAMES, greet, 0)
    sides = (lax.rem(plane + 1, PLANES), lax.rem(plane + PLANES - 1, PLANES))
    for there in sides:
        pl.semaphore_signal(barrier, inc=1, device_id=(there, me), device_id_type=MESH)
    pl.semaphore_wait(barrier, FRAMES - 1 + 2)

    mine = jnp.minimum(row, HEADS_HERE - 1)
    goal = attn.at[plane * HEADS_HERE + mine, :, column * 2 + core]

    def back(step):
        there = lax.rem(me + step, FRAMES)
        return pltpu.make_async_remote_copy(
            src_ref=o_ref.at[:, there],
            dst_ref=goal,
            send_sem=send.at[step],
            recv_sem=recv.at[mine],
            device_id=(plane, there),
            device_id_type=MESH,
        )

    def start(step, carry):
        back(step).start()
        return carry

    def end(step, carry):
        back(step).wait_send()
        return carry

    working = row < HEADS_HERE

    @pl.when(working)
    def _():
        lax.fori_loop(1, FRAMES, start, 0)
        pltpu.make_async_copy(o_ref.at[:, me], goal, recv.at[mine]).start()

    cut = SLOTS // 2

    def near(head, side):
        part = attn.at[plane * HEADS_HERE + head]
        return pltpu.make_async_remote_copy(
            src_ref=part,
            dst_ref=part,
            send_sem=x_send.at[head, side],
            recv_sem=x_recv.at[head, side],
            device_id=(sides[side], me),
            device_id_type=MESH,
        )

    def far(head, side):
        part = attn.at[sides[1 - side] * HEADS_HERE + head]
        part = part.at[pl.ds(0, cut)] if side == 0 else part.at[pl.ds(cut, SLOTS - cut)]
        return pltpu.make_async_remote_copy(
            src_ref=part,
            dst_ref=part,
            send_sem=x_send.at[head, 2 + side],
            recv_sem=x_recv.at[head, 2 + side],
            device_id=(sides[side], me),
            device_id_type=MESH,
        )

    for head in range(HEADS_HERE):
        part = attn.at[plane * HEADS_HERE + head]
        pltpu.make_async_copy(part, part, recv.at[head]).wait()
        for side in range(2):
            near(head, side).start()
    for head in range(HEADS_HERE):
        for side in range(2):
            near(head, side).wait_recv()
            far(head, side).start()

    @pl.when(working)
    def _():
        lax.fori_loop(1, FRAMES, end, 0)

    for head in range(HEADS_HERE):
        for side in range(2):
            near(head, side).wait_send()
            far(head, side).wait()


def collect(attended):
    return pl.pallas_call(
        collect_kernel,
        out_shape=jax.ShapeDtypeStruct(
            (PLANES * HEADS_HERE, SLOTS, WORKERS, SPOTS, DH), BF16
        ),
        in_specs=[pl.BlockSpec(memory_space=pl.ANY)],
        out_specs=pl.BlockSpec(memory_space=pl.ANY),
        scratch_shapes=[
            pltpu.SemaphoreType.DMA((FRAMES,)),
            pltpu.SemaphoreType.DMA((HEADS_HERE,)),
            pltpu.SemaphoreType.DMA((HEADS_HERE, 4)),
            pltpu.SemaphoreType.DMA((HEADS_HERE, 4)),
        ],
        compiler_params=pltpu.CompilerParams(
            collective_id=1, has_side_effects=True, vmem_limit_bytes=4 * 1024 * 1024
        ),
    )(attended)


def project_kernel(attn_ref, w_ref, out_ref):
    rows = out_ref.shape[0]
    heads = attn_ref.shape[0]
    wide = jnp.concatenate([attn_ref[h, :rows, :] for h in range(heads)], axis=1)
    out_ref[...] = jnp.dot(wide, w_ref[...], preferred_element_type=F32).astype(BF16)


def project(attn, weight, rows):
    columns = weight.shape[1]
    block = 256
    heads = attn.shape[0]
    return pl.pallas_call(
        project_kernel,
        out_shape=jax.ShapeDtypeStruct((rows, columns), BF16),
        grid=(columns // block,),
        in_specs=[
            pl.BlockSpec((heads, attn.shape[1], DH), lambda i: (0, 0, 0)),
            pl.BlockSpec((weight.shape[0], block), lambda i: (0, i)),
        ],
        out_specs=pl.BlockSpec((rows, block), lambda i: (0, i)),
        compiler_params=pltpu.CompilerParams(vmem_limit_bytes=24 * 1024 * 1024),
    )(attn, weight)


def arrange_kernel(pattern_ref, mask_ref, q_ref, k_ref, v_ref, q_out, kv_out, list_ref):
    me = lax.axis_index("ctx")
    row, column, core = where_is(me, lax.axis_index("heads"))
    rows = q_ref.shape[0]
    for head in range(HEADS_HERE):
        columns = slice(head * DH, (head + 1) * DH)
        q_out[head] = q_ref[:, columns]
        kv_out[head, :rows, :] = k_ref[:, columns]
        kv_out[head, rows:, :] = v_ref[:, columns]

    pattern = pattern_ref[jnp.minimum(row, HEADS_HERE - 1)]
    masks = []
    tiles = [slot * WORKERS + column * 2 + core for slot in range(SLOTS)]
    for tile in tiles:
        masks.append(jnp.where(row < HEADS_HERE, mask_ref[pattern, pl.ds(tile, 1), :], 0))
    seen = jnp.concatenate(masks, axis=0) == 1
    seen = jnp.where(seen, 1.0, 0.0).astype(F32)
    down = lax.broadcasted_iota(jnp.int32, (TILES, TILES), 0)
    along = lax.broadcasted_iota(jnp.int32, (TILES, TILES), 1)
    both = (((1,), (1,)), ((), ()))
    upto = jnp.where(along <= down, 1.0, 0.0).astype(BF16)
    same = jnp.where(along == down, 1.0, 0.0).astype(BF16)
    rank = lax.dot_general(upto, seen.astype(BF16), both, preferred_element_type=F32)
    turned = lax.dot_general(same, seen.astype(BF16), both, preferred_element_type=F32)
    rank = rank.astype(jnp.int32)
    spot = jnp.where(turned > 0.5, rank - 1, -1)
    for slot in range(SLOTS):
        hit = spot[:, slot : slot + 1] == along
        listed = jnp.sum(jnp.where(hit, down, 0), axis=0, keepdims=True)
        spare = along[:1, :] >= rank[TILES - 1 :, slot : slot + 1]
        list_ref[slot : slot + 1, :] = jnp.where(spare, tiles[slot], listed)
    last = jnp.concatenate(
        [rank[TILES - 1 :, :], jnp.zeros((1, TILES - SLOTS), jnp.int32)], axis=1
    )
    list_ref[SLOTS : SLOTS + 1, :] = last


def arrange(head_pattern, tile_masks, queries, key_rows, value_rows):
    rows = queries.shape[0]
    return pl.pallas_call(
        arrange_kernel,
        out_shape=(
            jax.ShapeDtypeStruct((HEADS_HERE, rows, DH), BF16),
            jax.ShapeDtypeStruct((HEADS_HERE, 2 * rows, DH), BF16),
            jax.ShapeDtypeStruct((SLOTS + 1, TILES), jnp.int32),
        ),
        in_specs=[pl.BlockSpec(memory_space=pltpu.SMEM)]
        + [pl.BlockSpec(memory_space=pltpu.VMEM)] * 4,
        out_specs=(pl.BlockSpec(memory_space=pltpu.VMEM),) * 3,
        compiler_params=pltpu.CompilerParams(vmem_limit_bytes=16 * 1024 * 1024),
    )(head_pattern, tile_masks, queries, key_rows, value_rows)


def body(queries, key_rows, value_rows, out_weight, tile_masks, head_pattern):
    rows = queries.shape[0]
    q_parts, kv_parts, lists = arrange(head_pattern, tile_masks, queries, key_rows, value_rows)
    q_all, kv_all, w_all = spread(
        q_parts.reshape(HEADS_HERE, SLOTS, WORKERS, SPOTS, DH),
        kv_parts.reshape(HEADS_HERE, 2 * TILES, SPOTS, DH),
        out_weight,
    )
    attended = attend(
        lists, q_all.reshape(SLOTS * TILE, DH), kv_all.reshape(WORKERS, 2 * TILES * PIECE, DH)
    )
    attn = collect(attended.reshape(SLOTS, FRAMES, SPOTS, DH))
    attn = attn.reshape(PLANES * HEADS_HERE, rows, DH)
    return project(attn, w_all, rows)


def solution(mesh):
    placed = (
        P("ctx", "heads"),
        P("ctx", "heads"),
        P("ctx", "heads"),
        P("heads", None),
        P(),
        P("heads"),
    )
    return jax.shard_map(
        body, mesh=mesh, in_specs=placed, out_specs=P("ctx", "heads"), check_vma=False
    )
```

```python
import math

import jax
import jax.numpy as jnp
from jax import lax
from jax.experimental import pallas as pl
from jax.experimental.pallas import tpu as pltpu
from jax.sharding import PartitionSpec as P

MESH = pl.DeviceIdType.MESH
DH = 128
TILE = 128
SPOTS = 4
FRAMES = 32
TILES = 128
PLANES = 4
SIDE = 4
HEADS_HERE = 3
WORKERS = 2 * SIDE
SLOTS = TILES // WORKERS
PARTS = 4
PART = 2 * TILES // PARTS
PIECE = TILE // WORKERS
GROUP = 8
BESIDE = 4
FAR = 2.0**64
LOW = -1e30
SCALE2 = math.log2(math.e) / math.sqrt(DH)
BF16 = jnp.bfloat16
F32 = jnp.float32


def where_is(device):
    return lax.div(device, WORKERS), lax.rem(lax.div(device, 2), SIDE), lax.rem(device, 2)


def device_at(row, column, core):
    return (lax.rem(row, SIDE) * SIDE + lax.rem(column, SIDE)) * 2 + core


def spread_kernel(
    q_ref, kv_ref, q_all, kv_all,
    q_send, q_recv, z_send, z_recv, y_send, y_recv, far_send, far_recv,
    core_send, core_recv, own_sem,
):
    plane = lax.axis_index("heads")
    me = lax.axis_index("ctx")
    row, column, core = where_is(me)
    working = row < HEADS_HERE
    own_row = jnp.minimum(row, HEADS_HERE - 1)
    sides = (1, SIDE - 1)

    barrier = pltpu.get_barrier_semaphore()

    def greet(step, carry):
        pl.semaphore_signal(
            barrier, inc=1, device_id=(plane, lax.rem(me + step, FRAMES)), device_id_type=MESH
        )
        return carry

    lax.fori_loop(1, FRAMES, greet, 0)
    pl.semaphore_wait(barrier, FRAMES - 1)

    def span(part):
        return pl.ds(part * PART, PART)

    own_copy = pltpu.make_async_copy(
        kv_ref.at[own_row], kv_all.at[column * 2 + core, :, 0], own_sem
    )

    def z_copy(part, hop):
        there = lax.rem(row + hop, SIDE)
        return pltpu.make_async_remote_copy(
            src_ref=kv_ref.at[there, span(part)],
            dst_ref=kv_all.at[column * 2 + core, span(part), hop],
            send_sem=z_send.at[part, hop],
            recv_sem=z_recv.at[part, hop],
            device_id=(plane, device_at(there, column, core)),
            device_id_type=MESH,
        )

    def piece(number, away):
        source = kv_all.at[lax.rem(column + away, SIDE) * 2 + core]
        if number == 0:
            return source.at[:, 0]
        return source.at[span(number - 1), pl.ds(1, SIDE - 1)]

    def y_copy(number, side):
        return pltpu.make_async_remote_copy(
            src_ref=kv_ref.at[own_row] if number == 0 else piece(number, 0),
            dst_ref=piece(number, 0),
            send_sem=y_send.at[number, side],
            recv_sem=y_recv.at[number, side],
            device_id=(plane, device_at(row, column + sides[side], core)),
            device_id_type=MESH,
        )

    def far_copy(number, side):
        source = kv_all.at[lax.rem(column + sides[1 - side], SIDE) * 2 + core]
        if number == 0:
            chunk = source.at[pl.ds(side * TILES, TILES), 0]
        else:
            chunk = source.at[
                pl.ds((number - 1) * PART + side * (PART // 2), PART // 2), pl.ds(1, SIDE - 1)
            ]
        return pltpu.make_async_remote_copy(
            src_ref=chunk,
            dst_ref=chunk,
            send_sem=far_send.at[number, side],
            recv_sem=far_recv.at[number, side],
            device_id=(plane, device_at(row, column + sides[side], core)),
            device_id_type=MESH,
        )

    def core_copy(number, away):
        return pltpu.make_async_remote_copy(
            src_ref=piece(number, away),
            dst_ref=piece(number, away),
            send_sem=core_send.at[number, away],
            recv_sem=core_recv,
            device_id=(plane, device_at(row, column, 1 - core)),
            device_id_type=MESH,
        )

    def q_copy(step):
        there = lax.rem(me + step, FRAMES)
        row_there, column_there, core_there = where_is(there)
        return row_there < HEADS_HERE, pltpu.make_async_remote_copy(
            src_ref=q_ref.at[
                jnp.minimum(row_there, HEADS_HERE - 1), :, column_there * 2 + core_there
            ],
            dst_ref=q_all.at[:, me],
            send_sem=q_send.at[step],
            recv_sem=q_recv,
            device_id=(plane, there),
            device_id_type=MESH,
        )

    def to_rows(part, work):
        for hop in range(1, SIDE):

            @pl.when(lax.rem(row + hop, SIDE) < HEADS_HERE)
            def _():
                work(z_copy(part, hop))

    def send_q(step, carry):
        wanted, copy = q_copy(step)

        @pl.when(wanted)
        def _():
            copy.start()

        return carry

    def sent_q(step, carry):
        wanted, copy = q_copy(step)

        @pl.when(wanted)
        def _():
            copy.wait_send()

        return carry

    @pl.when(working)
    def _():
        own_copy.start()
        for side in range(2):
            y_copy(0, side).start()

    to_rows(0, lambda copy: copy.start())
    lax.fori_loop(1, FRAMES, send_q, 0)

    def next_rows(part):
        to_rows(part, lambda copy: copy.wait_send())
        if part + 1 < PARTS:
            to_rows(part + 1, lambda copy: copy.start())

    @pl.when(jnp.logical_not(working))
    def _():
        for part in range(PARTS):
            next_rows(part)

    @pl.when(working)
    def _():
        pltpu.make_async_copy(
            q_ref.at[own_row, :, column * 2 + core], q_all.at[:, me], q_recv
        ).start()
        own_copy.wait()
        core_copy(0, 0).start()

        def pass_on(number):
            for side in range(2):
                y_copy(number, side).wait_recv()
                far_copy(number, side).start()
            for side in range(2):
                core_copy(number, sides[1 - side]).start()

        for part in range(PARTS):
            next_rows(part)
            for hop in range(1, SIDE):
                landed = kv_all.at[column * 2 + core, span(part), hop]
                pltpu.make_async_copy(landed, landed, z_recv.at[part, hop]).wait()
            for side in range(2):
                y_copy(part + 1, side).start()
            core_copy(part + 1, 0).start()
            pass_on(part)
        pass_on(PARTS)
        for number in range(PARTS + 1):
            for side in range(2):
                far_copy(number, side).wait_recv()
            core_copy(number, 2).start()

    @pl.when(working)
    def _():
        pltpu.make_async_copy(q_all, q_all, q_recv).wait()
        other = kv_all.at[pl.ds(0, SIDE)]
        pltpu.make_async_copy(other, other, core_recv).wait()
        for number in range(PARTS + 1):
            for side in range(2):
                y_copy(number, side).wait_send()
                far_copy(number, side).wait_send()
            for away in range(SIDE):
                core_copy(number, away).wait_send()

    lax.fori_loop(1, FRAMES, sent_q, 0)


def spread(q_parts, kv_parts):
    return pl.pallas_call(
        spread_kernel,
        out_shape=(
            jax.ShapeDtypeStruct((SLOTS, FRAMES, SPOTS, DH), BF16),
            jax.ShapeDtypeStruct((WORKERS, 2 * TILES, SIDE, SPOTS, DH), BF16),
        ),
        in_specs=[pl.BlockSpec(memory_space=pl.ANY)] * 2,
        out_specs=(pl.BlockSpec(memory_space=pl.ANY),) * 2,
        scratch_shapes=[
            pltpu.SemaphoreType.DMA((FRAMES,)),
            pltpu.SemaphoreType.DMA,
            pltpu.SemaphoreType.DMA((PARTS, SIDE)),
            pltpu.SemaphoreType.DMA((PARTS, SIDE)),
            pltpu.SemaphoreType.DMA((PARTS + 1, 2)),
            pltpu.SemaphoreType.DMA((PARTS + 1, 2)),
            pltpu.SemaphoreType.DMA((PARTS + 1, 2)),
            pltpu.SemaphoreType.DMA((PARTS + 1, 2)),
            pltpu.SemaphoreType.DMA((PARTS + 1, SIDE)),
            pltpu.SemaphoreType.DMA,
            pltpu.SemaphoreType.DMA,
        ],
        compiler_params=pltpu.CompilerParams(
            collective_id=0, has_side_effects=True, vmem_limit_bytes=4 * 1024 * 1024
        ),
    )(q_parts, kv_parts)


def attend_kernel(
    list_ref, q_ref, kv_ref, o_ref, keys_ref, values_ref, base_ref, peak_ref, sum_ref,
    slot_of, first_of, listed_of,
):
    _, column, core = where_is(lax.axis_index("ctx"))

    def loop(count, work):
        def one(step, carry):
            work(step)
            return carry

        lax.fori_loop(0, count, one, 0)

    def rows_of(slot):
        return pl.ds(pl.multiple_of(slot * TILE, TILE), TILE)

    def tile_at(tile):
        start = pl.multiple_of(tile * PIECE, PIECE)
        return jnp.concatenate(
            [kv_ref[worker, pl.ds(start, PIECE), :] for worker in range(WORKERS)], axis=0
        )

    def enlist(slot, total):
        count = list_ref[SLOTS, slot]
        steps = lax.div(count + GROUP - 1, GROUP)

        def one(step, carry):
            slot_of[total + step] = slot
            first_of[total + step] = step * GROUP
            listed_of[total + step] = count - step * GROUP
            return carry

        lax.fori_loop(0, steps, one, 0)
        return total + steps

    total = lax.fori_loop(0, SLOTS, enlist, 0)
    for spare in range(BESIDE - 1):
        slot_of[total + spare] = 0
        first_of[total + spare] = 0
        listed_of[total + spare] = 0
    turns = lax.div(total + BESIDE - 1, BESIDE)
    busy = jnp.where(total > 0, 1, 0)

    values_ref[TILES] = jnp.zeros((TILE, DH), BF16)

    def unpack(step):
        for u in range(GROUP):
            tile = step * GROUP + u
            keys_ref[tile] = tile_at(tile).T
            values_ref[tile] = tile_at(TILES + tile)

    loop(busy * (TILES // GROUP), unpack)

    def set_base(slot, base):
        base_ref[slot] = jnp.broadcast_to(base * SCALE2, (TILE, TILE))

    def own_base(step):
        for u in range(BESIDE):
            slot = step * BESIDE + u
            own = keys_ref[slot * WORKERS + column * 2 + core]
            scores = jnp.dot(q_ref[rows_of(slot), :], own, preferred_element_type=F32)
            set_base(slot, jnp.max(scores, axis=1, keepdims=True))

    loop(busy * (SLOTS // BESIDE), own_base)

    def tiles_of(number):
        slot, first = slot_of[number], first_of[number]
        return slot, [list_ref[slot, first + u] for u in range(GROUP)]

    def scores_of(slot, tiles):
        keys = jnp.concatenate([keys_ref[tile] for tile in tiles], axis=1)
        return jnp.dot(q_ref[rows_of(slot), :], keys, preferred_element_type=F32)

    def attend_steps(step):
        found = []
        for beside in range(BESIDE):
            number = step * BESIDE + beside
            slot, tiles = tiles_of(number)
            listed = listed_of[number]
            base = base_ref[slot]
            base = jnp.concatenate([base, base], axis=1)
            weights, values = [], []
            for u in range(0, GROUP, 2):
                scores = scores_of(slot, tiles[u : u + 2])
                weights.append(jnp.exp2(scores * SCALE2 - base).astype(BF16))
            for u in range(GROUP):
                value = values_ref[jnp.where(u < listed, tiles[u], TILES)]
                ones = jnp.where(u < listed, 1.0, 0.0).astype(BF16)
                ones = jnp.broadcast_to(ones, (TILE, DH))
                values.append(jnp.concatenate([value, ones], axis=1))
            added = jnp.dot(
                jnp.concatenate(weights, axis=1),
                jnp.concatenate(values, axis=0),
                preferred_element_type=F32,
            )
            found.append((slot, added))
        for slot, added in found:
            sum_ref[slot] += added

    def peak_steps(step):
        for beside in range(BESIDE):
            slot, tiles = tiles_of(step * BESIDE + beside)
            scores = scores_of(slot, tiles)
            peak = peak_ref[slot]
            for u in range(GROUP):
                peak = jnp.maximum(peak, scores[:, u * TILE : (u + 1) * TILE])
            peak_ref[slot] = peak

    def attempt(number, needed):
        def clear(slot):
            sum_ref[slot] = jnp.zeros((TILE, 2 * DH), F32)
            peak_ref[slot] = jnp.full((TILE, TILE), LOW, F32)

        loop(needed * SLOTS, clear)
        loop(needed * turns, attend_steps)
        beyond = jnp.zeros((TILE, DH), F32)
        for slot in range(SLOTS):
            beyond = jnp.where(sum_ref[slot, :, DH:] <= FAR, beyond, 1.0)
        again = needed * jnp.where(jnp.max(beyond) > 0.0, 1, 0)
        loop(again * turns, peak_steps)

        def rebase(slot):
            set_base(slot, jnp.max(peak_ref[slot], axis=1, keepdims=True))

        loop(again * SLOTS, rebase)
        return again

    lax.fori_loop(0, 2, attempt, busy)

    def finish(step):
        for u in range(BESIDE):
            slot = step * BESIDE + u
            o_ref[rows_of(slot), :] = (sum_ref[slot, :, :DH] / sum_ref[slot, :, DH:]).astype(BF16)

    loop(busy * (SLOTS // BESIDE), finish)


def attend(lists, query, kv):
    most = SLOTS * (TILES // GROUP) + BESIDE
    return pl.pallas_call(
        attend_kernel,
        out_shape=jax.ShapeDtypeStruct(query.shape, BF16),
        in_specs=[
            pl.BlockSpec(memory_space=pltpu.SMEM),
            pl.BlockSpec(memory_space=pltpu.VMEM),
            pl.BlockSpec(memory_space=pltpu.VMEM),
        ],
        out_specs=pl.BlockSpec(memory_space=pltpu.VMEM),
        scratch_shapes=[
            pltpu.VMEM((TILES, DH, TILE), BF16),
            pltpu.VMEM((TILES + 1, TILE, DH), BF16),
            pltpu.VMEM((SLOTS, TILE, TILE), F32),
            pltpu.VMEM((SLOTS, TILE, TILE), F32),
            pltpu.VMEM((SLOTS, TILE, 2 * DH), F32),
            pltpu.SMEM((most,), jnp.int32),
            pltpu.SMEM((most,), jnp.int32),
            pltpu.SMEM((most,), jnp.int32),
        ],
        compiler_params=pltpu.CompilerParams(vmem_limit_bytes=40 * 1024 * 1024),
        cost_estimate=pl.CostEstimate(
            flops=2 * 2 * SLOTS * TILE * TILES * TILE * DH,
            bytes_accessed=2 * TILES * TILE * DH * 2,
            transcendentals=SLOTS * TILE * TILES * TILE,
        ),
    )(lists, query, kv)


def collect_kernel(o_ref, attn, send, recv, x_send, x_recv):
    plane = lax.axis_index("heads")
    me = lax.axis_index("ctx")
    row, column, core = where_is(me)
    barrier = pltpu.get_barrier_semaphore()

    def greet(step, carry):
        pl.semaphore_signal(
            barrier, inc=1, device_id=(plane, lax.rem(me + step, FRAMES)), device_id_type=MESH
        )
        return carry

    lax.fori_loop(1, FRAMES, greet, 0)
    sides = (lax.rem(plane + 1, PLANES), lax.rem(plane + PLANES - 1, PLANES))
    for there in sides:
        pl.semaphore_signal(barrier, inc=1, device_id=(there, me), device_id_type=MESH)
    pl.semaphore_wait(barrier, FRAMES - 1 + 2)

    mine = jnp.minimum(row, HEADS_HERE - 1)
    goal = attn.at[plane * HEADS_HERE + mine, :, column * 2 + core]

    def back(step):
        there = lax.rem(me + step, FRAMES)
        return pltpu.make_async_remote_copy(
            src_ref=o_ref.at[:, there],
            dst_ref=goal,
            send_sem=send.at[step],
            recv_sem=recv.at[mine],
            device_id=(plane, there),
            device_id_type=MESH,
        )

    def start(step, carry):
        back(step).start()
        return carry

    def end(step, carry):
        back(step).wait_send()
        return carry

    working = row < HEADS_HERE

    @pl.when(working)
    def _():
        lax.fori_loop(1, FRAMES, start, 0)
        pltpu.make_async_copy(o_ref.at[:, me], goal, recv.at[mine]).start()

    cut = SLOTS // 2

    def near(head, side):
        part = attn.at[plane * HEADS_HERE + head]
        return pltpu.make_async_remote_copy(
            src_ref=part,
            dst_ref=part,
            send_sem=x_send.at[head, side],
            recv_sem=x_recv.at[head, side],
            device_id=(sides[side], me),
            device_id_type=MESH,
        )

    def far(head, side):
        part = attn.at[sides[1 - side] * HEADS_HERE + head]
        part = part.at[pl.ds(0, cut)] if side == 0 else part.at[pl.ds(cut, SLOTS - cut)]
        return pltpu.make_async_remote_copy(
            src_ref=part,
            dst_ref=part,
            send_sem=x_send.at[head, 2 + side],
            recv_sem=x_recv.at[head, 2 + side],
            device_id=(sides[side], me),
            device_id_type=MESH,
        )

    for head in range(HEADS_HERE):
        part = attn.at[plane * HEADS_HERE + head]
        pltpu.make_async_copy(part, part, recv.at[head]).wait()
        for side in range(2):
            near(head, side).start()
    for head in range(HEADS_HERE):
        for side in range(2):
            near(head, side).wait_recv()
            far(head, side).start()

    @pl.when(working)
    def _():
        lax.fori_loop(1, FRAMES, end, 0)

    for head in range(HEADS_HERE):
        for side in range(2):
            near(head, side).wait_send()
            far(head, side).wait()


def collect(attended):
    return pl.pallas_call(
        collect_kernel,
        out_shape=jax.ShapeDtypeStruct(
            (PLANES * HEADS_HERE, SLOTS, WORKERS, SPOTS, DH), BF16
        ),
        in_specs=[pl.BlockSpec(memory_space=pl.ANY)],
        out_specs=pl.BlockSpec(memory_space=pl.ANY),
        scratch_shapes=[
            pltpu.SemaphoreType.DMA((FRAMES,)),
            pltpu.SemaphoreType.DMA((HEADS_HERE,)),
            pltpu.SemaphoreType.DMA((HEADS_HERE, 4)),
            pltpu.SemaphoreType.DMA((HEADS_HERE, 4)),
        ],
        compiler_params=pltpu.CompilerParams(
            collective_id=1, has_side_effects=True, vmem_limit_bytes=4 * 1024 * 1024
        ),
    )(attended)


def project_kernel(attn_ref, *refs):
    weights, out_ref = refs[:-1], refs[-1]
    plane = lax.axis_index("heads")
    wide, tall = [], []
    for hop, weight in enumerate(weights):
        source = lax.rem(plane + PLANES - hop, PLANES)
        wide += [attn_ref[source * HEADS_HERE + h] for h in range(HEADS_HERE)]
        tall.append(weight[...])
    out_ref[...] = jnp.dot(
        jnp.concatenate(wide, axis=1),
        jnp.concatenate(tall, axis=0),
        preferred_element_type=F32,
    ).astype(BF16)


def project(attn, weights, rows):
    depth, columns = weights[0].shape
    block = 256
    return pl.pallas_call(
        project_kernel,
        out_shape=jax.ShapeDtypeStruct((rows, columns), BF16),
        grid=(columns // block,),
        in_specs=[pl.BlockSpec(attn.shape, lambda i: (0, 0, 0))]
        + [pl.BlockSpec((depth, block), lambda i: (0, i))] * len(weights),
        out_specs=pl.BlockSpec((rows, block), lambda i: (0, i)),
        compiler_params=pltpu.CompilerParams(vmem_limit_bytes=24 * 1024 * 1024),
    )(attn, *weights)


def arrange_kernel(pattern_ref, mask_ref, q_ref, k_ref, v_ref, w_ref, *refs):
    w_out, (q_out, kv_out, list_ref, sems) = refs[:PLANES], refs[PLANES:]
    plane = lax.axis_index("heads")
    width = w_out[0].shape[1]
    cuts = []
    for hop in range(PLANES):
        first = pl.multiple_of(lax.rem(plane + hop, PLANES) * width, 128)
        cuts.append(
            pltpu.make_async_copy(w_ref.at[:, pl.ds(first, width)], w_out[hop], sems.at[hop])
        )
        cuts[-1].start()
    me = lax.axis_index("ctx")
    row, column, core = where_is(me)
    rows = q_ref.shape[0]
    for head in range(HEADS_HERE):
        columns = slice(head * DH, (head + 1) * DH)
        q_out[head] = q_ref[:, columns]
        kv_out[head, :rows, :] = k_ref[:, columns]
        kv_out[head, rows:, :] = v_ref[:, columns]

    pattern = pattern_ref[jnp.minimum(row, HEADS_HERE - 1)]
    masks = []
    tiles = [slot * WORKERS + column * 2 + core for slot in range(SLOTS)]
    for tile in tiles:
        masks.append(jnp.where(row < HEADS_HERE, mask_ref[pattern, pl.ds(tile, 1), :], 0))
    seen = jnp.concatenate(masks, axis=0) == 1
    seen = jnp.where(seen, 1.0, 0.0).astype(F32)
    down = lax.broadcasted_iota(jnp.int32, (TILES, TILES), 0)
    along = lax.broadcasted_iota(jnp.int32, (TILES, TILES), 1)
    both = (((1,), (1,)), ((), ()))
    upto = jnp.where(along <= down, 1.0, 0.0).astype(BF16)
    same = jnp.where(along == down, 1.0, 0.0).astype(BF16)
    rank = lax.dot_general(upto, seen.astype(BF16), both, preferred_element_type=F32)
    turned = lax.dot_general(same, seen.astype(BF16), both, preferred_element_type=F32)
    rank = rank.astype(jnp.int32)
    spot = jnp.where(turned > 0.5, rank - 1, -1)
    for slot in range(SLOTS):
        hit = spot[:, slot : slot + 1] == along
        listed = jnp.sum(jnp.where(hit, down, 0), axis=0, keepdims=True)
        spare = along[:1, :] >= rank[TILES - 1 :, slot : slot + 1]
        list_ref[slot : slot + 1, :] = jnp.where(spare, tiles[slot], listed)
    last = jnp.concatenate(
        [rank[TILES - 1 :, :], jnp.zeros((1, TILES - SLOTS), jnp.int32)], axis=1
    )
    list_ref[SLOTS : SLOTS + 1, :] = last
    for cut in cuts:
        cut.wait()


def arrange(head_pattern, tile_masks, queries, key_rows, value_rows, out_weight):
    rows = queries.shape[0]
    depth, columns = out_weight.shape
    return pl.pallas_call(
        arrange_kernel,
        out_shape=(
            *[jax.ShapeDtypeStruct((depth, columns // PLANES), BF16)] * PLANES,
            jax.ShapeDtypeStruct((HEADS_HERE, rows, DH), BF16),
            jax.ShapeDtypeStruct((HEADS_HERE, 2 * rows, DH), BF16),
            jax.ShapeDtypeStruct((SLOTS + 1, TILES), jnp.int32),
        ),
        in_specs=[pl.BlockSpec(memory_space=pltpu.SMEM)]
        + [pl.BlockSpec(memory_space=pltpu.VMEM)] * 4
        + [pl.BlockSpec(memory_space=pl.ANY)],
        out_specs=(
            *[pl.BlockSpec(memory_space=pl.ANY)] * PLANES,
            *[pl.BlockSpec(memory_space=pltpu.VMEM)] * 3,
        ),
        scratch_shapes=[pltpu.SemaphoreType.DMA((PLANES,))],
        compiler_params=pltpu.CompilerParams(vmem_limit_bytes=16 * 1024 * 1024),
    )(head_pattern, tile_masks, queries, key_rows, value_rows, out_weight)


def body(queries, key_rows, value_rows, out_weight, tile_masks, head_pattern):
    rows = queries.shape[0]
    *weights, q_parts, kv_parts, lists = arrange(
        head_pattern, tile_masks, queries, key_rows, value_rows, out_weight
    )
    q_all, kv_all = spread(
        q_parts.reshape(HEADS_HERE, SLOTS, WORKERS, SPOTS, DH),
        kv_parts.reshape(HEADS_HERE, 2 * TILES, SPOTS, DH),
    )
    q_all, *weights = lax.optimization_barrier((q_all, *weights))
    for hop in range(1, PLANES):
        ring = [(plane, (plane + hop) % PLANES) for plane in range(PLANES)]
        weights[hop] = lax.ppermute(weights[hop], "heads", ring)
    attended = attend(
        lists,
        q_all.reshape(SLOTS * TILE, DH),
        kv_all.reshape(WORKERS, 2 * TILES * PIECE, DH),
    )
    attn = collect(attended.reshape(SLOTS, FRAMES, SPOTS, DH))
    attn = attn.reshape(PLANES * HEADS_HERE, rows, DH)
    return project(attn, weights, rows)


def solution(mesh):
    placed = (
        P("ctx", "heads"),
        P("ctx", "heads"),
        P("ctx", "heads"),
        P("heads", None),
        P(),
        P("heads"),
    )
    return jax.shard_map(
        body, mesh=mesh, in_specs=placed, out_specs=P("ctx", "heads"), check_vma=False
    )
```

```python
import math

import jax
import jax.numpy as jnp
from jax import lax
from jax.experimental import pallas as pl
from jax.experimental.pallas import tpu as pltpu
from jax.sharding import PartitionSpec as P

MESH = pl.DeviceIdType.MESH
DH = 128
TILE = 128
SPOTS = 4
FRAMES = 32
TILES = 128
PLANES = 4
SIDE = 4
HEADS_HERE = 3
WORKERS = 2 * SIDE
SLOTS = TILES // WORKERS
PARTS = 4
PART = 2 * TILES // PARTS
PIECES = ((0, TILES, 0, 1), (TILES, TILES, 0, 1)) + tuple(
    (part * PART, PART, 1, SIDE - 1) for part in range(PARTS)
)
ROUND = (1, 2)
PIECE = TILE // WORKERS
GROUP = 8
BESIDE = 4
FAR = 2.0**64
LOW = -1e30
SCALE2 = math.log2(math.e) / math.sqrt(DH)
BF16 = jnp.bfloat16
F32 = jnp.float32


def where_is(device, plane):
    z, y = lax.div(device, 2 * SIDE), lax.rem(lax.div(device, 2), SIDE)
    odd = lax.rem(plane, 2)
    return z + odd * (y - z), y + odd * (z - y), lax.rem(device, 2)


def device_at(row, column, core, plane):
    row, column = lax.rem(row, SIDE), lax.rem(column, SIDE)
    odd = lax.rem(plane, 2)
    return ((row + odd * (column - row)) * SIDE + column + odd * (row - column)) * 2 + core


def spread_kernel(
    q_ref, kv_ref, w_ref, q_all, kv_all, w_all,
    q_send, q_recv, z_send, z_recv, y_send, y_recv, far_send, far_recv,
    core_send, core_recv, w_send, w_recv, w_core_send, w_core_recv, own_sem,
    held_own, held_part, passed_own, passed_part, leg_send, leg_recv,
):
    plane = lax.axis_index("heads")
    me = lax.axis_index("ctx")
    row, column, core = where_is(me, plane)
    working = row < HEADS_HERE
    own_row = jnp.minimum(row, HEADS_HERE - 1)
    depth = w_ref.shape[0]
    width = w_all.shape[1]
    sides = (1, SIDE - 1)

    barrier = pltpu.get_barrier_semaphore()

    def greet(step, carry):
        pl.semaphore_signal(
            barrier, inc=1, device_id=(plane, lax.rem(me + step, FRAMES)), device_id_type=MESH
        )
        return carry

    lax.fori_loop(1, FRAMES, greet, 0)
    for hop in range(1, PLANES):
        pl.semaphore_signal(
            barrier, inc=1, device_id=(lax.rem(plane + hop, PLANES), me), device_id_type=MESH
        )
    pl.semaphore_wait(barrier, FRAMES - 1 + PLANES - 1)

    def span(part):
        return pl.ds(part * PART, PART)

    own_copy = pltpu.make_async_copy(
        kv_ref.at[own_row], kv_all.at[column * 2 + core, :, 0], own_sem
    )

    def z_copy(part, hop):
        there = lax.rem(row + hop, SIDE)
        return pltpu.make_async_remote_copy(
            src_ref=kv_ref.at[there, span(part)],
            dst_ref=kv_all.at[column * 2 + core, span(part), hop],
            send_sem=z_send.at[part, hop],
            recv_sem=z_recv.at[part, hop],
            device_id=(plane, device_at(there, column, core, plane)),
            device_id_type=MESH,
        )

    def cut(source, number, share=None):
        first, count, row_first, row_count = PIECES[number]
        if share is not None:
            first, count = first + share * (count // 2), count // 2
        return source.at[pl.ds(first, count), pl.ds(row_first, row_count)]

    def piece(number, away):
        return cut(kv_all.at[lax.rem(column + away, SIDE) * 2 + core], number)

    def y_copy(number, side):
        return pltpu.make_async_remote_copy(
            src_ref=piece(number, 0),
            dst_ref=piece(number, 0),
            send_sem=y_send.at[number, side],
            recv_sem=y_recv.at[number, side],
            device_id=(plane, device_at(row, column + sides[side], core, plane)),
            device_id_type=MESH,
        )

    def far_copy(number, side):
        chunk = cut(kv_all.at[lax.rem(column + sides[1 - side], SIDE) * 2 + core], number, side)
        return pltpu.make_async_remote_copy(
            src_ref=chunk,
            dst_ref=chunk,
            send_sem=far_send.at[number, side],
            recv_sem=far_recv.at[number, side],
            device_id=(plane, device_at(row, column + sides[side], core, plane)),
            device_id_type=MESH,
        )

    held, passed = (held_own, held_part), (passed_own, passed_part)

    other_row, other_column, _ = where_is(me, plane + 1)
    relaying = other_row < HEADS_HERE

    def next_plane(side):
        return lax.rem(plane + sides[side], PLANES)

    def first_leg(number, side):
        return pltpu.make_async_remote_copy(
            src_ref=piece(number, 0),
            dst_ref=held[ROUND.index(number)].at[side],
            send_sem=leg_send.at[0, number, side],
            recv_sem=leg_recv.at[0, number, side],
            device_id=(next_plane(side), me),
            device_id_type=MESH,
        )

    def second_leg(number, side):
        there = device_at(other_row, other_column + sides[side], core, plane + 1)
        return pltpu.make_async_remote_copy(
            src_ref=held[ROUND.index(number)].at[side],
            dst_ref=passed[ROUND.index(number)].at[side],
            send_sem=leg_send.at[1, number, side],
            recv_sem=leg_recv.at[1, number, side],
            device_id=(plane, there),
            device_id_type=MESH,
        )

    def third_leg(number, side):
        source = kv_all.at[lax.rem(other_column + sides[1 - side], SIDE) * 2 + core]
        return pltpu.make_async_remote_copy(
            src_ref=passed[ROUND.index(number)].at[side],
            dst_ref=cut(source, number),
            send_sem=leg_send.at[2, number, side],
            recv_sem=y_recv.at[number, side],
            device_id=(next_plane(1 - side), me),
            device_id_type=MESH,
        )

    def relay(leg, number):
        @pl.when(relaying)
        def _():
            for side in range(2):
                if leg == 1:
                    first_leg(number, side).wait_recv()
                    second_leg(number, side).start()
                else:
                    second_leg(number, side).wait_recv()
                    third_leg(number, side).start()

    def core_copy(number, away):
        return pltpu.make_async_remote_copy(
            src_ref=piece(number, away),
            dst_ref=piece(number, away),
            send_sem=core_send.at[number, away],
            recv_sem=core_recv,
            device_id=(plane, device_at(row, column, 1 - core, plane)),
            device_id_type=MESH,
        )

    half = depth // 2

    def w_rows(source, part):
        return w_all.at[pl.ds(pl.multiple_of(source * depth + part * half, 16), half)]

    def w_copy(hop):
        there = lax.rem(plane + hop, PLANES)
        return pltpu.make_async_remote_copy(
            src_ref=w_ref.at[
                pl.ds(pl.multiple_of(core * half, 16), half),
                pl.ds(pl.multiple_of(there * width, 128), width),
            ],
            dst_ref=w_rows(plane, core),
            send_sem=w_send.at[hop],
            recv_sem=w_recv.at[hop],
            device_id=(there, me),
            device_id_type=MESH,
        )

    def w_core_copy(hop):
        rows = w_rows(lax.rem(plane + PLANES - hop, PLANES), core)
        return pltpu.make_async_remote_copy(
            src_ref=rows,
            dst_ref=rows,
            send_sem=w_core_send.at[hop],
            recv_sem=w_core_recv.at[hop],
            device_id=(plane, device_at(row, column, 1 - core, plane)),
            device_id_type=MESH,
        )

    own_w = pltpu.make_async_copy(
        w_ref.at[:, pl.ds(pl.multiple_of(plane * width, 128), width)],
        w_all.at[pl.ds(pl.multiple_of(plane * depth, 128), depth)],
        w_recv.at[0],
    )

    def q_copy(step):
        there = lax.rem(me + step, FRAMES)
        row_there, column_there, core_there = where_is(there, plane)
        return row_there < HEADS_HERE, pltpu.make_async_remote_copy(
            src_ref=q_ref.at[
                jnp.minimum(row_there, HEADS_HERE - 1), :, column_there * 2 + core_there
            ],
            dst_ref=q_all.at[:, me],
            send_sem=q_send.at[step],
            recv_sem=q_recv,
            device_id=(plane, there),
            device_id_type=MESH,
        )

    def to_rows(part, work):
        for hop in range(1, SIDE):

            @pl.when(lax.rem(row + hop, SIDE) < HEADS_HERE)
            def _():
                work(z_copy(part, hop))

    def send_q(step, carry):
        wanted, copy = q_copy(step)

        @pl.when(wanted)
        def _():
            copy.start()

        return carry

    def sent_q(step, carry):
        wanted, copy = q_copy(step)

        @pl.when(wanted)
        def _():
            copy.wait_send()

        return carry

    def send_weights():
        for hop in range(1, PLANES):
            w_copy(hop).start()
        own_w.start()

    def send_on(number):
        for side in range(2):
            if number in ROUND:
                first_leg(number, side).start()
            else:
                y_copy(number, side).start()
        core_copy(number, 0).start()

    to_rows(0, lambda copy: copy.start())

    @pl.when(working)
    def _():
        own_copy.start()
        own_copy.wait()
        send_on(0)
        send_on(1)
        pltpu.make_async_copy(
            q_ref.at[own_row, :, column * 2 + core], q_all.at[:, me], q_recv
        ).start()

    lax.fori_loop(1, FRAMES, send_q, 0)

    def next_rows(part):
        to_rows(part, lambda copy: copy.wait_send())
        if part + 1 < PARTS:
            to_rows(part + 1, lambda copy: copy.start())

    def gathered(part):
        next_rows(part)

        @pl.when(working)
        def _():
            for hop in range(1, SIDE):
                landed = kv_all.at[column * 2 + core, span(part), hop]
                pltpu.make_async_copy(landed, landed, z_recv.at[part, hop]).wait()
            send_on(part + 2)

    def pass_on(number):
        @pl.when(working)
        def _():
            for side in range(2):
                y_copy(number, side).wait_recv()
                far_copy(number, side).start()
            for side in range(2):
                core_copy(number, sides[1 - side]).start()

    gathered(0)
    pass_on(0)
    relay(1, 1)
    gathered(1)
    relay(1, 2)
    send_weights()
    gathered(2)
    relay(2, 1)
    pass_on(3)
    gathered(3)
    relay(2, 2)
    pass_on(1)
    pass_on(4)
    pass_on(2)
    pass_on(5)

    @pl.when(working)
    def _():
        for number in (0, 3, 1, 4, 2, 5):
            for side in range(2):
                far_copy(number, side).wait_recv()
            core_copy(number, 2).start()

    for hop in range(1, PLANES):
        w_copy(hop).wait_recv()
        w_core_copy(hop).start()

    @pl.when(working)
    def _():
        pltpu.make_async_copy(q_all, q_all, q_recv).wait()
        other = kv_all.at[pl.ds(0, SIDE)]
        pltpu.make_async_copy(other, other, core_recv).wait()
        for number in range(len(PIECES)):
            for side in range(2):
                if number in ROUND:
                    first_leg(number, side).wait_send()
                else:
                    y_copy(number, side).wait_send()
                far_copy(number, side).wait_send()
            for away in range(SIDE):
                core_copy(number, away).wait_send()

    @pl.when(relaying)
    def _():
        for number in ROUND:
            for side in range(2):
                second_leg(number, side).wait_send()
                third_leg(number, side).wait_send()

    own_w.wait()
    lax.fori_loop(1, FRAMES, sent_q, 0)
    for hop in range(1, PLANES):
        w_copy(hop).wait_send()
        w_core_copy(hop).wait()


def spread(q_parts, kv_parts, out_weight):
    depth, columns = out_weight.shape
    return pl.pallas_call(
        spread_kernel,
        out_shape=(
            jax.ShapeDtypeStruct((SLOTS, FRAMES, SPOTS, DH), BF16),
            jax.ShapeDtypeStruct((WORKERS, 2 * TILES, SIDE, SPOTS, DH), BF16),
            jax.ShapeDtypeStruct((depth * PLANES, columns // PLANES), BF16),
        ),
        in_specs=[pl.BlockSpec(memory_space=pl.ANY)] * 3,
        out_specs=(pl.BlockSpec(memory_space=pl.ANY),) * 3,
        scratch_shapes=[
            pltpu.SemaphoreType.DMA((FRAMES,)),
            pltpu.SemaphoreType.DMA,
            pltpu.SemaphoreType.DMA((PARTS, SIDE)),
            pltpu.SemaphoreType.DMA((PARTS, SIDE)),
            pltpu.SemaphoreType.DMA((len(PIECES), 2)),
            pltpu.SemaphoreType.DMA((len(PIECES), 2)),
            pltpu.SemaphoreType.DMA((len(PIECES), 2)),
            pltpu.SemaphoreType.DMA((len(PIECES), 2)),
            pltpu.SemaphoreType.DMA((len(PIECES), SIDE)),
            pltpu.SemaphoreType.DMA,
            pltpu.SemaphoreType.DMA((PLANES,)),
            pltpu.SemaphoreType.DMA((PLANES,)),
            pltpu.SemaphoreType.DMA((PLANES,)),
            pltpu.SemaphoreType.DMA((PLANES,)),
            pltpu.SemaphoreType.DMA,
            *[
                pltpu.VMEM((2, PIECES[number][1], PIECES[number][3], SPOTS, DH), BF16)
                for number in ROUND + ROUND
            ],
            pltpu.SemaphoreType.DMA((3, len(PIECES), 2)),
            pltpu.SemaphoreType.DMA((2, len(PIECES), 2)),
        ],
        compiler_params=pltpu.CompilerParams(
            collective_id=0, has_side_effects=True, vmem_limit_bytes=12 * 1024 * 1024
        ),
    )(q_parts, kv_parts, out_weight)


def attend_kernel(
    list_ref, q_ref, kv_ref, o_ref, keys_ref, values_ref, base_ref, peak_ref, sum_ref,
    slot_of, first_of, listed_of,
):
    _, column, core = where_is(lax.axis_index("ctx"), lax.axis_index("heads"))

    def loop(count, work):
        def one(step, carry):
            work(step)
            return carry

        lax.fori_loop(0, count, one, 0)

    def rows_of(slot):
        return pl.ds(pl.multiple_of(slot * TILE, TILE), TILE)

    def tile_at(tile):
        start = pl.multiple_of(tile * PIECE, PIECE)
        return jnp.concatenate(
            [kv_ref[worker, pl.ds(start, PIECE), :] for worker in range(WORKERS)], axis=0
        )

    def enlist(slot, total):
        count = list_ref[SLOTS, slot]
        steps = lax.div(count + GROUP - 1, GROUP)

        def one(step, carry):
            slot_of[total + step] = slot
            first_of[total + step] = step * GROUP
            listed_of[total + step] = count - step * GROUP
            return carry

        lax.fori_loop(0, steps, one, 0)
        return total + steps

    total = lax.fori_loop(0, SLOTS, enlist, 0)
    for spare in range(BESIDE - 1):
        slot_of[total + spare] = 0
        first_of[total + spare] = 0
        listed_of[total + spare] = 0
    turns = lax.div(total + BESIDE - 1, BESIDE)
    busy = jnp.where(total > 0, 1, 0)

    values_ref[TILES] = jnp.zeros((TILE, DH), BF16)

    def unpack(step):
        for u in range(GROUP):
            tile = step * GROUP + u
            keys_ref[tile] = tile_at(tile).T
            values_ref[tile] = tile_at(TILES + tile)

    loop(busy * (TILES // GROUP), unpack)

    def set_base(slot, base):
        base_ref[slot] = jnp.broadcast_to(base * SCALE2, (TILE, TILE))

    def own_base(step):
        for u in range(BESIDE):
            slot = step * BESIDE + u
            own = keys_ref[slot * WORKERS + column * 2 + core]
            scores = jnp.dot(q_ref[rows_of(slot), :], own, preferred_element_type=F32)
            set_base(slot, jnp.max(scores, axis=1, keepdims=True))

    loop(busy * (SLOTS // BESIDE), own_base)

    def tiles_of(number):
        slot, first = slot_of[number], first_of[number]
        return slot, [list_ref[slot, first + u] for u in range(GROUP)]

    def scores_of(slot, tiles):
        keys = jnp.concatenate([keys_ref[tile] for tile in tiles], axis=1)
        return jnp.dot(q_ref[rows_of(slot), :], keys, preferred_element_type=F32)

    def attend_steps(step):
        found = []
        for beside in range(BESIDE):
            number = step * BESIDE + beside
            slot, tiles = tiles_of(number)
            listed = listed_of[number]
            base = base_ref[slot]
            base = jnp.concatenate([base, base], axis=1)
            weights, values = [], []
            for u in range(0, GROUP, 2):
                scores = scores_of(slot, tiles[u : u + 2])
                weights.append(jnp.exp2(scores * SCALE2 - base).astype(BF16))
            for u in range(GROUP):
                value = values_ref[jnp.where(u < listed, tiles[u], TILES)]
                ones = jnp.where(u < listed, 1.0, 0.0).astype(BF16)
                ones = jnp.broadcast_to(ones, (TILE, DH))
                values.append(jnp.concatenate([value, ones], axis=1))
            added = jnp.dot(
                jnp.concatenate(weights, axis=1),
                jnp.concatenate(values, axis=0),
                preferred_element_type=F32,
            )
            found.append((slot, added))
        for slot, added in found:
            sum_ref[slot] += added

    def peak_steps(step):
        for beside in range(BESIDE):
            slot, tiles = tiles_of(step * BESIDE + beside)
            scores = scores_of(slot, tiles)
            peak = peak_ref[slot]
            for u in range(GROUP):
                peak = jnp.maximum(peak, scores[:, u * TILE : (u + 1) * TILE])
            peak_ref[slot] = peak

    def attempt(number, needed):
        def clear(slot):
            sum_ref[slot] = jnp.zeros((TILE, 2 * DH), F32)
            peak_ref[slot] = jnp.full((TILE, TILE), LOW, F32)

        loop(needed * SLOTS, clear)
        loop(needed * turns, attend_steps)
        beyond = jnp.zeros((TILE, DH), F32)
        for slot in range(SLOTS):
            beyond = jnp.where(sum_ref[slot, :, DH:] <= FAR, beyond, 1.0)
        again = needed * jnp.where(jnp.max(beyond) > 0.0, 1, 0)
        loop(again * turns, peak_steps)

        def rebase(slot):
            set_base(slot, jnp.max(peak_ref[slot], axis=1, keepdims=True))

        loop(again * SLOTS, rebase)
        return again

    lax.fori_loop(0, 2, attempt, busy)

    def finish(step):
        for u in range(BESIDE):
            slot = step * BESIDE + u
            o_ref[rows_of(slot), :] = (sum_ref[slot, :, :DH] / sum_ref[slot, :, DH:]).astype(BF16)

    loop(busy * (SLOTS // BESIDE), finish)


def attend(lists, query, kv):
    most = SLOTS * (TILES // GROUP) + BESIDE
    return pl.pallas_call(
        attend_kernel,
        out_shape=jax.ShapeDtypeStruct(query.shape, BF16),
        in_specs=[
            pl.BlockSpec(memory_space=pltpu.SMEM),
            pl.BlockSpec(memory_space=pltpu.VMEM),
            pl.BlockSpec(memory_space=pltpu.VMEM),
        ],
        out_specs=pl.BlockSpec(memory_space=pltpu.VMEM),
        scratch_shapes=[
            pltpu.VMEM((TILES, DH, TILE), BF16),
            pltpu.VMEM((TILES + 1, TILE, DH), BF16),
            pltpu.VMEM((SLOTS, TILE, TILE), F32),
            pltpu.VMEM((SLOTS, TILE, TILE), F32),
            pltpu.VMEM((SLOTS, TILE, 2 * DH), F32),
            pltpu.SMEM((most,), jnp.int32),
            pltpu.SMEM((most,), jnp.int32),
            pltpu.SMEM((most,), jnp.int32),
        ],
        compiler_params=pltpu.CompilerParams(vmem_limit_bytes=40 * 1024 * 1024),
    )(lists, query, kv)


def collect_kernel(o_ref, attn, send, recv, x_send, x_recv):
    plane = lax.axis_index("heads")
    me = lax.axis_index("ctx")
    row, column, core = where_is(me, plane)
    barrier = pltpu.get_barrier_semaphore()

    def greet(step, carry):
        pl.semaphore_signal(
            barrier, inc=1, device_id=(plane, lax.rem(me + step, FRAMES)), device_id_type=MESH
        )
        return carry

    lax.fori_loop(1, FRAMES, greet, 0)
    sides = (lax.rem(plane + 1, PLANES), lax.rem(plane + PLANES - 1, PLANES))
    for there in sides:
        pl.semaphore_signal(barrier, inc=1, device_id=(there, me), device_id_type=MESH)
    pl.semaphore_wait(barrier, FRAMES - 1 + 2)

    mine = jnp.minimum(row, HEADS_HERE - 1)
    goal = attn.at[plane * HEADS_HERE + mine, :, column * 2 + core]

    def back(step):
        there = lax.rem(me + step, FRAMES)
        return pltpu.make_async_remote_copy(
            src_ref=o_ref.at[:, there],
            dst_ref=goal,
            send_sem=send.at[step],
            recv_sem=recv.at[mine],
            device_id=(plane, there),
            device_id_type=MESH,
        )

    def start(step, carry):
        back(step).start()
        return carry

    def end(step, carry):
        back(step).wait_send()
        return carry

    working = row < HEADS_HERE

    @pl.when(working)
    def _():
        lax.fori_loop(1, FRAMES, start, 0)
        pltpu.make_async_copy(o_ref.at[:, me], goal, recv.at[mine]).start()

    cut = SLOTS // 2

    def near(head, side):
        part = attn.at[plane * HEADS_HERE + head]
        return pltpu.make_async_remote_copy(
            src_ref=part,
            dst_ref=part,
            send_sem=x_send.at[head, side],
            recv_sem=x_recv.at[head, side],
            device_id=(sides[side], me),
            device_id_type=MESH,
        )

    def far(head, side):
        part = attn.at[sides[1 - side] * HEADS_HERE + head]
        part = part.at[pl.ds(0, cut)] if side == 0 else part.at[pl.ds(cut, SLOTS - cut)]
        return pltpu.make_async_remote_copy(
            src_ref=part,
            dst_ref=part,
            send_sem=x_send.at[head, 2 + side],
            recv_sem=x_recv.at[head, 2 + side],
            device_id=(sides[side], me),
            device_id_type=MESH,
        )

    for head in range(HEADS_HERE):
        part = attn.at[plane * HEADS_HERE + head]
        pltpu.make_async_copy(part, part, recv.at[head]).wait()
        for side in range(2):
            near(head, side).start()
    for head in range(HEADS_HERE):
        for side in range(2):
            near(head, side).wait_recv()
            far(head, side).start()

    @pl.when(working)
    def _():
        lax.fori_loop(1, FRAMES, end, 0)

    for head in range(HEADS_HERE):
        for side in range(2):
            near(head, side).wait_send()
            far(head, side).wait()


def collect(attended):
    return pl.pallas_call(
        collect_kernel,
        out_shape=jax.ShapeDtypeStruct(
            (PLANES * HEADS_HERE, SLOTS, WORKERS, SPOTS, DH), BF16
        ),
        in_specs=[pl.BlockSpec(memory_space=pl.ANY)],
        out_specs=pl.BlockSpec(memory_space=pl.ANY),
        scratch_shapes=[
            pltpu.SemaphoreType.DMA((FRAMES,)),
            pltpu.SemaphoreType.DMA((HEADS_HERE,)),
            pltpu.SemaphoreType.DMA((HEADS_HERE, 4)),
            pltpu.SemaphoreType.DMA((HEADS_HERE, 4)),
        ],
        compiler_params=pltpu.CompilerParams(
            collective_id=1, has_side_effects=True, vmem_limit_bytes=4 * 1024 * 1024
        ),
    )(attended)


def project_kernel(attn_ref, w_ref, out_ref):
    rows = out_ref.shape[0]
    heads = attn_ref.shape[0]
    wide = jnp.concatenate([attn_ref[h, :rows, :] for h in range(heads)], axis=1)
    out_ref[...] = jnp.dot(wide, w_ref[...], preferred_element_type=F32).astype(BF16)


def project(attn, weight, rows):
    columns = weight.shape[1]
    block = 256
    heads = attn.shape[0]
    return pl.pallas_call(
        project_kernel,
        out_shape=jax.ShapeDtypeStruct((rows, columns), BF16),
        grid=(columns // block,),
        in_specs=[
            pl.BlockSpec((heads, attn.shape[1], DH), lambda i: (0, 0, 0)),
            pl.BlockSpec((weight.shape[0], block), lambda i: (0, i)),
        ],
        out_specs=pl.BlockSpec((rows, block), lambda i: (0, i)),
        compiler_params=pltpu.CompilerParams(vmem_limit_bytes=24 * 1024 * 1024),
    )(attn, weight)


def arrange_kernel(pattern_ref, mask_ref, q_ref, k_ref, v_ref, q_out, kv_out, list_ref):
    me = lax.axis_index("ctx")
    row, column, core = where_is(me, lax.axis_index("heads"))
    rows = q_ref.shape[0]
    for head in range(HEADS_HERE):
        columns = slice(head * DH, (head + 1) * DH)
        q_out[head] = q_ref[:, columns]
        kv_out[head, :rows, :] = k_ref[:, columns]
        kv_out[head, rows:, :] = v_ref[:, columns]

    pattern = pattern_ref[jnp.minimum(row, HEADS_HERE - 1)]
    masks = []
    tiles = [slot * WORKERS + column * 2 + core for slot in range(SLOTS)]
    for tile in tiles:
        masks.append(jnp.where(row < HEADS_HERE, mask_ref[pattern, pl.ds(tile, 1), :], 0))
    seen = jnp.concatenate(masks, axis=0) == 1
    seen = jnp.where(seen, 1.0, 0.0).astype(F32)
    down = lax.broadcasted_iota(jnp.int32, (TILES, TILES), 0)
    along = lax.broadcasted_iota(jnp.int32, (TILES, TILES), 1)
    both = (((1,), (1,)), ((), ()))
    upto = jnp.where(along <= down, 1.0, 0.0).astype(BF16)
    same = jnp.where(along == down, 1.0, 0.0).astype(BF16)
    rank = lax.dot_general(upto, seen.astype(BF16), both, preferred_element_type=F32)
    turned = lax.dot_general(same, seen.astype(BF16), both, preferred_element_type=F32)
    rank = rank.astype(jnp.int32)
    spot = jnp.where(turned > 0.5, rank - 1, -1)
    for slot in range(SLOTS):
        hit = spot[:, slot : slot + 1] == along
        listed = jnp.sum(jnp.where(hit, down, 0), axis=0, keepdims=True)
        spare = along[:1, :] >= rank[TILES - 1 :, slot : slot + 1]
        list_ref[slot : slot + 1, :] = jnp.where(spare, tiles[slot], listed)
    last = jnp.concatenate(
        [rank[TILES - 1 :, :], jnp.zeros((1, TILES - SLOTS), jnp.int32)], axis=1
    )
    list_ref[SLOTS : SLOTS + 1, :] = last


def arrange(head_pattern, tile_masks, queries, key_rows, value_rows):
    rows = queries.shape[0]
    return pl.pallas_call(
        arrange_kernel,
        out_shape=(
            jax.ShapeDtypeStruct((HEADS_HERE, rows, DH), BF16),
            jax.ShapeDtypeStruct((HEADS_HERE, 2 * rows, DH), BF16),
            jax.ShapeDtypeStruct((SLOTS + 1, TILES), jnp.int32),
        ),
        in_specs=[pl.BlockSpec(memory_space=pltpu.SMEM)]
        + [pl.BlockSpec(memory_space=pltpu.VMEM)] * 4,
        out_specs=(pl.BlockSpec(memory_space=pltpu.VMEM),) * 3,
        compiler_params=pltpu.CompilerParams(vmem_limit_bytes=16 * 1024 * 1024),
    )(head_pattern, tile_masks, queries, key_rows, value_rows)


def body(queries, key_rows, value_rows, out_weight, tile_masks, head_pattern):
    rows = queries.shape[0]
    q_parts, kv_parts, lists = arrange(head_pattern, tile_masks, queries, key_rows, value_rows)
    q_all, kv_all, w_all = spread(
        q_parts.reshape(HEADS_HERE, SLOTS, WORKERS, SPOTS, DH),
        kv_parts.reshape(HEADS_HERE, 2 * TILES, SPOTS, DH),
        out_weight,
    )
    attended = attend(
        lists, q_all.reshape(SLOTS * TILE, DH), kv_all.reshape(WORKERS, 2 * TILES * PIECE, DH)
    )
    attn = collect(attended.reshape(SLOTS, FRAMES, SPOTS, DH))
    attn = attn.reshape(PLANES * HEADS_HERE, rows, DH)
    return project(attn, w_all, rows)


def solution(mesh):
    placed = (
        P("ctx", "heads"),
        P("ctx", "heads"),
        P("ctx", "heads"),
        P("heads", None),
        P(),
        P("heads"),
    )
    return jax.shard_map(
        body, mesh=mesh, in_specs=placed, out_specs=P("ctx", "heads"), check_vma=False
    )
```

```python
import math

import jax
import jax.numpy as jnp
from jax import lax
from jax.experimental import pallas as pl
from jax.experimental.pallas import tpu as pltpu
from jax.sharding import PartitionSpec as P

MESH = pl.DeviceIdType.MESH
DH = 128
TILE = 128
SPOTS = 4
FRAMES = 32
TILES = 128
PLANES = 4
SIDE = 4
HEADS_HERE = 3
WORKERS = 2 * SIDE
SLOTS = TILES // WORKERS
PARTS = 4
PART = 2 * TILES // PARTS
PIECE = TILE // WORKERS
GROUP = 8
CHUNK = 32
BESIDE = 4
FAR = 2.0**64
LOW = -1e30
SCALE2 = math.log2(math.e) / math.sqrt(DH)
BF16 = jnp.bfloat16
F32 = jnp.float32


def where_is(device):
    return lax.div(device, WORKERS), lax.rem(lax.div(device, 2), SIDE), lax.rem(device, 2)


def device_at(row, column, core):
    return (lax.rem(row, SIDE) * SIDE + lax.rem(column, SIDE)) * 2 + core


def spread_kernel(
    q_ref, kv_ref, w_ref, q_all, kv_all, w_all,
    q_send, q_recv, z_send, z_recv, y_send, y_recv, far_send, far_recv,
    core_send, core_recv, w_send, w_recv, w_core_send, w_core_recv, own_sem,
):
    plane = lax.axis_index("heads")
    me = lax.axis_index("ctx")
    row, column, core = where_is(me)
    working = row < HEADS_HERE
    own_row = jnp.minimum(row, HEADS_HERE - 1)
    depth = w_ref.shape[0]
    width = w_all.shape[1]
    sides = (1, SIDE - 1)

    barrier = pltpu.get_barrier_semaphore()

    def greet(step, carry):
        pl.semaphore_signal(
            barrier, inc=1, device_id=(plane, lax.rem(me + step, FRAMES)), device_id_type=MESH
        )
        return carry

    lax.fori_loop(1, FRAMES, greet, 0)
    for hop in range(1, PLANES):
        pl.semaphore_signal(
            barrier, inc=1, device_id=(lax.rem(plane + hop, PLANES), me), device_id_type=MESH
        )
    pl.semaphore_wait(barrier, FRAMES - 1 + PLANES - 1)

    def span(part):
        return pl.ds(part * PART, PART)

    own_copy = pltpu.make_async_copy(
        kv_ref.at[own_row], kv_all.at[column * 2 + core, :, 0], own_sem
    )

    def z_copy(part, hop):
        there = lax.rem(row + hop, SIDE)
        return pltpu.make_async_remote_copy(
            src_ref=kv_ref.at[there, span(part)],
            dst_ref=kv_all.at[column * 2 + core, span(part), hop],
            send_sem=z_send.at[part, hop],
            recv_sem=z_recv.at[part, hop],
            device_id=(plane, device_at(there, column, core)),
            device_id_type=MESH,
        )

    def piece(number, away):
        source = kv_all.at[lax.rem(column + away, SIDE) * 2 + core]
        if number == 0:
            return source.at[:, 0]
        return source.at[span(number - 1), pl.ds(1, SIDE - 1)]

    def y_copy(number, side):
        return pltpu.make_async_remote_copy(
            src_ref=kv_ref.at[own_row] if number == 0 else piece(number, 0),
            dst_ref=piece(number, 0),
            send_sem=y_send.at[number, side],
            recv_sem=y_recv.at[number, side],
            device_id=(plane, device_at(row, column + sides[side], core)),
            device_id_type=MESH,
        )

    def far_copy(number, side):
        source = kv_all.at[lax.rem(column + sides[1 - side], SIDE) * 2 + core]
        if number == 0:
            chunk = source.at[pl.ds(side * TILES, TILES), 0]
        else:
            chunk = source.at[
                pl.ds((number - 1) * PART + side * (PART // 2), PART // 2), pl.ds(1, SIDE - 1)
            ]
        return pltpu.make_async_remote_copy(
            src_ref=chunk,
            dst_ref=chunk,
            send_sem=far_send.at[number, side],
            recv_sem=far_recv.at[number, side],
            device_id=(plane, device_at(row, column + sides[side], core)),
            device_id_type=MESH,
        )

    def core_copy(number, away):
        return pltpu.make_async_remote_copy(
            src_ref=piece(number, away),
            dst_ref=piece(number, away),
            send_sem=core_send.at[number, away],
            recv_sem=core_recv,
            device_id=(plane, device_at(row, column, 1 - core)),
            device_id_type=MESH,
        )

    half = depth // 2

    def w_rows(source, part):
        return w_all.at[pl.ds(pl.multiple_of(source * depth + part * half, 16), half)]

    def w_copy(hop):
        there = lax.rem(plane + hop, PLANES)
        return pltpu.make_async_remote_copy(
            src_ref=w_ref.at[
                pl.ds(pl.multiple_of(core * half, 16), half),
                pl.ds(pl.multiple_of(there * width, 128), width),
            ],
            dst_ref=w_rows(plane, core),
            send_sem=w_send.at[hop],
            recv_sem=w_recv.at[hop],
            device_id=(there, me),
            device_id_type=MESH,
        )

    def w_core_copy(hop):
        rows = w_rows(lax.rem(plane + PLANES - hop, PLANES), core)
        return pltpu.make_async_remote_copy(
            src_ref=rows,
            dst_ref=rows,
            send_sem=w_core_send.at[hop],
            recv_sem=w_core_recv.at[hop],
            device_id=(plane, device_at(row, column, 1 - core)),
            device_id_type=MESH,
        )

    own_w = pltpu.make_async_copy(
        w_ref.at[:, pl.ds(pl.multiple_of(plane * width, 128), width)],
        w_all.at[pl.ds(pl.multiple_of(plane * depth, 128), depth)],
        w_recv.at[0],
    )

    def q_copy(step):
        there = lax.rem(me + step, FRAMES)
        row_there, column_there, core_there = where_is(there)
        return row_there < HEADS_HERE, pltpu.make_async_remote_copy(
            src_ref=q_ref.at[
                jnp.minimum(row_there, HEADS_HERE - 1), :, column_there * 2 + core_there
            ],
            dst_ref=q_all.at[:, me],
            send_sem=q_send.at[step],
            recv_sem=q_recv,
            device_id=(plane, there),
            device_id_type=MESH,
        )

    def to_rows(part, work):
        for hop in range(1, SIDE):

            @pl.when(lax.rem(row + hop, SIDE) < HEADS_HERE)
            def _():
                work(z_copy(part, hop))

    def send_q(step, carry):
        wanted, copy = q_copy(step)

        @pl.when(wanted)
        def _():
            copy.start()

        return carry

    def sent_q(step, carry):
        wanted, copy = q_copy(step)

        @pl.when(wanted)
        def _():
            copy.wait_send()

        return carry

    def send_small():
        for hop in range(1, PLANES):
            w_copy(hop).start()
        own_w.start()
        lax.fori_loop(1, FRAMES, send_q, 0)

    @pl.when(working)
    def _():
        own_copy.start()
        for side in range(2):
            y_copy(0, side).start()

    to_rows(0, lambda copy: copy.start())
    send_small()

    def next_rows(part):
        to_rows(part, lambda copy: copy.wait_send())
        if part + 1 < PARTS:
            to_rows(part + 1, lambda copy: copy.start())

    @pl.when(jnp.logical_not(working))
    def _():
        for part in range(PARTS):
            next_rows(part)

    @pl.when(working)
    def _():
        pltpu.make_async_copy(
            q_ref.at[own_row, :, column * 2 + core], q_all.at[:, me], q_recv
        ).start()
        own_copy.wait()
        core_copy(0, 0).start()

        def pass_on(number):
            for side in range(2):
                y_copy(number, side).wait_recv()
                far_copy(number, side).start()
            for side in range(2):
                core_copy(number, sides[1 - side]).start()

        for part in range(PARTS):
            next_rows(part)
            for hop in range(1, SIDE):
                landed = kv_all.at[column * 2 + core, span(part), hop]
                pltpu.make_async_copy(landed, landed, z_recv.at[part, hop]).wait()
            for side in range(2):
                y_copy(part + 1, side).start()
            core_copy(part + 1, 0).start()
            pass_on(part)
        pass_on(PARTS)
        for number in range(PARTS + 1):
            for side in range(2):
                far_copy(number, side).wait_recv()
            core_copy(number, 2).start()

    for hop in range(1, PLANES):
        w_copy(hop).wait_recv()
        w_core_copy(hop).start()

    @pl.when(working)
    def _():
        pltpu.make_async_copy(q_all, q_all, q_recv).wait()
        other = kv_all.at[pl.ds(0, SIDE)]
        pltpu.make_async_copy(other, other, core_recv).wait()
        for number in range(PARTS + 1):
            for side in range(2):
                y_copy(number, side).wait_send()
                far_copy(number, side).wait_send()
            for away in range(SIDE):
                core_copy(number, away).wait_send()

    own_w.wait()
    lax.fori_loop(1, FRAMES, sent_q, 0)
    for hop in range(1, PLANES):
        w_copy(hop).wait_send()
        w_core_copy(hop).wait()


def spread(q_parts, kv_parts, out_weight):
    depth, columns = out_weight.shape
    return pl.pallas_call(
        spread_kernel,
        out_shape=(
            jax.ShapeDtypeStruct((SLOTS, FRAMES, SPOTS, DH), BF16),
            jax.ShapeDtypeStruct((WORKERS, 2 * TILES, SIDE, SPOTS, DH), BF16),
            jax.ShapeDtypeStruct((depth * PLANES, columns // PLANES), BF16),
        ),
        in_specs=[pl.BlockSpec(memory_space=pl.ANY)] * 3,
        out_specs=(pl.BlockSpec(memory_space=pl.ANY),) * 3,
        scratch_shapes=[
            pltpu.SemaphoreType.DMA((FRAMES,)),
            pltpu.SemaphoreType.DMA,
            pltpu.SemaphoreType.DMA((PARTS, SIDE)),
            pltpu.SemaphoreType.DMA((PARTS, SIDE)),
            pltpu.SemaphoreType.DMA((PARTS + 1, 2)),
            pltpu.SemaphoreType.DMA((PARTS + 1, 2)),
            pltpu.SemaphoreType.DMA((PARTS + 1, 2)),
            pltpu.SemaphoreType.DMA((PARTS + 1, 2)),
            pltpu.SemaphoreType.DMA((PARTS + 1, SIDE)),
            pltpu.SemaphoreType.DMA,
            pltpu.SemaphoreType.DMA((PLANES,)),
            pltpu.SemaphoreType.DMA((PLANES,)),
            pltpu.SemaphoreType.DMA((PLANES,)),
            pltpu.SemaphoreType.DMA((PLANES,)),
            pltpu.SemaphoreType.DMA,
        ],
        compiler_params=pltpu.CompilerParams(
            collective_id=0, has_side_effects=True, vmem_limit_bytes=57 * 1024 * 1024
        ),
    )(q_parts, kv_parts, out_weight)


def attend_kernel(
    list_ref, q_ref, kv_hbm, o_ref, kv_ref, keys_ref, values_ref, base_ref, peak_ref, sum_ref,
    slot_of, first_of, listed_of, kv_sem,
):
    def chunk(number, first):
        rows = pl.ds((first + number * CHUNK) * PIECE, CHUNK * PIECE)
        return pltpu.make_async_copy(
            kv_hbm.at[:, rows], kv_ref.at[:, rows], kv_sem.at[number, min(first, 1)]
        )

    for number in range(TILES // CHUNK):
        chunk(number, 0).start()
        chunk(number, TILES).start()

    _, column, core = where_is(lax.axis_index("ctx"))

    def loop(count, work):
        def one(step, carry):
            work(step)
            return carry

        lax.fori_loop(0, count, one, 0)

    def rows_of(slot):
        return pl.ds(pl.multiple_of(slot * TILE, TILE), TILE)

    def tile_at(tile):
        start = pl.multiple_of(tile * PIECE, PIECE)
        return jnp.concatenate(
            [kv_ref[worker, pl.ds(start, PIECE), :] for worker in range(WORKERS)], axis=0
        )

    def enlist(slot, total):
        count = list_ref[SLOTS, slot]
        steps = lax.div(count + GROUP - 1, GROUP)

        def one(step, carry):
            slot_of[total + step] = slot
            first_of[total + step] = step * GROUP
            listed_of[total + step] = count - step * GROUP
            return carry

        lax.fori_loop(0, steps, one, 0)
        return total + steps

    total = lax.fori_loop(0, SLOTS, enlist, 0)
    for spare in range(BESIDE - 1):
        slot_of[total + spare] = 0
        first_of[total + spare] = 0
        listed_of[total + spare] = 0
    turns = lax.div(total + BESIDE - 1, BESIDE)
    busy = jnp.where(total > 0, 1, 0)

    values_ref[TILES] = jnp.zeros((TILE, DH), BF16)

    def unpack(step):
        for u in range(GROUP):
            tile = step * GROUP + u
            keys_ref[tile] = tile_at(tile).T
            values_ref[tile] = tile_at(TILES + tile)

    for number in range(TILES // CHUNK):
        chunk(number, 0).wait()
        chunk(number, TILES).wait()
        steps = CHUNK // GROUP
        loop(busy * steps, lambda step: unpack(step + number * steps))

    def set_base(slot, base):
        base_ref[slot] = jnp.broadcast_to(base * SCALE2, (TILE, TILE))

    def own_base(step):
        for u in range(BESIDE):
            slot = step * BESIDE + u
            own = keys_ref[slot * WORKERS + column * 2 + core]
            scores = jnp.dot(q_ref[rows_of(slot), :], own, preferred_element_type=F32)
            set_base(slot, jnp.max(scores, axis=1, keepdims=True))

    loop(busy * (SLOTS // BESIDE), own_base)

    def tiles_of(number):
        slot, first = slot_of[number], first_of[number]
        return slot, [list_ref[slot, first + u] for u in range(GROUP)]

    def scores_of(slot, tiles):
        keys = jnp.concatenate([keys_ref[tile] for tile in tiles], axis=1)
        return jnp.dot(q_ref[rows_of(slot), :], keys, preferred_element_type=F32)

    def attend_steps(step):
        found = []
        for beside in range(BESIDE):
            number = step * BESIDE + beside
            slot, tiles = tiles_of(number)
            listed = listed_of[number]
            base = base_ref[slot]
            base = jnp.concatenate([base, base], axis=1)
            weights, values = [], []
            for u in range(0, GROUP, 2):
                scores = scores_of(slot, tiles[u : u + 2])
                weights.append(jnp.exp2(scores * SCALE2 - base).astype(BF16))
            for u in range(GROUP):
                value = values_ref[jnp.where(u < listed, tiles[u], TILES)]
                ones = jnp.where(u < listed, 1.0, 0.0).astype(BF16)
                ones = jnp.broadcast_to(ones, (TILE, DH))
                values.append(jnp.concatenate([value, ones], axis=1))
            added = jnp.dot(
                jnp.concatenate(weights, axis=1),
                jnp.concatenate(values, axis=0),
                preferred_element_type=F32,
            )
            found.append((slot, added))
        for slot, added in found:
            sum_ref[slot] += added

    def peak_steps(step):
        for beside in range(BESIDE):
            slot, tiles = tiles_of(step * BESIDE + beside)
            scores = scores_of(slot, tiles)
            peak = peak_ref[slot]
            for u in range(GROUP):
                peak = jnp.maximum(peak, scores[:, u * TILE : (u + 1) * TILE])
            peak_ref[slot] = peak

    def attempt(number, needed):
        def clear(slot):
            sum_ref[slot] = jnp.zeros((TILE, 2 * DH), F32)
            peak_ref[slot] = jnp.full((TILE, TILE), LOW, F32)

        loop(needed * SLOTS, clear)
        loop(needed * turns, attend_steps)
        beyond = jnp.zeros((TILE, DH), F32)
        for slot in range(SLOTS):
            beyond = jnp.where(sum_ref[slot, :, DH:] <= FAR, beyond, 1.0)
        again = needed * jnp.where(jnp.max(beyond) > 0.0, 1, 0)
        loop(again * turns, peak_steps)

        def rebase(slot):
            set_base(slot, jnp.max(peak_ref[slot], axis=1, keepdims=True))

        loop(again * SLOTS, rebase)
        return again

    lax.fori_loop(0, 2, attempt, busy)

    def finish(step):
        for u in range(BESIDE):
            slot = step * BESIDE + u
            o_ref[rows_of(slot), :] = (sum_ref[slot, :, :DH] / sum_ref[slot, :, DH:]).astype(BF16)

    loop(busy * (SLOTS // BESIDE), finish)


def attend(lists, query, kv):
    most = SLOTS * (TILES // GROUP) + BESIDE
    return pl.pallas_call(
        attend_kernel,
        out_shape=jax.ShapeDtypeStruct(query.shape, BF16),
        in_specs=[
            pl.BlockSpec(memory_space=pltpu.SMEM),
            pl.BlockSpec(memory_space=pltpu.VMEM),
            pl.BlockSpec(memory_space=pl.ANY),
        ],
        out_specs=pl.BlockSpec(memory_space=pltpu.VMEM),
        scratch_shapes=[
            pltpu.VMEM(kv.shape, BF16),
            pltpu.VMEM((TILES, DH, TILE), BF16),
            pltpu.VMEM((TILES + 1, TILE, DH), BF16),
            pltpu.VMEM((SLOTS, TILE, TILE), F32),
            pltpu.VMEM((SLOTS, TILE, TILE), F32),
            pltpu.VMEM((SLOTS, TILE, 2 * DH), F32),
            pltpu.SMEM((most,), jnp.int32),
            pltpu.SMEM((most,), jnp.int32),
            pltpu.SMEM((most,), jnp.int32),
            pltpu.SemaphoreType.DMA((TILES // CHUNK, 2)),
        ],
        compiler_params=pltpu.CompilerParams(vmem_limit_bytes=57 * 1024 * 1024),
    )(lists, query, kv)


def collect_kernel(o_ref, attn, send, recv, x_send, x_recv):
    plane = lax.axis_index("heads")
    me = lax.axis_index("ctx")
    row, column, core = where_is(me)
    barrier = pltpu.get_barrier_semaphore()

    def greet(step, carry):
        pl.semaphore_signal(
            barrier, inc=1, device_id=(plane, lax.rem(me + step, FRAMES)), device_id_type=MESH
        )
        return carry

    lax.fori_loop(1, FRAMES, greet, 0)
    sides = (lax.rem(plane + 1, PLANES), lax.rem(plane + PLANES - 1, PLANES))
    for there in sides:
        pl.semaphore_signal(barrier, inc=1, device_id=(there, me), device_id_type=MESH)
    pl.semaphore_wait(barrier, FRAMES - 1 + 2)

    mine = jnp.minimum(row, HEADS_HERE - 1)
    goal = attn.at[plane * HEADS_HERE + mine, :, column * 2 + core]

    def back(step):
        there = lax.rem(me + step, FRAMES)
        return pltpu.make_async_remote_copy(
            src_ref=o_ref.at[:, there],
            dst_ref=goal,
            send_sem=send.at[step],
            recv_sem=recv.at[mine],
            device_id=(plane, there),
            device_id_type=MESH,
        )

    def start(step, carry):
        back(step).start()
        return carry

    def end(step, carry):
        back(step).wait_send()
        return carry

    working = row < HEADS_HERE

    @pl.when(working)
    def _():
        lax.fori_loop(1, FRAMES, start, 0)
        pltpu.make_async_copy(o_ref.at[:, me], goal, recv.at[mine]).start()

    cut = SLOTS // 2

    def near(head, side):
        part = attn.at[plane * HEADS_HERE + head]
        return pltpu.make_async_remote_copy(
            src_ref=part,
            dst_ref=part,
            send_sem=x_send.at[head, side],
            recv_sem=x_recv.at[head, side],
            device_id=(sides[side], me),
            device_id_type=MESH,
        )

    def far(head, side):
        part = attn.at[sides[1 - side] * HEADS_HERE + head]
        part = part.at[pl.ds(0, cut)] if side == 0 else part.at[pl.ds(cut, SLOTS - cut)]
        return pltpu.make_async_remote_copy(
            src_ref=part,
            dst_ref=part,
            send_sem=x_send.at[head, 2 + side],
            recv_sem=x_recv.at[head, 2 + side],
            device_id=(sides[side], me),
            device_id_type=MESH,
        )

    for head in range(HEADS_HERE):
        part = attn.at[plane * HEADS_HERE + head]
        pltpu.make_async_copy(part, part, recv.at[head]).wait()
        for side in range(2):
            near(head, side).start()
    for head in range(HEADS_HERE):
        for side in range(2):
            near(head, side).wait_recv()
            far(head, side).start()

    @pl.when(working)
    def _():
        lax.fori_loop(1, FRAMES, end, 0)

    for head in range(HEADS_HERE):
        for side in range(2):
            near(head, side).wait_send()
            far(head, side).wait()


def collect(attended):
    return pl.pallas_call(
        collect_kernel,
        out_shape=jax.ShapeDtypeStruct(
            (PLANES * HEADS_HERE, SLOTS, WORKERS, SPOTS, DH), BF16
        ),
        in_specs=[pl.BlockSpec(memory_space=pl.ANY)],
        out_specs=pl.BlockSpec(memory_space=pl.ANY),
        scratch_shapes=[
            pltpu.SemaphoreType.DMA((FRAMES,)),
            pltpu.SemaphoreType.DMA((HEADS_HERE,)),
            pltpu.SemaphoreType.DMA((HEADS_HERE, 4)),
            pltpu.SemaphoreType.DMA((HEADS_HERE, 4)),
        ],
        compiler_params=pltpu.CompilerParams(
            collective_id=1, has_side_effects=True, vmem_limit_bytes=4 * 1024 * 1024
        ),
    )(attended)


def project_kernel(attn_ref, w_ref, out_ref):
    heads = attn_ref.shape[0]
    wide = jnp.concatenate([attn_ref[h] for h in range(heads)], axis=1)
    block = 256
    for first in range(0, out_ref.shape[1], block):
        columns = slice(first, first + block)
        out_ref[:, columns] = jnp.dot(
            wide, w_ref[:, columns], preferred_element_type=F32
        ).astype(BF16)


def project(attn, weight, rows):
    return pl.pallas_call(
        project_kernel,
        out_shape=jax.ShapeDtypeStruct((rows, weight.shape[1]), BF16),
        in_specs=[pl.BlockSpec(memory_space=pltpu.VMEM)] * 2,
        out_specs=pl.BlockSpec(memory_space=pltpu.VMEM),
        compiler_params=pltpu.CompilerParams(vmem_limit_bytes=24 * 1024 * 1024),
    )(attn, weight)


def arrange_kernel(
    pattern_ref, mask_hbm, q_hbm, k_hbm, v_hbm, q_out, kv_out, list_ref,
    mask_ref, q_ref, k_ref, v_ref, sems,
):
    sources = (mask_hbm, q_hbm, k_hbm, v_hbm)
    targets = (mask_ref, q_ref, k_ref, v_ref)
    moves = [
        pltpu.make_async_copy(source, target, sems.at[i])
        for i, (source, target) in enumerate(zip(sources, targets))
    ]
    for move in moves:
        move.start()
    me = lax.axis_index("ctx")
    row, column, core = where_is(me)
    moves[0].wait()
    pattern = pattern_ref[jnp.minimum(row, HEADS_HERE - 1)]
    masks = []
    tiles = [slot * WORKERS + column * 2 + core for slot in range(SLOTS)]
    for tile in tiles:
        masks.append(jnp.where(row < HEADS_HERE, mask_ref[pattern, pl.ds(tile, 1), :], 0))
    seen = jnp.concatenate(masks, axis=0) == 1
    seen = jnp.where(seen, 1.0, 0.0).astype(F32)
    down = lax.broadcasted_iota(jnp.int32, (TILES, TILES), 0)
    along = lax.broadcasted_iota(jnp.int32, (TILES, TILES), 1)
    both = (((1,), (1,)), ((), ()))
    upto = jnp.where(along <= down, 1.0, 0.0).astype(BF16)
    same = jnp.where(along == down, 1.0, 0.0).astype(BF16)
    rank = lax.dot_general(upto, seen.astype(BF16), both, preferred_element_type=F32)
    turned = lax.dot_general(same, seen.astype(BF16), both, preferred_element_type=F32)
    rank = rank.astype(jnp.int32)
    spot = jnp.where(turned > 0.5, rank - 1, -1)
    for slot in range(SLOTS):
        hit = spot[:, slot : slot + 1] == along
        listed = jnp.sum(jnp.where(hit, down, 0), axis=0, keepdims=True)
        spare = along[:1, :] >= rank[TILES - 1 :, slot : slot + 1]
        list_ref[slot : slot + 1, :] = jnp.where(spare, tiles[slot], listed)
    last = jnp.concatenate(
        [rank[TILES - 1 :, :], jnp.zeros((1, TILES - SLOTS), jnp.int32)], axis=1
    )
    list_ref[SLOTS : SLOTS + 1, :] = last


    rows = q_ref.shape[0]
    for move, source, target, first in (
        (moves[1], q_ref, q_out, 0),
        (moves[2], k_ref, kv_out, 0),
        (moves[3], v_ref, kv_out, rows),
    ):
        move.wait()
        for head in range(HEADS_HERE):
            target[head, first : first + rows, :] = source[:, head * DH : (head + 1) * DH]


def arrange(head_pattern, tile_masks, queries, key_rows, value_rows):
    rows = queries.shape[0]
    return pl.pallas_call(
        arrange_kernel,
        out_shape=(
            jax.ShapeDtypeStruct((HEADS_HERE, rows, DH), BF16),
            jax.ShapeDtypeStruct((HEADS_HERE, 2 * rows, DH), BF16),
            jax.ShapeDtypeStruct((SLOTS + 1, TILES), jnp.int32),
        ),
        in_specs=[pl.BlockSpec(memory_space=pltpu.SMEM)]
        + [pl.BlockSpec(memory_space=pl.ANY)] * 4,
        out_specs=(pl.BlockSpec(memory_space=pltpu.VMEM),) * 3,
        scratch_shapes=[
            pltpu.VMEM(tile_masks.shape, jnp.int32),
            pltpu.VMEM(queries.shape, BF16),
            pltpu.VMEM(queries.shape, BF16),
            pltpu.VMEM(queries.shape, BF16),
            pltpu.SemaphoreType.DMA((4,)),
        ],
        compiler_params=pltpu.CompilerParams(vmem_limit_bytes=57 * 1024 * 1024),
    )(head_pattern, tile_masks, queries, key_rows, value_rows)


def body(queries, key_rows, value_rows, out_weight, tile_masks, head_pattern):
    rows = queries.shape[0]
    q_parts, kv_parts, lists = arrange(head_pattern, tile_masks, queries, key_rows, value_rows)
    q_all, kv_all, w_all = spread(
        q_parts.reshape(HEADS_HERE, SLOTS, WORKERS, SPOTS, DH),
        kv_parts.reshape(HEADS_HERE, 2 * TILES, SPOTS, DH),
        out_weight,
    )
    attended = attend(
        lists, q_all.reshape(SLOTS * TILE, DH), kv_all.reshape(WORKERS, 2 * TILES * PIECE, DH)
    )
    attn = collect(attended.reshape(SLOTS, FRAMES, SPOTS, DH))
    attn = attn.reshape(PLANES * HEADS_HERE, rows, DH)
    return project(attn, w_all, rows)


def solution(mesh):
    placed = (
        P("ctx", "heads"),
        P("ctx", "heads"),
        P("ctx", "heads"),
        P("heads", None),
        P(),
        P("heads"),
    )
    return jax.shard_map(
        body, mesh=mesh, in_specs=placed, out_specs=P("ctx", "heads"), check_vma=False
    )
```

```python
import math

import jax
import jax.numpy as jnp
from jax import lax
from jax.experimental import pallas as pl
from jax.experimental.pallas import tpu as pltpu
from jax.sharding import PartitionSpec as P

MESH = pl.DeviceIdType.MESH
DH = 128
TILE = 128
SPOTS = 4
FRAMES = 32
TILES = 128
PLANES = 4
SIDE = 4
HEADS_HERE = 3
WORKERS = 2 * SIDE
SLOTS = TILES // WORKERS
PARTS = 4
PART = 2 * TILES // PARTS
PIECE = TILE // WORKERS
GROUP = 4
CHUNK = 16
UNPACK = 8
BESIDE = 8
FAR = 2.0**64
LOW = -1e30
SCALE2 = math.log2(math.e) / math.sqrt(DH)
BF16 = jnp.bfloat16
F32 = jnp.float32


def where_is(device):
    return lax.div(device, WORKERS), lax.rem(lax.div(device, 2), SIDE), lax.rem(device, 2)


def device_at(row, column, core):
    return (lax.rem(row, SIDE) * SIDE + lax.rem(column, SIDE)) * 2 + core


def spread_kernel(
    q_ref, kv_ref, w_ref, q_all, kv_all, w_all,
    q_send, q_recv, z_send, z_recv, y_send, y_recv, far_send, far_recv,
    core_send, core_recv, w_send, w_recv, w_core_send, w_core_recv, own_sem,
):
    plane = lax.axis_index("heads")
    me = lax.axis_index("ctx")
    row, column, core = where_is(me)
    working = row < HEADS_HERE
    own_row = jnp.minimum(row, HEADS_HERE - 1)
    depth = w_ref.shape[0]
    width = w_all.shape[1]
    sides = (1, SIDE - 1)

    barrier = pltpu.get_barrier_semaphore()

    def greet(step, carry):
        pl.semaphore_signal(
            barrier, inc=1, device_id=(plane, lax.rem(me + step, FRAMES)), device_id_type=MESH
        )
        return carry

    lax.fori_loop(1, FRAMES, greet, 0)
    for hop in range(1, PLANES):
        pl.semaphore_signal(
            barrier, inc=1, device_id=(lax.rem(plane + hop, PLANES), me), device_id_type=MESH
        )
    pl.semaphore_wait(barrier, FRAMES - 1 + PLANES - 1)

    def span(part):
        return pl.ds(part * PART, PART)

    own_copy = pltpu.make_async_copy(
        kv_ref.at[own_row], kv_all.at[column * 2 + core, :, 0], own_sem
    )

    def z_copy(part, hop):
        there = lax.rem(row + hop, SIDE)
        return pltpu.make_async_remote_copy(
            src_ref=kv_ref.at[there, span(part)],
            dst_ref=kv_all.at[column * 2 + core, span(part), hop],
            send_sem=z_send.at[part, hop],
            recv_sem=z_recv.at[part, hop],
            device_id=(plane, device_at(there, column, core)),
            device_id_type=MESH,
        )

    def piece(number, away):
        source = kv_all.at[lax.rem(column + away, SIDE) * 2 + core]
        if number == 0:
            return source.at[:, 0]
        return source.at[span(number - 1), pl.ds(1, SIDE - 1)]

    def y_copy(number, side):
        return pltpu.make_async_remote_copy(
            src_ref=kv_ref.at[own_row] if number == 0 else piece(number, 0),
            dst_ref=piece(number, 0),
            send_sem=y_send.at[number, side],
            recv_sem=y_recv.at[number, side],
            device_id=(plane, device_at(row, column + sides[side], core)),
            device_id_type=MESH,
        )

    def far_copy(number, side):
        source = kv_all.at[lax.rem(column + sides[1 - side], SIDE) * 2 + core]
        if number == 0:
            chunk = source.at[pl.ds(side * TILES, TILES), 0]
        else:
            chunk = source.at[
                pl.ds((number - 1) * PART + side * (PART // 2), PART // 2), pl.ds(1, SIDE - 1)
            ]
        return pltpu.make_async_remote_copy(
            src_ref=chunk,
            dst_ref=chunk,
            send_sem=far_send.at[number, side],
            recv_sem=far_recv.at[number, side],
            device_id=(plane, device_at(row, column + sides[side], core)),
            device_id_type=MESH,
        )

    def core_copy(number, away):
        return pltpu.make_async_remote_copy(
            src_ref=piece(number, away),
            dst_ref=piece(number, away),
            send_sem=core_send.at[number, away],
            recv_sem=core_recv,
            device_id=(plane, device_at(row, column, 1 - core)),
            device_id_type=MESH,
        )

    half = depth // 2

    def w_rows(source, part):
        return w_all.at[pl.ds(pl.multiple_of(source * depth + part * half, 16), half)]

    def w_copy(hop):
        there = lax.rem(plane + hop, PLANES)
        return pltpu.make_async_remote_copy(
            src_ref=w_ref.at[
                pl.ds(pl.multiple_of(core * half, 16), half),
                pl.ds(pl.multiple_of(there * width, 128), width),
            ],
            dst_ref=w_rows(plane, core),
            send_sem=w_send.at[hop],
            recv_sem=w_recv.at[hop],
            device_id=(there, me),
            device_id_type=MESH,
        )

    def w_core_copy(hop):
        rows = w_rows(lax.rem(plane + PLANES - hop, PLANES), core)
        return pltpu.make_async_remote_copy(
            src_ref=rows,
            dst_ref=rows,
            send_sem=w_core_send.at[hop],
            recv_sem=w_core_recv.at[hop],
            device_id=(plane, device_at(row, column, 1 - core)),
            device_id_type=MESH,
        )

    own_w = pltpu.make_async_copy(
        w_ref.at[:, pl.ds(pl.multiple_of(plane * width, 128), width)],
        w_all.at[pl.ds(pl.multiple_of(plane * depth, 128), depth)],
        w_recv.at[0],
    )

    def q_copy(step):
        there = lax.rem(me + step, FRAMES)
        row_there, column_there, core_there = where_is(there)
        return row_there < HEADS_HERE, pltpu.make_async_remote_copy(
            src_ref=q_ref.at[
                jnp.minimum(row_there, HEADS_HERE - 1), :, column_there * 2 + core_there
            ],
            dst_ref=q_all.at[:, me],
            send_sem=q_send.at[step],
            recv_sem=q_recv,
            device_id=(plane, there),
            device_id_type=MESH,
        )

    def to_rows(part, work):
        for hop in range(1, SIDE):

            @pl.when(lax.rem(row + hop, SIDE) < HEADS_HERE)
            def _():
                work(z_copy(part, hop))

    def send_q(step, carry):
        wanted, copy = q_copy(step)

        @pl.when(wanted)
        def _():
            copy.start()

        return carry

    def sent_q(step, carry):
        wanted, copy = q_copy(step)

        @pl.when(wanted)
        def _():
            copy.wait_send()

        return carry

    def send_small():
        for hop in range(1, PLANES):
            w_copy(hop).start()
        own_w.start()
        lax.fori_loop(1, FRAMES, send_q, 0)

    @pl.when(working)
    def _():
        own_copy.start()
        for side in range(2):
            y_copy(0, side).start()

    to_rows(0, lambda copy: copy.start())
    send_small()

    def next_rows(part):
        to_rows(part, lambda copy: copy.wait_send())
        if part + 1 < PARTS:
            to_rows(part + 1, lambda copy: copy.start())

    @pl.when(jnp.logical_not(working))
    def _():
        for part in range(PARTS):
            next_rows(part)

    @pl.when(working)
    def _():
        pltpu.make_async_copy(
            q_ref.at[own_row, :, column * 2 + core], q_all.at[:, me], q_recv
        ).start()
        own_copy.wait()
        core_copy(0, 0).start()

        def pass_on(number):
            for side in range(2):
                y_copy(number, side).wait_recv()
                far_copy(number, side).start()
            for side in range(2):
                core_copy(number, sides[1 - side]).start()

        for part in range(PARTS):
            next_rows(part)
            for hop in range(1, SIDE):
                landed = kv_all.at[column * 2 + core, span(part), hop]
                pltpu.make_async_copy(landed, landed, z_recv.at[part, hop]).wait()
            for side in range(2):
                y_copy(part + 1, side).start()
            core_copy(part + 1, 0).start()
            pass_on(part)
        pass_on(PARTS)
        for number in range(PARTS + 1):
            for side in range(2):
                far_copy(number, side).wait_recv()
            core_copy(number, 2).start()

    for hop in range(1, PLANES):
        w_copy(hop).wait_recv()
        w_core_copy(hop).start()

    @pl.when(working)
    def _():
        pltpu.make_async_copy(q_all, q_all, q_recv).wait()
        other = kv_all.at[pl.ds(0, SIDE)]
        pltpu.make_async_copy(other, other, core_recv).wait()
        for number in range(PARTS + 1):
            for side in range(2):
                y_copy(number, side).wait_send()
                far_copy(number, side).wait_send()
            for away in range(SIDE):
                core_copy(number, away).wait_send()

    own_w.wait()
    lax.fori_loop(1, FRAMES, sent_q, 0)
    for hop in range(1, PLANES):
        w_copy(hop).wait_send()
        w_core_copy(hop).wait()


def spread(q_parts, kv_parts, out_weight):
    depth, columns = out_weight.shape
    return pl.pallas_call(
        spread_kernel,
        out_shape=(
            jax.ShapeDtypeStruct((SLOTS, FRAMES, SPOTS, DH), BF16),
            jax.ShapeDtypeStruct((WORKERS, 2 * TILES, SIDE, SPOTS, DH), BF16),
            jax.ShapeDtypeStruct((depth * PLANES, columns // PLANES), BF16),
        ),
        in_specs=[pl.BlockSpec(memory_space=pl.ANY)] * 3,
        out_specs=(pl.BlockSpec(memory_space=pl.ANY),) * 3,
        scratch_shapes=[
            pltpu.SemaphoreType.DMA((FRAMES,)),
            pltpu.SemaphoreType.DMA,
            pltpu.SemaphoreType.DMA((PARTS, SIDE)),
            pltpu.SemaphoreType.DMA((PARTS, SIDE)),
            pltpu.SemaphoreType.DMA((PARTS + 1, 2)),
            pltpu.SemaphoreType.DMA((PARTS + 1, 2)),
            pltpu.SemaphoreType.DMA((PARTS + 1, 2)),
            pltpu.SemaphoreType.DMA((PARTS + 1, 2)),
            pltpu.SemaphoreType.DMA((PARTS + 1, SIDE)),
            pltpu.SemaphoreType.DMA,
            pltpu.SemaphoreType.DMA((PLANES,)),
            pltpu.SemaphoreType.DMA((PLANES,)),
            pltpu.SemaphoreType.DMA((PLANES,)),
            pltpu.SemaphoreType.DMA((PLANES,)),
            pltpu.SemaphoreType.DMA,
        ],
        compiler_params=pltpu.CompilerParams(
            collective_id=0, has_side_effects=True, vmem_limit_bytes=57 * 1024 * 1024
        ),
    )(q_parts, kv_parts, out_weight)


def attend_kernel(
    list_ref, q_ref, kv_hbm, o_ref, kv_ref, keys_ref, values_ref, base_ref, peak_ref, sum_ref,
    slot_of, first_of, listed_of, kv_sem,
):
    def chunk(number, first):
        rows = pl.ds((first + number * CHUNK) * PIECE, CHUNK * PIECE)
        return pltpu.make_async_copy(
            kv_hbm.at[:, rows], kv_ref.at[:, rows], kv_sem.at[number, min(first, 1)]
        )

    def bring(number):
        if number < TILES // CHUNK:
            chunk(number, 0).start()
            chunk(number, TILES).start()

    bring(0)
    bring(1)

    _, column, core = where_is(lax.axis_index("ctx"))

    def loop(count, work):
        def one(step, carry):
            work(step)
            return carry

        lax.fori_loop(0, count, one, 0)

    def rows_of(slot):
        return pl.ds(pl.multiple_of(slot * TILE, TILE), TILE)

    def tile_at(tile):
        start = pl.multiple_of(tile * PIECE, PIECE)
        return jnp.concatenate(
            [kv_ref[worker, pl.ds(start, PIECE), :] for worker in range(WORKERS)], axis=0
        )

    def enlist(slot, total):
        count = list_ref[SLOTS, slot]
        steps = lax.div(count + GROUP - 1, GROUP)

        def one(step, carry):
            slot_of[total + step] = slot
            first_of[total + step] = step * GROUP
            listed_of[total + step] = count - step * GROUP
            return carry

        lax.fori_loop(0, steps, one, 0)
        return total + steps

    total = lax.fori_loop(0, SLOTS, enlist, 0)
    for spare in range(BESIDE - 1):
        slot_of[total + spare] = 0
        first_of[total + spare] = 0
        listed_of[total + spare] = 0
    turns = lax.div(total + BESIDE - 1, BESIDE)
    busy = jnp.where(total > 0, 1, 0)

    values_ref[TILES] = jnp.zeros((TILE, DH), BF16)

    def unpack(step):
        for u in range(UNPACK):
            tile = step * UNPACK + u
            keys_ref[tile] = tile_at(tile).T
            values_ref[tile] = tile_at(TILES + tile)

    for number in range(TILES // CHUNK):
        chunk(number, 0).wait()
        chunk(number, TILES).wait()
        bring(number + 2)
        steps = CHUNK // UNPACK
        loop(busy * steps, lambda step: unpack(step + number * steps))

    def set_base(slot, base):
        base_ref[slot] = jnp.broadcast_to(base * SCALE2, (TILE, TILE))

    def own_base(step):
        for u in range(BESIDE):
            slot = step * BESIDE + u
            own = keys_ref[slot * WORKERS + column * 2 + core]
            scores = jnp.dot(q_ref[rows_of(slot), :], own, preferred_element_type=F32)
            set_base(slot, jnp.max(scores, axis=1, keepdims=True))

    loop(busy * (SLOTS // BESIDE), own_base)

    def tiles_of(number):
        slot, first = slot_of[number], first_of[number]
        return slot, [list_ref[slot, first + u] for u in range(GROUP)]

    def scores_of(slot, tiles):
        keys = jnp.concatenate([keys_ref[tile] for tile in tiles], axis=1)
        return jnp.dot(q_ref[rows_of(slot), :], keys, preferred_element_type=F32)

    def attend_steps(step):
        found = []
        for beside in range(BESIDE):
            number = step * BESIDE + beside
            slot, tiles = tiles_of(number)
            listed = listed_of[number]
            base = base_ref[slot]
            base = jnp.concatenate([base, base], axis=1)
            weights, values = [], []
            for u in range(0, GROUP, 2):
                scores = scores_of(slot, tiles[u : u + 2])
                weights.append(jnp.exp2(scores * SCALE2 - base).astype(BF16))
            for u in range(GROUP):
                value = values_ref[jnp.where(u < listed, tiles[u], TILES)]
                ones = jnp.where(u < listed, 1.0, 0.0).astype(BF16)
                ones = jnp.broadcast_to(ones, (TILE, DH))
                values.append(jnp.concatenate([value, ones], axis=1))
            added = jnp.dot(
                jnp.concatenate(weights, axis=1),
                jnp.concatenate(values, axis=0),
                preferred_element_type=F32,
            )
            found.append((slot, added))
        for slot, added in found:
            sum_ref[slot] += added

    def peak_steps(step):
        for beside in range(BESIDE):
            slot, tiles = tiles_of(step * BESIDE + beside)
            scores = scores_of(slot, tiles)
            peak = peak_ref[slot]
            for u in range(GROUP):
                peak = jnp.maximum(peak, scores[:, u * TILE : (u + 1) * TILE])
            peak_ref[slot] = peak

    def attempt(number, needed):
        def clear(slot):
            sum_ref[slot] = jnp.zeros((TILE, 2 * DH), F32)
            peak_ref[slot] = jnp.full((TILE, TILE), LOW, F32)

        loop(needed * SLOTS, clear)
        loop(needed * turns, attend_steps)
        beyond = jnp.zeros((TILE, DH), F32)
        for slot in range(SLOTS):
            beyond = jnp.where(sum_ref[slot, :, DH:] <= FAR, beyond, 1.0)
        again = needed * jnp.where(jnp.max(beyond) > 0.0, 1, 0)
        loop(again * turns, peak_steps)

        def rebase(slot):
            set_base(slot, jnp.max(peak_ref[slot], axis=1, keepdims=True))

        loop(again * SLOTS, rebase)
        return again

    lax.fori_loop(0, 2, attempt, busy)

    def finish(step):
        for u in range(BESIDE):
            slot = step * BESIDE + u
            o_ref[rows_of(slot), :] = (sum_ref[slot, :, :DH] / sum_ref[slot, :, DH:]).astype(BF16)

    loop(busy * (SLOTS // BESIDE), finish)


def attend(lists, query, kv):
    most = SLOTS * (TILES // GROUP) + BESIDE
    return pl.pallas_call(
        attend_kernel,
        out_shape=jax.ShapeDtypeStruct(query.shape, BF16),
        in_specs=[
            pl.BlockSpec(memory_space=pltpu.SMEM),
            pl.BlockSpec(memory_space=pltpu.VMEM),
            pl.BlockSpec(memory_space=pl.ANY),
        ],
        out_specs=pl.BlockSpec(memory_space=pltpu.VMEM),
        scratch_shapes=[
            pltpu.VMEM(kv.shape, BF16),
            pltpu.VMEM((TILES, DH, TILE), BF16),
            pltpu.VMEM((TILES + 1, TILE, DH), BF16),
            pltpu.VMEM((SLOTS, TILE, TILE), F32),
            pltpu.VMEM((SLOTS, TILE, TILE), F32),
            pltpu.VMEM((SLOTS, TILE, 2 * DH), F32),
            pltpu.SMEM((most,), jnp.int32),
            pltpu.SMEM((most,), jnp.int32),
            pltpu.SMEM((most,), jnp.int32),
            pltpu.SemaphoreType.DMA((TILES // CHUNK, 2)),
        ],
        compiler_params=pltpu.CompilerParams(vmem_limit_bytes=57 * 1024 * 1024),
    )(lists, query, kv)


def collect_kernel(o_ref, attn, send, recv, x_send, x_recv):
    plane = lax.axis_index("heads")
    me = lax.axis_index("ctx")
    row, column, core = where_is(me)
    barrier = pltpu.get_barrier_semaphore()

    def greet(step, carry):
        pl.semaphore_signal(
            barrier, inc=1, device_id=(plane, lax.rem(me + step, FRAMES)), device_id_type=MESH
        )
        return carry

    lax.fori_loop(1, FRAMES, greet, 0)
    sides = (lax.rem(plane + 1, PLANES), lax.rem(plane + PLANES - 1, PLANES))
    for there in sides:
        pl.semaphore_signal(barrier, inc=1, device_id=(there, me), device_id_type=MESH)
    pl.semaphore_wait(barrier, FRAMES - 1 + 2)

    mine = jnp.minimum(row, HEADS_HERE - 1)
    goal = attn.at[plane * HEADS_HERE + mine, :, column * 2 + core]

    def back(step):
        there = lax.rem(me + step, FRAMES)
        return pltpu.make_async_remote_copy(
            src_ref=o_ref.at[:, there],
            dst_ref=goal,
            send_sem=send.at[step],
            recv_sem=recv.at[mine],
            device_id=(plane, there),
            device_id_type=MESH,
        )

    def start(step, carry):
        back(step).start()
        return carry

    def end(step, carry):
        back(step).wait_send()
        return carry

    working = row < HEADS_HERE

    @pl.when(working)
    def _():
        lax.fori_loop(1, FRAMES, start, 0)
        pltpu.make_async_copy(o_ref.at[:, me], goal, recv.at[mine]).start()

    cut = SLOTS // 2

    def near(head, side):
        part = attn.at[plane * HEADS_HERE + head]
        return pltpu.make_async_remote_copy(
            src_ref=part,
            dst_ref=part,
            send_sem=x_send.at[head, side],
            recv_sem=x_recv.at[head, side],
            device_id=(sides[side], me),
            device_id_type=MESH,
        )

    def far(head, side):
        part = attn.at[sides[1 - side] * HEADS_HERE + head]
        part = part.at[pl.ds(0, cut)] if side == 0 else part.at[pl.ds(cut, SLOTS - cut)]
        return pltpu.make_async_remote_copy(
            src_ref=part,
            dst_ref=part,
            send_sem=x_send.at[head, 2 + side],
            recv_sem=x_recv.at[head, 2 + side],
            device_id=(sides[side], me),
            device_id_type=MESH,
        )

    for head in range(HEADS_HERE):
        part = attn.at[plane * HEADS_HERE + head]
        pltpu.make_async_copy(part, part, recv.at[head]).wait()
        for side in range(2):
            near(head, side).start()
    for head in range(HEADS_HERE):
        for side in range(2):
            near(head, side).wait_recv()
            far(head, side).start()

    @pl.when(working)
    def _():
        lax.fori_loop(1, FRAMES, end, 0)

    for head in range(HEADS_HERE):
        for side in range(2):
            near(head, side).wait_send()
            far(head, side).wait()


def collect(attended):
    return pl.pallas_call(
        collect_kernel,
        out_shape=jax.ShapeDtypeStruct(
            (PLANES * HEADS_HERE, SLOTS, WORKERS, SPOTS, DH), BF16
        ),
        in_specs=[pl.BlockSpec(memory_space=pl.ANY)],
        out_specs=pl.BlockSpec(memory_space=pl.ANY),
        scratch_shapes=[
            pltpu.SemaphoreType.DMA((FRAMES,)),
            pltpu.SemaphoreType.DMA((HEADS_HERE,)),
            pltpu.SemaphoreType.DMA((HEADS_HERE, 4)),
            pltpu.SemaphoreType.DMA((HEADS_HERE, 4)),
        ],
        compiler_params=pltpu.CompilerParams(
            collective_id=1, has_side_effects=True, vmem_limit_bytes=4 * 1024 * 1024
        ),
    )(attended)


def project_kernel(attn_ref, w_ref, out_ref):
    heads = attn_ref.shape[0]
    wide = jnp.concatenate([attn_ref[h] for h in range(heads)], axis=1)
    block = 256
    for first in range(0, out_ref.shape[1], block):
        columns = slice(first, first + block)
        out_ref[:, columns] = jnp.dot(
            wide, w_ref[:, columns], preferred_element_type=F32
        ).astype(BF16)


def project(attn, weight, rows):
    return pl.pallas_call(
        project_kernel,
        out_shape=jax.ShapeDtypeStruct((rows, weight.shape[1]), BF16),
        in_specs=[pl.BlockSpec(memory_space=pltpu.VMEM)] * 2,
        out_specs=pl.BlockSpec(memory_space=pltpu.VMEM),
        compiler_params=pltpu.CompilerParams(vmem_limit_bytes=24 * 1024 * 1024),
    )(attn, weight)


def arrange_kernel(
    pattern_ref, mask_hbm, q_hbm, k_hbm, v_hbm, q_out, kv_out, list_ref,
    mask_ref, q_ref, k_ref, v_ref, sems,
):
    sources = (mask_hbm, q_hbm, k_hbm, v_hbm)
    targets = (mask_ref, q_ref, k_ref, v_ref)
    moves = [
        pltpu.make_async_copy(source, target, sems.at[i])
        for i, (source, target) in enumerate(zip(sources, targets))
    ]
    for move in moves:
        move.start()
    me = lax.axis_index("ctx")
    row, column, core = where_is(me)
    moves[0].wait()
    pattern = pattern_ref[jnp.minimum(row, HEADS_HERE - 1)]
    masks = []
    tiles = [slot * WORKERS + column * 2 + core for slot in range(SLOTS)]
    for tile in tiles:
        masks.append(jnp.where(row < HEADS_HERE, mask_ref[pattern, pl.ds(tile, 1), :], 0))
    seen = jnp.concatenate(masks, axis=0) == 1
    seen = jnp.where(seen, 1.0, 0.0).astype(F32)
    down = lax.broadcasted_iota(jnp.int32, (TILES, TILES), 0)
    along = lax.broadcasted_iota(jnp.int32, (TILES, TILES), 1)
    both = (((1,), (1,)), ((), ()))
    upto = jnp.where(along <= down, 1.0, 0.0).astype(BF16)
    same = jnp.where(along == down, 1.0, 0.0).astype(BF16)
    rank = lax.dot_general(upto, seen.astype(BF16), both, preferred_element_type=F32)
    turned = lax.dot_general(same, seen.astype(BF16), both, preferred_element_type=F32)
    rank = rank.astype(jnp.int32)
    spot = jnp.where(turned > 0.5, rank - 1, -1)
    for slot in range(SLOTS):
        hit = spot[:, slot : slot + 1] == along
        listed = jnp.sum(jnp.where(hit, down, 0), axis=0, keepdims=True)
        spare = along[:1, :] >= rank[TILES - 1 :, slot : slot + 1]
        list_ref[slot : slot + 1, :] = jnp.where(spare, tiles[slot], listed)
    last = jnp.concatenate(
        [rank[TILES - 1 :, :], jnp.zeros((1, TILES - SLOTS), jnp.int32)], axis=1
    )
    list_ref[SLOTS : SLOTS + 1, :] = last


    rows = q_ref.shape[0]
    for move, source, target, first in (
        (moves[1], q_ref, q_out, 0),
        (moves[2], k_ref, kv_out, 0),
        (moves[3], v_ref, kv_out, rows),
    ):
        move.wait()
        for head in range(HEADS_HERE):
            target[head, first : first + rows, :] = source[:, head * DH : (head + 1) * DH]


def arrange(head_pattern, tile_masks, queries, key_rows, value_rows):
    rows = queries.shape[0]
    return pl.pallas_call(
        arrange_kernel,
        out_shape=(
            jax.ShapeDtypeStruct((HEADS_HERE, rows, DH), BF16),
            jax.ShapeDtypeStruct((HEADS_HERE, 2 * rows, DH), BF16),
            jax.ShapeDtypeStruct((SLOTS + 1, TILES), jnp.int32),
        ),
        in_specs=[pl.BlockSpec(memory_space=pltpu.SMEM)]
        + [pl.BlockSpec(memory_space=pl.ANY)] * 4,
        out_specs=(pl.BlockSpec(memory_space=pltpu.VMEM),) * 3,
        scratch_shapes=[
            pltpu.VMEM(tile_masks.shape, jnp.int32),
            pltpu.VMEM(queries.shape, BF16),
            pltpu.VMEM(queries.shape, BF16),
            pltpu.VMEM(queries.shape, BF16),
            pltpu.SemaphoreType.DMA((4,)),
        ],
        compiler_params=pltpu.CompilerParams(vmem_limit_bytes=57 * 1024 * 1024),
    )(head_pattern, tile_masks, queries, key_rows, value_rows)


def body(queries, key_rows, value_rows, out_weight, tile_masks, head_pattern):
    rows = queries.shape[0]
    q_parts, kv_parts, lists = arrange(head_pattern, tile_masks, queries, key_rows, value_rows)
    q_all, kv_all, w_all = spread(
        q_parts.reshape(HEADS_HERE, SLOTS, WORKERS, SPOTS, DH),
        kv_parts.reshape(HEADS_HERE, 2 * TILES, SPOTS, DH),
        out_weight,
    )
    attended = attend(
        lists, q_all.reshape(SLOTS * TILE, DH), kv_all.reshape(WORKERS, 2 * TILES * PIECE, DH)
    )
    attn = collect(attended.reshape(SLOTS, FRAMES, SPOTS, DH))
    attn = attn.reshape(PLANES * HEADS_HERE, rows, DH)
    return project(attn, w_all, rows)


def solution(mesh):
    placed = (
        P("ctx", "heads"),
        P("ctx", "heads"),
        P("ctx", "heads"),
        P("heads", None),
        P(),
        P("heads"),
    )
    return jax.shard_map(
        body, mesh=mesh, in_specs=placed, out_specs=P("ctx", "heads"), check_vma=False
    )
```

```python
import math

import jax
import jax.numpy as jnp
from jax import lax
from jax.experimental import pallas as pl
from jax.experimental.pallas import tpu as pltpu
from jax.sharding import PartitionSpec as P

MESH = pl.DeviceIdType.MESH
DH = 128
TILE = 128
SPOTS = 4
FRAMES = 32
TILES = 128
PLANES = 4
SIDE = 4
HEADS_HERE = 3
WORKERS = 2 * SIDE
SLOTS = TILES // WORKERS
PARTS = 4
PART = 2 * TILES // PARTS
PIECE = TILE // WORKERS
GROUP = 8
CHUNK = 32
BESIDE = 4
FAR = 2.0**64
LOW = -1e30
SCALE2 = math.log2(math.e) / math.sqrt(DH)
BF16 = jnp.bfloat16
F32 = jnp.float32


def where_is(device):
    return lax.div(device, WORKERS), lax.rem(lax.div(device, 2), SIDE), lax.rem(device, 2)


def device_at(row, column, core):
    return (lax.rem(row, SIDE) * SIDE + lax.rem(column, SIDE)) * 2 + core


def spread_kernel(
    q_ref, kv_ref, w_ref, kv_all, w_all,
    q_send, q_recv, z_send, z_recv, y_send, y_recv, far_send, far_recv,
    core_send, core_recv, w_send, w_recv, w_core_send, w_core_recv, own_sem,
):
    plane = lax.axis_index("heads")
    me = lax.axis_index("ctx")
    row, column, core = where_is(me)
    working = row < HEADS_HERE
    own_row = jnp.minimum(row, HEADS_HERE - 1)
    depth = w_ref.shape[0]
    width = w_all.shape[1]
    sides = (1, SIDE - 1)

    barrier = pltpu.get_barrier_semaphore()

    def greet(step, carry):
        pl.semaphore_signal(
            barrier, inc=1, device_id=(plane, lax.rem(me + step, FRAMES)), device_id_type=MESH
        )
        return carry

    lax.fori_loop(1, FRAMES, greet, 0)
    for hop in range(1, PLANES):
        pl.semaphore_signal(
            barrier, inc=1, device_id=(lax.rem(plane + hop, PLANES), me), device_id_type=MESH
        )
    pl.semaphore_wait(barrier, FRAMES - 1 + PLANES - 1)

    def span(part):
        return pl.ds(part * PART, PART)

    own_copy = pltpu.make_async_copy(
        kv_ref.at[own_row], kv_all.at[column * 2 + core, pl.ds(0, 2 * TILES), 0], own_sem
    )

    def z_copy(part, hop):
        there = lax.rem(row + hop, SIDE)
        return pltpu.make_async_remote_copy(
            src_ref=kv_ref.at[there, span(part)],
            dst_ref=kv_all.at[column * 2 + core, span(part), hop],
            send_sem=z_send.at[part, hop],
            recv_sem=z_recv.at[part, hop],
            device_id=(plane, device_at(there, column, core)),
            device_id_type=MESH,
        )

    def piece(number, away):
        source = kv_all.at[lax.rem(column + away, SIDE) * 2 + core]
        if number == 0:
            return source.at[pl.ds(0, 2 * TILES), 0]
        return source.at[span(number - 1), pl.ds(1, SIDE - 1)]

    def y_copy(number, side):
        return pltpu.make_async_remote_copy(
            src_ref=kv_ref.at[own_row] if number == 0 else piece(number, 0),
            dst_ref=piece(number, 0),
            send_sem=y_send.at[number, side],
            recv_sem=y_recv.at[number, side],
            device_id=(plane, device_at(row, column + sides[side], core)),
            device_id_type=MESH,
        )

    def far_copy(number, side):
        source = kv_all.at[lax.rem(column + sides[1 - side], SIDE) * 2 + core]
        if number == 0:
            chunk = source.at[pl.ds(side * TILES, TILES), 0]
        else:
            chunk = source.at[
                pl.ds((number - 1) * PART + side * (PART // 2), PART // 2), pl.ds(1, SIDE - 1)
            ]
        return pltpu.make_async_remote_copy(
            src_ref=chunk,
            dst_ref=chunk,
            send_sem=far_send.at[number, side],
            recv_sem=far_recv.at[number, side],
            device_id=(plane, device_at(row, column + sides[side], core)),
            device_id_type=MESH,
        )

    def core_copy(number, away):
        return pltpu.make_async_remote_copy(
            src_ref=piece(number, away),
            dst_ref=piece(number, away),
            send_sem=core_send.at[number, away],
            recv_sem=core_recv,
            device_id=(plane, device_at(row, column, 1 - core)),
            device_id_type=MESH,
        )

    half = depth // 2

    def w_rows(source, part):
        return w_all.at[pl.ds(pl.multiple_of(source * depth + part * half, 16), half)]

    def w_copy(hop):
        there = lax.rem(plane + hop, PLANES)
        return pltpu.make_async_remote_copy(
            src_ref=w_ref.at[
                pl.ds(pl.multiple_of(core * half, 16), half),
                pl.ds(pl.multiple_of(there * width, 128), width),
            ],
            dst_ref=w_rows(plane, core),
            send_sem=w_send.at[hop],
            recv_sem=w_recv.at[hop],
            device_id=(there, me),
            device_id_type=MESH,
        )

    def w_core_copy(hop):
        rows = w_rows(lax.rem(plane + PLANES - hop, PLANES), core)
        return pltpu.make_async_remote_copy(
            src_ref=rows,
            dst_ref=rows,
            send_sem=w_core_send.at[hop],
            recv_sem=w_core_recv.at[hop],
            device_id=(plane, device_at(row, column, 1 - core)),
            device_id_type=MESH,
        )

    own_w = pltpu.make_async_copy(
        w_ref.at[:, pl.ds(pl.multiple_of(plane * width, 128), width)],
        w_all.at[pl.ds(pl.multiple_of(plane * depth, 128), depth)],
        w_recv.at[0],
    )

    queries = kv_all.at[:, pl.ds(2 * TILES, SLOTS)]

    def q_copy(step):
        there = lax.rem(me + step, FRAMES)
        row_there, column_there, core_there = where_is(there)
        return row_there < HEADS_HERE, pltpu.make_async_remote_copy(
            src_ref=q_ref.at[
                jnp.minimum(row_there, HEADS_HERE - 1), :, column_there * 2 + core_there
            ],
            dst_ref=queries.at[column * 2 + core, :, lax.rem(row_there - row + SIDE, SIDE)],
            send_sem=q_send.at[step],
            recv_sem=q_recv,
            device_id=(plane, there),
            device_id_type=MESH,
        )

    def to_rows(part, work):
        for hop in range(1, SIDE):

            @pl.when(lax.rem(row + hop, SIDE) < HEADS_HERE)
            def _():
                work(z_copy(part, hop))

    def send_q(step, carry):
        wanted, copy = q_copy(step)

        @pl.when(wanted)
        def _():
            copy.start()

        return carry

    def sent_q(step, carry):
        wanted, copy = q_copy(step)

        @pl.when(wanted)
        def _():
            copy.wait_send()

        return carry

    def send_small():
        for hop in range(1, PLANES):
            w_copy(hop).start()
        own_w.start()
        lax.fori_loop(1, FRAMES, send_q, 0)

    @pl.when(working)
    def _():
        own_copy.start()
        for side in range(2):
            y_copy(0, side).start()

    to_rows(0, lambda copy: copy.start())
    send_small()

    def next_rows(part):
        to_rows(part, lambda copy: copy.wait_send())
        if part + 1 < PARTS:
            to_rows(part + 1, lambda copy: copy.start())

    @pl.when(jnp.logical_not(working))
    def _():
        for part in range(PARTS):
            next_rows(part)

    @pl.when(working)
    def _():
        pltpu.make_async_copy(
            q_ref.at[own_row, :, column * 2 + core], queries.at[column * 2 + core, :, 0], q_recv
        ).start()
        own_copy.wait()
        core_copy(0, 0).start()

        def pass_on(number):
            for side in range(2):
                y_copy(number, side).wait_recv()
                far_copy(number, side).start()
            for side in range(2):
                core_copy(number, sides[1 - side]).start()

        for part in range(PARTS):
            next_rows(part)
            for hop in range(1, SIDE):
                landed = kv_all.at[column * 2 + core, span(part), hop]
                pltpu.make_async_copy(landed, landed, z_recv.at[part, hop]).wait()
            for side in range(2):
                y_copy(part + 1, side).start()
            core_copy(part + 1, 0).start()
            pass_on(part)
        pass_on(PARTS)
        for number in range(PARTS + 1):
            for side in range(2):
                far_copy(number, side).wait_recv()
            core_copy(number, 2).start()

    for hop in range(1, PLANES):
        w_copy(hop).wait_recv()
        w_core_copy(hop).start()

    @pl.when(working)
    def _():
        pltpu.make_async_copy(queries, queries, q_recv).wait()
        other = kv_all.at[pl.ds(0, SIDE), pl.ds(0, 2 * TILES)]
        pltpu.make_async_copy(other, other, core_recv).wait()
        for number in range(PARTS + 1):
            for side in range(2):
                y_copy(number, side).wait_send()
                far_copy(number, side).wait_send()
            for away in range(SIDE):
                core_copy(number, away).wait_send()

    own_w.wait()
    lax.fori_loop(1, FRAMES, sent_q, 0)
    for hop in range(1, PLANES):
        w_copy(hop).wait_send()
        w_core_copy(hop).wait()


def spread(q_parts, kv_parts, out_weight):
    depth, columns = out_weight.shape
    return pl.pallas_call(
        spread_kernel,
        out_shape=(
            jax.ShapeDtypeStruct((WORKERS, 2 * TILES + SLOTS, SIDE, SPOTS, DH), BF16),
            jax.ShapeDtypeStruct((depth * PLANES, columns // PLANES), BF16),
        ),
        in_specs=[pl.BlockSpec(memory_space=pl.ANY)] * 3,
        out_specs=(pl.BlockSpec(memory_space=pl.ANY),) * 2,
        scratch_shapes=[
            pltpu.SemaphoreType.DMA((FRAMES,)),
            pltpu.SemaphoreType.DMA,
            pltpu.SemaphoreType.DMA((PARTS, SIDE)),
            pltpu.SemaphoreType.DMA((PARTS, SIDE)),
            pltpu.SemaphoreType.DMA((PARTS + 1, 2)),
            pltpu.SemaphoreType.DMA((PARTS + 1, 2)),
            pltpu.SemaphoreType.DMA((PARTS + 1, 2)),
            pltpu.SemaphoreType.DMA((PARTS + 1, 2)),
            pltpu.SemaphoreType.DMA((PARTS + 1, SIDE)),
            pltpu.SemaphoreType.DMA,
            pltpu.SemaphoreType.DMA((PLANES,)),
            pltpu.SemaphoreType.DMA((PLANES,)),
            pltpu.SemaphoreType.DMA((PLANES,)),
            pltpu.SemaphoreType.DMA((PLANES,)),
            pltpu.SemaphoreType.DMA,
        ],
        compiler_params=pltpu.CompilerParams(
            collective_id=0, has_side_effects=True, vmem_limit_bytes=57 * 1024 * 1024
        ),
    )(q_parts, kv_parts, out_weight)


def attend_kernel(
    list_ref, kv_hbm, o_ref, kv_ref, q_ref, keys_ref, base_ref, peak_ref, sum_ref,
    slot_of, first_of, listed_of, kv_sem,
):
    def bring(number, first, tiles):
        rows = pl.ds(first * PIECE, tiles * PIECE)
        return pltpu.make_async_copy(kv_hbm.at[:, rows], kv_ref.at[:, rows], kv_sem.at[number])

    chunks = TILES // CHUNK
    moves = [bring(number, number * CHUNK, CHUNK) for number in range(chunks)]
    moves.append(bring(chunks, 2 * TILES, SLOTS))
    moves.append(bring(chunks + 1, TILES, TILES))
    for move in moves:
        move.start()

    _, column, core = where_is(lax.axis_index("ctx"))

    def loop(count, work):
        def one(step, carry):
            work(step)
            return carry

        lax.fori_loop(0, count, one, 0)

    def rows_of(slot):
        return pl.ds(pl.multiple_of(slot * TILE, TILE), TILE)

    def tile_at(tile):
        start = pl.multiple_of(tile * PIECE, PIECE)
        return jnp.concatenate(
            [kv_ref[worker, pl.ds(start, PIECE), :] for worker in range(WORKERS)], axis=0
        )

    def enlist(slot, total):
        count = list_ref[SLOTS, slot]
        steps = lax.div(count + GROUP - 1, GROUP)

        def one(step, carry):
            slot_of[total + step] = slot
            first_of[total + step] = step * GROUP
            listed_of[total + step] = count - step * GROUP
            return carry

        lax.fori_loop(0, steps, one, 0)
        return total + steps

    total = lax.fori_loop(0, SLOTS, enlist, 0)
    for spare in range(BESIDE - 1):
        slot_of[total + spare] = 0
        first_of[total + spare] = 0
        listed_of[total + spare] = 0
    turns = lax.div(total + BESIDE - 1, BESIDE)
    busy = jnp.where(total > 0, 1, 0)

    def unpack(step):
        for u in range(GROUP):
            tile = step * GROUP + u
            keys_ref[tile] = tile_at(tile).T

    for number in range(chunks):
        moves[number].wait()
        steps = CHUNK // GROUP
        loop(busy * steps, lambda step: unpack(step + number * steps))
    moves[chunks].wait()

    def set_base(slot, base):
        base_ref[slot] = jnp.broadcast_to(base * SCALE2, (TILE, TILE))

    def own_base(step):
        for u in range(BESIDE):
            slot = step * BESIDE + u
            own = keys_ref[slot * WORKERS + column * 2 + core]
            query = tile_at(2 * TILES + slot)
            q_ref[rows_of(slot), :] = query
            scores = jnp.dot(query, own, preferred_element_type=F32)
            set_base(slot, jnp.max(scores, axis=1, keepdims=True))

    loop(busy * (SLOTS // BESIDE), own_base)
    moves[chunks + 1].wait()

    def tiles_of(number):
        slot, first = slot_of[number], first_of[number]
        return slot, [list_ref[slot, first + u] for u in range(GROUP)]

    def scores_of(slot, tiles):
        keys = jnp.concatenate([keys_ref[tile] for tile in tiles], axis=1)
        return jnp.dot(q_ref[rows_of(slot), :], keys, preferred_element_type=F32)

    def attend_steps(step):
        found = []
        for beside in range(BESIDE):
            number = step * BESIDE + beside
            slot, tiles = tiles_of(number)
            listed = listed_of[number]
            base = base_ref[slot]
            scores = scores_of(slot, tiles)
            weights, values = [], []
            for u in range(GROUP):
                part = scores[:, u * TILE : (u + 1) * TILE]
                weights.append(jnp.exp2(part * SCALE2 - base).astype(BF16))
                value = jnp.where(u < listed, tile_at(TILES + tiles[u]), 0).astype(BF16)
                ones = jnp.where(u < listed, 1.0, 0.0).astype(BF16)
                ones = jnp.broadcast_to(ones, (TILE, DH))
                values.append(jnp.concatenate([value, ones], axis=1))
            added = jnp.dot(
                jnp.concatenate(weights, axis=1),
                jnp.concatenate(values, axis=0),
                preferred_element_type=F32,
            )
            found.append((slot, added))
        for slot, added in found:
            sum_ref[slot] += added

    def peak_steps(step):
        for beside in range(BESIDE):
            slot, tiles = tiles_of(step * BESIDE + beside)
            scores = scores_of(slot, tiles)
            peak = peak_ref[slot]
            for u in range(GROUP):
                peak = jnp.maximum(peak, scores[:, u * TILE : (u + 1) * TILE])
            peak_ref[slot] = peak

    def attempt(number, needed):
        def clear(slot):
            sum_ref[slot] = jnp.zeros((TILE, 2 * DH), F32)
            peak_ref[slot] = jnp.full((TILE, TILE), LOW, F32)

        loop(needed * SLOTS, clear)
        loop(needed * turns, attend_steps)
        beyond = jnp.zeros((TILE, DH), F32)
        for slot in range(SLOTS):
            beyond = jnp.where(sum_ref[slot, :, DH:] <= FAR, beyond, 1.0)
        again = needed * jnp.where(jnp.max(beyond) > 0.0, 1, 0)
        loop(again * turns, peak_steps)

        def rebase(slot):
            set_base(slot, jnp.max(peak_ref[slot], axis=1, keepdims=True))

        loop(again * SLOTS, rebase)
        return again

    lax.fori_loop(0, 2, attempt, busy)

    def finish(step):
        for u in range(BESIDE):
            slot = step * BESIDE + u
            o_ref[rows_of(slot), :] = (sum_ref[slot, :, :DH] / sum_ref[slot, :, DH:]).astype(BF16)

    loop(busy * (SLOTS // BESIDE), finish)


def attend(lists, kv):
    most = SLOTS * (TILES // GROUP) + BESIDE
    return pl.pallas_call(
        attend_kernel,
        out_shape=jax.ShapeDtypeStruct((SLOTS * TILE, DH), BF16),
        in_specs=[pl.BlockSpec(memory_space=pltpu.SMEM), pl.BlockSpec(memory_space=pl.ANY)],
        out_specs=pl.BlockSpec(memory_space=pltpu.VMEM),
        scratch_shapes=[
            pltpu.VMEM(kv.shape, BF16),
            pltpu.VMEM((SLOTS * TILE, DH), BF16),
            pltpu.VMEM((TILES, DH, TILE), BF16),
            pltpu.VMEM((SLOTS, TILE, TILE), F32),
            pltpu.VMEM((SLOTS, TILE, TILE), F32),
            pltpu.VMEM((SLOTS, TILE, 2 * DH), F32),
            pltpu.SMEM((most,), jnp.int32),
            pltpu.SMEM((most,), jnp.int32),
            pltpu.SMEM((most,), jnp.int32),
            pltpu.SemaphoreType.DMA((TILES // CHUNK + 2,)),
        ],
        compiler_params=pltpu.CompilerParams(vmem_limit_bytes=50 * 1024 * 1024),
    )(lists, kv)


def collect_kernel(o_ref, attn, send, recv, x_send, x_recv):
    plane = lax.axis_index("heads")
    me = lax.axis_index("ctx")
    row, column, core = where_is(me)
    barrier = pltpu.get_barrier_semaphore()

    def greet(step, carry):
        pl.semaphore_signal(
            barrier, inc=1, device_id=(plane, lax.rem(me + step, FRAMES)), device_id_type=MESH
        )
        return carry

    lax.fori_loop(1, FRAMES, greet, 0)
    sides = (lax.rem(plane + 1, PLANES), lax.rem(plane + PLANES - 1, PLANES))
    for there in sides:
        pl.semaphore_signal(barrier, inc=1, device_id=(there, me), device_id_type=MESH)
    pl.semaphore_wait(barrier, FRAMES - 1 + 2)

    mine = jnp.minimum(row, HEADS_HERE - 1)
    goal = attn.at[plane * HEADS_HERE + mine, :, column * 2 + core]

    def rows_for(there):
        row_there, column_there, core_there = where_is(there)
        above = lax.rem(row - row_there + SIDE, SIDE)
        return o_ref.at[:, column_there * 2 + core_there, above]

    def back(step):
        there = lax.rem(me + step, FRAMES)
        return pltpu.make_async_remote_copy(
            src_ref=rows_for(there),
            dst_ref=goal,
            send_sem=send.at[step],
            recv_sem=recv.at[mine],
            device_id=(plane, there),
            device_id_type=MESH,
        )

    def start(step, carry):
        back(step).start()
        return carry

    def end(step, carry):
        back(step).wait_send()
        return carry

    working = row < HEADS_HERE

    @pl.when(working)
    def _():
        lax.fori_loop(1, FRAMES, start, 0)
        pltpu.make_async_copy(rows_for(me), goal, recv.at[mine]).start()

    cut = SLOTS // 2

    def near(head, side):
        part = attn.at[plane * HEADS_HERE + head]
        return pltpu.make_async_remote_copy(
            src_ref=part,
            dst_ref=part,
            send_sem=x_send.at[head, side],
            recv_sem=x_recv.at[head, side],
            device_id=(sides[side], me),
            device_id_type=MESH,
        )

    def far(head, side):
        part = attn.at[sides[1 - side] * HEADS_HERE + head]
        part = part.at[pl.ds(0, cut)] if side == 0 else part.at[pl.ds(cut, SLOTS - cut)]
        return pltpu.make_async_remote_copy(
            src_ref=part,
            dst_ref=part,
            send_sem=x_send.at[head, 2 + side],
            recv_sem=x_recv.at[head, 2 + side],
            device_id=(sides[side], me),
            device_id_type=MESH,
        )

    for head in range(HEADS_HERE):
        part = attn.at[plane * HEADS_HERE + head]
        pltpu.make_async_copy(part, part, recv.at[head]).wait()
        for side in range(2):
            near(head, side).start()
    for head in range(HEADS_HERE):
        for side in range(2):
            near(head, side).wait_recv()
            far(head, side).start()

    @pl.when(working)
    def _():
        lax.fori_loop(1, FRAMES, end, 0)

    for head in range(HEADS_HERE):
        for side in range(2):
            near(head, side).wait_send()
            far(head, side).wait()


def collect(attended):
    return pl.pallas_call(
        collect_kernel,
        out_shape=jax.ShapeDtypeStruct(
            (PLANES * HEADS_HERE, SLOTS, WORKERS, SPOTS, DH), BF16
        ),
        in_specs=[pl.BlockSpec(memory_space=pl.ANY)],
        out_specs=pl.BlockSpec(memory_space=pl.ANY),
        scratch_shapes=[
            pltpu.SemaphoreType.DMA((FRAMES,)),
            pltpu.SemaphoreType.DMA((HEADS_HERE,)),
            pltpu.SemaphoreType.DMA((HEADS_HERE, 4)),
            pltpu.SemaphoreType.DMA((HEADS_HERE, 4)),
        ],
        compiler_params=pltpu.CompilerParams(
            collective_id=1, has_side_effects=True, vmem_limit_bytes=4 * 1024 * 1024
        ),
    )(attended)


def project_kernel(attn_ref, w_ref, out_ref):
    heads = attn_ref.shape[0]
    wide = jnp.concatenate([attn_ref[h] for h in range(heads)], axis=1)
    block = 256
    for first in range(0, out_ref.shape[1], block):
        columns = slice(first, first + block)
        out_ref[:, columns] = jnp.dot(
            wide, w_ref[:, columns], preferred_element_type=F32
        ).astype(BF16)


def project(attn, weight, rows):
    return pl.pallas_call(
        project_kernel,
        out_shape=jax.ShapeDtypeStruct((rows, weight.shape[1]), BF16),
        in_specs=[pl.BlockSpec(memory_space=pltpu.VMEM)] * 2,
        out_specs=pl.BlockSpec(memory_space=pltpu.VMEM),
        compiler_params=pltpu.CompilerParams(vmem_limit_bytes=24 * 1024 * 1024),
    )(attn, weight)


def arrange_kernel(
    pattern_ref, mask_hbm, q_hbm, k_hbm, v_hbm, q_out, kv_out, list_ref,
    mask_ref, q_ref, k_ref, v_ref, sems,
):
    sources = (mask_hbm, q_hbm, k_hbm, v_hbm)
    targets = (mask_ref, q_ref, k_ref, v_ref)
    moves = [
        pltpu.make_async_copy(source, target, sems.at[i])
        for i, (source, target) in enumerate(zip(sources, targets))
    ]
    for move in moves:
        move.start()
    me = lax.axis_index("ctx")
    row, column, core = where_is(me)
    moves[0].wait()
    pattern = pattern_ref[jnp.minimum(row, HEADS_HERE - 1)]
    masks = []
    tiles = [slot * WORKERS + column * 2 + core for slot in range(SLOTS)]
    for tile in tiles:
        masks.append(jnp.where(row < HEADS_HERE, mask_ref[pattern, pl.ds(tile, 1), :], 0))
    seen = jnp.concatenate(masks, axis=0) == 1
    seen = jnp.where(seen, 1.0, 0.0).astype(F32)
    down = lax.broadcasted_iota(jnp.int32, (TILES, TILES), 0)
    along = lax.broadcasted_iota(jnp.int32, (TILES, TILES), 1)
    both = (((1,), (1,)), ((), ()))
    upto = jnp.where(along <= down, 1.0, 0.0).astype(BF16)
    same = jnp.where(along == down, 1.0, 0.0).astype(BF16)
    rank = lax.dot_general(upto, seen.astype(BF16), both, preferred_element_type=F32)
    turned = lax.dot_general(same, seen.astype(BF16), both, preferred_element_type=F32)
    rank = rank.astype(jnp.int32)
    spot = jnp.where(turned > 0.5, rank - 1, -1)
    for slot in range(SLOTS):
        hit = spot[:, slot : slot + 1] == along
        listed = jnp.sum(jnp.where(hit, down, 0), axis=0, keepdims=True)
        spare = along[:1, :] >= rank[TILES - 1 :, slot : slot + 1]
        list_ref[slot : slot + 1, :] = jnp.where(spare, tiles[slot], listed)
    last = jnp.concatenate(
        [rank[TILES - 1 :, :], jnp.zeros((1, TILES - SLOTS), jnp.int32)], axis=1
    )
    list_ref[SLOTS : SLOTS + 1, :] = last


    rows = q_ref.shape[0]
    for move, source, target, first in (
        (moves[1], q_ref, q_out, 0),
        (moves[2], k_ref, kv_out, 0),
        (moves[3], v_ref, kv_out, rows),
    ):
        move.wait()
        for head in range(HEADS_HERE):
            target[head, first : first + rows, :] = source[:, head * DH : (head + 1) * DH]


def arrange(head_pattern, tile_masks, queries, key_rows, value_rows):
    rows = queries.shape[0]
    return pl.pallas_call(
        arrange_kernel,
        out_shape=(
            jax.ShapeDtypeStruct((HEADS_HERE, rows, DH), BF16),
            jax.ShapeDtypeStruct((HEADS_HERE, 2 * rows, DH), BF16),
            jax.ShapeDtypeStruct((SLOTS + 1, TILES), jnp.int32),
        ),
        in_specs=[pl.BlockSpec(memory_space=pltpu.SMEM)]
        + [pl.BlockSpec(memory_space=pl.ANY)] * 4,
        out_specs=(pl.BlockSpec(memory_space=pltpu.VMEM),) * 3,
        scratch_shapes=[
            pltpu.VMEM(tile_masks.shape, jnp.int32),
            pltpu.VMEM(queries.shape, BF16),
            pltpu.VMEM(queries.shape, BF16),
            pltpu.VMEM(queries.shape, BF16),
            pltpu.SemaphoreType.DMA((4,)),
        ],
        compiler_params=pltpu.CompilerParams(vmem_limit_bytes=57 * 1024 * 1024),
    )(head_pattern, tile_masks, queries, key_rows, value_rows)


def body(queries, key_rows, value_rows, out_weight, tile_masks, head_pattern):
    rows = queries.shape[0]
    q_parts, kv_parts, lists = arrange(head_pattern, tile_masks, queries, key_rows, value_rows)
    kv_all, w_all = spread(
        q_parts.reshape(HEADS_HERE, SLOTS, WORKERS, SPOTS, DH),
        kv_parts.reshape(HEADS_HERE, 2 * TILES, SPOTS, DH),
        out_weight,
    )
    attended = attend(lists, kv_all.reshape(WORKERS, (2 * TILES + SLOTS) * PIECE, DH))
    attn = collect(attended.reshape(SLOTS, WORKERS, SIDE, SPOTS, DH))
    attn = attn.reshape(PLANES * HEADS_HERE, rows, DH)
    return project(attn, w_all, rows)


def solution(mesh):
    placed = (
        P("ctx", "heads"),
        P("ctx", "heads"),
        P("ctx", "heads"),
        P("heads", None),
        P(),
        P("heads"),
    )
    return jax.shard_map(
        body, mesh=mesh, in_specs=placed, out_specs=P("ctx", "heads"), check_vma=False
    )
```

```python
import math

import jax
import jax.numpy as jnp
from jax import lax
from jax.experimental import pallas as pl
from jax.experimental.pallas import tpu as pltpu
from jax.sharding import PartitionSpec as P

MESH = pl.DeviceIdType.MESH
DH = 128
TILE = 128
SPOTS = 4
FRAMES = 32
TILES = 128
PLANES = 4
SIDE = 4
HEADS_HERE = 3
WORKERS = 2 * SIDE
SLOTS = TILES // WORKERS
PARTS = 4
PART = 2 * TILES // PARTS
PIECE = TILE // WORKERS
GROUP = 8
CHUNK = 32
BESIDE = 4
FAR = 2.0**64
LOW = -1e30
SCALE2 = math.log2(math.e) / math.sqrt(DH)
BF16 = jnp.bfloat16
F32 = jnp.float32


def where_is(device):
    return lax.div(device, WORKERS), lax.rem(lax.div(device, 2), SIDE), lax.rem(device, 2)


def device_at(row, column, core):
    return (lax.rem(row, SIDE) * SIDE + lax.rem(column, SIDE)) * 2 + core


def spread_kernel(
    q_ref, kv_ref, w_ref, kv_all, w_all,
    q_send, q_recv, z_send, z_recv, y_send, y_recv, far_send, far_recv,
    core_send, core_recv, w_send, w_recv, w_core_send, w_core_recv, own_sem,
):
    plane = lax.axis_index("heads")
    me = lax.axis_index("ctx")
    row, column, core = where_is(me)
    working = row < HEADS_HERE
    own_row = jnp.minimum(row, HEADS_HERE - 1)
    depth = w_ref.shape[0]
    width = w_all.shape[1]
    sides = (1, SIDE - 1)

    barrier = pltpu.get_barrier_semaphore()

    def greet(step, carry):
        pl.semaphore_signal(
            barrier, inc=1, device_id=(plane, lax.rem(me + step, FRAMES)), device_id_type=MESH
        )
        return carry

    lax.fori_loop(1, FRAMES, greet, 0)
    for hop in range(1, PLANES):
        pl.semaphore_signal(
            barrier, inc=1, device_id=(lax.rem(plane + hop, PLANES), me), device_id_type=MESH
        )
    pl.semaphore_wait(barrier, FRAMES - 1 + PLANES - 1)

    def span(part):
        return pl.ds(part * PART, PART)

    own_copy = pltpu.make_async_copy(
        kv_ref.at[own_row], kv_all.at[column * 2 + core, pl.ds(0, 2 * TILES), 0], own_sem
    )

    def z_copy(part, hop):
        there = lax.rem(row + hop, SIDE)
        return pltpu.make_async_remote_copy(
            src_ref=kv_ref.at[there, span(part)],
            dst_ref=kv_all.at[column * 2 + core, span(part), hop],
            send_sem=z_send.at[part, hop],
            recv_sem=z_recv.at[part, hop],
            device_id=(plane, device_at(there, column, core)),
            device_id_type=MESH,
        )

    def piece(number, away):
        source = kv_all.at[lax.rem(column + away, SIDE) * 2 + core]
        if number == 0:
            return source.at[pl.ds(0, 2 * TILES), 0]
        return source.at[span(number - 1), pl.ds(1, SIDE - 1)]

    def y_copy(number, side):
        return pltpu.make_async_remote_copy(
            src_ref=kv_ref.at[own_row] if number == 0 else piece(number, 0),
            dst_ref=piece(number, 0),
            send_sem=y_send.at[number, side],
            recv_sem=y_recv.at[number, side],
            device_id=(plane, device_at(row, column + sides[side], core)),
            device_id_type=MESH,
        )

    def far_copy(number, side):
        source = kv_all.at[lax.rem(column + sides[1 - side], SIDE) * 2 + core]
        if number == 0:
            chunk = source.at[pl.ds(side * TILES, TILES), 0]
        else:
            chunk = source.at[
                pl.ds((number - 1) * PART + side * (PART // 2), PART // 2), pl.ds(1, SIDE - 1)
            ]
        return pltpu.make_async_remote_copy(
            src_ref=chunk,
            dst_ref=chunk,
            send_sem=far_send.at[number, side],
            recv_sem=far_recv.at[number, side],
            device_id=(plane, device_at(row, column + sides[side], core)),
            device_id_type=MESH,
        )

    def core_copy(number, away):
        return pltpu.make_async_remote_copy(
            src_ref=piece(number, away),
            dst_ref=piece(number, away),
            send_sem=core_send.at[number, away],
            recv_sem=core_recv,
            device_id=(plane, device_at(row, column, 1 - core)),
            device_id_type=MESH,
        )

    half = depth // 2

    def w_rows(source, part):
        return w_all.at[pl.ds(pl.multiple_of(source * depth + part * half, 16), half)]

    def w_copy(hop):
        there = lax.rem(plane + hop, PLANES)
        return pltpu.make_async_remote_copy(
            src_ref=w_ref.at[
                pl.ds(pl.multiple_of(core * half, 16), half),
                pl.ds(pl.multiple_of(there * width, 128), width),
            ],
            dst_ref=w_rows(plane, core),
            send_sem=w_send.at[hop],
            recv_sem=w_recv.at[hop],
            device_id=(there, me),
            device_id_type=MESH,
        )

    def w_core_copy(hop):
        rows = w_rows(lax.rem(plane + PLANES - hop, PLANES), core)
        return pltpu.make_async_remote_copy(
            src_ref=rows,
            dst_ref=rows,
            send_sem=w_core_send.at[hop],
            recv_sem=w_core_recv.at[hop],
            device_id=(plane, device_at(row, column, 1 - core)),
            device_id_type=MESH,
        )

    own_w = pltpu.make_async_copy(
        w_ref.at[:, pl.ds(pl.multiple_of(plane * width, 128), width)],
        w_all.at[pl.ds(pl.multiple_of(plane * depth, 128), depth)],
        w_recv.at[0],
    )

    queries = kv_all.at[:, pl.ds(2 * TILES, SLOTS)]

    def q_copy(step):
        there = lax.rem(me + step, FRAMES)
        row_there, column_there, core_there = where_is(there)
        return row_there < HEADS_HERE, pltpu.make_async_remote_copy(
            src_ref=q_ref.at[
                jnp.minimum(row_there, HEADS_HERE - 1), :, column_there * 2 + core_there
            ],
            dst_ref=queries.at[column * 2 + core, :, lax.rem(row_there - row + SIDE, SIDE)],
            send_sem=q_send.at[step],
            recv_sem=q_recv,
            device_id=(plane, there),
            device_id_type=MESH,
        )

    def to_rows(part, work):
        for hop in range(1, SIDE):

            @pl.when(lax.rem(row + hop, SIDE) < HEADS_HERE)
            def _():
                work(z_copy(part, hop))

    def send_q(step, carry):
        wanted, copy = q_copy(step)

        @pl.when(wanted)
        def _():
            copy.start()

        return carry

    def sent_q(step, carry):
        wanted, copy = q_copy(step)

        @pl.when(wanted)
        def _():
            copy.wait_send()

        return carry

    def send_small():
        for hop in range(1, PLANES):
            w_copy(hop).start()
        own_w.start()
        lax.fori_loop(1, FRAMES, send_q, 0)

    @pl.when(working)
    def _():
        own_copy.start()
        for side in range(2):
            y_copy(0, side).start()

    to_rows(0, lambda copy: copy.start())
    to_rows(1, lambda copy: copy.start())
    send_small()

    def next_rows(part):
        to_rows(part, lambda copy: copy.wait_send())
        if part + 2 < PARTS:
            to_rows(part + 2, lambda copy: copy.start())

    @pl.when(jnp.logical_not(working))
    def _():
        for part in range(PARTS):
            next_rows(part)

    @pl.when(working)
    def _():
        pltpu.make_async_copy(
            q_ref.at[own_row, :, column * 2 + core], queries.at[column * 2 + core, :, 0], q_recv
        ).start()
        own_copy.wait()
        core_copy(0, 0).start()

        def pass_on(number):
            for side in range(2):
                y_copy(number, side).wait_recv()
                far_copy(number, side).start()
            for side in range(2):
                core_copy(number, sides[1 - side]).start()

        for part in range(PARTS):
            next_rows(part)
            for hop in range(1, SIDE):
                landed = kv_all.at[column * 2 + core, span(part), hop]
                pltpu.make_async_copy(landed, landed, z_recv.at[part, hop]).wait()
            for side in range(2):
                y_copy(part + 1, side).start()
            core_copy(part + 1, 0).start()
            pass_on(part)
        pass_on(PARTS)
        for number in range(PARTS + 1):
            for side in range(2):
                far_copy(number, side).wait_recv()
            core_copy(number, 2).start()

    for hop in range(1, PLANES):
        w_copy(hop).wait_recv()
        w_core_copy(hop).start()

    @pl.when(working)
    def _():
        pltpu.make_async_copy(queries, queries, q_recv).wait()
        other = kv_all.at[pl.ds(0, SIDE), pl.ds(0, 2 * TILES)]
        pltpu.make_async_copy(other, other, core_recv).wait()
        for number in range(PARTS + 1):
            for side in range(2):
                y_copy(number, side).wait_send()
                far_copy(number, side).wait_send()
            for away in range(SIDE):
                core_copy(number, away).wait_send()

    own_w.wait()
    lax.fori_loop(1, FRAMES, sent_q, 0)
    for hop in range(1, PLANES):
        w_copy(hop).wait_send()
        w_core_copy(hop).wait()


def spread(q_parts, kv_parts, out_weight):
    depth, columns = out_weight.shape
    return pl.pallas_call(
        spread_kernel,
        out_shape=(
            jax.ShapeDtypeStruct((WORKERS, 2 * TILES + SLOTS, SIDE, SPOTS, DH), BF16),
            jax.ShapeDtypeStruct((depth * PLANES, columns // PLANES), BF16),
        ),
        in_specs=[pl.BlockSpec(memory_space=pl.ANY)] * 3,
        out_specs=(pl.BlockSpec(memory_space=pl.ANY),) * 2,
        scratch_shapes=[
            pltpu.SemaphoreType.DMA((FRAMES,)),
            pltpu.SemaphoreType.DMA,
            pltpu.SemaphoreType.DMA((PARTS, SIDE)),
            pltpu.SemaphoreType.DMA((PARTS, SIDE)),
            pltpu.SemaphoreType.DMA((PARTS + 1, 2)),
            pltpu.SemaphoreType.DMA((PARTS + 1, 2)),
            pltpu.SemaphoreType.DMA((PARTS + 1, 2)),
            pltpu.SemaphoreType.DMA((PARTS + 1, 2)),
            pltpu.SemaphoreType.DMA((PARTS + 1, SIDE)),
            pltpu.SemaphoreType.DMA,
            pltpu.SemaphoreType.DMA((PLANES,)),
            pltpu.SemaphoreType.DMA((PLANES,)),
            pltpu.SemaphoreType.DMA((PLANES,)),
            pltpu.SemaphoreType.DMA((PLANES,)),
            pltpu.SemaphoreType.DMA,
        ],
        compiler_params=pltpu.CompilerParams(
            collective_id=0, has_side_effects=True, vmem_limit_bytes=57 * 1024 * 1024
        ),
    )(q_parts, kv_parts, out_weight)


def turned_rows(rows):
    to = lax.broadcasted_iota(jnp.int32, (rows, rows), 0)
    source = lax.broadcasted_iota(jnp.int32, (rows, rows), 1)
    group = WORKERS * SPOTS
    place = lax.div(lax.rem(to, group), SPOTS)
    wanted = to + (WORKERS - 1 - 2 * place) * SPOTS
    return jnp.where(source == wanted, 1.0, 0.0).astype(BF16)


def attend_kernel(
    list_ref, kv_hbm, o_ref, kv_ref, q_ref, keys_ref, base_ref, peak_ref, sum_ref,
    slot_of, first_of, listed_of, kv_sem,
):
    def bring(number, first, tiles):
        rows = pl.ds(first * PIECE, tiles * PIECE)
        return pltpu.make_async_copy(kv_hbm.at[:, rows], kv_ref.at[:, rows], kv_sem.at[number])

    chunks = TILES // CHUNK
    moves = [bring(number, number * CHUNK, CHUNK) for number in range(chunks)]
    moves.append(bring(chunks, 2 * TILES, SLOTS))
    moves.append(bring(chunks + 1, TILES, TILES))
    for move in moves:
        move.start()

    _, column, core = where_is(lax.axis_index("ctx"))

    def loop(count, work):
        def one(step, carry):
            work(step)
            return carry

        lax.fori_loop(0, count, one, 0)

    def rows_of(slot):
        return pl.ds(pl.multiple_of(slot * TILE, TILE), TILE)

    def tile_at(tile):
        start = pl.multiple_of(tile * PIECE, PIECE)
        return jnp.concatenate(
            [kv_ref[worker, pl.ds(start, PIECE), :] for worker in range(WORKERS)], axis=0
        )

    def enlist(slot, total):
        count = list_ref[SLOTS, slot]
        steps = lax.div(count + GROUP - 1, GROUP)

        def one(step, carry):
            slot_of[total + step] = slot
            first_of[total + step] = step * GROUP
            listed_of[total + step] = count - step * GROUP
            return carry

        lax.fori_loop(0, steps, one, 0)
        return total + steps

    total = lax.fori_loop(0, SLOTS, enlist, 0)
    for spare in range(BESIDE - 1):
        slot_of[total + spare] = 0
        first_of[total + spare] = 0
        listed_of[total + spare] = 0
    turns = lax.div(total + BESIDE - 1, BESIDE)
    busy = jnp.where(total > 0, 1, 0)

    def unpack(step):
        for u in range(GROUP):
            tile = step * GROUP + u
            keys_ref[tile] = tile_at(tile).T

    for number in range(chunks):
        moves[number].wait()
        steps = CHUNK // GROUP
        loop(busy * steps, lambda step: unpack(step + number * steps))
    moves[chunks].wait()

    def set_base(slot, base):
        base_ref[slot] = jnp.broadcast_to(base * SCALE2, (TILE, TILE))

    def own_base(step):
        for u in range(BESIDE):
            slot = step * BESIDE + u
            place = column * 2 + core
            late = jnp.where(slot < SLOTS // 2, 0, WORKERS - 1 - 2 * place)
            own = keys_ref[slot * WORKERS + place + late]
            query = tile_at(2 * TILES + slot)
            q_ref[rows_of(slot), :] = query
            scores = jnp.dot(query, own, preferred_element_type=F32)
            set_base(slot, jnp.max(scores, axis=1, keepdims=True))

    loop(busy * (SLOTS // BESIDE), own_base)
    moves[chunks + 1].wait()

    def tiles_of(number):
        slot, first = slot_of[number], first_of[number]
        return slot, [list_ref[slot, first + u] for u in range(GROUP)]

    def scores_of(slot, tiles):
        keys = jnp.concatenate([keys_ref[tile] for tile in tiles], axis=1)
        return jnp.dot(q_ref[rows_of(slot), :], keys, preferred_element_type=F32)

    def attend_steps(step):
        found = []
        for beside in range(BESIDE):
            number = step * BESIDE + beside
            slot, tiles = tiles_of(number)
            listed = listed_of[number]
            base = base_ref[slot]
            scores = scores_of(slot, tiles)
            weights, values = [], []
            for u in range(GROUP):
                part = scores[:, u * TILE : (u + 1) * TILE]
                weights.append(jnp.exp2(part * SCALE2 - base).astype(BF16))
                value = jnp.where(u < listed, tile_at(TILES + tiles[u]), 0).astype(BF16)
                ones = jnp.where(u < listed, 1.0, 0.0).astype(BF16)
                ones = jnp.broadcast_to(ones, (TILE, DH))
                values.append(jnp.concatenate([value, ones], axis=1))
            added = jnp.dot(
                jnp.concatenate(weights, axis=1),
                jnp.concatenate(values, axis=0),
                preferred_element_type=F32,
            )
            found.append((slot, added))
        for slot, added in found:
            sum_ref[slot] += added

    def peak_steps(step):
        for beside in range(BESIDE):
            slot, tiles = tiles_of(step * BESIDE + beside)
            scores = scores_of(slot, tiles)
            peak = peak_ref[slot]
            for u in range(GROUP):
                peak = jnp.maximum(peak, scores[:, u * TILE : (u + 1) * TILE])
            peak_ref[slot] = peak

    def attempt(number, needed):
        def clear(slot):
            sum_ref[slot] = jnp.zeros((TILE, 2 * DH), F32)
            peak_ref[slot] = jnp.full((TILE, TILE), LOW, F32)

        loop(needed * SLOTS, clear)
        loop(needed * turns, attend_steps)
        beyond = jnp.zeros((TILE, DH), F32)
        for slot in range(SLOTS):
            beyond = jnp.where(sum_ref[slot, :, DH:] <= FAR, beyond, 1.0)
        again = needed * jnp.where(jnp.max(beyond) > 0.0, 1, 0)
        loop(again * turns, peak_steps)

        def rebase(slot):
            set_base(slot, jnp.max(peak_ref[slot], axis=1, keepdims=True))

        loop(again * SLOTS, rebase)
        return again

    lax.fori_loop(0, 2, attempt, busy)

    def finish(step):
        for u in range(BESIDE):
            slot = step * BESIDE + u
            o_ref[rows_of(slot), :] = (sum_ref[slot, :, :DH] / sum_ref[slot, :, DH:]).astype(BF16)

    loop(busy * (SLOTS // BESIDE), finish)


def attend(lists, kv):
    most = SLOTS * (TILES // GROUP) + BESIDE
    return pl.pallas_call(
        attend_kernel,
        out_shape=jax.ShapeDtypeStruct((SLOTS * TILE, DH), BF16),
        in_specs=[pl.BlockSpec(memory_space=pltpu.SMEM), pl.BlockSpec(memory_space=pl.ANY)],
        out_specs=pl.BlockSpec(memory_space=pltpu.VMEM),
        scratch_shapes=[
            pltpu.VMEM(kv.shape, BF16),
            pltpu.VMEM((SLOTS * TILE, DH), BF16),
            pltpu.VMEM((TILES, DH, TILE), BF16),
            pltpu.VMEM((SLOTS, TILE, TILE), F32),
            pltpu.VMEM((SLOTS, TILE, TILE), F32),
            pltpu.VMEM((SLOTS, TILE, 2 * DH), F32),
            pltpu.SMEM((most,), jnp.int32),
            pltpu.SMEM((most,), jnp.int32),
            pltpu.SMEM((most,), jnp.int32),
            pltpu.SemaphoreType.DMA((TILES // CHUNK + 2,)),
        ],
        compiler_params=pltpu.CompilerParams(vmem_limit_bytes=50 * 1024 * 1024),
    )(lists, kv)


def collect_kernel(o_ref, attn, send, recv, x_send, x_recv):
    plane = lax.axis_index("heads")
    me = lax.axis_index("ctx")
    row, column, core = where_is(me)
    barrier = pltpu.get_barrier_semaphore()

    def greet(step, carry):
        pl.semaphore_signal(
            barrier, inc=1, device_id=(plane, lax.rem(me + step, FRAMES)), device_id_type=MESH
        )
        return carry

    lax.fori_loop(1, FRAMES, greet, 0)
    sides = (lax.rem(plane + 1, PLANES), lax.rem(plane + PLANES - 1, PLANES))
    for there in sides:
        pl.semaphore_signal(barrier, inc=1, device_id=(there, me), device_id_type=MESH)
    pl.semaphore_wait(barrier, FRAMES - 1 + 2)

    mine = jnp.minimum(row, HEADS_HERE - 1)
    goal = attn.at[plane * HEADS_HERE + mine, :, column * 2 + core]

    def rows_for(there):
        row_there, column_there, core_there = where_is(there)
        above = lax.rem(row - row_there + SIDE, SIDE)
        return o_ref.at[:, column_there * 2 + core_there, above]

    def back(step):
        there = lax.rem(me + step, FRAMES)
        return pltpu.make_async_remote_copy(
            src_ref=rows_for(there),
            dst_ref=goal,
            send_sem=send.at[step],
            recv_sem=recv.at[mine],
            device_id=(plane, there),
            device_id_type=MESH,
        )

    def start(step, carry):
        back(step).start()
        return carry

    def end(step, carry):
        back(step).wait_send()
        return carry

    working = row < HEADS_HERE

    @pl.when(working)
    def _():
        lax.fori_loop(1, FRAMES, start, 0)
        pltpu.make_async_copy(rows_for(me), goal, recv.at[mine]).start()

    cut = SLOTS // 2

    def near(head, side):
        part = attn.at[plane * HEADS_HERE + head]
        return pltpu.make_async_remote_copy(
            src_ref=part,
            dst_ref=part,
            send_sem=x_send.at[head, side],
            recv_sem=x_recv.at[head, side],
            device_id=(sides[side], me),
            device_id_type=MESH,
        )

    def far(head, side):
        part = attn.at[sides[1 - side] * HEADS_HERE + head]
        part = part.at[pl.ds(0, cut)] if side == 0 else part.at[pl.ds(cut, SLOTS - cut)]
        return pltpu.make_async_remote_copy(
            src_ref=part,
            dst_ref=part,
            send_sem=x_send.at[head, 2 + side],
            recv_sem=x_recv.at[head, 2 + side],
            device_id=(sides[side], me),
            device_id_type=MESH,
        )

    for head in range(HEADS_HERE):
        part = attn.at[plane * HEADS_HERE + head]
        pltpu.make_async_copy(part, part, recv.at[head]).wait()
        for side in range(2):
            near(head, side).start()
    for head in range(HEADS_HERE):
        for side in range(2):
            near(head, side).wait_recv()
            far(head, side).start()

    @pl.when(working)
    def _():
        lax.fori_loop(1, FRAMES, end, 0)

    for head in range(HEADS_HERE):
        for side in range(2):
            near(head, side).wait_send()
            far(head, side).wait()


def collect(attended):
    return pl.pallas_call(
        collect_kernel,
        out_shape=jax.ShapeDtypeStruct(
            (PLANES * HEADS_HERE, SLOTS, WORKERS, SPOTS, DH), BF16
        ),
        in_specs=[pl.BlockSpec(memory_space=pl.ANY)],
        out_specs=pl.BlockSpec(memory_space=pl.ANY),
        scratch_shapes=[
            pltpu.SemaphoreType.DMA((FRAMES,)),
            pltpu.SemaphoreType.DMA((HEADS_HERE,)),
            pltpu.SemaphoreType.DMA((HEADS_HERE, 4)),
            pltpu.SemaphoreType.DMA((HEADS_HERE, 4)),
        ],
        compiler_params=pltpu.CompilerParams(
            collective_id=1, has_side_effects=True, vmem_limit_bytes=4 * 1024 * 1024
        ),
    )(attended)


def project_kernel(attn_ref, w_ref, out_ref):
    heads = attn_ref.shape[0]
    half = out_ref.shape[0] // 2
    wide = jnp.concatenate([attn_ref[h] for h in range(heads)], axis=1)
    block = 256
    for first in range(0, out_ref.shape[1], block):
        columns = slice(first, first + block)
        mixed = jnp.dot(wide, w_ref[:, columns], preferred_element_type=F32).astype(BF16)
        out_ref[:half, columns] = mixed[:half]
        out_ref[half:, columns] = jnp.dot(
            turned_rows(half), mixed[half:], preferred_element_type=F32
        ).astype(BF16)


def project(attn, weight, rows):
    return pl.pallas_call(
        project_kernel,
        out_shape=jax.ShapeDtypeStruct((rows, weight.shape[1]), BF16),
        in_specs=[pl.BlockSpec(memory_space=pltpu.VMEM)] * 2,
        out_specs=pl.BlockSpec(memory_space=pltpu.VMEM),
        compiler_params=pltpu.CompilerParams(vmem_limit_bytes=24 * 1024 * 1024),
    )(attn, weight)


def arrange_kernel(
    pattern_ref, mask_hbm, q_hbm, k_hbm, v_hbm, q_out, kv_out, list_ref,
    mask_ref, q_ref, k_ref, v_ref, sems,
):
    sources = (mask_hbm, q_hbm, k_hbm, v_hbm)
    targets = (mask_ref, q_ref, k_ref, v_ref)
    moves = [
        pltpu.make_async_copy(source, target, sems.at[i])
        for i, (source, target) in enumerate(zip(sources, targets))
    ]
    for move in moves:
        move.start()
    me = lax.axis_index("ctx")
    row, column, core = where_is(me)
    moves[0].wait()
    pattern = pattern_ref[jnp.minimum(row, HEADS_HERE - 1)]
    masks = []
    place = column * 2 + core
    tiles = [
        slot * WORKERS + (place if slot < SLOTS // 2 else WORKERS - 1 - place)
        for slot in range(SLOTS)
    ]
    for tile in tiles:
        masks.append(jnp.where(row < HEADS_HERE, mask_ref[pattern, pl.ds(tile, 1), :], 0))
    seen = jnp.concatenate(masks, axis=0) == 1
    seen = jnp.where(seen, 1.0, 0.0).astype(F32)
    down = lax.broadcasted_iota(jnp.int32, (TILES, TILES), 0)
    along = lax.broadcasted_iota(jnp.int32, (TILES, TILES), 1)
    both = (((1,), (1,)), ((), ()))
    upto = jnp.where(along <= down, 1.0, 0.0).astype(BF16)
    same = jnp.where(along == down, 1.0, 0.0).astype(BF16)
    rank = lax.dot_general(upto, seen.astype(BF16), both, preferred_element_type=F32)
    turned = lax.dot_general(same, seen.astype(BF16), both, preferred_element_type=F32)
    rank = rank.astype(jnp.int32)
    spot = jnp.where(turned > 0.5, rank - 1, -1)
    for slot in range(SLOTS):
        hit = spot[:, slot : slot + 1] == along
        listed = jnp.sum(jnp.where(hit, down, 0), axis=0, keepdims=True)
        spare = along[:1, :] >= rank[TILES - 1 :, slot : slot + 1]
        list_ref[slot : slot + 1, :] = jnp.where(spare, tiles[slot], listed)
    last = jnp.concatenate(
        [rank[TILES - 1 :, :], jnp.zeros((1, TILES - SLOTS), jnp.int32)], axis=1
    )
    list_ref[SLOTS : SLOTS + 1, :] = last


    rows = q_ref.shape[0]
    for move, source, target, first in (
        (moves[1], q_ref, q_out, 0),
        (moves[2], k_ref, kv_out, 0),
        (moves[3], v_ref, kv_out, rows),
    ):
        move.wait()
        for head in range(HEADS_HERE):
            target[head, first : first + rows, :] = source[:, head * DH : (head + 1) * DH]
    half = rows // 2
    later = jnp.dot(turned_rows(half), q_ref[half:, :], preferred_element_type=F32).astype(BF16)
    for head in range(HEADS_HERE):
        q_out[head, half:, :] = later[:, head * DH : (head + 1) * DH]


def arrange(head_pattern, tile_masks, queries, key_rows, value_rows):
    rows = queries.shape[0]
    return pl.pallas_call(
        arrange_kernel,
        out_shape=(
            jax.ShapeDtypeStruct((HEADS_HERE, rows, DH), BF16),
            jax.ShapeDtypeStruct((HEADS_HERE, 2 * rows, DH), BF16),
            jax.ShapeDtypeStruct((SLOTS + 1, TILES), jnp.int32),
        ),
        in_specs=[pl.BlockSpec(memory_space=pltpu.SMEM)]
        + [pl.BlockSpec(memory_space=pl.ANY)] * 4,
        out_specs=(pl.BlockSpec(memory_space=pltpu.VMEM),) * 3,
        scratch_shapes=[
            pltpu.VMEM(tile_masks.shape, jnp.int32),
            pltpu.VMEM(queries.shape, BF16),
            pltpu.VMEM(queries.shape, BF16),
            pltpu.VMEM(queries.shape, BF16),
            pltpu.SemaphoreType.DMA((4,)),
        ],
        compiler_params=pltpu.CompilerParams(vmem_limit_bytes=57 * 1024 * 1024),
    )(head_pattern, tile_masks, queries, key_rows, value_rows)


def body(queries, key_rows, value_rows, out_weight, tile_masks, head_pattern):
    rows = queries.shape[0]
    q_parts, kv_parts, lists = arrange(head_pattern, tile_masks, queries, key_rows, value_rows)
    kv_all, w_all = spread(
        q_parts.reshape(HEADS_HERE, SLOTS, WORKERS, SPOTS, DH),
        kv_parts.reshape(HEADS_HERE, 2 * TILES, SPOTS, DH),
        out_weight,
    )
    attended = attend(lists, kv_all.reshape(WORKERS, (2 * TILES + SLOTS) * PIECE, DH))
    attn = collect(attended.reshape(SLOTS, WORKERS, SIDE, SPOTS, DH))
    attn = attn.reshape(PLANES * HEADS_HERE, rows, DH)
    return project(attn, w_all, rows)


def solution(mesh):
    placed = (
        P("ctx", "heads"),
        P("ctx", "heads"),
        P("ctx", "heads"),
        P("heads", None),
        P(),
        P("heads"),
    )
    return jax.shard_map(
        body, mesh=mesh, in_specs=placed, out_specs=P("ctx", "heads"), check_vma=False
    )
```

```python
import math

import jax
import jax.numpy as jnp
from jax import lax
from jax.experimental import pallas as pl
from jax.experimental.pallas import tpu as pltpu
from jax.sharding import PartitionSpec as P

MESH = pl.DeviceIdType.MESH
DH = 128
TILE = 128
SPOTS = 4
FRAMES = 32
TILES = 128
PLANES = 4
SIDE = 4
HEADS_HERE = 3
WORKERS = 2 * SIDE
SLOTS = TILES // WORKERS
SIZES = (80, 80, 64, 32)
PARTS = len(SIZES)
PIECE = TILE // WORKERS
GROUP = 8
CHUNK = 32
BESIDE = 4
FAR = 2.0**64
LOW = -1e30
SCALE2 = math.log2(math.e) / math.sqrt(DH)
BF16 = jnp.bfloat16
F32 = jnp.float32


def where_is(device):
    return lax.div(device, WORKERS), lax.rem(lax.div(device, 2), SIDE), lax.rem(device, 2)


def device_at(row, column, core):
    return (lax.rem(row, SIDE) * SIDE + lax.rem(column, SIDE)) * 2 + core


def spread_kernel(
    q_ref, kv_ref, w_ref, kv_all, w_all,
    q_send, q_recv, z_send, z_recv, y_send, y_recv, far_send, far_recv,
    core_send, core_recv, w_send, w_recv, w_core_send, w_core_recv, own_sem,
):
    plane = lax.axis_index("heads")
    me = lax.axis_index("ctx")
    row, column, core = where_is(me)
    working = row < HEADS_HERE
    own_row = jnp.minimum(row, HEADS_HERE - 1)
    depth = w_ref.shape[0]
    width = w_all.shape[1]
    sides = (1, SIDE - 1)

    barrier = pltpu.get_barrier_semaphore()

    def greet(step, carry):
        pl.semaphore_signal(
            barrier, inc=1, device_id=(plane, lax.rem(me + step, FRAMES)), device_id_type=MESH
        )
        return carry

    lax.fori_loop(1, FRAMES, greet, 0)
    for hop in range(1, PLANES):
        pl.semaphore_signal(
            barrier, inc=1, device_id=(lax.rem(plane + hop, PLANES), me), device_id_type=MESH
        )
    pl.semaphore_wait(barrier, FRAMES - 1 + PLANES - 1)

    def span(part):
        return pl.ds(sum(SIZES[:part]), SIZES[part])

    own_copy = pltpu.make_async_copy(
        kv_ref.at[own_row], kv_all.at[column * 2 + core, pl.ds(0, 2 * TILES), 0], own_sem
    )

    def z_copy(part, hop):
        there = lax.rem(row + hop, SIDE)
        return pltpu.make_async_remote_copy(
            src_ref=kv_ref.at[there, span(part)],
            dst_ref=kv_all.at[column * 2 + core, span(part), hop],
            send_sem=z_send.at[part, hop],
            recv_sem=z_recv.at[part, hop],
            device_id=(plane, device_at(there, column, core)),
            device_id_type=MESH,
        )

    def piece(number, away):
        source = kv_all.at[lax.rem(column + away, SIDE) * 2 + core]
        if number == 0:
            return source.at[pl.ds(0, 2 * TILES), 0]
        return source.at[span(number - 1), pl.ds(1, SIDE - 1)]

    def y_copy(number, side):
        return pltpu.make_async_remote_copy(
            src_ref=kv_ref.at[own_row] if number == 0 else piece(number, 0),
            dst_ref=piece(number, 0),
            send_sem=y_send.at[number, side],
            recv_sem=y_recv.at[number, side],
            device_id=(plane, device_at(row, column + sides[side], core)),
            device_id_type=MESH,
        )

    def far_copy(number, side):
        source = kv_all.at[lax.rem(column + sides[1 - side], SIDE) * 2 + core]
        first, count = (0, 2 * TILES) if number == 0 else (sum(SIZES[: number - 1]), SIZES[number - 1])
        share = count * 3 // 8
        tiles = pl.ds(first + share, count - share) if side else pl.ds(first, share)
        chunk = source.at[tiles, 0] if number == 0 else source.at[tiles, pl.ds(1, SIDE - 1)]
        return pltpu.make_async_remote_copy(
            src_ref=chunk,
            dst_ref=chunk,
            send_sem=far_send.at[number, side],
            recv_sem=far_recv.at[number, side],
            device_id=(plane, device_at(row, column + sides[side], core)),
            device_id_type=MESH,
        )

    def core_copy(number, away):
        return pltpu.make_async_remote_copy(
            src_ref=piece(number, away),
            dst_ref=piece(number, away),
            send_sem=core_send.at[number, away],
            recv_sem=core_recv,
            device_id=(plane, device_at(row, column, 1 - core)),
            device_id_type=MESH,
        )

    half = depth // 2

    def w_rows(source, part):
        return w_all.at[pl.ds(pl.multiple_of(source * depth + part * half, 16), half)]

    def w_copy(hop):
        there = lax.rem(plane + hop, PLANES)
        return pltpu.make_async_remote_copy(
            src_ref=w_ref.at[
                pl.ds(pl.multiple_of(core * half, 16), half),
                pl.ds(pl.multiple_of(there * width, 128), width),
            ],
            dst_ref=w_rows(plane, core),
            send_sem=w_send.at[hop],
            recv_sem=w_recv.at[hop],
            device_id=(there, me),
            device_id_type=MESH,
        )

    def w_core_copy(hop):
        rows = w_rows(lax.rem(plane + PLANES - hop, PLANES), core)
        return pltpu.make_async_remote_copy(
            src_ref=rows,
            dst_ref=rows,
            send_sem=w_core_send.at[hop],
            recv_sem=w_core_recv.at[hop],
            device_id=(plane, device_at(row, column, 1 - core)),
            device_id_type=MESH,
        )

    own_w = pltpu.make_async_copy(
        w_ref.at[:, pl.ds(pl.multiple_of(plane * width, 128), width)],
        w_all.at[pl.ds(pl.multiple_of(plane * depth, 128), depth)],
        w_recv.at[0],
    )

    queries = kv_all.at[:, pl.ds(2 * TILES, SLOTS)]

    def q_copy(step):
        there = lax.rem(me + step, FRAMES)
        row_there, column_there, core_there = where_is(there)
        return row_there < HEADS_HERE, pltpu.make_async_remote_copy(
            src_ref=q_ref.at[
                jnp.minimum(row_there, HEADS_HERE - 1), :, column_there * 2 + core_there
            ],
            dst_ref=queries.at[column * 2 + core, :, lax.rem(row_there - row + SIDE, SIDE)],
            send_sem=q_send.at[step],
            recv_sem=q_recv,
            device_id=(plane, there),
            device_id_type=MESH,
        )

    def to_rows(part, work):
        for hop in range(1, SIDE):

            @pl.when(lax.rem(row + hop, SIDE) < HEADS_HERE)
            def _():
                work(z_copy(part, hop))

    def send_q(step, carry):
        wanted, copy = q_copy(step)

        @pl.when(wanted)
        def _():
            copy.start()

        return carry

    def sent_q(step, carry):
        wanted, copy = q_copy(step)

        @pl.when(wanted)
        def _():
            copy.wait_send()

        return carry

    def send_small():
        for hop in range(1, PLANES):
            w_copy(hop).start()
        own_w.start()
        lax.fori_loop(1, FRAMES, send_q, 0)

    @pl.when(working)
    def _():
        own_copy.start()
        for side in range(2):
            y_copy(0, side).start()

    to_rows(0, lambda copy: copy.start())
    send_small()

    def next_rows(part):
        to_rows(part, lambda copy: copy.wait_send())
        if part + 1 < PARTS:
            to_rows(part + 1, lambda copy: copy.start())

    @pl.when(jnp.logical_not(working))
    def _():
        for part in range(PARTS):
            next_rows(part)

    @pl.when(working)
    def _():
        pltpu.make_async_copy(
            q_ref.at[own_row, :, column * 2 + core], queries.at[column * 2 + core, :, 0], q_recv
        ).start()
        own_copy.wait()
        core_copy(0, 0).start()

        def pass_on(number):
            for side in range(2):
                y_copy(number, side).wait_recv()
                far_copy(number, side).start()
            for side in range(2):
                core_copy(number, sides[1 - side]).start()

        for part in range(PARTS):
            next_rows(part)
            for hop in range(1, SIDE):
                landed = kv_all.at[column * 2 + core, span(part), hop]
                pltpu.make_async_copy(landed, landed, z_recv.at[part, hop]).wait()
            for side in range(2):
                y_copy(part + 1, side).start()
            core_copy(part + 1, 0).start()
            pass_on(part)
        pass_on(PARTS)
        for number in range(PARTS + 1):
            for side in range(2):
                far_copy(number, side).wait_recv()
            core_copy(number, 2).start()

    for hop in range(1, PLANES):
        w_copy(hop).wait_recv()
        w_core_copy(hop).start()

    @pl.when(working)
    def _():
        pltpu.make_async_copy(queries, queries, q_recv).wait()
        other = kv_all.at[pl.ds(0, SIDE), pl.ds(0, 2 * TILES)]
        pltpu.make_async_copy(other, other, core_recv).wait()
        for number in range(PARTS + 1):
            for side in range(2):
                y_copy(number, side).wait_send()
                far_copy(number, side).wait_send()
            for away in range(SIDE):
                core_copy(number, away).wait_send()

    own_w.wait()
    lax.fori_loop(1, FRAMES, sent_q, 0)
    for hop in range(1, PLANES):
        w_copy(hop).wait_send()
        w_core_copy(hop).wait()


def spread(q_parts, kv_parts, out_weight):
    depth, columns = out_weight.shape
    return pl.pallas_call(
        spread_kernel,
        out_shape=(
            jax.ShapeDtypeStruct((WORKERS, 2 * TILES + SLOTS, SIDE, SPOTS, DH), BF16),
            jax.ShapeDtypeStruct((depth * PLANES, columns // PLANES), BF16),
        ),
        in_specs=[pl.BlockSpec(memory_space=pl.ANY)] * 3,
        out_specs=(pl.BlockSpec(memory_space=pl.ANY),) * 2,
        scratch_shapes=[
            pltpu.SemaphoreType.DMA((FRAMES,)),
            pltpu.SemaphoreType.DMA,
            pltpu.SemaphoreType.DMA((PARTS, SIDE)),
            pltpu.SemaphoreType.DMA((PARTS, SIDE)),
            pltpu.SemaphoreType.DMA((PARTS + 1, 2)),
            pltpu.SemaphoreType.DMA((PARTS + 1, 2)),
            pltpu.SemaphoreType.DMA((PARTS + 1, 2)),
            pltpu.SemaphoreType.DMA((PARTS + 1, 2)),
            pltpu.SemaphoreType.DMA((PARTS + 1, SIDE)),
            pltpu.SemaphoreType.DMA,
            pltpu.SemaphoreType.DMA((PLANES,)),
            pltpu.SemaphoreType.DMA((PLANES,)),
            pltpu.SemaphoreType.DMA((PLANES,)),
            pltpu.SemaphoreType.DMA((PLANES,)),
            pltpu.SemaphoreType.DMA,
        ],
        compiler_params=pltpu.CompilerParams(
            collective_id=0, has_side_effects=True, vmem_limit_bytes=57 * 1024 * 1024
        ),
    )(q_parts, kv_parts, out_weight)


def turned_rows(rows):
    to = lax.broadcasted_iota(jnp.int32, (rows, rows), 0)
    source = lax.broadcasted_iota(jnp.int32, (rows, rows), 1)
    group = WORKERS * SPOTS
    place = lax.div(lax.rem(to, group), SPOTS)
    wanted = to + (WORKERS - 1 - 2 * place) * SPOTS
    return jnp.where(source == wanted, 1.0, 0.0).astype(BF16)


def attend_kernel(
    list_ref, kv_hbm, o_ref, kv_ref, q_ref, keys_ref, base_ref, peak_ref, sum_ref,
    slot_of, first_of, listed_of, kv_sem,
):
    def bring(number, first, tiles):
        rows = pl.ds(first * PIECE, tiles * PIECE)
        return pltpu.make_async_copy(kv_hbm.at[:, rows], kv_ref.at[:, rows], kv_sem.at[number])

    chunks = TILES // CHUNK
    moves = [bring(number, number * CHUNK, CHUNK) for number in range(chunks)]
    moves.append(bring(chunks, 2 * TILES, SLOTS))
    moves.append(bring(chunks + 1, TILES, TILES))
    for move in moves:
        move.start()

    _, column, core = where_is(lax.axis_index("ctx"))

    def loop(count, work):
        def one(step, carry):
            work(step)
            return carry

        lax.fori_loop(0, count, one, 0)

    def rows_of(slot):
        return pl.ds(pl.multiple_of(slot * TILE, TILE), TILE)

    def tile_at(tile):
        start = pl.multiple_of(tile * PIECE, PIECE)
        return jnp.concatenate(
            [kv_ref[worker, pl.ds(start, PIECE), :] for worker in range(WORKERS)], axis=0
        )

    def enlist(slot, total):
        count = list_ref[SLOTS, slot]
        steps = lax.div(count + GROUP - 1, GROUP)

        def one(step, carry):
            slot_of[total + step] = slot
            first_of[total + step] = step * GROUP
            listed_of[total + step] = count - step * GROUP
            return carry

        lax.fori_loop(0, steps, one, 0)
        return total + steps

    total = lax.fori_loop(0, SLOTS, enlist, 0)
    for spare in range(BESIDE - 1):
        slot_of[total + spare] = 0
        first_of[total + spare] = 0
        listed_of[total + spare] = 0
    turns = lax.div(total + BESIDE - 1, BESIDE)
    busy = jnp.where(total > 0, 1, 0)

    def unpack(step):
        for u in range(GROUP):
            tile = step * GROUP + u
            keys_ref[tile] = tile_at(tile).T

    for number in range(chunks):
        moves[number].wait()
        steps = CHUNK // GROUP
        loop(busy * steps, lambda step: unpack(step + number * steps))
    moves[chunks].wait()

    def set_base(slot, base):
        base_ref[slot] = jnp.broadcast_to(base * SCALE2, (TILE, TILE))

    def own_base(step):
        for u in range(BESIDE):
            slot = step * BESIDE + u
            place = column * 2 + core
            late = jnp.where(slot < SLOTS // 2, 0, WORKERS - 1 - 2 * place)
            own = keys_ref[slot * WORKERS + place + late]
            query = tile_at(2 * TILES + slot)
            q_ref[rows_of(slot), :] = query
            scores = jnp.dot(query, own, preferred_element_type=F32)
            set_base(slot, jnp.max(scores, axis=1, keepdims=True))

    loop(busy * (SLOTS // BESIDE), own_base)
    moves[chunks + 1].wait()

    def tiles_of(number):
        slot, first = slot_of[number], first_of[number]
        return slot, [list_ref[slot, first + u] for u in range(GROUP)]

    def scores_of(slot, tiles):
        keys = jnp.concatenate([keys_ref[tile] for tile in tiles], axis=1)
        return jnp.dot(q_ref[rows_of(slot), :], keys, preferred_element_type=F32)

    def attend_steps(step):
        found = []
        for beside in range(BESIDE):
            number = step * BESIDE + beside
            slot, tiles = tiles_of(number)
            listed = listed_of[number]
            base = base_ref[slot]
            scores = scores_of(slot, tiles)
            weights, values = [], []
            for u in range(GROUP):
                part = scores[:, u * TILE : (u + 1) * TILE]
                weights.append(jnp.exp2(part * SCALE2 - base).astype(BF16))
                value = jnp.where(u < listed, tile_at(TILES + tiles[u]), 0).astype(BF16)
                ones = jnp.where(u < listed, 1.0, 0.0).astype(BF16)
                ones = jnp.broadcast_to(ones, (TILE, DH))
                values.append(jnp.concatenate([value, ones], axis=1))
            added = jnp.dot(
                jnp.concatenate(weights, axis=1),
                jnp.concatenate(values, axis=0),
                preferred_element_type=F32,
            )
            found.append((slot, added))
        for slot, added in found:
            sum_ref[slot] += added

    def peak_steps(step):
        for beside in range(BESIDE):
            slot, tiles = tiles_of(step * BESIDE + beside)
            scores = scores_of(slot, tiles)
            peak = peak_ref[slot]
            for u in range(GROUP):
                peak = jnp.maximum(peak, scores[:, u * TILE : (u + 1) * TILE])
            peak_ref[slot] = peak

    def attempt(number, needed):
        def clear(slot):
            sum_ref[slot] = jnp.zeros((TILE, 2 * DH), F32)
            peak_ref[slot] = jnp.full((TILE, TILE), LOW, F32)

        loop(needed * SLOTS, clear)
        loop(needed * turns, attend_steps)
        beyond = jnp.zeros((TILE, DH), F32)
        for slot in range(SLOTS):
            beyond = jnp.where(sum_ref[slot, :, DH:] <= FAR, beyond, 1.0)
        again = needed * jnp.where(jnp.max(beyond) > 0.0, 1, 0)
        loop(again * turns, peak_steps)

        def rebase(slot):
            set_base(slot, jnp.max(peak_ref[slot], axis=1, keepdims=True))

        loop(again * SLOTS, rebase)
        return again

    lax.fori_loop(0, 2, attempt, busy)

    def finish(step):
        for u in range(BESIDE):
            slot = step * BESIDE + u
            o_ref[rows_of(slot), :] = (sum_ref[slot, :, :DH] / sum_ref[slot, :, DH:]).astype(BF16)

    loop(busy * (SLOTS // BESIDE), finish)


def attend(lists, kv):
    most = SLOTS * (TILES // GROUP) + BESIDE
    return pl.pallas_call(
        attend_kernel,
        out_shape=jax.ShapeDtypeStruct((SLOTS * TILE, DH), BF16),
        in_specs=[pl.BlockSpec(memory_space=pltpu.SMEM), pl.BlockSpec(memory_space=pl.ANY)],
        out_specs=pl.BlockSpec(memory_space=pltpu.VMEM),
        scratch_shapes=[
            pltpu.VMEM(kv.shape, BF16),
            pltpu.VMEM((SLOTS * TILE, DH), BF16),
            pltpu.VMEM((TILES, DH, TILE), BF16),
            pltpu.VMEM((SLOTS, TILE, TILE), F32),
            pltpu.VMEM((SLOTS, TILE, TILE), F32),
            pltpu.VMEM((SLOTS, TILE, 2 * DH), F32),
            pltpu.SMEM((most,), jnp.int32),
            pltpu.SMEM((most,), jnp.int32),
            pltpu.SMEM((most,), jnp.int32),
            pltpu.SemaphoreType.DMA((TILES // CHUNK + 2,)),
        ],
        compiler_params=pltpu.CompilerParams(vmem_limit_bytes=50 * 1024 * 1024),
    )(lists, kv)


def collect_kernel(o_ref, attn, send, recv, x_send, x_recv):
    plane = lax.axis_index("heads")
    me = lax.axis_index("ctx")
    row, column, core = where_is(me)
    barrier = pltpu.get_barrier_semaphore()

    def greet(step, carry):
        pl.semaphore_signal(
            barrier, inc=1, device_id=(plane, lax.rem(me + step, FRAMES)), device_id_type=MESH
        )
        return carry

    lax.fori_loop(1, FRAMES, greet, 0)
    sides = (lax.rem(plane + 1, PLANES), lax.rem(plane + PLANES - 1, PLANES))
    for there in sides:
        pl.semaphore_signal(barrier, inc=1, device_id=(there, me), device_id_type=MESH)
    pl.semaphore_wait(barrier, FRAMES - 1 + 2)

    mine = jnp.minimum(row, HEADS_HERE - 1)
    goal = attn.at[plane * HEADS_HERE + mine, :, column * 2 + core]

    def rows_for(there):
        row_there, column_there, core_there = where_is(there)
        above = lax.rem(row - row_there + SIDE, SIDE)
        return o_ref.at[:, column_there * 2 + core_there, above]

    def back(step):
        there = lax.rem(me + step, FRAMES)
        return pltpu.make_async_remote_copy(
            src_ref=rows_for(there),
            dst_ref=goal,
            send_sem=send.at[step],
            recv_sem=recv.at[mine],
            device_id=(plane, there),
            device_id_type=MESH,
        )

    def start(step, carry):
        back(step).start()
        return carry

    def end(step, carry):
        back(step).wait_send()
        return carry

    working = row < HEADS_HERE

    @pl.when(working)
    def _():
        lax.fori_loop(1, FRAMES, start, 0)
        pltpu.make_async_copy(rows_for(me), goal, recv.at[mine]).start()

    cut = SLOTS // 2

    def near(head, side):
        part = attn.at[plane * HEADS_HERE + head]
        return pltpu.make_async_remote_copy(
            src_ref=part,
            dst_ref=part,
            send_sem=x_send.at[head, side],
            recv_sem=x_recv.at[head, side],
            device_id=(sides[side], me),
            device_id_type=MESH,
        )

    def far(head, side):
        part = attn.at[sides[1 - side] * HEADS_HERE + head]
        part = part.at[pl.ds(0, cut)] if side == 0 else part.at[pl.ds(cut, SLOTS - cut)]
        return pltpu.make_async_remote_copy(
            src_ref=part,
            dst_ref=part,
            send_sem=x_send.at[head, 2 + side],
            recv_sem=x_recv.at[head, 2 + side],
            device_id=(sides[side], me),
            device_id_type=MESH,
        )

    for head in range(HEADS_HERE):
        part = attn.at[plane * HEADS_HERE + head]
        pltpu.make_async_copy(part, part, recv.at[head]).wait()
        for side in range(2):
            near(head, side).start()
    for head in range(HEADS_HERE):
        for side in range(2):
            near(head, side).wait_recv()
            far(head, side).start()

    @pl.when(working)
    def _():
        lax.fori_loop(1, FRAMES, end, 0)

    for head in range(HEADS_HERE):
        for side in range(2):
            near(head, side).wait_send()
            far(head, side).wait()


def collect(attended):
    return pl.pallas_call(
        collect_kernel,
        out_shape=jax.ShapeDtypeStruct(
            (PLANES * HEADS_HERE, SLOTS, WORKERS, SPOTS, DH), BF16
        ),
        in_specs=[pl.BlockSpec(memory_space=pl.ANY)],
        out_specs=pl.BlockSpec(memory_space=pl.ANY),
        scratch_shapes=[
            pltpu.SemaphoreType.DMA((FRAMES,)),
            pltpu.SemaphoreType.DMA((HEADS_HERE,)),
            pltpu.SemaphoreType.DMA((HEADS_HERE, 4)),
            pltpu.SemaphoreType.DMA((HEADS_HERE, 4)),
        ],
        compiler_params=pltpu.CompilerParams(
            collective_id=1, has_side_effects=True, vmem_limit_bytes=4 * 1024 * 1024
        ),
    )(attended)


def project_kernel(attn_ref, w_ref, out_ref):
    heads = attn_ref.shape[0]
    half = out_ref.shape[0] // 2
    wide = jnp.concatenate([attn_ref[h] for h in range(heads)], axis=1)
    block = 256
    for first in range(0, out_ref.shape[1], block):
        columns = slice(first, first + block)
        mixed = jnp.dot(wide, w_ref[:, columns], preferred_element_type=F32)
        out_ref[:half, columns] = mixed[:half].astype(BF16)
        group, pair = WORKERS * SPOTS, 2 * SPOTS
        blocks = []
        for start in range(half, 2 * half, group):
            for last in range(start + group, start, -pair):
                blocks.append(pltpu.roll(mixed[last - pair : last], SPOTS, 0))
        out_ref[half:, columns] = jnp.concatenate(blocks, axis=0).astype(BF16)


def project(attn, weight, rows):
    return pl.pallas_call(
        project_kernel,
        out_shape=jax.ShapeDtypeStruct((rows, weight.shape[1]), BF16),
        in_specs=[pl.BlockSpec(memory_space=pltpu.VMEM)] * 2,
        out_specs=pl.BlockSpec(memory_space=pltpu.VMEM),
        compiler_params=pltpu.CompilerParams(vmem_limit_bytes=24 * 1024 * 1024),
    )(attn, weight)


def arrange_kernel(
    pattern_ref, mask_hbm, q_hbm, k_hbm, v_hbm, q_out, kv_out, list_ref,
    mask_ref, q_ref, k_ref, v_ref, sems,
):
    sources = (mask_hbm, q_hbm, k_hbm, v_hbm)
    targets = (mask_ref, q_ref, k_ref, v_ref)
    moves = [
        pltpu.make_async_copy(source, target, sems.at[i])
        for i, (source, target) in enumerate(zip(sources, targets))
    ]
    for move in moves:
        move.start()
    me = lax.axis_index("ctx")
    row, column, core = where_is(me)
    moves[0].wait()
    pattern = pattern_ref[jnp.minimum(row, HEADS_HERE - 1)]
    masks = []
    place = column * 2 + core
    tiles = [
        slot * WORKERS + (place if slot < SLOTS // 2 else WORKERS - 1 - place)
        for slot in range(SLOTS)
    ]
    for tile in tiles:
        masks.append(jnp.where(row < HEADS_HERE, mask_ref[pattern, pl.ds(tile, 1), :], 0))
    seen = jnp.concatenate(masks, axis=0) == 1
    seen = jnp.where(seen, 1.0, 0.0).astype(F32)
    down = lax.broadcasted_iota(jnp.int32, (TILES, TILES), 0)
    along = lax.broadcasted_iota(jnp.int32, (TILES, TILES), 1)
    both = (((1,), (1,)), ((), ()))
    upto = jnp.where(along <= down, 1.0, 0.0).astype(BF16)
    same = jnp.where(along == down, 1.0, 0.0).astype(BF16)
    rank = lax.dot_general(upto, seen.astype(BF16), both, preferred_element_type=F32)
    turned = lax.dot_general(same, seen.astype(BF16), both, preferred_element_type=F32)
    rank = rank.astype(jnp.int32)
    spot = jnp.where(turned > 0.5, rank - 1, -1)
    for slot in range(SLOTS):
        hit = spot[:, slot : slot + 1] == along
        listed = jnp.sum(jnp.where(hit, down, 0), axis=0, keepdims=True)
        spare = along[:1, :] >= rank[TILES - 1 :, slot : slot + 1]
        list_ref[slot : slot + 1, :] = jnp.where(spare, tiles[slot], listed)
    last = jnp.concatenate(
        [rank[TILES - 1 :, :], jnp.zeros((1, TILES - SLOTS), jnp.int32)], axis=1
    )
    list_ref[SLOTS : SLOTS + 1, :] = last


    rows = q_ref.shape[0]
    for move, source, target, first in (
        (moves[1], q_ref, q_out, 0),
        (moves[2], k_ref, kv_out, 0),
        (moves[3], v_ref, kv_out, rows),
    ):
        move.wait()
        for head in range(HEADS_HERE):
            target[head, first : first + rows, :] = source[:, head * DH : (head + 1) * DH]
    half = rows // 2
    later = jnp.dot(turned_rows(half), q_ref[half:, :], preferred_element_type=F32).astype(BF16)
    for head in range(HEADS_HERE):
        q_out[head, half:, :] = later[:, head * DH : (head + 1) * DH]


def arrange(head_pattern, tile_masks, queries, key_rows, value_rows):
    rows = queries.shape[0]
    return pl.pallas_call(
        arrange_kernel,
        out_shape=(
            jax.ShapeDtypeStruct((HEADS_HERE, rows, DH), BF16),
            jax.ShapeDtypeStruct((HEADS_HERE, 2 * rows, DH), BF16),
            jax.ShapeDtypeStruct((SLOTS + 1, TILES), jnp.int32),
        ),
        in_specs=[pl.BlockSpec(memory_space=pltpu.SMEM)]
        + [pl.BlockSpec(memory_space=pl.ANY)] * 4,
        out_specs=(pl.BlockSpec(memory_space=pltpu.VMEM),) * 3,
        scratch_shapes=[
            pltpu.VMEM(tile_masks.shape, jnp.int32),
            pltpu.VMEM(queries.shape, BF16),
            pltpu.VMEM(queries.shape, BF16),
            pltpu.VMEM(queries.shape, BF16),
            pltpu.SemaphoreType.DMA((4,)),
        ],
        compiler_params=pltpu.CompilerParams(vmem_limit_bytes=57 * 1024 * 1024),
    )(head_pattern, tile_masks, queries, key_rows, value_rows)


def body(queries, key_rows, value_rows, out_weight, tile_masks, head_pattern):
    rows = queries.shape[0]
    q_parts, kv_parts, lists = arrange(head_pattern, tile_masks, queries, key_rows, value_rows)
    kv_all, w_all = spread(
        q_parts.reshape(HEADS_HERE, SLOTS, WORKERS, SPOTS, DH),
        kv_parts.reshape(HEADS_HERE, 2 * TILES, SPOTS, DH),
        out_weight,
    )
    attended = attend(lists, kv_all.reshape(WORKERS, (2 * TILES + SLOTS) * PIECE, DH))
    attn = collect(attended.reshape(SLOTS, WORKERS, SIDE, SPOTS, DH))
    attn = attn.reshape(PLANES * HEADS_HERE, rows, DH)
    return project(attn, w_all, rows)


def solution(mesh):
    placed = (
        P("ctx", "heads"),
        P("ctx", "heads"),
        P("ctx", "heads"),
        P("heads", None),
        P(),
        P("heads"),
    )
    return jax.shard_map(
        body, mesh=mesh, in_specs=placed, out_specs=P("ctx", "heads"), check_vma=False
    )
```

```python
import math

import jax
import jax.numpy as jnp
from jax import lax
from jax.experimental import pallas as pl
from jax.experimental.pallas import tpu as pltpu
from jax.sharding import PartitionSpec as P

MESH = pl.DeviceIdType.MESH
DH = 128
TILE = 128
SPOTS = 4
FRAMES = 32
TILES = 128
PLANES = 4
SIDE = 4
HEADS_HERE = 3
WORKERS = 2 * SIDE
SLOTS = TILES // WORKERS
SIZES = (64, 64, 64, 64)
PARTS = len(SIZES)
PIECE = TILE // WORKERS
GROUP = 8
CHUNK = 32
BESIDE = 4
FAR = 2.0**64
LOW = -1e30
SCALE2 = math.log2(math.e) / math.sqrt(DH)
BF16 = jnp.bfloat16
F32 = jnp.float32


def where_is(device):
    return lax.div(device, WORKERS), lax.rem(lax.div(device, 2), SIDE), lax.rem(device, 2)


def device_at(row, column, core):
    return (lax.rem(row, SIDE) * SIDE + lax.rem(column, SIDE)) * 2 + core


def spread_kernel(
    q_ref, kv_ref, w_ref, kv_all, w_all,
    q_send, q_recv, z_send, z_recv, y_send, y_recv, far_send, far_recv,
    core_send, core_recv, w_send, w_recv, w_core_send, w_core_recv, own_sem,
):
    plane = lax.axis_index("heads")
    me = lax.axis_index("ctx")
    row, column, core = where_is(me)
    working = row < HEADS_HERE
    own_row = jnp.minimum(row, HEADS_HERE - 1)
    depth = w_ref.shape[0]
    width = w_all.shape[1]
    sides = (1, SIDE - 1)

    barrier = pltpu.get_barrier_semaphore()

    def greet(step, carry):
        pl.semaphore_signal(
            barrier, inc=1, device_id=(plane, lax.rem(me + step, FRAMES)), device_id_type=MESH
        )
        return carry

    lax.fori_loop(1, FRAMES, greet, 0)
    for hop in range(1, PLANES):
        pl.semaphore_signal(
            barrier, inc=1, device_id=(lax.rem(plane + hop, PLANES), me), device_id_type=MESH
        )
    pl.semaphore_wait(barrier, FRAMES - 1 + PLANES - 1)

    def span(part):
        return pl.ds(sum(SIZES[:part]), SIZES[part])

    own_copy = pltpu.make_async_copy(
        kv_ref.at[own_row], kv_all.at[column * 2 + core, pl.ds(0, 2 * TILES), 0], own_sem
    )

    def z_copy(part, hop):
        there = lax.rem(row + hop, SIDE)
        return pltpu.make_async_remote_copy(
            src_ref=kv_ref.at[there, span(part)],
            dst_ref=kv_all.at[column * 2 + core, span(part), hop],
            send_sem=z_send.at[part, hop],
            recv_sem=z_recv.at[part, hop],
            device_id=(plane, device_at(there, column, core)),
            device_id_type=MESH,
        )

    def piece(number, away):
        source = kv_all.at[lax.rem(column + away, SIDE) * 2 + core]
        if number == 0:
            return source.at[pl.ds(0, 2 * TILES), 0]
        return source.at[span(number - 1), pl.ds(1, SIDE - 1)]

    def y_copy(number, side):
        return pltpu.make_async_remote_copy(
            src_ref=kv_ref.at[own_row] if number == 0 else piece(number, 0),
            dst_ref=piece(number, 0),
            send_sem=y_send.at[number, side],
            recv_sem=y_recv.at[number, side],
            device_id=(plane, device_at(row, column + sides[side], core)),
            device_id_type=MESH,
        )

    def far_copy(number, side):
        source = kv_all.at[lax.rem(column + sides[1 - side], SIDE) * 2 + core]
        first, count = (0, 2 * TILES) if number == 0 else (sum(SIZES[: number - 1]), SIZES[number - 1])
        share = count * 5 // 8
        tiles = pl.ds(first + share, count - share) if side else pl.ds(first, share)
        chunk = source.at[tiles, 0] if number == 0 else source.at[tiles, pl.ds(1, SIDE - 1)]
        return pltpu.make_async_remote_copy(
            src_ref=chunk,
            dst_ref=chunk,
            send_sem=far_send.at[number, side],
            recv_sem=far_recv.at[number, side],
            device_id=(plane, device_at(row, column + sides[side], core)),
            device_id_type=MESH,
        )

    def core_copy(number, away):
        return pltpu.make_async_remote_copy(
            src_ref=piece(number, away),
            dst_ref=piece(number, away),
            send_sem=core_send.at[number, away],
            recv_sem=core_recv,
            device_id=(plane, device_at(row, column, 1 - core)),
            device_id_type=MESH,
        )

    half = depth // 2

    def w_rows(source, part):
        return w_all.at[pl.ds(pl.multiple_of(source * depth + part * half, 16), half)]

    def w_copy(hop):
        there = lax.rem(plane + hop, PLANES)
        return pltpu.make_async_remote_copy(
            src_ref=w_ref.at[
                pl.ds(pl.multiple_of(core * half, 16), half),
                pl.ds(pl.multiple_of(there * width, 128), width),
            ],
            dst_ref=w_rows(plane, core),
            send_sem=w_send.at[hop],
            recv_sem=w_recv.at[hop],
            device_id=(there, me),
            device_id_type=MESH,
        )

    def w_core_copy(hop):
        rows = w_rows(lax.rem(plane + PLANES - hop, PLANES), core)
        return pltpu.make_async_remote_copy(
            src_ref=rows,
            dst_ref=rows,
            send_sem=w_core_send.at[hop],
            recv_sem=w_core_recv.at[hop],
            device_id=(plane, device_at(row, column, 1 - core)),
            device_id_type=MESH,
        )

    own_w = pltpu.make_async_copy(
        w_ref.at[:, pl.ds(pl.multiple_of(plane * width, 128), width)],
        w_all.at[pl.ds(pl.multiple_of(plane * depth, 128), depth)],
        w_recv.at[0],
    )

    queries = kv_all.at[:, pl.ds(2 * TILES, SLOTS)]

    def q_copy(step):
        there = lax.rem(me + step, FRAMES)
        row_there, column_there, core_there = where_is(there)
        return row_there < HEADS_HERE, pltpu.make_async_remote_copy(
            src_ref=q_ref.at[
                jnp.minimum(row_there, HEADS_HERE - 1), :, column_there * 2 + core_there
            ],
            dst_ref=queries.at[column * 2 + core, :, lax.rem(row_there - row + SIDE, SIDE)],
            send_sem=q_send.at[step],
            recv_sem=q_recv,
            device_id=(plane, there),
            device_id_type=MESH,
        )

    def to_rows(part, work):
        for hop in range(1, SIDE):

            @pl.when(lax.rem(row + hop, SIDE) < HEADS_HERE)
            def _():
                work(z_copy(part, hop))

    def send_q(step, carry):
        wanted, copy = q_copy(step)

        @pl.when(wanted)
        def _():
            copy.start()

        return carry

    def sent_q(step, carry):
        wanted, copy = q_copy(step)

        @pl.when(wanted)
        def _():
            copy.wait_send()

        return carry

    def send_small():
        for hop in range(1, PLANES):
            w_copy(hop).start()
        own_w.start()
        lax.fori_loop(1, FRAMES, send_q, 0)

    @pl.when(working)
    def _():
        own_copy.start()
        for side in range(2):
            y_copy(0, side).start()

    to_rows(0, lambda copy: copy.start())
    send_small()

    def next_rows(part):
        to_rows(part, lambda copy: copy.wait_send())
        if part + 1 < PARTS:
            to_rows(part + 1, lambda copy: copy.start())

    @pl.when(jnp.logical_not(working))
    def _():
        for part in range(PARTS):
            next_rows(part)

    @pl.when(working)
    def _():
        pltpu.make_async_copy(
            q_ref.at[own_row, :, column * 2 + core], queries.at[column * 2 + core, :, 0], q_recv
        ).start()
        own_copy.wait()
        core_copy(0, 0).start()

        def pass_on(number):
            for side in range(2):
                y_copy(number, side).wait_recv()
                far_copy(number, side).start()
            for side in range(2):
                core_copy(number, sides[1 - side]).start()

        for part in range(PARTS):
            next_rows(part)
            for hop in range(1, SIDE):
                landed = kv_all.at[column * 2 + core, span(part), hop]
                pltpu.make_async_copy(landed, landed, z_recv.at[part, hop]).wait()
            for side in range(2):
                y_copy(part + 1, side).start()
            core_copy(part + 1, 0).start()
            pass_on(part)
        pass_on(PARTS)
        for number in range(PARTS + 1):
            for side in range(2):
                far_copy(number, side).wait_recv()
            core_copy(number, 2).start()

    for hop in range(1, PLANES):
        w_copy(hop).wait_recv()
        w_core_copy(hop).start()

    @pl.when(working)
    def _():
        pltpu.make_async_copy(queries, queries, q_recv).wait()
        other = kv_all.at[pl.ds(0, SIDE), pl.ds(0, 2 * TILES)]
        pltpu.make_async_copy(other, other, core_recv).wait()
        for number in range(PARTS + 1):
            for side in range(2):
                y_copy(number, side).wait_send()
                far_copy(number, side).wait_send()
            for away in range(SIDE):
                core_copy(number, away).wait_send()

    own_w.wait()
    lax.fori_loop(1, FRAMES, sent_q, 0)
    for hop in range(1, PLANES):
        w_copy(hop).wait_send()
        w_core_copy(hop).wait()


def spread(q_parts, kv_parts, out_weight):
    depth, columns = out_weight.shape
    return pl.pallas_call(
        spread_kernel,
        out_shape=(
            jax.ShapeDtypeStruct((WORKERS, 2 * TILES + SLOTS, SIDE, SPOTS, DH), BF16),
            jax.ShapeDtypeStruct((depth * PLANES, columns // PLANES), BF16),
        ),
        in_specs=[pl.BlockSpec(memory_space=pl.ANY)] * 3,
        out_specs=(pl.BlockSpec(memory_space=pl.ANY),) * 2,
        scratch_shapes=[
            pltpu.SemaphoreType.DMA((FRAMES,)),
            pltpu.SemaphoreType.DMA,
            pltpu.SemaphoreType.DMA((PARTS, SIDE)),
            pltpu.SemaphoreType.DMA((PARTS, SIDE)),
            pltpu.SemaphoreType.DMA((PARTS + 1, 2)),
            pltpu.SemaphoreType.DMA((PARTS + 1, 2)),
            pltpu.SemaphoreType.DMA((PARTS + 1, 2)),
            pltpu.SemaphoreType.DMA((PARTS + 1, 2)),
            pltpu.SemaphoreType.DMA((PARTS + 1, SIDE)),
            pltpu.SemaphoreType.DMA,
            pltpu.SemaphoreType.DMA((PLANES,)),
            pltpu.SemaphoreType.DMA((PLANES,)),
            pltpu.SemaphoreType.DMA((PLANES,)),
            pltpu.SemaphoreType.DMA((PLANES,)),
            pltpu.SemaphoreType.DMA,
        ],
        compiler_params=pltpu.CompilerParams(
            collective_id=0, has_side_effects=True, vmem_limit_bytes=57 * 1024 * 1024
        ),
    )(q_parts, kv_parts, out_weight)


def turned_rows(rows):
    to = lax.broadcasted_iota(jnp.int32, (rows, rows), 0)
    source = lax.broadcasted_iota(jnp.int32, (rows, rows), 1)
    group = WORKERS * SPOTS
    place = lax.div(lax.rem(to, group), SPOTS)
    wanted = to + (WORKERS - 1 - 2 * place) * SPOTS
    return jnp.where(source == wanted, 1.0, 0.0).astype(BF16)


def attend_kernel(
    list_ref, kv_hbm, o_ref, kv_ref, q_ref, keys_ref, base_ref, peak_ref, sum_ref,
    slot_of, first_of, listed_of, kv_sem,
):
    def bring(number, first, tiles):
        rows = pl.ds(first * PIECE, tiles * PIECE)
        return pltpu.make_async_copy(kv_hbm.at[:, rows], kv_ref.at[:, rows], kv_sem.at[number])

    chunks = TILES // CHUNK
    moves = [bring(number, number * CHUNK, CHUNK) for number in range(chunks)]
    moves.append(bring(chunks, 2 * TILES, SLOTS))
    moves.append(bring(chunks + 1, TILES, TILES))
    for move in moves:
        move.start()

    _, column, core = where_is(lax.axis_index("ctx"))

    def loop(count, work):
        def one(step, carry):
            work(step)
            return carry

        lax.fori_loop(0, count, one, 0)

    def rows_of(slot):
        return pl.ds(pl.multiple_of(slot * TILE, TILE), TILE)

    def tile_at(tile):
        start = pl.multiple_of(tile * PIECE, PIECE)
        return jnp.concatenate(
            [kv_ref[worker, pl.ds(start, PIECE), :] for worker in range(WORKERS)], axis=0
        )

    def enlist(slot, total):
        count = list_ref[SLOTS, slot]
        steps = lax.div(count + GROUP - 1, GROUP)

        def one(step, carry):
            slot_of[total + step] = slot
            first_of[total + step] = step * GROUP
            listed_of[total + step] = count - step * GROUP
            return carry

        lax.fori_loop(0, steps, one, 0)
        return total + steps

    total = lax.fori_loop(0, SLOTS, enlist, 0)
    for spare in range(BESIDE - 1):
        slot_of[total + spare] = 0
        first_of[total + spare] = 0
        listed_of[total + spare] = 0
    turns = lax.div(total + BESIDE - 1, BESIDE)
    busy = jnp.where(total > 0, 1, 0)

    def unpack(step):
        for u in range(GROUP):
            tile = step * GROUP + u
            keys_ref[tile] = tile_at(tile).T

    for number in range(chunks):
        moves[number].wait()
        steps = CHUNK // GROUP
        loop(busy * steps, lambda step: unpack(step + number * steps))
    moves[chunks].wait()

    def set_base(slot, base):
        base_ref[slot] = jnp.broadcast_to(base * SCALE2, (TILE, TILE))

    def own_base(step):
        for u in range(BESIDE):
            slot = step * BESIDE + u
            place = column * 2 + core
            late = jnp.where(slot < SLOTS // 2, 0, WORKERS - 1 - 2 * place)
            own = keys_ref[slot * WORKERS + place + late]
            query = tile_at(2 * TILES + slot)
            q_ref[rows_of(slot), :] = query
            scores = jnp.dot(query, own, preferred_element_type=F32)
            set_base(slot, jnp.max(scores, axis=1, keepdims=True))

    loop(busy * (SLOTS // BESIDE), own_base)
    moves[chunks + 1].wait()

    def tiles_of(number):
        slot, first = slot_of[number], first_of[number]
        return slot, [list_ref[slot, first + u] for u in range(GROUP)]

    def scores_of(slot, tiles):
        keys = jnp.concatenate([keys_ref[tile] for tile in tiles], axis=1)
        return jnp.dot(q_ref[rows_of(slot), :], keys, preferred_element_type=F32)

    def attend_steps(step):
        found = []
        for beside in range(BESIDE):
            number = step * BESIDE + beside
            slot, tiles = tiles_of(number)
            listed = listed_of[number]
            base = base_ref[slot]
            scores = scores_of(slot, tiles)
            weights, values = [], []
            for u in range(GROUP):
                part = scores[:, u * TILE : (u + 1) * TILE]
                weights.append(jnp.exp2(part * SCALE2 - base).astype(BF16))
                value = jnp.where(u < listed, tile_at(TILES + tiles[u]), 0).astype(BF16)
                ones = jnp.where(u < listed, 1.0, 0.0).astype(BF16)
                ones = jnp.broadcast_to(ones, (TILE, DH))
                values.append(jnp.concatenate([value, ones], axis=1))
            added = jnp.dot(
                jnp.concatenate(weights, axis=1),
                jnp.concatenate(values, axis=0),
                preferred_element_type=F32,
            )
            found.append((slot, added))
        for slot, added in found:
            sum_ref[slot] += added

    def peak_steps(step):
        for beside in range(BESIDE):
            slot, tiles = tiles_of(step * BESIDE + beside)
            scores = scores_of(slot, tiles)
            peak = peak_ref[slot]
            for u in range(GROUP):
                peak = jnp.maximum(peak, scores[:, u * TILE : (u + 1) * TILE])
            peak_ref[slot] = peak

    def attempt(number, needed):
        def clear(slot):
            sum_ref[slot] = jnp.zeros((TILE, 2 * DH), F32)
            peak_ref[slot] = jnp.full((TILE, TILE), LOW, F32)

        loop(needed * SLOTS, clear)
        loop(needed * turns, attend_steps)
        beyond = jnp.zeros((TILE, DH), F32)
        for slot in range(SLOTS):
            beyond = jnp.where(sum_ref[slot, :, DH:] <= FAR, beyond, 1.0)
        again = needed * jnp.where(jnp.max(beyond) > 0.0, 1, 0)
        loop(again * turns, peak_steps)

        def rebase(slot):
            set_base(slot, jnp.max(peak_ref[slot], axis=1, keepdims=True))

        loop(again * SLOTS, rebase)
        return again

    lax.fori_loop(0, 2, attempt, busy)

    def finish(step):
        for u in range(BESIDE):
            slot = step * BESIDE + u
            o_ref[rows_of(slot), :] = (sum_ref[slot, :, :DH] / sum_ref[slot, :, DH:]).astype(BF16)

    loop(busy * (SLOTS // BESIDE), finish)


def attend(lists, kv):
    most = SLOTS * (TILES // GROUP) + BESIDE
    return pl.pallas_call(
        attend_kernel,
        out_shape=jax.ShapeDtypeStruct((SLOTS * TILE, DH), BF16),
        in_specs=[pl.BlockSpec(memory_space=pltpu.SMEM), pl.BlockSpec(memory_space=pl.ANY)],
        out_specs=pl.BlockSpec(memory_space=pltpu.VMEM),
        scratch_shapes=[
            pltpu.VMEM(kv.shape, BF16),
            pltpu.VMEM((SLOTS * TILE, DH), BF16),
            pltpu.VMEM((TILES, DH, TILE), BF16),
            pltpu.VMEM((SLOTS, TILE, TILE), F32),
            pltpu.VMEM((SLOTS, TILE, TILE), F32),
            pltpu.VMEM((SLOTS, TILE, 2 * DH), F32),
            pltpu.SMEM((most,), jnp.int32),
            pltpu.SMEM((most,), jnp.int32),
            pltpu.SMEM((most,), jnp.int32),
            pltpu.SemaphoreType.DMA((TILES // CHUNK + 2,)),
        ],
        compiler_params=pltpu.CompilerParams(vmem_limit_bytes=50 * 1024 * 1024),
    )(lists, kv)


def collect_kernel(o_ref, attn, send, recv, x_send, x_recv):
    plane = lax.axis_index("heads")
    me = lax.axis_index("ctx")
    row, column, core = where_is(me)
    barrier = pltpu.get_barrier_semaphore()

    def greet(step, carry):
        pl.semaphore_signal(
            barrier, inc=1, device_id=(plane, lax.rem(me + step, FRAMES)), device_id_type=MESH
        )
        return carry

    lax.fori_loop(1, FRAMES, greet, 0)
    sides = (lax.rem(plane + 1, PLANES), lax.rem(plane + PLANES - 1, PLANES))
    for there in sides:
        pl.semaphore_signal(barrier, inc=1, device_id=(there, me), device_id_type=MESH)
    pl.semaphore_wait(barrier, FRAMES - 1 + 2)

    mine = jnp.minimum(row, HEADS_HERE - 1)
    goal = attn.at[plane * HEADS_HERE + mine, :, column * 2 + core]

    def rows_for(there):
        row_there, column_there, core_there = where_is(there)
        above = lax.rem(row - row_there + SIDE, SIDE)
        return o_ref.at[:, column_there * 2 + core_there, above]

    def back(step):
        there = lax.rem(me + step, FRAMES)
        return pltpu.make_async_remote_copy(
            src_ref=rows_for(there),
            dst_ref=goal,
            send_sem=send.at[step],
            recv_sem=recv.at[mine],
            device_id=(plane, there),
            device_id_type=MESH,
        )

    def start(step, carry):
        back(step).start()
        return carry

    def end(step, carry):
        back(step).wait_send()
        return carry

    working = row < HEADS_HERE

    @pl.when(working)
    def _():
        lax.fori_loop(1, FRAMES, start, 0)
        pltpu.make_async_copy(rows_for(me), goal, recv.at[mine]).start()

    cut = SLOTS // 2

    def near(head, side):
        part = attn.at[plane * HEADS_HERE + head]
        return pltpu.make_async_remote_copy(
            src_ref=part,
            dst_ref=part,
            send_sem=x_send.at[head, side],
            recv_sem=x_recv.at[head, side],
            device_id=(sides[side], me),
            device_id_type=MESH,
        )

    def far(head, side):
        part = attn.at[sides[1 - side] * HEADS_HERE + head]
        part = part.at[pl.ds(0, cut)] if side == 0 else part.at[pl.ds(cut, SLOTS - cut)]
        return pltpu.make_async_remote_copy(
            src_ref=part,
            dst_ref=part,
            send_sem=x_send.at[head, 2 + side],
            recv_sem=x_recv.at[head, 2 + side],
            device_id=(sides[side], me),
            device_id_type=MESH,
        )

    for head in range(HEADS_HERE):
        part = attn.at[plane * HEADS_HERE + head]
        pltpu.make_async_copy(part, part, recv.at[head]).wait()
        for side in range(2):
            near(head, side).start()
    for head in range(HEADS_HERE):
        for side in range(2):
            near(head, side).wait_recv()
            far(head, side).start()

    @pl.when(working)
    def _():
        lax.fori_loop(1, FRAMES, end, 0)

    for head in range(HEADS_HERE):
        for side in range(2):
            near(head, side).wait_send()
            far(head, side).wait()


def collect(attended):
    return pl.pallas_call(
        collect_kernel,
        out_shape=jax.ShapeDtypeStruct(
            (PLANES * HEADS_HERE, SLOTS, WORKERS, SPOTS, DH), BF16
        ),
        in_specs=[pl.BlockSpec(memory_space=pl.ANY)],
        out_specs=pl.BlockSpec(memory_space=pl.ANY),
        scratch_shapes=[
            pltpu.SemaphoreType.DMA((FRAMES,)),
            pltpu.SemaphoreType.DMA((HEADS_HERE,)),
            pltpu.SemaphoreType.DMA((HEADS_HERE, 4)),
            pltpu.SemaphoreType.DMA((HEADS_HERE, 4)),
        ],
        compiler_params=pltpu.CompilerParams(
            collective_id=1, has_side_effects=True, vmem_limit_bytes=4 * 1024 * 1024
        ),
    )(attended)


def project_kernel(attn_ref, w_ref, out_ref):
    heads = attn_ref.shape[0]
    half = out_ref.shape[0] // 2
    wide = jnp.concatenate([attn_ref[h] for h in range(heads)], axis=1)
    block = 256
    for first in range(0, out_ref.shape[1], block):
        columns = slice(first, first + block)
        mixed = jnp.dot(wide, w_ref[:, columns], preferred_element_type=F32)
        out_ref[:half, columns] = mixed[:half].astype(BF16)
        group, pair = WORKERS * SPOTS, 2 * SPOTS
        blocks = []
        for start in range(half, 2 * half, group):
            for last in range(start + group, start, -pair):
                blocks.append(pltpu.roll(mixed[last - pair : last], SPOTS, 0))
        out_ref[half:, columns] = jnp.concatenate(blocks, axis=0).astype(BF16)


def project(attn, weight, rows):
    return pl.pallas_call(
        project_kernel,
        out_shape=jax.ShapeDtypeStruct((rows, weight.shape[1]), BF16),
        in_specs=[pl.BlockSpec(memory_space=pltpu.VMEM)] * 2,
        out_specs=pl.BlockSpec(memory_space=pltpu.VMEM),
        compiler_params=pltpu.CompilerParams(vmem_limit_bytes=24 * 1024 * 1024),
    )(attn, weight)


def arrange_kernel(
    pattern_ref, mask_hbm, q_hbm, k_hbm, v_hbm, q_out, kv_out, list_ref,
    mask_ref, q_ref, k_ref, v_ref, sems,
):
    sources = (mask_hbm, q_hbm, k_hbm, v_hbm)
    targets = (mask_ref, q_ref, k_ref, v_ref)
    moves = [
        pltpu.make_async_copy(source, target, sems.at[i])
        for i, (source, target) in enumerate(zip(sources, targets))
    ]
    for move in moves:
        move.start()
    me = lax.axis_index("ctx")
    row, column, core = where_is(me)
    moves[0].wait()
    pattern = pattern_ref[jnp.minimum(row, HEADS_HERE - 1)]
    masks = []
    place = column * 2 + core
    tiles = [
        slot * WORKERS + (place if slot < SLOTS // 2 else WORKERS - 1 - place)
        for slot in range(SLOTS)
    ]
    for tile in tiles:
        masks.append(jnp.where(row < HEADS_HERE, mask_ref[pattern, pl.ds(tile, 1), :], 0))
    seen = jnp.concatenate(masks, axis=0) == 1
    seen = jnp.where(seen, 1.0, 0.0).astype(F32)
    down = lax.broadcasted_iota(jnp.int32, (TILES, TILES), 0)
    along = lax.broadcasted_iota(jnp.int32, (TILES, TILES), 1)
    both = (((1,), (1,)), ((), ()))
    upto = jnp.where(along <= down, 1.0, 0.0).astype(BF16)
    same = jnp.where(along == down, 1.0, 0.0).astype(BF16)
    rank = lax.dot_general(upto, seen.astype(BF16), both, preferred_element_type=F32)
    turned = lax.dot_general(same, seen.astype(BF16), both, preferred_element_type=F32)
    rank = rank.astype(jnp.int32)
    spot = jnp.where(turned > 0.5, rank - 1, -1)
    for slot in range(SLOTS):
        hit = spot[:, slot : slot + 1] == along
        listed = jnp.sum(jnp.where(hit, down, 0), axis=0, keepdims=True)
        spare = along[:1, :] >= rank[TILES - 1 :, slot : slot + 1]
        list_ref[slot : slot + 1, :] = jnp.where(spare, tiles[slot], listed)
    last = jnp.concatenate(
        [rank[TILES - 1 :, :], jnp.zeros((1, TILES - SLOTS), jnp.int32)], axis=1
    )
    list_ref[SLOTS : SLOTS + 1, :] = last


    rows = q_ref.shape[0]
    for move, source, target, first in (
        (moves[1], q_ref, q_out, 0),
        (moves[2], k_ref, kv_out, 0),
        (moves[3], v_ref, kv_out, rows),
    ):
        move.wait()
        for head in range(HEADS_HERE):
            target[head, first : first + rows, :] = source[:, head * DH : (head + 1) * DH]
    half = rows // 2
    later = jnp.dot(turned_rows(half), q_ref[half:, :], preferred_element_type=F32).astype(BF16)
    for head in range(HEADS_HERE):
        q_out[head, half:, :] = later[:, head * DH : (head + 1) * DH]


def arrange(head_pattern, tile_masks, queries, key_rows, value_rows):
    rows = queries.shape[0]
    return pl.pallas_call(
        arrange_kernel,
        out_shape=(
            jax.ShapeDtypeStruct((HEADS_HERE, rows, DH), BF16),
            jax.ShapeDtypeStruct((HEADS_HERE, 2 * rows, DH), BF16),
            jax.ShapeDtypeStruct((SLOTS + 1, TILES), jnp.int32),
        ),
        in_specs=[pl.BlockSpec(memory_space=pltpu.SMEM)]
        + [pl.BlockSpec(memory_space=pl.ANY)] * 4,
        out_specs=(pl.BlockSpec(memory_space=pltpu.VMEM),) * 3,
        scratch_shapes=[
            pltpu.VMEM(tile_masks.shape, jnp.int32),
            pltpu.VMEM(queries.shape, BF16),
            pltpu.VMEM(queries.shape, BF16),
            pltpu.VMEM(queries.shape, BF16),
            pltpu.SemaphoreType.DMA((4,)),
        ],
        compiler_params=pltpu.CompilerParams(vmem_limit_bytes=57 * 1024 * 1024),
    )(head_pattern, tile_masks, queries, key_rows, value_rows)


def body(queries, key_rows, value_rows, out_weight, tile_masks, head_pattern):
    rows = queries.shape[0]
    q_parts, kv_parts, lists = arrange(head_pattern, tile_masks, queries, key_rows, value_rows)
    kv_all, w_all = spread(
        q_parts.reshape(HEADS_HERE, SLOTS, WORKERS, SPOTS, DH),
        kv_parts.reshape(HEADS_HERE, 2 * TILES, SPOTS, DH),
        out_weight,
    )
    attended = attend(lists, kv_all.reshape(WORKERS, (2 * TILES + SLOTS) * PIECE, DH))
    attn = collect(attended.reshape(SLOTS, WORKERS, SIDE, SPOTS, DH))
    attn = attn.reshape(PLANES * HEADS_HERE, rows, DH)
    return project(attn, w_all, rows)


def solution(mesh):
    placed = (
        P("ctx", "heads"),
        P("ctx", "heads"),
        P("ctx", "heads"),
        P("heads", None),
        P(),
        P("heads"),
    )
    return jax.shard_map(
        body, mesh=mesh, in_specs=placed, out_specs=P("ctx", "heads"), check_vma=False
    )
```

```python
import math

import jax
import jax.numpy as jnp
from jax import lax
from jax.experimental import pallas as pl
from jax.experimental.pallas import tpu as pltpu
from jax.sharding import PartitionSpec as P

MESH = pl.DeviceIdType.MESH
DH = 128
TILE = 128
SPOTS = 4
FRAMES = 32
TILES = 128
PLANES = 4
SIDE = 4
HEADS_HERE = 3
WORKERS = 2 * SIDE
SLOTS = TILES // WORKERS
SIZES = (64, 64, 64, 64)
PARTS = len(SIZES)
PIECE = TILE // WORKERS
GROUP = 8
CHUNK = 32
BESIDE = 4
FAR = 2.0**64
LOW = -1e30
SCALE2 = math.log2(math.e) / math.sqrt(DH)
BF16 = jnp.bfloat16
F32 = jnp.float32


def where_is(device):
    return lax.div(device, WORKERS), lax.rem(lax.div(device, 2), SIDE), lax.rem(device, 2)


def device_at(row, column, core):
    return (lax.rem(row, SIDE) * SIDE + lax.rem(column, SIDE)) * 2 + core


def spread_kernel(
    q_ref, kv_ref, w_ref, kv_all, w_all,
    q_send, q_recv, z_send, z_recv, y_send, y_recv, far_send, far_recv,
    core_send, core_recv, last_recv, w_send, w_recv, w_core_send, w_core_recv, own_sem,
):
    plane = lax.axis_index("heads")
    me = lax.axis_index("ctx")
    row, column, core = where_is(me)
    working = row < HEADS_HERE
    own_row = jnp.minimum(row, HEADS_HERE - 1)
    depth = w_ref.shape[0]
    width = w_all.shape[1]
    sides = (1, SIDE - 1)

    barrier = pltpu.get_barrier_semaphore()

    def greet(step, carry):
        pl.semaphore_signal(
            barrier, inc=1, device_id=(plane, lax.rem(me + step, FRAMES)), device_id_type=MESH
        )
        return carry

    lax.fori_loop(1, FRAMES, greet, 0)
    for hop in range(1, PLANES):
        pl.semaphore_signal(
            barrier, inc=1, device_id=(lax.rem(plane + hop, PLANES), me), device_id_type=MESH
        )
    pl.semaphore_wait(barrier, FRAMES - 1 + PLANES - 1)

    def span(part):
        return pl.ds(sum(SIZES[:part]), SIZES[part])

    own_copy = pltpu.make_async_copy(
        kv_ref.at[own_row], kv_all.at[column * 2 + core, pl.ds(0, 2 * TILES), 0], own_sem
    )

    def z_copy(part, hop):
        there = lax.rem(row + hop, SIDE)
        return pltpu.make_async_remote_copy(
            src_ref=kv_ref.at[there, span(part)],
            dst_ref=kv_all.at[column * 2 + core, span(part), hop],
            send_sem=z_send.at[part, hop],
            recv_sem=z_recv.at[part, hop],
            device_id=(plane, device_at(there, column, core)),
            device_id_type=MESH,
        )

    def piece(number, away):
        source = kv_all.at[lax.rem(column + away, SIDE) * 2 + core]
        if number == 0:
            return source.at[pl.ds(0, 2 * TILES), 0]
        return source.at[span(number - 1), pl.ds(1, SIDE - 1)]

    def y_copy(number, side):
        return pltpu.make_async_remote_copy(
            src_ref=kv_ref.at[own_row] if number == 0 else piece(number, 0),
            dst_ref=piece(number, 0),
            send_sem=y_send.at[number, side],
            recv_sem=y_recv.at[number, side],
            device_id=(plane, device_at(row, column + sides[side], core)),
            device_id_type=MESH,
        )

    def far_copy(number, side, over=0):
        source = kv_all.at[lax.rem(column + sides[1 - side], SIDE) * 2 + core]
        first, count = (0, 2 * TILES) if number == 0 else (sum(SIZES[: number - 1]), SIZES[number - 1])
        share = count // 2
        tiles = pl.ds(first + share, count - share) if side else pl.ds(first, share)
        chunk = source.at[tiles, 0] if number == 0 else source.at[tiles, pl.ds(1, SIDE - 1)]
        return pltpu.make_async_remote_copy(
            src_ref=chunk,
            dst_ref=chunk,
            send_sem=far_send.at[number, side, over],
            recv_sem=far_recv.at[number, side, over],
            device_id=(
                plane,
                device_at(row, column + sides[side], core + over - 2 * core * over),
            ),
            device_id_type=MESH,
        )

    def core_copy(number, away):
        return pltpu.make_async_remote_copy(
            src_ref=piece(number, away),
            dst_ref=piece(number, away),
            send_sem=core_send.at[number, away],
            recv_sem=last_recv if number == PARTS else core_recv,
            device_id=(plane, device_at(row, column, 1 - core)),
            device_id_type=MESH,
        )

    half = depth // 2

    def w_rows(source, part):
        return w_all.at[pl.ds(pl.multiple_of(source * depth + part * half, 16), half)]

    def w_copy(hop):
        there = lax.rem(plane + hop, PLANES)
        return pltpu.make_async_remote_copy(
            src_ref=w_ref.at[
                pl.ds(pl.multiple_of(core * half, 16), half),
                pl.ds(pl.multiple_of(there * width, 128), width),
            ],
            dst_ref=w_rows(plane, core),
            send_sem=w_send.at[hop],
            recv_sem=w_recv.at[hop],
            device_id=(there, me),
            device_id_type=MESH,
        )

    def w_core_copy(hop):
        rows = w_rows(lax.rem(plane + PLANES - hop, PLANES), core)
        return pltpu.make_async_remote_copy(
            src_ref=rows,
            dst_ref=rows,
            send_sem=w_core_send.at[hop],
            recv_sem=w_core_recv.at[hop],
            device_id=(plane, device_at(row, column, 1 - core)),
            device_id_type=MESH,
        )

    own_w = pltpu.make_async_copy(
        w_ref.at[:, pl.ds(pl.multiple_of(plane * width, 128), width)],
        w_all.at[pl.ds(pl.multiple_of(plane * depth, 128), depth)],
        w_recv.at[0],
    )

    queries = kv_all.at[:, pl.ds(2 * TILES, SLOTS)]

    def q_copy(step):
        there = lax.rem(me + step, FRAMES)
        row_there, column_there, core_there = where_is(there)
        return row_there < HEADS_HERE, pltpu.make_async_remote_copy(
            src_ref=q_ref.at[
                jnp.minimum(row_there, HEADS_HERE - 1), :, column_there * 2 + core_there
            ],
            dst_ref=queries.at[column * 2 + core, :, lax.rem(row_there - row + SIDE, SIDE)],
            send_sem=q_send.at[step],
            recv_sem=q_recv,
            device_id=(plane, there),
            device_id_type=MESH,
        )

    def to_rows(part, work):
        for hop in range(1, SIDE):

            @pl.when(lax.rem(row + hop, SIDE) < HEADS_HERE)
            def _():
                work(z_copy(part, hop))

    def send_q(step, carry):
        wanted, copy = q_copy(step)

        @pl.when(wanted)
        def _():
            copy.start()

        return carry

    def sent_q(step, carry):
        wanted, copy = q_copy(step)

        @pl.when(wanted)
        def _():
            copy.wait_send()

        return carry

    def send_small():
        for hop in range(1, PLANES):
            w_copy(hop).start()
        own_w.start()
        lax.fori_loop(1, FRAMES, send_q, 0)

    @pl.when(working)
    def _():
        own_copy.start()
        for side in range(2):
            y_copy(0, side).start()

    to_rows(0, lambda copy: copy.start())
    send_small()

    def next_rows(part):
        to_rows(part, lambda copy: copy.wait_send())
        if part + 1 < PARTS:
            to_rows(part + 1, lambda copy: copy.start())

    @pl.when(jnp.logical_not(working))
    def _():
        for part in range(PARTS):
            next_rows(part)

    @pl.when(working)
    def _():
        pltpu.make_async_copy(
            q_ref.at[own_row, :, column * 2 + core], queries.at[column * 2 + core, :, 0], q_recv
        ).start()
        own_copy.wait()
        core_copy(0, 0).start()

        def pass_on(number):
            for side in range(2):
                y_copy(number, side).wait_recv()
                far_copy(number, side).start()
                if number == PARTS:
                    far_copy(number, side, 1).start()
            for side in range(2):
                core_copy(number, sides[1 - side]).start()

        for part in range(PARTS):
            next_rows(part)
            for hop in range(1, SIDE):
                landed = kv_all.at[column * 2 + core, span(part), hop]
                pltpu.make_async_copy(landed, landed, z_recv.at[part, hop]).wait()
            for side in range(2):
                y_copy(part + 1, side).start()
            core_copy(part + 1, 0).start()
            pass_on(part)
        pass_on(PARTS)
        for number in range(PARTS + 1):
            for side in range(2):
                far_copy(number, side).wait_recv()
                if number == PARTS:
                    far_copy(number, side, 1).wait_recv()
            if number < PARTS:
                core_copy(number, 2).start()

    for hop in range(1, PLANES):
        w_copy(hop).wait_recv()
        w_core_copy(hop).start()

    @pl.when(working)
    def _():
        pltpu.make_async_copy(queries, queries, q_recv).wait()
        last = SIZES[-1]
        early = (2 * TILES + (2 * TILES - last) * (SIDE - 1)) // SIDE
        other = kv_all.at[pl.ds(0, SIDE), pl.ds(0, early)]
        pltpu.make_async_copy(other, other, core_recv).wait()
        other = kv_all.at[pl.ds(0, SIDE - 1), pl.ds(0, last), pl.ds(0, SIDE - 1)]
        pltpu.make_async_copy(other, other, last_recv).wait()
        for number in range(PARTS + 1):
            for side in range(2):
                y_copy(number, side).wait_send()
                far_copy(number, side).wait_send()
                if number == PARTS:
                    far_copy(number, side, 1).wait_send()
            for away in range(SIDE):
                if number < PARTS or away != 2:
                    core_copy(number, away).wait_send()

    own_w.wait()
    lax.fori_loop(1, FRAMES, sent_q, 0)
    for hop in range(1, PLANES):
        w_copy(hop).wait_send()
        w_core_copy(hop).wait()


def spread(q_parts, kv_parts, out_weight):
    depth, columns = out_weight.shape
    return pl.pallas_call(
        spread_kernel,
        out_shape=(
            jax.ShapeDtypeStruct((WORKERS, 2 * TILES + SLOTS, SIDE, SPOTS, DH), BF16),
            jax.ShapeDtypeStruct((depth * PLANES, columns // PLANES), BF16),
        ),
        in_specs=[pl.BlockSpec(memory_space=pl.ANY)] * 3,
        out_specs=(pl.BlockSpec(memory_space=pl.ANY),) * 2,
        scratch_shapes=[
            pltpu.SemaphoreType.DMA((FRAMES,)),
            pltpu.SemaphoreType.DMA,
            pltpu.SemaphoreType.DMA((PARTS, SIDE)),
            pltpu.SemaphoreType.DMA((PARTS, SIDE)),
            pltpu.SemaphoreType.DMA((PARTS + 1, 2)),
            pltpu.SemaphoreType.DMA((PARTS + 1, 2)),
            pltpu.SemaphoreType.DMA((PARTS + 1, 2, 2)),
            pltpu.SemaphoreType.DMA((PARTS + 1, 2, 2)),
            pltpu.SemaphoreType.DMA((PARTS + 1, SIDE)),
            pltpu.SemaphoreType.DMA,
            pltpu.SemaphoreType.DMA,
            pltpu.SemaphoreType.DMA((PLANES,)),
            pltpu.SemaphoreType.DMA((PLANES,)),
            pltpu.SemaphoreType.DMA((PLANES,)),
            pltpu.SemaphoreType.DMA((PLANES,)),
            pltpu.SemaphoreType.DMA,
        ],
        compiler_params=pltpu.CompilerParams(
            collective_id=0, has_side_effects=True, vmem_limit_bytes=57 * 1024 * 1024
        ),
    )(q_parts, kv_parts, out_weight)


def turned_rows(rows):
    to = lax.broadcasted_iota(jnp.int32, (rows, rows), 0)
    source = lax.broadcasted_iota(jnp.int32, (rows, rows), 1)
    group = WORKERS * SPOTS
    place = lax.div(lax.rem(to, group), SPOTS)
    wanted = to + (WORKERS - 1 - 2 * place) * SPOTS
    return jnp.where(source == wanted, 1.0, 0.0).astype(BF16)


def attend_kernel(
    list_ref, kv_hbm, o_ref, kv_ref, q_ref, keys_ref, base_ref, peak_ref, sum_ref,
    slot_of, first_of, listed_of, kv_sem,
):
    def bring(number, first, tiles):
        rows = pl.ds(first * PIECE, tiles * PIECE)
        return pltpu.make_async_copy(kv_hbm.at[:, rows], kv_ref.at[:, rows], kv_sem.at[number])

    chunks = TILES // CHUNK
    moves = [bring(number, number * CHUNK, CHUNK) for number in range(chunks)]
    moves.append(bring(chunks, 2 * TILES, SLOTS))
    moves.append(bring(chunks + 1, TILES, TILES))
    for move in moves:
        move.start()

    _, column, core = where_is(lax.axis_index("ctx"))

    def loop(count, work):
        def one(step, carry):
            work(step)
            return carry

        lax.fori_loop(0, count, one, 0)

    def rows_of(slot):
        return pl.ds(pl.multiple_of(slot * TILE, TILE), TILE)

    def tile_at(tile):
        start = pl.multiple_of(tile * PIECE, PIECE)
        return jnp.concatenate(
            [kv_ref[worker, pl.ds(start, PIECE), :] for worker in range(WORKERS)], axis=0
        )

    def enlist(slot, total):
        count = list_ref[SLOTS, slot]
        steps = lax.div(count + GROUP - 1, GROUP)

        def one(step, carry):
            slot_of[total + step] = slot
            first_of[total + step] = step * GROUP
            listed_of[total + step] = count - step * GROUP
            return carry

        lax.fori_loop(0, steps, one, 0)
        return total + steps

    total = lax.fori_loop(0, SLOTS, enlist, 0)
    for spare in range(BESIDE - 1):
        slot_of[total + spare] = 0
        first_of[total + spare] = 0
        listed_of[total + spare] = 0
    turns = lax.div(total + BESIDE - 1, BESIDE)
    busy = jnp.where(total > 0, 1, 0)

    def unpack(step):
        for u in range(GROUP):
            tile = step * GROUP + u
            keys_ref[tile] = tile_at(tile).T

    for number in range(chunks):
        moves[number].wait()
        steps = CHUNK // GROUP
        loop(busy * steps, lambda step: unpack(step + number * steps))
    moves[chunks].wait()

    def set_base(slot, base):
        base_ref[slot] = jnp.broadcast_to(base * SCALE2, (TILE, TILE))

    def own_base(step):
        for u in range(BESIDE):
            slot = step * BESIDE + u
            place = column * 2 + core
            late = jnp.where(slot < SLOTS // 2, 0, WORKERS - 1 - 2 * place)
            own = keys_ref[slot * WORKERS + place + late]
            query = tile_at(2 * TILES + slot)
            q_ref[rows_of(slot), :] = query
            scores = jnp.dot(query, own, preferred_element_type=F32)
            set_base(slot, jnp.max(scores, axis=1, keepdims=True))

    loop(busy * (SLOTS // BESIDE), own_base)
    moves[chunks + 1].wait()

    def tiles_of(number):
        slot, first = slot_of[number], first_of[number]
        return slot, [list_ref[slot, first + u] for u in range(GROUP)]

    def scores_of(slot, tiles):
        keys = jnp.concatenate([keys_ref[tile] for tile in tiles], axis=1)
        return jnp.dot(q_ref[rows_of(slot), :], keys, preferred_element_type=F32)

    def attend_steps(step):
        found = []
        for beside in range(BESIDE):
            number = step * BESIDE + beside
            slot, tiles = tiles_of(number)
            listed = listed_of[number]
            base = base_ref[slot]
            scores = scores_of(slot, tiles)
            weights, values = [], []
            for u in range(GROUP):
                part = scores[:, u * TILE : (u + 1) * TILE]
                weights.append(jnp.exp2(part * SCALE2 - base).astype(BF16))
                value = jnp.where(u < listed, tile_at(TILES + tiles[u]), 0).astype(BF16)
                ones = jnp.where(u < listed, 1.0, 0.0).astype(BF16)
                ones = jnp.broadcast_to(ones, (TILE, DH))
                values.append(jnp.concatenate([value, ones], axis=1))
            added = jnp.dot(
                jnp.concatenate(weights, axis=1),
                jnp.concatenate(values, axis=0),
                preferred_element_type=F32,
            )
            found.append((slot, added))
        for slot, added in found:
            sum_ref[slot] += added

    def peak_steps(step):
        for beside in range(BESIDE):
            slot, tiles = tiles_of(step * BESIDE + beside)
            scores = scores_of(slot, tiles)
            peak = peak_ref[slot]
            for u in range(GROUP):
                peak = jnp.maximum(peak, scores[:, u * TILE : (u + 1) * TILE])
            peak_ref[slot] = peak

    def attempt(number, needed):
        def clear(slot):
            sum_ref[slot] = jnp.zeros((TILE, 2 * DH), F32)
            peak_ref[slot] = jnp.full((TILE, TILE), LOW, F32)

        loop(needed * SLOTS, clear)
        loop(needed * turns, attend_steps)
        beyond = jnp.zeros((TILE, DH), F32)
        for slot in range(SLOTS):
            beyond = jnp.where(sum_ref[slot, :, DH:] <= FAR, beyond, 1.0)
        again = needed * jnp.where(jnp.max(beyond) > 0.0, 1, 0)
        loop(again * turns, peak_steps)

        def rebase(slot):
            set_base(slot, jnp.max(peak_ref[slot], axis=1, keepdims=True))

        loop(again * SLOTS, rebase)
        return again

    lax.fori_loop(0, 2, attempt, busy)

    def finish(step):
        for u in range(BESIDE):
            slot = step * BESIDE + u
            o_ref[rows_of(slot), :] = (sum_ref[slot, :, :DH] / sum_ref[slot, :, DH:]).astype(BF16)

    loop(busy * (SLOTS // BESIDE), finish)


def attend(lists, kv):
    most = SLOTS * (TILES // GROUP) + BESIDE
    return pl.pallas_call(
        attend_kernel,
        out_shape=jax.ShapeDtypeStruct((SLOTS * TILE, DH), BF16),
        in_specs=[pl.BlockSpec(memory_space=pltpu.SMEM), pl.BlockSpec(memory_space=pl.ANY)],
        out_specs=pl.BlockSpec(memory_space=pltpu.VMEM),
        scratch_shapes=[
            pltpu.VMEM(kv.shape, BF16),
            pltpu.VMEM((SLOTS * TILE, DH), BF16),
            pltpu.VMEM((TILES, DH, TILE), BF16),
            pltpu.VMEM((SLOTS, TILE, TILE), F32),
            pltpu.VMEM((SLOTS, TILE, TILE), F32),
            pltpu.VMEM((SLOTS, TILE, 2 * DH), F32),
            pltpu.SMEM((most,), jnp.int32),
            pltpu.SMEM((most,), jnp.int32),
            pltpu.SMEM((most,), jnp.int32),
            pltpu.SemaphoreType.DMA((TILES // CHUNK + 2,)),
        ],
        compiler_params=pltpu.CompilerParams(vmem_limit_bytes=50 * 1024 * 1024),
    )(lists, kv)


def collect_kernel(o_ref, attn, send, recv, x_send, x_recv):
    plane = lax.axis_index("heads")
    me = lax.axis_index("ctx")
    row, column, core = where_is(me)
    barrier = pltpu.get_barrier_semaphore()

    def greet(step, carry):
        pl.semaphore_signal(
            barrier, inc=1, device_id=(plane, lax.rem(me + step, FRAMES)), device_id_type=MESH
        )
        return carry

    lax.fori_loop(1, FRAMES, greet, 0)
    sides = (lax.rem(plane + 1, PLANES), lax.rem(plane + PLANES - 1, PLANES))
    for there in sides:
        pl.semaphore_signal(barrier, inc=1, device_id=(there, me), device_id_type=MESH)
    pl.semaphore_wait(barrier, FRAMES - 1 + 2)

    mine = jnp.minimum(row, HEADS_HERE - 1)
    goal = attn.at[plane * HEADS_HERE + mine, :, column * 2 + core]

    def rows_for(there):
        row_there, column_there, core_there = where_is(there)
        above = lax.rem(row - row_there + SIDE, SIDE)
        return o_ref.at[:, column_there * 2 + core_there, above]

    def back(step):
        there = lax.rem(me + step, FRAMES)
        return pltpu.make_async_remote_copy(
            src_ref=rows_for(there),
            dst_ref=goal,
            send_sem=send.at[step],
            recv_sem=recv.at[mine],
            device_id=(plane, there),
            device_id_type=MESH,
        )

    def start(step, carry):
        back(step).start()
        return carry

    def end(step, carry):
        back(step).wait_send()
        return carry

    working = row < HEADS_HERE

    @pl.when(working)
    def _():
        lax.fori_loop(1, FRAMES, start, 0)
        pltpu.make_async_copy(rows_for(me), goal, recv.at[mine]).start()

    cut = SLOTS // 2

    def near(head, side):
        part = attn.at[plane * HEADS_HERE + head]
        return pltpu.make_async_remote_copy(
            src_ref=part,
            dst_ref=part,
            send_sem=x_send.at[head, side],
            recv_sem=x_recv.at[head, side],
            device_id=(sides[side], me),
            device_id_type=MESH,
        )

    def far(head, side):
        part = attn.at[sides[1 - side] * HEADS_HERE + head]
        part = part.at[pl.ds(0, cut)] if side == 0 else part.at[pl.ds(cut, SLOTS - cut)]
        return pltpu.make_async_remote_copy(
            src_ref=part,
            dst_ref=part,
            send_sem=x_send.at[head, 2 + side],
            recv_sem=x_recv.at[head, 2 + side],
            device_id=(sides[side], me),
            device_id_type=MESH,
        )

    for head in range(HEADS_HERE):
        part = attn.at[plane * HEADS_HERE + head]
        pltpu.make_async_copy(part, part, recv.at[head]).wait()
        for side in range(2):
            near(head, side).start()
    for head in range(HEADS_HERE):
        for side in range(2):
            near(head, side).wait_recv()
            far(head, side).start()

    @pl.when(working)
    def _():
        lax.fori_loop(1, FRAMES, end, 0)

    for head in range(HEADS_HERE):
        for side in range(2):
            near(head, side).wait_send()
            far(head, side).wait()


def collect(attended):
    return pl.pallas_call(
        collect_kernel,
        out_shape=jax.ShapeDtypeStruct(
            (PLANES * HEADS_HERE, SLOTS, WORKERS, SPOTS, DH), BF16
        ),
        in_specs=[pl.BlockSpec(memory_space=pl.ANY)],
        out_specs=pl.BlockSpec(memory_space=pl.ANY),
        scratch_shapes=[
            pltpu.SemaphoreType.DMA((FRAMES,)),
            pltpu.SemaphoreType.DMA((HEADS_HERE,)),
            pltpu.SemaphoreType.DMA((HEADS_HERE, 4)),
            pltpu.SemaphoreType.DMA((HEADS_HERE, 4)),
        ],
        compiler_params=pltpu.CompilerParams(
            collective_id=1, has_side_effects=True, vmem_limit_bytes=4 * 1024 * 1024
        ),
    )(attended)


def project_kernel(attn_ref, w_ref, out_ref):
    heads = attn_ref.shape[0]
    half = out_ref.shape[0] // 2
    wide = jnp.concatenate([attn_ref[h] for h in range(heads)], axis=1)
    block = 256
    for first in range(0, out_ref.shape[1], block):
        columns = slice(first, first + block)
        mixed = jnp.dot(wide, w_ref[:, columns], preferred_element_type=F32)
        out_ref[:half, columns] = mixed[:half].astype(BF16)
        group, pair = WORKERS * SPOTS, 2 * SPOTS
        blocks = []
        for start in range(half, 2 * half, group):
            for last in range(start + group, start, -pair):
                blocks.append(pltpu.roll(mixed[last - pair : last], SPOTS, 0))
        out_ref[half:, columns] = jnp.concatenate(blocks, axis=0).astype(BF16)


def project(attn, weight, rows):
    return pl.pallas_call(
        project_kernel,
        out_shape=jax.ShapeDtypeStruct((rows, weight.shape[1]), BF16),
        in_specs=[pl.BlockSpec(memory_space=pltpu.VMEM)] * 2,
        out_specs=pl.BlockSpec(memory_space=pltpu.VMEM),
        compiler_params=pltpu.CompilerParams(vmem_limit_bytes=24 * 1024 * 1024),
    )(attn, weight)


def arrange_kernel(
    pattern_ref, mask_hbm, q_hbm, k_hbm, v_hbm, q_out, kv_out, list_ref,
    mask_ref, q_ref, k_ref, v_ref, sems,
):
    sources = (mask_hbm, q_hbm, k_hbm, v_hbm)
    targets = (mask_ref, q_ref, k_ref, v_ref)
    moves = [
        pltpu.make_async_copy(source, target, sems.at[i])
        for i, (source, target) in enumerate(zip(sources, targets))
    ]
    for move in moves:
        move.start()
    me = lax.axis_index("ctx")
    row, column, core = where_is(me)
    moves[0].wait()
    pattern = pattern_ref[jnp.minimum(row, HEADS_HERE - 1)]
    masks = []
    place = column * 2 + core
    tiles = [
        slot * WORKERS + (place if slot < SLOTS // 2 else WORKERS - 1 - place)
        for slot in range(SLOTS)
    ]
    for tile in tiles:
        masks.append(jnp.where(row < HEADS_HERE, mask_ref[pattern, pl.ds(tile, 1), :], 0))
    seen = jnp.concatenate(masks, axis=0) == 1
    seen = jnp.where(seen, 1.0, 0.0).astype(F32)
    down = lax.broadcasted_iota(jnp.int32, (TILES, TILES), 0)
    along = lax.broadcasted_iota(jnp.int32, (TILES, TILES), 1)
    both = (((1,), (1,)), ((), ()))
    upto = jnp.where(along <= down, 1.0, 0.0).astype(BF16)
    same = jnp.where(along == down, 1.0, 0.0).astype(BF16)
    rank = lax.dot_general(upto, seen.astype(BF16), both, preferred_element_type=F32)
    turned = lax.dot_general(same, seen.astype(BF16), both, preferred_element_type=F32)
    rank = rank.astype(jnp.int32)
    spot = jnp.where(turned > 0.5, rank - 1, -1)
    for slot in range(SLOTS):
        hit = spot[:, slot : slot + 1] == along
        listed = jnp.sum(jnp.where(hit, down, 0), axis=0, keepdims=True)
        spare = along[:1, :] >= rank[TILES - 1 :, slot : slot + 1]
        list_ref[slot : slot + 1, :] = jnp.where(spare, tiles[slot], listed)
    last = jnp.concatenate(
        [rank[TILES - 1 :, :], jnp.zeros((1, TILES - SLOTS), jnp.int32)], axis=1
    )
    list_ref[SLOTS : SLOTS + 1, :] = last


    rows = q_ref.shape[0]
    for move, source, target, first in (
        (moves[1], q_ref, q_out, 0),
        (moves[2], k_ref, kv_out, 0),
        (moves[3], v_ref, kv_out, rows),
    ):
        move.wait()
        for head in range(HEADS_HERE):
            target[head, first : first + rows, :] = source[:, head * DH : (head + 1) * DH]
    half = rows // 2
    later = jnp.dot(turned_rows(half), q_ref[half:, :], preferred_element_type=F32).astype(BF16)
    for head in range(HEADS_HERE):
        q_out[head, half:, :] = later[:, head * DH : (head + 1) * DH]


def arrange(head_pattern, tile_masks, queries, key_rows, value_rows):
    rows = queries.shape[0]
    return pl.pallas_call(
        arrange_kernel,
        out_shape=(
            jax.ShapeDtypeStruct((HEADS_HERE, rows, DH), BF16),
            jax.ShapeDtypeStruct((HEADS_HERE, 2 * rows, DH), BF16),
            jax.ShapeDtypeStruct((SLOTS + 1, TILES), jnp.int32),
        ),
        in_specs=[pl.BlockSpec(memory_space=pltpu.SMEM)]
        + [pl.BlockSpec(memory_space=pl.ANY)] * 4,
        out_specs=(pl.BlockSpec(memory_space=pltpu.VMEM),) * 3,
        scratch_shapes=[
            pltpu.VMEM(tile_masks.shape, jnp.int32),
            pltpu.VMEM(queries.shape, BF16),
            pltpu.VMEM(queries.shape, BF16),
            pltpu.VMEM(queries.shape, BF16),
            pltpu.SemaphoreType.DMA((4,)),
        ],
        compiler_params=pltpu.CompilerParams(vmem_limit_bytes=57 * 1024 * 1024),
    )(head_pattern, tile_masks, queries, key_rows, value_rows)


def body(queries, key_rows, value_rows, out_weight, tile_masks, head_pattern):
    rows = queries.shape[0]
    q_parts, kv_parts, lists = arrange(head_pattern, tile_masks, queries, key_rows, value_rows)
    kv_all, w_all = spread(
        q_parts.reshape(HEADS_HERE, SLOTS, WORKERS, SPOTS, DH),
        kv_parts.reshape(HEADS_HERE, 2 * TILES, SPOTS, DH),
        out_weight,
    )
    attended = attend(lists, kv_all.reshape(WORKERS, (2 * TILES + SLOTS) * PIECE, DH))
    attn = collect(attended.reshape(SLOTS, WORKERS, SIDE, SPOTS, DH))
    attn = attn.reshape(PLANES * HEADS_HERE, rows, DH)
    return project(attn, w_all, rows)


def solution(mesh):
    placed = (
        P("ctx", "heads"),
        P("ctx", "heads"),
        P("ctx", "heads"),
        P("heads", None),
        P(),
        P("heads"),
    )
    return jax.shard_map(
        body, mesh=mesh, in_specs=placed, out_specs=P("ctx", "heads"), check_vma=False
    )
```

```python
import math

import jax
import jax.numpy as jnp
from jax import lax
from jax.experimental import pallas as pl
from jax.experimental.pallas import tpu as pltpu
from jax.sharding import PartitionSpec as P

MESH = pl.DeviceIdType.MESH
DH = 128
TILE = 128
SPOTS = 4
FRAMES = 32
TILES = 128
PLANES = 4
SIDE = 4
HEADS_HERE = 3
WORKERS = 2 * SIDE
SLOTS = TILES // WORKERS
SIZES = (64, 64, 64, 64)
PARTS = len(SIZES)
PIECE = TILE // WORKERS
GROUP = 8
CHUNK = 32
BESIDE = 4
FAR = 2.0**64
LOW = -1e30
SCALE2 = math.log2(math.e) / math.sqrt(DH)
BF16 = jnp.bfloat16
F32 = jnp.float32


def where_is(device):
    return lax.div(device, WORKERS), lax.rem(lax.div(device, 2), SIDE), lax.rem(device, 2)


def device_at(row, column, core):
    return (lax.rem(row, SIDE) * SIDE + lax.rem(column, SIDE)) * 2 + core


def spread_kernel(
    q_ref, kv_ref, w_ref, kv_all, w_all,
    q_send, q_recv, z_send, z_recv, y_send, y_recv, far_send, far_recv,
    core_send, core_recv, w_send, w_recv, w_core_send, w_core_recv, own_sem,
):
    plane = lax.axis_index("heads")
    me = lax.axis_index("ctx")
    row, column, core = where_is(me)
    working = row < HEADS_HERE
    own_row = jnp.minimum(row, HEADS_HERE - 1)
    depth = w_ref.shape[0]
    width = w_all.shape[1]
    sides = (1, SIDE - 1)

    barrier = pltpu.get_barrier_semaphore()

    def greet(step, carry):
        pl.semaphore_signal(
            barrier, inc=1, device_id=(plane, lax.rem(me + step, FRAMES)), device_id_type=MESH
        )
        return carry

    lax.fori_loop(1, FRAMES, greet, 0)
    for hop in range(1, PLANES):
        pl.semaphore_signal(
            barrier, inc=1, device_id=(lax.rem(plane + hop, PLANES), me), device_id_type=MESH
        )
    pl.semaphore_wait(barrier, FRAMES - 1 + PLANES - 1)

    def span(part):
        return pl.ds(sum(SIZES[:part]), SIZES[part])

    own_copy = pltpu.make_async_copy(
        kv_ref.at[own_row], kv_all.at[column * 2 + core, pl.ds(0, 2 * TILES), 0], own_sem
    )

    def z_copy(part, hop):
        there = lax.rem(row + hop, SIDE)
        return pltpu.make_async_remote_copy(
            src_ref=kv_ref.at[there, span(part)],
            dst_ref=kv_all.at[column * 2 + core, span(part), hop],
            send_sem=z_send.at[part, hop],
            recv_sem=z_recv.at[part, hop],
            device_id=(plane, device_at(there, column, core)),
            device_id_type=MESH,
        )

    def piece(number, away):
        source = kv_all.at[lax.rem(column + away, SIDE) * 2 + core]
        if number == 0:
            return source.at[pl.ds(0, 2 * TILES), 0]
        return source.at[span(number - 1), pl.ds(1, SIDE - 1)]

    def y_copy(number, side):
        return pltpu.make_async_remote_copy(
            src_ref=kv_ref.at[own_row] if number == 0 else piece(number, 0),
            dst_ref=piece(number, 0),
            send_sem=y_send.at[number, side],
            recv_sem=y_recv.at[number, side],
            device_id=(plane, device_at(row, column + sides[side], core)),
            device_id_type=MESH,
        )

    def far_copy(number, side):
        source = kv_all.at[lax.rem(column + sides[1 - side], SIDE) * 2 + core]
        first, count = (0, 2 * TILES) if number == 0 else (sum(SIZES[: number - 1]), SIZES[number - 1])
        share = count // 2
        tiles = pl.ds(first + share, count - share) if side else pl.ds(first, share)
        chunk = source.at[tiles, 0] if number == 0 else source.at[tiles, pl.ds(1, SIDE - 1)]
        return pltpu.make_async_remote_copy(
            src_ref=chunk,
            dst_ref=chunk,
            send_sem=far_send.at[number, side],
            recv_sem=far_recv.at[number, side],
            device_id=(plane, device_at(row, column + sides[side], core)),
            device_id_type=MESH,
        )

    def core_copy(number, away):
        return pltpu.make_async_remote_copy(
            src_ref=piece(number, away),
            dst_ref=piece(number, away),
            send_sem=core_send.at[number, away],
            recv_sem=core_recv,
            device_id=(plane, device_at(row, column, 1 - core)),
            device_id_type=MESH,
        )

    half = depth // 2

    def w_rows(source, part):
        return w_all.at[pl.ds(pl.multiple_of(source * depth + part * half, 16), half)]

    def w_copy(hop):
        there = lax.rem(plane + hop, PLANES)
        return pltpu.make_async_remote_copy(
            src_ref=w_ref.at[
                pl.ds(pl.multiple_of(core * half, 16), half),
                pl.ds(pl.multiple_of(there * width, 128), width),
            ],
            dst_ref=w_rows(plane, core),
            send_sem=w_send.at[hop],
            recv_sem=w_recv.at[hop],
            device_id=(there, me),
            device_id_type=MESH,
        )

    def w_core_copy(hop):
        rows = w_rows(lax.rem(plane + PLANES - hop, PLANES), core)
        return pltpu.make_async_remote_copy(
            src_ref=rows,
            dst_ref=rows,
            send_sem=w_core_send.at[hop],
            recv_sem=w_core_recv.at[hop],
            device_id=(plane, device_at(row, column, 1 - core)),
            device_id_type=MESH,
        )

    own_w = pltpu.make_async_copy(
        w_ref.at[:, pl.ds(pl.multiple_of(plane * width, 128), width)],
        w_all.at[pl.ds(pl.multiple_of(plane * depth, 128), depth)],
        w_recv.at[0],
    )

    queries = kv_all.at[:, pl.ds(2 * TILES, SLOTS)]

    def q_copy(step):
        there = lax.rem(me + step, FRAMES)
        row_there, column_there, core_there = where_is(there)
        return row_there < HEADS_HERE, pltpu.make_async_remote_copy(
            src_ref=q_ref.at[
                jnp.minimum(row_there, HEADS_HERE - 1), :, column_there * 2 + core_there
            ],
            dst_ref=queries.at[column * 2 + core, :, lax.rem(row_there - row + SIDE, SIDE)],
            send_sem=q_send.at[step],
            recv_sem=q_recv,
            device_id=(plane, there),
            device_id_type=MESH,
        )

    def to_rows(part, work):
        for hop in range(1, SIDE):

            @pl.when(lax.rem(row + hop, SIDE) < HEADS_HERE)
            def _():
                work(z_copy(part, hop))

    def send_q(step, carry):
        wanted, copy = q_copy(step)

        @pl.when(wanted)
        def _():
            copy.start()

        return carry

    def sent_q(step, carry):
        wanted, copy = q_copy(step)

        @pl.when(wanted)
        def _():
            copy.wait_send()

        return carry

    def send_small():
        for hop in range(1, PLANES):
            w_copy(hop).start()
        own_w.start()
        lax.fori_loop(1, FRAMES, send_q, 0)

    @pl.when(working)
    def _():
        own_copy.start()
        for side in range(2):
            y_copy(0, side).start()

    to_rows(0, lambda copy: copy.start())
    send_small()

    def next_rows(part):
        to_rows(part, lambda copy: copy.wait_send())
        if part + 1 < PARTS:
            to_rows(part + 1, lambda copy: copy.start())

    @pl.when(jnp.logical_not(working))
    def _():
        for part in range(PARTS):
            next_rows(part)

    @pl.when(working)
    def _():
        pltpu.make_async_copy(
            q_ref.at[own_row, :, column * 2 + core], queries.at[column * 2 + core, :, 0], q_recv
        ).start()
        own_copy.wait()
        core_copy(0, 0).start()

        def pass_on(number):
            for side in range(2):
                y_copy(number, side).wait_recv()
                far_copy(number, side).start()
            for side in range(2):
                core_copy(number, sides[1 - side]).start()

        for part in range(PARTS):
            next_rows(part)
            for hop in range(1, SIDE):
                landed = kv_all.at[column * 2 + core, span(part), hop]
                pltpu.make_async_copy(landed, landed, z_recv.at[part, hop]).wait()
            for side in range(2):
                y_copy(part + 1, side).start()
            core_copy(part + 1, 0).start()
            pass_on(part)
        pass_on(PARTS)
        for number in range(PARTS + 1):
            for side in range(2):
                far_copy(number, side).wait_recv()
            core_copy(number, 2).start()

    for hop in range(1, PLANES):
        w_copy(hop).wait_recv()
        w_core_copy(hop).start()

    @pl.when(working)
    def _():
        pltpu.make_async_copy(queries, queries, q_recv).wait()
        other = kv_all.at[pl.ds(0, SIDE), pl.ds(0, 2 * TILES)]
        pltpu.make_async_copy(other, other, core_recv).wait()
        for number in range(PARTS + 1):
            for side in range(2):
                y_copy(number, side).wait_send()
                far_copy(number, side).wait_send()
            for away in range(SIDE):
                core_copy(number, away).wait_send()

    own_w.wait()
    lax.fori_loop(1, FRAMES, sent_q, 0)
    for hop in range(1, PLANES):
        w_copy(hop).wait_send()
        w_core_copy(hop).wait()


def spread(q_parts, kv_parts, out_weight):
    depth, columns = out_weight.shape
    return pl.pallas_call(
        spread_kernel,
        out_shape=(
            jax.ShapeDtypeStruct((WORKERS, 2 * TILES + SLOTS, SIDE, SPOTS, DH), BF16),
            jax.ShapeDtypeStruct((depth * PLANES, columns // PLANES), BF16),
        ),
        in_specs=[pl.BlockSpec(memory_space=pl.ANY)] * 3,
        out_specs=(pl.BlockSpec(memory_space=pl.ANY),) * 2,
        scratch_shapes=[
            pltpu.SemaphoreType.DMA((FRAMES,)),
            pltpu.SemaphoreType.DMA,
            pltpu.SemaphoreType.DMA((PARTS, SIDE)),
            pltpu.SemaphoreType.DMA((PARTS, SIDE)),
            pltpu.SemaphoreType.DMA((PARTS + 1, 2)),
            pltpu.SemaphoreType.DMA((PARTS + 1, 2)),
            pltpu.SemaphoreType.DMA((PARTS + 1, 2)),
            pltpu.SemaphoreType.DMA((PARTS + 1, 2)),
            pltpu.SemaphoreType.DMA((PARTS + 1, SIDE)),
            pltpu.SemaphoreType.DMA,
            pltpu.SemaphoreType.DMA((PLANES,)),
            pltpu.SemaphoreType.DMA((PLANES,)),
            pltpu.SemaphoreType.DMA((PLANES,)),
            pltpu.SemaphoreType.DMA((PLANES,)),
            pltpu.SemaphoreType.DMA,
        ],
        compiler_params=pltpu.CompilerParams(
            collective_id=0, has_side_effects=True, vmem_limit_bytes=57 * 1024 * 1024
        ),
    )(q_parts, kv_parts, out_weight)


def turned_rows(rows):
    to = lax.broadcasted_iota(jnp.int32, (rows, rows), 0)
    source = lax.broadcasted_iota(jnp.int32, (rows, rows), 1)
    group = WORKERS * SPOTS
    place = lax.div(lax.rem(to, group), SPOTS)
    wanted = to + (WORKERS - 1 - 2 * place) * SPOTS
    return jnp.where(source == wanted, 1.0, 0.0).astype(BF16)


def attend_kernel(
    list_ref, kv_hbm, o_ref, kv_ref, q_ref, keys_ref, base_ref, peak_ref, sum_ref,
    slot_of, first_of, listed_of, kv_sem,
):
    def bring(number, first, tiles):
        rows = pl.ds(first * PIECE, tiles * PIECE)
        return pltpu.make_async_copy(kv_hbm.at[:, rows], kv_ref.at[:, rows], kv_sem.at[number])

    chunks = TILES // CHUNK
    moves = [bring(number, number * CHUNK, CHUNK) for number in range(chunks)]
    moves.append(bring(chunks, 2 * TILES, SLOTS))
    moves.append(bring(chunks + 1, TILES, TILES))
    for move in moves:
        move.start()

    _, column, core = where_is(lax.axis_index("ctx"))

    def loop(count, work):
        def one(step, carry):
            work(step)
            return carry

        lax.fori_loop(0, count, one, 0)

    def rows_of(slot):
        return pl.ds(pl.multiple_of(slot * TILE, TILE), TILE)

    def tile_at(tile):
        start = pl.multiple_of(tile * PIECE, PIECE)
        return jnp.concatenate(
            [kv_ref[worker, pl.ds(start, PIECE), :] for worker in range(WORKERS)], axis=0
        )

    def enlist(slot, total):
        count = list_ref[SLOTS, slot]
        steps = lax.div(count + GROUP - 1, GROUP)

        def one(step, carry):
            slot_of[total + step] = slot
            first_of[total + step] = step * GROUP
            listed_of[total + step] = count - step * GROUP
            return carry

        lax.fori_loop(0, steps, one, 0)
        return total + steps

    total = lax.fori_loop(0, SLOTS, enlist, 0)
    for spare in range(BESIDE - 1):
        slot_of[total + spare] = 0
        first_of[total + spare] = 0
        listed_of[total + spare] = 0
    turns = lax.div(total + BESIDE - 1, BESIDE)
    busy = jnp.where(total > 0, 1, 0)

    def unpack(step):
        for u in range(GROUP):
            tile = step * GROUP + u
            keys_ref[tile] = tile_at(tile).T

    for number in range(chunks):
        moves[number].wait()
        steps = CHUNK // GROUP
        loop(busy * steps, lambda step: unpack(step + number * steps))
    moves[chunks].wait()

    def set_base(slot, base):
        base_ref[slot] = jnp.broadcast_to(base * SCALE2, (TILE, TILE))

    def own_base(step):
        for u in range(BESIDE):
            slot = step * BESIDE + u
            place = column * 2 + core
            late = jnp.where(slot < SLOTS // 2, 0, WORKERS - 1 - 2 * place)
            own = keys_ref[slot * WORKERS + place + late]
            query = tile_at(2 * TILES + slot)
            q_ref[rows_of(slot), :] = query
            scores = jnp.dot(query, own, preferred_element_type=F32)
            set_base(slot, jnp.max(scores, axis=1, keepdims=True))

    loop(busy * (SLOTS // BESIDE), own_base)
    moves[chunks + 1].wait()

    def tiles_of(number):
        slot, first = slot_of[number], first_of[number]
        return slot, [list_ref[slot, first + u] for u in range(GROUP)]

    def scores_of(slot, tiles):
        keys = jnp.concatenate([keys_ref[tile] for tile in tiles], axis=1)
        return jnp.dot(q_ref[rows_of(slot), :], keys, preferred_element_type=F32)

    def attend_steps(step):
        found = []
        for beside in range(BESIDE):
            number = step * BESIDE + beside
            slot, tiles = tiles_of(number)
            listed = listed_of[number]
            base = base_ref[slot]
            scores = scores_of(slot, tiles)
            weights, values = [], []
            for u in range(GROUP):
                part = scores[:, u * TILE : (u + 1) * TILE]
                weights.append(jnp.exp2(part * SCALE2 - base).astype(BF16))
                value = jnp.where(u < listed, tile_at(TILES + tiles[u]), 0).astype(BF16)
                ones = jnp.where(u < listed, 1.0, 0.0).astype(BF16)
                ones = jnp.broadcast_to(ones, (TILE, DH))
                values.append(jnp.concatenate([value, ones], axis=1))
            added = jnp.dot(
                jnp.concatenate(weights, axis=1),
                jnp.concatenate(values, axis=0),
                preferred_element_type=F32,
            )
            found.append((slot, added))
        for slot, added in found:
            sum_ref[slot] += added

    def peak_steps(step):
        for beside in range(BESIDE):
            slot, tiles = tiles_of(step * BESIDE + beside)
            scores = scores_of(slot, tiles)
            peak = peak_ref[slot]
            for u in range(GROUP):
                peak = jnp.maximum(peak, scores[:, u * TILE : (u + 1) * TILE])
            peak_ref[slot] = peak

    def attempt(number, needed):
        def clear(slot):
            sum_ref[slot] = jnp.zeros((TILE, 2 * DH), F32)
            peak_ref[slot] = jnp.full((TILE, TILE), LOW, F32)

        loop(needed * SLOTS, clear)
        loop(needed * turns, attend_steps)
        beyond = jnp.zeros((TILE, DH), F32)
        for slot in range(SLOTS):
            beyond = jnp.where(sum_ref[slot, :, DH:] <= FAR, beyond, 1.0)
        again = needed * jnp.where(jnp.max(beyond) > 0.0, 1, 0)
        loop(again * turns, peak_steps)

        def rebase(slot):
            set_base(slot, jnp.max(peak_ref[slot], axis=1, keepdims=True))

        loop(again * SLOTS, rebase)
        return again

    lax.fori_loop(0, 2, attempt, busy)

    def finish(step):
        for u in range(BESIDE):
            slot = step * BESIDE + u
            o_ref[rows_of(slot), :] = (sum_ref[slot, :, :DH] / sum_ref[slot, :, DH:]).astype(BF16)

    loop(busy * (SLOTS // BESIDE), finish)


def attend(lists, kv):
    most = SLOTS * (TILES // GROUP) + BESIDE
    return pl.pallas_call(
        attend_kernel,
        out_shape=jax.ShapeDtypeStruct((SLOTS * TILE, DH), BF16),
        in_specs=[pl.BlockSpec(memory_space=pltpu.SMEM), pl.BlockSpec(memory_space=pl.ANY)],
        out_specs=pl.BlockSpec(memory_space=pltpu.VMEM),
        scratch_shapes=[
            pltpu.VMEM(kv.shape, BF16),
            pltpu.VMEM((SLOTS * TILE, DH), BF16),
            pltpu.VMEM((TILES, DH, TILE), BF16),
            pltpu.VMEM((SLOTS, TILE, TILE), F32),
            pltpu.VMEM((SLOTS, TILE, TILE), F32),
            pltpu.VMEM((SLOTS, TILE, 2 * DH), F32),
            pltpu.SMEM((most,), jnp.int32),
            pltpu.SMEM((most,), jnp.int32),
            pltpu.SMEM((most,), jnp.int32),
            pltpu.SemaphoreType.DMA((TILES // CHUNK + 2,)),
        ],
        compiler_params=pltpu.CompilerParams(vmem_limit_bytes=50 * 1024 * 1024),
    )(lists, kv)


def collect_kernel(o_ref, attn, send, recv, x_send, x_recv):
    plane = lax.axis_index("heads")
    me = lax.axis_index("ctx")
    row, column, core = where_is(me)
    barrier = pltpu.get_barrier_semaphore()

    def greet(step, carry):
        pl.semaphore_signal(
            barrier, inc=1, device_id=(plane, lax.rem(me + step, FRAMES)), device_id_type=MESH
        )
        return carry

    lax.fori_loop(1, FRAMES, greet, 0)
    sides = (lax.rem(plane + 1, PLANES), lax.rem(plane + PLANES - 1, PLANES))
    for there in sides:
        pl.semaphore_signal(barrier, inc=1, device_id=(there, me), device_id_type=MESH)
    pl.semaphore_wait(barrier, FRAMES - 1 + 2)

    mine = jnp.minimum(row, HEADS_HERE - 1)
    goal = attn.at[plane * HEADS_HERE + mine, :, column * 2 + core]

    def rows_for(there):
        row_there, column_there, core_there = where_is(there)
        above = lax.rem(row - row_there + SIDE, SIDE)
        return o_ref.at[:, column_there * 2 + core_there, above]

    def back(step):
        there = lax.rem(me + step, FRAMES)
        return pltpu.make_async_remote_copy(
            src_ref=rows_for(there),
            dst_ref=goal,
            send_sem=send.at[step],
            recv_sem=recv.at[mine],
            device_id=(plane, there),
            device_id_type=MESH,
        )

    def start(step, carry):
        back(step).start()
        return carry

    def end(step, carry):
        back(step).wait_send()
        return carry

    working = row < HEADS_HERE

    @pl.when(working)
    def _():
        lax.fori_loop(1, FRAMES, start, 0)
        pltpu.make_async_copy(rows_for(me), goal, recv.at[mine]).start()

    cut = SLOTS // 2

    def near(head, side):
        part = attn.at[plane * HEADS_HERE + head]
        return pltpu.make_async_remote_copy(
            src_ref=part,
            dst_ref=part,
            send_sem=x_send.at[head, side],
            recv_sem=x_recv.at[head, side],
            device_id=(sides[side], me),
            device_id_type=MESH,
        )

    def far(head, side):
        part = attn.at[sides[1 - side] * HEADS_HERE + head]
        part = part.at[pl.ds(0, cut)] if side == 0 else part.at[pl.ds(cut, SLOTS - cut)]
        return pltpu.make_async_remote_copy(
            src_ref=part,
            dst_ref=part,
            send_sem=x_send.at[head, 2 + side],
            recv_sem=x_recv.at[head, 2 + side],
            device_id=(sides[side], me),
            device_id_type=MESH,
        )

    for head in range(HEADS_HERE):
        part = attn.at[plane * HEADS_HERE + head]
        pltpu.make_async_copy(part, part, recv.at[head]).wait()
        for side in range(2):
            near(head, side).start()
    for head in range(HEADS_HERE):
        for side in range(2):
            near(head, side).wait_recv()
            far(head, side).start()

    @pl.when(working)
    def _():
        lax.fori_loop(1, FRAMES, end, 0)

    for head in range(HEADS_HERE):
        for side in range(2):
            near(head, side).wait_send()
            far(head, side).wait()


def collect(attended):
    return pl.pallas_call(
        collect_kernel,
        out_shape=jax.ShapeDtypeStruct(
            (PLANES * HEADS_HERE, SLOTS, WORKERS, SPOTS, DH), BF16
        ),
        in_specs=[pl.BlockSpec(memory_space=pl.ANY)],
        out_specs=pl.BlockSpec(memory_space=pl.ANY),
        scratch_shapes=[
            pltpu.SemaphoreType.DMA((FRAMES,)),
            pltpu.SemaphoreType.DMA((HEADS_HERE,)),
            pltpu.SemaphoreType.DMA((HEADS_HERE, 4)),
            pltpu.SemaphoreType.DMA((HEADS_HERE, 4)),
        ],
        compiler_params=pltpu.CompilerParams(
            collective_id=1, has_side_effects=True, vmem_limit_bytes=4 * 1024 * 1024
        ),
    )(attended)


def project_kernel(attn_ref, w_ref, out_ref):
    heads = attn_ref.shape[0]
    half = out_ref.shape[0] // 2
    wide = jnp.concatenate([attn_ref[h] for h in range(heads)], axis=1)
    block = 256
    for first in range(0, out_ref.shape[1], block):
        columns = slice(first, first + block)
        mixed = jnp.dot(wide, w_ref[:, columns], preferred_element_type=F32)
        out_ref[:half, columns] = mixed[:half].astype(BF16)
        group, pair = WORKERS * SPOTS, 2 * SPOTS
        blocks = []
        for start in range(half, 2 * half, group):
            for last in range(start + group, start, -pair):
                blocks.append(pltpu.roll(mixed[last - pair : last], SPOTS, 0))
        out_ref[half:, columns] = jnp.concatenate(blocks, axis=0).astype(BF16)


def project(attn, weight, rows):
    return pl.pallas_call(
        project_kernel,
        out_shape=jax.ShapeDtypeStruct((rows, weight.shape[1]), BF16),
        in_specs=[pl.BlockSpec(memory_space=pltpu.VMEM)] * 2,
        out_specs=pl.BlockSpec(memory_space=pltpu.VMEM),
        compiler_params=pltpu.CompilerParams(vmem_limit_bytes=24 * 1024 * 1024),
    )(attn, weight)


def arrange_kernel(
    pattern_ref, mask_hbm, q_hbm, k_hbm, v_hbm, q_out, kv_out, list_ref,
    mask_ref, q_ref, k_ref, v_ref, sems,
):
    sources = (mask_hbm, q_hbm, k_hbm, v_hbm)
    targets = (mask_ref, q_ref, k_ref, v_ref)
    moves = [
        pltpu.make_async_copy(source, target, sems.at[i])
        for i, (source, target) in enumerate(zip(sources, targets))
    ]
    for move in moves:
        move.start()
    me = lax.axis_index("ctx")
    row, column, core = where_is(me)
    moves[0].wait()
    pattern = pattern_ref[jnp.minimum(row, HEADS_HERE - 1)]
    masks = []
    place = column * 2 + core
    tiles = [
        slot * WORKERS + (place if slot < SLOTS // 2 else WORKERS - 1 - place)
        for slot in range(SLOTS)
    ]
    for tile in tiles:
        masks.append(jnp.where(row < HEADS_HERE, mask_ref[pattern, pl.ds(tile, 1), :], 0))
    seen = jnp.concatenate(masks, axis=0) == 1
    seen = jnp.where(seen, 1.0, 0.0).astype(F32)
    down = lax.broadcasted_iota(jnp.int32, (TILES, TILES), 0)
    along = lax.broadcasted_iota(jnp.int32, (TILES, TILES), 1)
    both = (((1,), (1,)), ((), ()))
    upto = jnp.where(along <= down, 1.0, 0.0).astype(BF16)
    same = jnp.where(along == down, 1.0, 0.0).astype(BF16)
    rank = lax.dot_general(upto, seen.astype(BF16), both, preferred_element_type=F32)
    turned = lax.dot_general(same, seen.astype(BF16), both, preferred_element_type=F32)
    rank = rank.astype(jnp.int32)
    spot = jnp.where(turned > 0.5, rank - 1, -1)
    for slot in range(SLOTS):
        hit = spot[:, slot : slot + 1] == along
        listed = jnp.sum(jnp.where(hit, down, 0), axis=0, keepdims=True)
        spare = along[:1, :] >= rank[TILES - 1 :, slot : slot + 1]
        list_ref[slot : slot + 1, :] = jnp.where(spare, tiles[slot], listed)
    last = jnp.concatenate(
        [rank[TILES - 1 :, :], jnp.zeros((1, TILES - SLOTS), jnp.int32)], axis=1
    )
    list_ref[SLOTS : SLOTS + 1, :] = last


    rows = q_ref.shape[0]
    for move, source, target, first in (
        (moves[1], q_ref, q_out, 0),
        (moves[2], k_ref, kv_out, 0),
        (moves[3], v_ref, kv_out, rows),
    ):
        move.wait()
        for head in range(HEADS_HERE):
            target[head, first : first + rows, :] = source[:, head * DH : (head + 1) * DH]
    half = rows // 2
    later = jnp.dot(turned_rows(half), q_ref[half:, :], preferred_element_type=F32).astype(BF16)
    for head in range(HEADS_HERE):
        q_out[head, half:, :] = later[:, head * DH : (head + 1) * DH]


def arrange(head_pattern, tile_masks, queries, key_rows, value_rows):
    rows = queries.shape[0]
    return pl.pallas_call(
        arrange_kernel,
        out_shape=(
            jax.ShapeDtypeStruct((HEADS_HERE, rows, DH), BF16),
            jax.ShapeDtypeStruct((HEADS_HERE, 2 * rows, DH), BF16),
            jax.ShapeDtypeStruct((SLOTS + 1, TILES), jnp.int32),
        ),
        in_specs=[pl.BlockSpec(memory_space=pltpu.SMEM)]
        + [pl.BlockSpec(memory_space=pl.ANY)] * 4,
        out_specs=(pl.BlockSpec(memory_space=pltpu.VMEM),) * 3,
        scratch_shapes=[
            pltpu.VMEM(tile_masks.shape, jnp.int32),
            pltpu.VMEM(queries.shape, BF16),
            pltpu.VMEM(queries.shape, BF16),
            pltpu.VMEM(queries.shape, BF16),
            pltpu.SemaphoreType.DMA((4,)),
        ],
        compiler_params=pltpu.CompilerParams(vmem_limit_bytes=57 * 1024 * 1024),
    )(head_pattern, tile_masks, queries, key_rows, value_rows)


def body(queries, key_rows, value_rows, out_weight, tile_masks, head_pattern):
    rows = queries.shape[0]
    q_parts, kv_parts, lists = arrange(head_pattern, tile_masks, queries, key_rows, value_rows)
    kv_all, w_all = spread(
        q_parts.reshape(HEADS_HERE, SLOTS, WORKERS, SPOTS, DH),
        kv_parts.reshape(HEADS_HERE, 2 * TILES, SPOTS, DH),
        out_weight,
    )
    attended = attend(lists, kv_all.reshape(WORKERS, (2 * TILES + SLOTS) * PIECE, DH))
    attn = collect(attended.reshape(SLOTS, WORKERS, SIDE, SPOTS, DH))
    attn = attn.reshape(PLANES * HEADS_HERE, rows, DH)
    return project(attn, w_all, rows)


def solution(mesh):
    placed = (
        P("ctx", "heads"),
        P("ctx", "heads"),
        P("ctx", "heads"),
        P("heads", None),
        P(),
        P("heads"),
    )
    return jax.shard_map(
        body, mesh=mesh, in_specs=placed, out_specs=P("ctx", "heads"), check_vma=False
    )
```

```python
import math

import jax
import jax.numpy as jnp
from jax import lax
from jax.experimental import pallas as pl
from jax.experimental.pallas import tpu as pltpu
from jax.sharding import PartitionSpec as P

MESH = pl.DeviceIdType.MESH
DH = 128
TILE = 128
SPOTS = 4
FRAMES = 32
TILES = 128
PLANES = 4
SIDE = 4
HEADS_HERE = 3
WORKERS = 2 * SIDE
SLOTS = TILES // WORKERS
SIZES = (64, 64, 64, 64)
PARTS = len(SIZES)
PIECE = TILE // WORKERS
GROUP = 8
CHUNK = 32
BESIDE = 8
FAR = 2.0**64
LOW = -1e30
SCALE2 = math.log2(math.e) / math.sqrt(DH)
BF16 = jnp.bfloat16
F32 = jnp.float32


def where_is(device):
    return lax.div(device, WORKERS), lax.rem(lax.div(device, 2), SIDE), lax.rem(device, 2)


def device_at(row, column, core):
    return (lax.rem(row, SIDE) * SIDE + lax.rem(column, SIDE)) * 2 + core


def spread_kernel(
    q_ref, kv_ref, w_ref, kv_all, w_all,
    q_send, q_recv, z_send, z_recv, y_send, y_recv, far_send, far_recv,
    core_send, core_recv, w_send, w_recv, w_core_send, w_core_recv, own_sem,
):
    plane = lax.axis_index("heads")
    me = lax.axis_index("ctx")
    row, column, core = where_is(me)
    working = row < HEADS_HERE
    own_row = jnp.minimum(row, HEADS_HERE - 1)
    depth = w_ref.shape[0]
    width = w_all.shape[1]
    sides = (1, SIDE - 1)

    barrier = pltpu.get_barrier_semaphore()

    def greet(step, carry):
        pl.semaphore_signal(
            barrier, inc=1, device_id=(plane, lax.rem(me + step, FRAMES)), device_id_type=MESH
        )
        return carry

    lax.fori_loop(1, FRAMES, greet, 0)
    for hop in range(1, PLANES):
        pl.semaphore_signal(
            barrier, inc=1, device_id=(lax.rem(plane + hop, PLANES), me), device_id_type=MESH
        )
    pl.semaphore_wait(barrier, FRAMES - 1 + PLANES - 1)

    def span(part):
        return pl.ds(sum(SIZES[:part]), SIZES[part])

    own_copy = pltpu.make_async_copy(
        kv_ref.at[own_row], kv_all.at[column * 2 + core, pl.ds(0, 2 * TILES), 0], own_sem
    )

    def z_copy(part, hop):
        there = lax.rem(row + hop, SIDE)
        return pltpu.make_async_remote_copy(
            src_ref=kv_ref.at[there, span(part)],
            dst_ref=kv_all.at[column * 2 + core, span(part), hop],
            send_sem=z_send.at[part, hop],
            recv_sem=z_recv.at[part, hop],
            device_id=(plane, device_at(there, column, core)),
            device_id_type=MESH,
        )

    def piece(number, away):
        source = kv_all.at[lax.rem(column + away, SIDE) * 2 + core]
        if number == 0:
            return source.at[pl.ds(0, 2 * TILES), 0]
        return source.at[span(number - 1), pl.ds(1, SIDE - 1)]

    def y_copy(number, side):
        return pltpu.make_async_remote_copy(
            src_ref=kv_ref.at[own_row] if number == 0 else piece(number, 0),
            dst_ref=piece(number, 0),
            send_sem=y_send.at[number, side],
            recv_sem=y_recv.at[number, side],
            device_id=(plane, device_at(row, column + sides[side], core)),
            device_id_type=MESH,
        )

    def far_copy(number, side):
        source = kv_all.at[lax.rem(column + sides[1 - side], SIDE) * 2 + core]
        first, count = (0, 2 * TILES) if number == 0 else (sum(SIZES[: number - 1]), SIZES[number - 1])
        share = count // 2
        tiles = pl.ds(first + share, count - share) if side else pl.ds(first, share)
        chunk = source.at[tiles, 0] if number == 0 else source.at[tiles, pl.ds(1, SIDE - 1)]
        return pltpu.make_async_remote_copy(
            src_ref=chunk,
            dst_ref=chunk,
            send_sem=far_send.at[number, side],
            recv_sem=far_recv.at[number, side],
            device_id=(plane, device_at(row, column + sides[side], core)),
            device_id_type=MESH,
        )

    def core_copy(number, away):
        return pltpu.make_async_remote_copy(
            src_ref=piece(number, away),
            dst_ref=piece(number, away),
            send_sem=core_send.at[number, away],
            recv_sem=core_recv,
            device_id=(plane, device_at(row, column, 1 - core)),
            device_id_type=MESH,
        )

    half = depth // 2

    def w_rows(source, part):
        return w_all.at[pl.ds(pl.multiple_of(source * depth + part * half, 16), half)]

    def w_copy(hop):
        there = lax.rem(plane + hop, PLANES)
        return pltpu.make_async_remote_copy(
            src_ref=w_ref.at[
                pl.ds(pl.multiple_of(core * half, 16), half),
                pl.ds(pl.multiple_of(there * width, 128), width),
            ],
            dst_ref=w_rows(plane, core),
            send_sem=w_send.at[hop],
            recv_sem=w_recv.at[hop],
            device_id=(there, me),
            device_id_type=MESH,
        )

    def w_core_copy(hop):
        rows = w_rows(lax.rem(plane + PLANES - hop, PLANES), core)
        return pltpu.make_async_remote_copy(
            src_ref=rows,
            dst_ref=rows,
            send_sem=w_core_send.at[hop],
            recv_sem=w_core_recv.at[hop],
            device_id=(plane, device_at(row, column, 1 - core)),
            device_id_type=MESH,
        )

    own_w = pltpu.make_async_copy(
        w_ref.at[:, pl.ds(pl.multiple_of(plane * width, 128), width)],
        w_all.at[pl.ds(pl.multiple_of(plane * depth, 128), depth)],
        w_recv.at[0],
    )

    queries = kv_all.at[:, pl.ds(2 * TILES, SLOTS)]

    def q_copy(step):
        there = lax.rem(me + step, FRAMES)
        row_there, column_there, core_there = where_is(there)
        return row_there < HEADS_HERE, pltpu.make_async_remote_copy(
            src_ref=q_ref.at[
                jnp.minimum(row_there, HEADS_HERE - 1), :, column_there * 2 + core_there
            ],
            dst_ref=queries.at[column * 2 + core, :, lax.rem(row_there - row + SIDE, SIDE)],
            send_sem=q_send.at[step],
            recv_sem=q_recv,
            device_id=(plane, there),
            device_id_type=MESH,
        )

    def to_rows(part, work):
        for hop in range(1, SIDE):

            @pl.when(lax.rem(row + hop, SIDE) < HEADS_HERE)
            def _():
                work(z_copy(part, hop))

    def send_q(step, carry):
        wanted, copy = q_copy(step)

        @pl.when(wanted)
        def _():
            copy.start()

        return carry

    def sent_q(step, carry):
        wanted, copy = q_copy(step)

        @pl.when(wanted)
        def _():
            copy.wait_send()

        return carry

    def send_small():
        for hop in range(1, PLANES):
            w_copy(hop).start()
        own_w.start()
        lax.fori_loop(1, FRAMES, send_q, 0)

    @pl.when(working)
    def _():
        own_copy.start()
        for side in range(2):
            y_copy(0, side).start()

    to_rows(0, lambda copy: copy.start())
    send_small()

    def next_rows(part):
        to_rows(part, lambda copy: copy.wait_send())
        if part + 1 < PARTS:
            to_rows(part + 1, lambda copy: copy.start())

    @pl.when(jnp.logical_not(working))
    def _():
        for part in range(PARTS):
            next_rows(part)

    @pl.when(working)
    def _():
        pltpu.make_async_copy(
            q_ref.at[own_row, :, column * 2 + core], queries.at[column * 2 + core, :, 0], q_recv
        ).start()
        own_copy.wait()
        core_copy(0, 0).start()

        def pass_on(number):
            for side in range(2):
                y_copy(number, side).wait_recv()
                far_copy(number, side).start()
            for side in range(2):
                core_copy(number, sides[1 - side]).start()

        for part in range(PARTS):
            next_rows(part)
            for hop in range(1, SIDE):
                landed = kv_all.at[column * 2 + core, span(part), hop]
                pltpu.make_async_copy(landed, landed, z_recv.at[part, hop]).wait()
            for side in range(2):
                y_copy(part + 1, side).start()
            core_copy(part + 1, 0).start()
            pass_on(part)
        pass_on(PARTS)
        for number in range(PARTS + 1):
            for side in range(2):
                far_copy(number, side).wait_recv()
            core_copy(number, 2).start()

    for hop in range(1, PLANES):
        w_copy(hop).wait_recv()
        w_core_copy(hop).start()

    @pl.when(working)
    def _():
        pltpu.make_async_copy(queries, queries, q_recv).wait()
        other = kv_all.at[pl.ds(0, SIDE), pl.ds(0, 2 * TILES)]
        pltpu.make_async_copy(other, other, core_recv).wait()
        for number in range(PARTS + 1):
            for side in range(2):
                y_copy(number, side).wait_send()
                far_copy(number, side).wait_send()
            for away in range(SIDE):
                core_copy(number, away).wait_send()

    own_w.wait()
    lax.fori_loop(1, FRAMES, sent_q, 0)
    for hop in range(1, PLANES):
        w_copy(hop).wait_send()
        w_core_copy(hop).wait()


def spread(q_parts, kv_parts, out_weight):
    depth, columns = out_weight.shape
    return pl.pallas_call(
        spread_kernel,
        out_shape=(
            jax.ShapeDtypeStruct((WORKERS, 2 * TILES + SLOTS, SIDE, SPOTS, DH), BF16),
            jax.ShapeDtypeStruct((depth * PLANES, columns // PLANES), BF16),
        ),
        in_specs=[pl.BlockSpec(memory_space=pl.ANY)] * 3,
        out_specs=(pl.BlockSpec(memory_space=pl.ANY),) * 2,
        scratch_shapes=[
            pltpu.SemaphoreType.DMA((FRAMES,)),
            pltpu.SemaphoreType.DMA,
            pltpu.SemaphoreType.DMA((PARTS, SIDE)),
            pltpu.SemaphoreType.DMA((PARTS, SIDE)),
            pltpu.SemaphoreType.DMA((PARTS + 1, 2)),
            pltpu.SemaphoreType.DMA((PARTS + 1, 2)),
            pltpu.SemaphoreType.DMA((PARTS + 1, 2)),
            pltpu.SemaphoreType.DMA((PARTS + 1, 2)),
            pltpu.SemaphoreType.DMA((PARTS + 1, SIDE)),
            pltpu.SemaphoreType.DMA,
            pltpu.SemaphoreType.DMA((PLANES,)),
            pltpu.SemaphoreType.DMA((PLANES,)),
            pltpu.SemaphoreType.DMA((PLANES,)),
            pltpu.SemaphoreType.DMA((PLANES,)),
            pltpu.SemaphoreType.DMA,
        ],
        compiler_params=pltpu.CompilerParams(
            collective_id=0, has_side_effects=True, vmem_limit_bytes=57 * 1024 * 1024
        ),
    )(q_parts, kv_parts, out_weight)


def turned_rows(rows):
    to = lax.broadcasted_iota(jnp.int32, (rows, rows), 0)
    source = lax.broadcasted_iota(jnp.int32, (rows, rows), 1)
    group = WORKERS * SPOTS
    place = lax.div(lax.rem(to, group), SPOTS)
    wanted = to + (WORKERS - 1 - 2 * place) * SPOTS
    return jnp.where(source == wanted, 1.0, 0.0).astype(BF16)


def attend_kernel(
    list_ref, kv_hbm, o_ref, kv_ref, q_ref, keys_ref, base_ref, peak_ref, sum_ref,
    slot_of, first_of, listed_of, kv_sem,
):
    def bring(number, first, tiles):
        rows = pl.ds(first * PIECE, tiles * PIECE)
        return pltpu.make_async_copy(kv_hbm.at[:, rows], kv_ref.at[:, rows], kv_sem.at[number])

    chunks = TILES // CHUNK
    moves = [bring(number, number * CHUNK, CHUNK) for number in range(chunks)]
    moves.append(bring(chunks, 2 * TILES, SLOTS))
    moves.append(bring(chunks + 1, TILES, TILES))
    for move in moves:
        move.start()

    _, column, core = where_is(lax.axis_index("ctx"))

    def loop(count, work):
        def one(step, carry):
            work(step)
            return carry

        lax.fori_loop(0, count, one, 0)

    def rows_of(slot):
        return pl.ds(pl.multiple_of(slot * TILE, TILE), TILE)

    def tile_at(tile):
        start = pl.multiple_of(tile * PIECE, PIECE)
        return jnp.concatenate(
            [kv_ref[worker, pl.ds(start, PIECE), :] for worker in range(WORKERS)], axis=0
        )

    def enlist(slot, total):
        count = list_ref[SLOTS, slot]
        steps = lax.div(count + GROUP - 1, GROUP)

        def one(step, carry):
            slot_of[total + step] = slot
            first_of[total + step] = step * GROUP
            listed_of[total + step] = count - step * GROUP
            return carry

        lax.fori_loop(0, steps, one, 0)
        return total + steps

    total = lax.fori_loop(0, SLOTS, enlist, 0)
    for spare in range(BESIDE - 1):
        slot_of[total + spare] = 0
        first_of[total + spare] = 0
        listed_of[total + spare] = 0
    turns = lax.div(total + BESIDE - 1, BESIDE)
    busy = jnp.where(total > 0, 1, 0)

    def unpack(step):
        for u in range(GROUP):
            tile = step * GROUP + u
            keys_ref[tile] = tile_at(tile).T

    for number in range(chunks):
        moves[number].wait()
        steps = CHUNK // GROUP
        loop(busy * steps, lambda step: unpack(step + number * steps))
    moves[chunks].wait()

    def set_base(slot, base):
        base_ref[slot] = jnp.broadcast_to(base * SCALE2, (TILE, TILE))

    def own_base(step):
        for u in range(BESIDE):
            slot = step * BESIDE + u
            place = column * 2 + core
            late = jnp.where(slot < SLOTS // 2, 0, WORKERS - 1 - 2 * place)
            own = keys_ref[slot * WORKERS + place + late]
            query = tile_at(2 * TILES + slot)
            q_ref[rows_of(slot), :] = query
            scores = jnp.dot(query, own, preferred_element_type=F32)
            set_base(slot, jnp.max(scores, axis=1, keepdims=True))

    loop(busy * (SLOTS // BESIDE), own_base)
    moves[chunks + 1].wait()

    def tiles_of(number):
        slot, first = slot_of[number], first_of[number]
        return slot, [list_ref[slot, first + u] for u in range(GROUP)]

    def scores_of(slot, tiles):
        keys = jnp.concatenate([keys_ref[tile] for tile in tiles], axis=1)
        return jnp.dot(q_ref[rows_of(slot), :], keys, preferred_element_type=F32)

    def attend_steps(step):
        found = []
        for beside in range(BESIDE):
            number = step * BESIDE + beside
            slot, tiles = tiles_of(number)
            listed = listed_of[number]
            base = base_ref[slot]
            scores = scores_of(slot, tiles)
            weights, values = [], []
            for u in range(GROUP):
                part = scores[:, u * TILE : (u + 1) * TILE]
                weights.append(jnp.exp2(part * SCALE2 - base).astype(BF16))
                value = jnp.where(u < listed, tile_at(TILES + tiles[u]), 0).astype(BF16)
                ones = jnp.where(u < listed, 1.0, 0.0).astype(BF16)
                ones = jnp.broadcast_to(ones, (TILE, DH))
                values.append(jnp.concatenate([value, ones], axis=1))
            added = jnp.dot(
                jnp.concatenate(weights, axis=1),
                jnp.concatenate(values, axis=0),
                preferred_element_type=F32,
            )
            found.append((slot, added))
        for slot, added in found:
            sum_ref[slot] += added

    def peak_steps(step):
        for beside in range(BESIDE):
            slot, tiles = tiles_of(step * BESIDE + beside)
            scores = scores_of(slot, tiles)
            peak = peak_ref[slot]
            for u in range(GROUP):
                peak = jnp.maximum(peak, scores[:, u * TILE : (u + 1) * TILE])
            peak_ref[slot] = peak

    def attempt(number, needed):
        def clear(slot):
            sum_ref[slot] = jnp.zeros((TILE, 2 * DH), F32)
            peak_ref[slot] = jnp.full((TILE, TILE), LOW, F32)

        loop(needed * SLOTS, clear)
        loop(needed * turns, attend_steps)
        beyond = jnp.zeros((TILE, DH), F32)
        for slot in range(SLOTS):
            beyond = jnp.where(sum_ref[slot, :, DH:] <= FAR, beyond, 1.0)
        again = needed * jnp.where(jnp.max(beyond) > 0.0, 1, 0)
        loop(again * turns, peak_steps)

        def rebase(slot):
            set_base(slot, jnp.max(peak_ref[slot], axis=1, keepdims=True))

        loop(again * SLOTS, rebase)
        return again

    lax.fori_loop(0, 2, attempt, busy)

    def finish(step):
        for u in range(BESIDE):
            slot = step * BESIDE + u
            o_ref[rows_of(slot), :] = (sum_ref[slot, :, :DH] / sum_ref[slot, :, DH:]).astype(BF16)

    loop(busy * (SLOTS // BESIDE), finish)


def attend(lists, kv):
    most = SLOTS * (TILES // GROUP) + BESIDE
    return pl.pallas_call(
        attend_kernel,
        out_shape=jax.ShapeDtypeStruct((SLOTS * TILE, DH), BF16),
        in_specs=[pl.BlockSpec(memory_space=pltpu.SMEM), pl.BlockSpec(memory_space=pl.ANY)],
        out_specs=pl.BlockSpec(memory_space=pltpu.VMEM),
        scratch_shapes=[
            pltpu.VMEM(kv.shape, BF16),
            pltpu.VMEM((SLOTS * TILE, DH), BF16),
            pltpu.VMEM((TILES, DH, TILE), BF16),
            pltpu.VMEM((SLOTS, TILE, TILE), F32),
            pltpu.VMEM((SLOTS, TILE, TILE), F32),
            pltpu.VMEM((SLOTS, TILE, 2 * DH), F32),
            pltpu.SMEM((most,), jnp.int32),
            pltpu.SMEM((most,), jnp.int32),
            pltpu.SMEM((most,), jnp.int32),
            pltpu.SemaphoreType.DMA((TILES // CHUNK + 2,)),
        ],
        compiler_params=pltpu.CompilerParams(vmem_limit_bytes=50 * 1024 * 1024),
    )(lists, kv)


def collect_kernel(o_ref, attn, send, recv, x_send, x_recv):
    plane = lax.axis_index("heads")
    me = lax.axis_index("ctx")
    row, column, core = where_is(me)
    barrier = pltpu.get_barrier_semaphore()

    def greet(step, carry):
        pl.semaphore_signal(
            barrier, inc=1, device_id=(plane, lax.rem(me + step, FRAMES)), device_id_type=MESH
        )
        return carry

    lax.fori_loop(1, FRAMES, greet, 0)
    sides = (lax.rem(plane + 1, PLANES), lax.rem(plane + PLANES - 1, PLANES))
    for there in sides:
        pl.semaphore_signal(barrier, inc=1, device_id=(there, me), device_id_type=MESH)
    pl.semaphore_wait(barrier, FRAMES - 1 + 2)

    mine = jnp.minimum(row, HEADS_HERE - 1)
    goal = attn.at[plane * HEADS_HERE + mine, :, column * 2 + core]

    def rows_for(there):
        row_there, column_there, core_there = where_is(there)
        above = lax.rem(row - row_there + SIDE, SIDE)
        return o_ref.at[:, column_there * 2 + core_there, above]

    def back(step):
        there = lax.rem(me + step, FRAMES)
        return pltpu.make_async_remote_copy(
            src_ref=rows_for(there),
            dst_ref=goal,
            send_sem=send.at[step],
            recv_sem=recv.at[mine],
            device_id=(plane, there),
            device_id_type=MESH,
        )

    def start(step, carry):
        back(step).start()
        return carry

    def end(step, carry):
        back(step).wait_send()
        return carry

    working = row < HEADS_HERE

    @pl.when(working)
    def _():
        lax.fori_loop(1, FRAMES, start, 0)
        pltpu.make_async_copy(rows_for(me), goal, recv.at[mine]).start()

    cut = SLOTS // 2

    def near(head, side):
        part = attn.at[plane * HEADS_HERE + head]
        return pltpu.make_async_remote_copy(
            src_ref=part,
            dst_ref=part,
            send_sem=x_send.at[head, side],
            recv_sem=x_recv.at[head, side],
            device_id=(sides[side], me),
            device_id_type=MESH,
        )

    def far(head, side):
        part = attn.at[sides[1 - side] * HEADS_HERE + head]
        part = part.at[pl.ds(0, cut)] if side == 0 else part.at[pl.ds(cut, SLOTS - cut)]
        return pltpu.make_async_remote_copy(
            src_ref=part,
            dst_ref=part,
            send_sem=x_send.at[head, 2 + side],
            recv_sem=x_recv.at[head, 2 + side],
            device_id=(sides[side], me),
            device_id_type=MESH,
        )

    for head in range(HEADS_HERE):
        part = attn.at[plane * HEADS_HERE + head]
        pltpu.make_async_copy(part, part, recv.at[head]).wait()
        for side in range(2):
            near(head, side).start()
    for head in range(HEADS_HERE):
        for side in range(2):
            near(head, side).wait_recv()
            far(head, side).start()

    @pl.when(working)
    def _():
        lax.fori_loop(1, FRAMES, end, 0)

    for head in range(HEADS_HERE):
        for side in range(2):
            near(head, side).wait_send()
            far(head, side).wait()


def collect(attended):
    return pl.pallas_call(
        collect_kernel,
        out_shape=jax.ShapeDtypeStruct(
            (PLANES * HEADS_HERE, SLOTS, WORKERS, SPOTS, DH), BF16
        ),
        in_specs=[pl.BlockSpec(memory_space=pl.ANY)],
        out_specs=pl.BlockSpec(memory_space=pl.ANY),
        scratch_shapes=[
            pltpu.SemaphoreType.DMA((FRAMES,)),
            pltpu.SemaphoreType.DMA((HEADS_HERE,)),
            pltpu.SemaphoreType.DMA((HEADS_HERE, 4)),
            pltpu.SemaphoreType.DMA((HEADS_HERE, 4)),
        ],
        compiler_params=pltpu.CompilerParams(
            collective_id=1, has_side_effects=True, vmem_limit_bytes=4 * 1024 * 1024
        ),
    )(attended)


def project_kernel(attn_ref, w_ref, out_ref):
    heads = attn_ref.shape[0]
    half = out_ref.shape[0] // 2
    wide = jnp.concatenate([attn_ref[h] for h in range(heads)], axis=1)
    block = 256
    for first in range(0, out_ref.shape[1], block):
        columns = slice(first, first + block)
        mixed = jnp.dot(wide, w_ref[:, columns], preferred_element_type=F32)
        out_ref[:half, columns] = mixed[:half].astype(BF16)
        group, pair = WORKERS * SPOTS, 2 * SPOTS
        blocks = []
        for start in range(half, 2 * half, group):
            for last in range(start + group, start, -pair):
                blocks.append(pltpu.roll(mixed[last - pair : last], SPOTS, 0))
        out_ref[half:, columns] = jnp.concatenate(blocks, axis=0).astype(BF16)


def project(attn, weight, rows):
    return pl.pallas_call(
        project_kernel,
        out_shape=jax.ShapeDtypeStruct((rows, weight.shape[1]), BF16),
        in_specs=[pl.BlockSpec(memory_space=pltpu.VMEM)] * 2,
        out_specs=pl.BlockSpec(memory_space=pltpu.VMEM),
        compiler_params=pltpu.CompilerParams(vmem_limit_bytes=24 * 1024 * 1024),
    )(attn, weight)


def arrange_kernel(
    pattern_ref, mask_hbm, q_hbm, k_hbm, v_hbm, q_out, kv_out, list_ref,
    mask_ref, q_ref, k_ref, v_ref, sems,
):
    sources = (mask_hbm, q_hbm, k_hbm, v_hbm)
    targets = (mask_ref, q_ref, k_ref, v_ref)
    moves = [
        pltpu.make_async_copy(source, target, sems.at[i])
        for i, (source, target) in enumerate(zip(sources, targets))
    ]
    for move in moves:
        move.start()
    me = lax.axis_index("ctx")
    row, column, core = where_is(me)
    moves[0].wait()
    pattern = pattern_ref[jnp.minimum(row, HEADS_HERE - 1)]
    masks = []
    place = column * 2 + core
    tiles = [
        slot * WORKERS + (place if slot < SLOTS // 2 else WORKERS - 1 - place)
        for slot in range(SLOTS)
    ]
    for tile in tiles:
        masks.append(jnp.where(row < HEADS_HERE, mask_ref[pattern, pl.ds(tile, 1), :], 0))
    seen = jnp.concatenate(masks, axis=0) == 1
    seen = jnp.where(seen, 1.0, 0.0).astype(F32)
    down = lax.broadcasted_iota(jnp.int32, (TILES, TILES), 0)
    along = lax.broadcasted_iota(jnp.int32, (TILES, TILES), 1)
    both = (((1,), (1,)), ((), ()))
    upto = jnp.where(along <= down, 1.0, 0.0).astype(BF16)
    same = jnp.where(along == down, 1.0, 0.0).astype(BF16)
    rank = lax.dot_general(upto, seen.astype(BF16), both, preferred_element_type=F32)
    turned = lax.dot_general(same, seen.astype(BF16), both, preferred_element_type=F32)
    rank = rank.astype(jnp.int32)
    spot = jnp.where(turned > 0.5, rank - 1, -1)
    for slot in range(SLOTS):
        hit = spot[:, slot : slot + 1] == along
        listed = jnp.sum(jnp.where(hit, down, 0), axis=0, keepdims=True)
        spare = along[:1, :] >= rank[TILES - 1 :, slot : slot + 1]
        list_ref[slot : slot + 1, :] = jnp.where(spare, tiles[slot], listed)
    last = jnp.concatenate(
        [rank[TILES - 1 :, :], jnp.zeros((1, TILES - SLOTS), jnp.int32)], axis=1
    )
    list_ref[SLOTS : SLOTS + 1, :] = last


    rows = q_ref.shape[0]
    for move, source, target, first in (
        (moves[1], q_ref, q_out, 0),
        (moves[2], k_ref, kv_out, 0),
        (moves[3], v_ref, kv_out, rows),
    ):
        move.wait()
        for head in range(HEADS_HERE):
            target[head, first : first + rows, :] = source[:, head * DH : (head + 1) * DH]
    half = rows // 2
    later = jnp.dot(turned_rows(half), q_ref[half:, :], preferred_element_type=F32).astype(BF16)
    for head in range(HEADS_HERE):
        q_out[head, half:, :] = later[:, head * DH : (head + 1) * DH]


def arrange(head_pattern, tile_masks, queries, key_rows, value_rows):
    rows = queries.shape[0]
    return pl.pallas_call(
        arrange_kernel,
        out_shape=(
            jax.ShapeDtypeStruct((HEADS_HERE, rows, DH), BF16),
            jax.ShapeDtypeStruct((HEADS_HERE, 2 * rows, DH), BF16),
            jax.ShapeDtypeStruct((SLOTS + 1, TILES), jnp.int32),
        ),
        in_specs=[pl.BlockSpec(memory_space=pltpu.SMEM)]
        + [pl.BlockSpec(memory_space=pl.ANY)] * 4,
        out_specs=(pl.BlockSpec(memory_space=pltpu.VMEM),) * 3,
        scratch_shapes=[
            pltpu.VMEM(tile_masks.shape, jnp.int32),
            pltpu.VMEM(queries.shape, BF16),
            pltpu.VMEM(queries.shape, BF16),
            pltpu.VMEM(queries.shape, BF16),
            pltpu.SemaphoreType.DMA((4,)),
        ],
        compiler_params=pltpu.CompilerParams(vmem_limit_bytes=57 * 1024 * 1024),
    )(head_pattern, tile_masks, queries, key_rows, value_rows)


def body(queries, key_rows, value_rows, out_weight, tile_masks, head_pattern):
    rows = queries.shape[0]
    q_parts, kv_parts, lists = arrange(head_pattern, tile_masks, queries, key_rows, value_rows)
    kv_all, w_all = spread(
        q_parts.reshape(HEADS_HERE, SLOTS, WORKERS, SPOTS, DH),
        kv_parts.reshape(HEADS_HERE, 2 * TILES, SPOTS, DH),
        out_weight,
    )
    attended = attend(lists, kv_all.reshape(WORKERS, (2 * TILES + SLOTS) * PIECE, DH))
    attn = collect(attended.reshape(SLOTS, WORKERS, SIDE, SPOTS, DH))
    attn = attn.reshape(PLANES * HEADS_HERE, rows, DH)
    return project(attn, w_all, rows)


def solution(mesh):
    placed = (
        P("ctx", "heads"),
        P("ctx", "heads"),
        P("ctx", "heads"),
        P("heads", None),
        P(),
        P("heads"),
    )
    return jax.shard_map(
        body, mesh=mesh, in_specs=placed, out_specs=P("ctx", "heads"), check_vma=False
    )
```
